32 devices in a mesh: dp: 8 (over y, x, core), chan: 4 (over z).
Axes of the slice: x: 2, y: 2, z: 4, core: 2. Of those that a mesh axis runs over, the one named last changes fastest.
Arguments:
- spectra: bfloat16 [16, 256, 3072], P('dp', 'chan'), may hold values from -6 to 6
- lengths: int32 [16], P('dp'), may hold values from 25 to 384, as said below
- weight_in: bfloat16 [9, 512, 256], P(None, 'chan'), may hold values from -0.125 to 0.125
- gamma_in: float32 [512], P('chan'), may hold values from 0.5 to 2
- beta_in: float32 [512], P('chan'), may hold values from -2 to 2
- weight_mid: bfloat16 [9, 512, 512], P(None, 'chan'), may hold values from -0.09375 to 0.09375
- gamma_mid: float32 [512], P('chan'), may hold values from 0.5 to 2
- beta_mid: float32 [512], P('chan'), may hold values from -2 to 2
- cotangent: bfloat16 [16, 512, 768], P('dp', 'chan'), may hold values from -6 to 6
Outputs:
- block_out: bfloat16 [16, 512, 768], P('dp', 'chan')
- spectra_grad: float32 [16, 256, 3072], P('dp', 'chan')
- weight_in_grad: float32 [9, 512, 256], P(None, 'chan')
- gamma_in_grad: float32 [512], P('chan')
- beta_in_grad: float32 [512], P('chan')
- weight_mid_grad: float32 [9, 512, 512], P(None, 'chan')
- gamma_mid_grad: float32 [512], P('chan')
- beta_mid_grad: float32 [512], P('chan')
- root_squares: float32 [4], replicated
The draws below stay inside these ranges and needn't reach their ends.
Inputs may be any that keep to these rules, and one draw needn't show every extreme that they name: `lengths`: some clip has exactly 384 valid frames.
All inputs are finite; a program needn't handle non-finite values.
Results may differ from the reference program's by a relative error of at most 0.014.
Values may be sent and summed in bfloat16 or wider, within the bound.
No kernel may reach another device: no remote copies, remote signals or barrier semaphores. Data moves between devices by JAX's collectives and lax.ppermute only.
A program may use at most 256 MiB of HBM per device.

```python
import math
import jax
import jax.numpy as jnp
from jax import lax

C_IN = 256
C_MID = 512
MEL = 8
FRAMES = 384
SHORTEST = 25
CLIPS_DEV = 2
CLIPS = 16


def draw_lengths(key, part):
    key = jax.random.fold_in(key, 11)
    first_key = jax.random.fold_in(key, 1)
    second_key = jax.random.fold_in(key, 2)
    indices = jnp.arange(CLIPS, dtype=jnp.int32)
    spread = FRAMES - SHORTEST
    low_end = SHORTEST + spread * 2 * indices // (3 * CLIPS)
    picked = jax.random.randint(first_key, (CLIPS,), 0, spread // 3 + 1, dtype=jnp.int32)
    drawn = jnp.minimum(low_end + picked, FRAMES)
    longest = jax.random.randint(second_key, (), CLIPS - CLIPS_DEV, CLIPS, dtype=jnp.int32)
    return jnp.where(indices == longest, FRAMES, drawn).astype(jnp.int32)


def shard_levels(rng, dims, split, least, top_value):
    def one(position, parts):
        steps = jax.random.uniform(jax.random.fold_in(jax.random.fold_in(rng, 6), position), (parts,), jnp.float32, least / len(split), top_value / len(split))
        return jnp.repeat(jnp.exp(steps), dims[position] // parts).reshape((-1,) + (1,) * (len(dims) - position - 1))

    loudness = one(*split[0])
    for cut in split[1:]:
        loudness = loudness * one(*cut)
    return loudness


def gaussian(own_key, shape, scale, bound, split=(), kind=jnp.bfloat16):
    array = scale * jax.random.normal(own_key, shape, jnp.float32)
    if split:
        array = array * shard_levels(own_key, shape, split, -0.22, 0.18)
    return jnp.clip(array, -bound, bound).astype(kind)


def setup_inputs(seed: int = 0) -> dict:
    seeds = jax.random.split(jax.random.key(seed), 10)
    return {
        "spectra": gaussian(seeds[0], (CLIPS, C_IN, FRAMES * MEL), 1.0, 6.0, ((0, 8), (1, 4))),
        "lengths": draw_lengths(jax.random.fold_in(seeds[9], 71), 0),
        "weight_in": gaussian(seeds[2], (9, C_MID, C_IN), (9 * C_IN) ** -0.5, 0.125, ((1, 4),)),
        "gamma_in": jnp.clip(jnp.exp(math.log(2.0) - 1.3862944 * jax.random.uniform(seeds[3], (C_MID,), jnp.float32) ** shard_levels(seeds[3], (C_MID,), ((0, 4),), -0.2, 0.2)), 0.5, 2.0),
        "beta_in": gaussian(seeds[4], (C_MID,), 0.5, 2.0, ((0, 4),), jnp.float32),
        "weight_mid": gaussian(seeds[5], (9, C_MID, C_MID), (9 * C_MID) ** -0.5, 0.09375, ((1, 4),)),
        "gamma_mid": jnp.clip(jnp.exp(math.log(2.0) - 1.3862944 * jax.random.uniform(seeds[6], (C_MID,), jnp.float32) ** shard_levels(seeds[6], (C_MID,), ((0, 4),), -0.2, 0.2)), 0.5, 2.0),
        "beta_mid": gaussian(seeds[7], (C_MID,), 0.5, 2.0, ((0, 4),), jnp.float32),
        "cotangent": gaussian(seeds[8], (CLIPS, C_MID, FRAMES * MEL // 4), 1.0, 6.0, ((0, 8), (1, 4))),
    }


@jax.custom_vjp
def low(v):
    return lax.optimization_barrier(v.astype(jnp.bfloat16)).astype(jnp.float32)

@jax.custom_vjp
def low_back(v):
    return v

def low_keep(v):
    return (low(v), None)

def low_pass(kept, grad):
    return (grad,)

def back_keep(v):
    return (v, None)

def back_low(kept, grad):
    return (low(grad),)
low.defvjp(low_keep, low_pass)
low_back.defvjp(back_keep, back_low)

def conv_taps(field, weight):
    kernel = jnp.transpose(weight.reshape(3, 3, weight.shape[1], weight.shape[2]), (2, 3, 0, 1))
    return lax.conv_general_dilated(field, kernel, (1, 1), ((1, 1), (1, 1)), dimension_numbers=('NCHW', 'OIHW', 'NCHW'), precision=lax.Precision.HIGHEST)

def normalize(pre, mask, count, gamma, beta):
    mean = lax.optimization_barrier(jnp.sum(pre * mask, axis=(0, 2, 3))) / count
    second = lax.optimization_barrier(jnp.sum(pre * pre * mask, axis=(0, 2, 3))) / count
    inverse = lax.rsqrt(second - mean * mean + 1e-05)
    scaled = (pre - mean[None, :, None, None]) * inverse[None, :, None, None]
    affine = gamma[None, :, None, None] * scaled + beta[None, :, None, None]
    return jax.nn.silu(affine) * mask

def reference(spectra, lengths, weight_in, gamma_in, beta_in, weight_mid, gamma_mid, beta_mid, cotangent):
    clips = spectra.shape[0]
    frames = jnp.arange(FRAMES, dtype=jnp.int32)
    mask = (frames[None, :] < lengths[:, None]).astype(jnp.float32)[:, None, :, None]
    starts = 2 * jnp.arange(FRAMES // 2, dtype=jnp.int32)
    inside = jnp.clip(lengths[:, None] - starts[None, :], 0, 2)
    divisor = (2.0 * jnp.maximum(inside, 1).astype(jnp.float32))[:, None, :, None]
    count = MEL * jnp.sum(lengths).astype(jnp.float32)
    pooled_count = MEL // 2 * jnp.sum((lengths + 1) // 2).astype(jnp.float32)
    field = spectra.astype(jnp.float32).reshape(clips, C_IN, FRAMES, MEL)

    def forward(field, weight_in, gamma_in, beta_in, weight_mid, gamma_mid, beta_mid):
        masked = field * mask
        first_pre = low_back(conv_taps(masked, weight_in))
        first_act = normalize(first_pre, mask, count, gamma_in, beta_in)
        second_pre = low_back(conv_taps(low(first_act), weight_mid))
        second_act = normalize(second_pre, mask, count, gamma_mid, beta_mid)
        pooled = second_act.reshape(clips, C_MID, FRAMES // 2, 2, MEL // 2, 2).sum(axis=(3, 5)) / divisor
        totals = jnp.stack([jnp.sum(masked * masked), jnp.sum(first_act * first_act), jnp.sum(second_act * second_act), jnp.sum(pooled * pooled)])
        return (pooled, totals)
    pooled, pullback, totals = jax.vjp(forward, field, weight_in.astype(jnp.float32), gamma_in, beta_in, weight_mid.astype(jnp.float32), gamma_mid, beta_mid, has_aux=True)
    grads = pullback(cotangent.astype(jnp.float32).reshape(clips, C_MID, FRAMES // 2, MEL // 2))
    denominators = jnp.stack([count * C_IN, count * C_MID, count * C_MID, pooled_count * C_MID])
    root_squares = jnp.sqrt(totals / denominators)
    block_out = pooled.reshape(clips, C_MID, -1).astype(jnp.bfloat16)
    spectra_grad = grads[0].reshape(clips, C_IN, FRAMES * MEL)
    return (block_out, spectra_grad, grads[1], grads[2], grads[3], grads[4], grads[5], grads[6], root_squares)
```

```python
import functools

import jax
import jax.numpy as jnp
from jax import lax
from jax.experimental import pallas as pl
from jax.experimental.pallas import tpu as pltpu
from jax.sharding import PartitionSpec as P

MEL = 8
HALO = 16
BF = jnp.bfloat16
F32 = jnp.float32
MIB = 1024 * 1024


class Geometry:
    def __init__(self, ndp, nch, clips, frames, c_in, c_mid):
        self.ndp, self.nch, self.ndev = ndp, nch, ndp * nch
        self.clips, self.frames = clips, frames
        self.ci_all, self.cm = c_in, c_mid
        self.ci, self.co = c_in // nch, c_mid // nch
        self.segs = nch // clips
        self.seg = frames // self.segs
        sides = min(self.segs - 1, 2)
        self.win = self.seg + HALO * sides
        self.starts = [
            min(max(s * self.seg - HALO, 0), frames - self.win) for s in range(self.segs)
        ]
        self.cwin = min(frames, (self.win + 48 + 63) // 64 * 64)
        self.cstarts = [min(s // 64 * 64, frames - self.cwin) for s in self.starts]
        self.rows = max(16, self.co // ndp)
        self.pieces = self.co // self.rows
        self.planes = self.pieces // 2


def dot(a, b, contract):
    return lax.dot_general(a, b, ((contract[0], contract[1]), ((), ())), preferred_element_type=F32)


def params(limit=56):
    return pltpu.CompilerParams(vmem_limit_bytes=limit * MIB)


def cost(flops, nbytes):
    return pl.CostEstimate(flops=int(flops), bytes_accessed=int(nbytes), transcendentals=0)


VMEM = pl.BlockSpec(memory_space=pltpu.VMEM)
SMEM = pl.BlockSpec(memory_space=pltpu.SMEM)
ANY = pl.BlockSpec(memory_space=pl.ANY)

LENGTH, START, OFF, QOFF, ZED, DEE = range(6)


def row_masks(g, info):
    r = lax.broadcasted_iota(jnp.int32, (g.win, 1), 0)
    valid = (r + info[START]) < info[LENGTH]
    own = valid & (r >= info[OFF]) & (r < info[OFF] + g.seg)
    return valid.astype(F32), own.astype(F32)


def shifted(x):
    n = x.shape[0]
    r = lax.broadcasted_iota(jnp.int32, (n, 1), 0)
    before = jnp.where(r == 0, 0.0, pltpu.roll(x, 1, 0))
    after = jnp.where(r == n - 1, 0.0, pltpu.roll(x, n - 1, 0))
    return before, after


def grid_order(rows=16):
    n = MEL * rows
    r = lax.broadcasted_iota(jnp.int32, (n, n), 0)
    c = lax.broadcasted_iota(jnp.int32, (n, n), 1)
    return (c == (r % rows) * MEL + r // rows).astype(BF)


def lanes(vector):
    n = vector.shape[1] // 128
    return jnp.concatenate([vector[:, 128 * i : 128 * (i + 1)] for i in range(n)], axis=0)


def unlanes(rows):
    return jnp.concatenate([rows[i : i + 1] for i in range(rows.shape[0])], axis=1)


def misc_row(*scalars):
    lane = lax.broadcasted_iota(jnp.int32, (1, 128), 1)
    row = jnp.zeros((1, 128), F32)
    for i, s in enumerate(scalars):
        row = jnp.where(lane == i, s, row)
    return row


def pick(row, i):
    lane = lax.broadcasted_iota(jnp.int32, (1, 128), 1)
    return jnp.sum(jnp.where(lane == i, row, 0.0), axis=1, keepdims=True)


def send_payload(ref, first, second, *extra):
    rows = [lanes(first), lanes(second), *extra]
    have = sum(r.shape[0] for r in rows)
    total = ref.shape[1]
    if have < total:
        rows.append(jnp.zeros((total - have, 128), F32))
    block = jnp.concatenate(rows, axis=0)
    ref[...] = jnp.broadcast_to(block[None], ref.shape)


def total_of(g, ref):
    n = g.cm // 128
    block = jnp.sum(ref[:, : 2 * n, :], axis=0)
    return unlanes(block[:n]), unlanes(block[n:])


def misc_of(g, ref):
    n = 2 * (g.cm // 128)
    return jnp.sum(ref[:, n, :], axis=0, keepdims=True)


def cut_kernel(g, info, spec, cot, w_in, w_mid, *rest):
    n = g.nch
    xs, cs, wi, wm, sems = rest[:n], rest[n : 2 * n], rest[2 * n], rest[2 * n + 1], rest[2 * n + 2]
    copies = []

    def add(src, dst):
        c = pltpu.make_async_copy(src, dst, sems.at[len(copies)])
        c.start()
        copies.append(c)

    piece = lax.rem(info[DEE], g.pieces)
    rows = pl.ds(pl.multiple_of(piece * g.rows, 16), g.rows)
    add(w_in.at[:, rows, :], wi)
    add(w_mid.at[:, rows, :], wm)
    for k in range(n):
        to = lax.rem(info[ZED] + k, n)
        clip, seg = to // g.segs, lax.rem(to, g.segs)
        start = jnp.clip(seg * g.seg - HALO, 0, g.frames - g.win)
        cstart = jnp.minimum(start // 64 * 64, g.frames - g.cwin)
        add(spec.at[clip, :, pl.ds(pl.multiple_of(start * MEL, 128), g.win * MEL)], xs[k])
        add(cot.at[clip, :, pl.ds(pl.multiple_of(cstart * 2, 128), g.cwin * 2)], cs[k])
    for c in copies:
        c.wait()


def cut(g, info, spec, cot, w_in, w_mid):
    n = g.nch
    shapes = (
        [jax.ShapeDtypeStruct((g.ci, g.win * MEL), BF)] * n
        + [jax.ShapeDtypeStruct((g.co, g.cwin * 2), BF)] * n
        + [
            jax.ShapeDtypeStruct((9, g.rows, g.ci_all), BF),
            jax.ShapeDtypeStruct((9, g.rows, g.cm), BF),
        ]
    )
    out = pl.pallas_call(
        functools.partial(cut_kernel, g),
        out_shape=shapes,
        in_specs=[SMEM] + [ANY] * 4,
        out_specs=[ANY] * len(shapes),
        scratch_shapes=[pltpu.SemaphoreType.DMA((2 * n + 2,))],
        compiler_params=params(8),
        name="cut",
    )(info, spec, cot, w_in, w_mid)
    return out[:n], out[n : 2 * n], out[2 * n], out[2 * n + 1]


def join_kernel(g, info, own, *rest):
    parts, out = rest[:-1], rest[-1]
    z = info[ZED]
    out[:, pl.ds(pl.multiple_of(z * g.co, 16), g.co), :] = own[...]
    for q in range(g.pieces):
        piece = lax.rem(info[DEE], g.pieces) ^ q
        for k in range(1, g.nch):
            source = lax.rem(z + g.nch - k, g.nch)
            at = pl.multiple_of(source * g.co + piece * g.rows, 16)
            out[:, pl.ds(at, g.rows), :] = parts[q][k - 1]


def join(g, info, own, parts, depth, name):
    return pl.pallas_call(
        functools.partial(join_kernel, g),
        out_shape=jax.ShapeDtypeStruct((9, g.cm, depth), BF),
        in_specs=[SMEM] + [VMEM] * (1 + len(parts)),
        out_specs=VMEM,
        compiler_params=params(24),
        cost_estimate=cost(0, 4 * 9 * g.cm * depth),
        name=name,
    )(info, own, *parts)


def conv_rows(m, x3, weight):
    total = None
    for b in range(3):
        if 0 <= m + b - 1 < MEL:
            term = dot(x3[m + b - 1], weight(b), ((1,), (1,)))
            total = term if total is None else total + term
    return total


def conv_back_rows(m, g3, weight):
    total = None
    for b in range(3):
        if 0 <= m - b + 1 < MEL:
            term = dot(g3[m - b + 1], weight(b), ((1,), (0,)))
            total = term if total is None else total + term
    return total


def side_by_side(ref):
    return lambda b: jnp.concatenate([ref[b], ref[3 + b], ref[6 + b]], axis=1)


def stacked(ref):
    return lambda b: jnp.concatenate([ref[b], ref[3 + b], ref[6 + b]], axis=0)


def first_kernel(g, info, lens, gains, *rest):
    n = g.nch
    xs, w, pre, x3, pay, held = rest[:n], rest[n], rest[n + 1], rest[n + 2], rest[n + 3], rest[n + 4]
    c = g.ci_all
    for k in range(n):
        source = lax.rem(info[ZED] + n - k, n)
        held[pl.ds(pl.multiple_of(source * g.ci, 16), g.ci), :] = xs[k][...]
    valid, own = row_masks(g, info)
    order = grid_order()
    square = jnp.zeros((1, c), F32)
    for j in range(g.win // 16):
        block = dot(order, held[:, 128 * j : 128 * (j + 1)], ((1,), (1,)))
        v = valid[16 * j : 16 * (j + 1)]
        o = own[16 * j : 16 * (j + 1)]
        for m in range(MEL):
            part = block[16 * m : 16 * (m + 1)] * v
            square = square + jnp.sum(part * part * o, axis=0, keepdims=True)
            x3[m, 16 * j : 16 * (j + 1), c : 2 * c] = part.astype(BF)
    for m in range(MEL):
        before, after = shifted(x3[m, :, c : 2 * c].astype(F32))
        x3[m, :, 0:c] = before.astype(BF)
        x3[m, :, 2 * c : 3 * c] = after.astype(BF)
    one = jnp.zeros((1, g.cm), F32)
    two = jnp.zeros((1, g.cm), F32)
    weight = side_by_side(w)
    for m in range(MEL):
        total = conv_rows(m, x3, weight)
        pre[m] = total
        kept = total * own
        one = one + jnp.sum(kept, axis=0, keepdims=True)
        two = two + jnp.sum(kept * total, axis=0, keepdims=True)
    frame_total = 0
    pair_total = 0
    for i in range(g.clips):
        frame_total = frame_total + lens[i]
        pair_total = pair_total + (lens[i] + 1) // 2
    row = misc_row(
        frame_total.astype(F32), pair_total.astype(F32), jnp.sum(square, axis=1, keepdims=True)
    )
    send_payload(pay, one, two, row, gains[...])


def first(g, info, lens, gains, xs, w):
    return pl.pallas_call(
        functools.partial(first_kernel, g),
        out_shape=[
            jax.ShapeDtypeStruct((MEL, g.win, g.cm), F32),
            jax.ShapeDtypeStruct((MEL, g.win, 3 * g.ci_all), BF),
            jax.ShapeDtypeStruct((g.ndev, 16, 128), F32),
        ],
        in_specs=[SMEM, SMEM] + [VMEM] * (2 + g.nch),
        out_specs=[VMEM] * 3,
        scratch_shapes=[pltpu.VMEM((g.ci_all, g.win * MEL), BF)],
        compiler_params=params(32),
        cost_estimate=cost(2 * 9 * MEL * g.win * g.ci_all * g.cm, 10 * MIB),
        name="first_conv",
    )(info, lens, gains, *xs, w)


MEAN1, INV1, GAMMA1, BETA1, GAMMA2, BETA2, COUNT, PAIRS, SQ0, MEAN2, INV2, SQ1 = range(12)
TABLE = 16


def second_kernel(g, info, got, pre1, w, pre, x3, table, pay):
    c = g.cm
    one, two = total_of(g, got)
    misc = misc_of(g, got)
    count = MEL * pick(misc, 0) / g.nch
    pairs = (MEL // 2) * pick(misc, 1) / g.nch
    at = 2 * (c // 128) + 1
    vectors = [
        jnp.concatenate([got[zz, at + i : at + i + 1, : g.co] for zz in range(g.nch)], axis=1)
        for i in range(4)
    ]
    gamma, beta = vectors[0], vectors[1]
    mean = one / count
    inverse = lax.rsqrt(two / count - mean * mean + 1e-05)
    wide = jnp.zeros((1, c), F32)
    table[...] = jnp.concatenate(
        [mean, inverse, *vectors, wide + count, wide + pairs, wide + pick(misc, 2)]
        + [wide] * (TABLE - 9),
        axis=0,
    )
    valid, own = row_masks(g, info)
    square = jnp.zeros((1, c), F32)
    for m in range(MEL):
        affine = gamma * ((pre1[m] - mean) * inverse) + beta
        act = affine / (1.0 + jnp.exp(-affine)) * valid
        square = square + jnp.sum(act * act * own, axis=0, keepdims=True)
        low = act.astype(BF)
        before, after = shifted(low.astype(F32))
        x3[m, :, 0:c] = before.astype(BF)
        x3[m, :, c : 2 * c] = low
        x3[m, :, 2 * c : 3 * c] = after.astype(BF)
    one = jnp.zeros((1, c), F32)
    two = jnp.zeros((1, c), F32)
    weight = side_by_side(w)
    for m in range(MEL):
        total = conv_rows(m, x3, weight)
        pre[m] = total
        kept = total * own
        one = one + jnp.sum(kept, axis=0, keepdims=True)
        two = two + jnp.sum(kept * total, axis=0, keepdims=True)
    send_payload(pay, one, two, misc_row(jnp.sum(square, axis=1, keepdims=True)))


def second(g, info, got, pre1, w):
    return pl.pallas_call(
        functools.partial(second_kernel, g),
        out_shape=[
            jax.ShapeDtypeStruct((MEL, g.win, g.cm), F32),
            jax.ShapeDtypeStruct((MEL, g.win, 3 * g.cm), BF),
            jax.ShapeDtypeStruct((TABLE, g.cm), F32),
            jax.ShapeDtypeStruct((g.ndev, 16, 128), F32),
        ],
        in_specs=[SMEM] + [VMEM] * 3,
        out_specs=[VMEM] * 4,
        compiler_params=params(40),
        cost_estimate=cost(2 * 9 * MEL * g.win * g.cm * g.cm, 17 * MIB),
        name="second_conv",
    )(info, got, pre1, w)


def pool_kernel(g, info, got, table1, pre2, *rest):
    n, c = g.nch, g.cm
    cs, outs = rest[:n], rest[n : 2 * n]
    local_ref, table, pay, held, grads, pooled_ref, flat = rest[2 * n :]
    one, two = total_of(g, got)
    misc = misc_of(g, got)
    old = table1[...]
    count = old[COUNT : COUNT + 1]
    gamma, beta = old[GAMMA2 : GAMMA2 + 1], old[BETA2 : BETA2 + 1]
    mean = one / count
    inverse = lax.rsqrt(two / count - mean * mean + 1e-05)
    wide = jnp.zeros((1, c), F32)
    table[...] = jnp.concatenate(
        [old[:MEAN2], mean, inverse, wide + pick(misc, 0)] + [wide] * (TABLE - 12), axis=0
    )
    for k in range(n):
        source = lax.rem(info[ZED] + n - k, n)
        held[pl.ds(pl.multiple_of(source * g.co, 16), g.co), :] = cs[k][...]
    r = lax.broadcasted_iota(jnp.int32, (256, 128), 0)
    l = lax.broadcasted_iota(jnp.int32, (256, 128), 1)
    spread = (l == (r % 64) // 2 * 4 + r // 64).astype(BF)
    for j in range(g.cwin // 64):
        block = dot(spread, held[:, 128 * j : 128 * (j + 1)], ((1,), (1,)))
        for k in range(MEL // 2):
            grads[k, 64 * j : 64 * (j + 1), :] = block[64 * k : 64 * (k + 1)]
    valid, own = row_masks(g, info)
    r = lax.broadcasted_iota(jnp.int32, (g.win, 1), 0) + info[START]
    share = jnp.where(info[LENGTH] - r // 2 * 2 >= 2, 0.25, 0.5)
    window = pl.ds(pl.multiple_of(info[QOFF], 16), g.win)
    segment = pl.ds(pl.multiple_of(info[OFF], 16), g.seg)
    beta_sum = gamma_sum = square = jnp.zeros((1, c), F32)
    for k in range(MEL // 2):
        given = grads[k, window, :] * (share * valid)
        pair = None
        for m in (2 * k, 2 * k + 1):
            scaled = (pre2[m] - mean) * inverse
            affine = gamma * scaled + beta
            sigma = 1.0 / (1.0 + jnp.exp(-affine))
            act = affine * sigma * valid
            square = square + jnp.sum(act * act * own, axis=0, keepdims=True)
            local = given * sigma * (1.0 + affine * (1.0 - sigma))
            local_ref[m] = local
            kept = local * own
            beta_sum = beta_sum + jnp.sum(kept, axis=0, keepdims=True)
            gamma_sum = gamma_sum + jnp.sum(kept * scaled, axis=0, keepdims=True)
            pair = act if pair is None else pair + act
        pooled_ref[k] = pair * share
    wide_rows = (MEL // 2) * g.seg
    values = jnp.concatenate([pooled_ref[k, segment, :] for k in range(MEL // 2)], axis=0)
    high = values.astype(BF)
    low = (values - high.astype(F32)).astype(BF)
    r = lax.broadcasted_iota(jnp.int32, (wide_rows, 2 * g.seg), 0)
    l = lax.broadcasted_iota(jnp.int32, (wide_rows, 2 * g.seg), 1)
    gather = (l == (r % g.seg) // 2 * 4 + r // g.seg).astype(BF)
    pooled = dot(high, gather, ((0,), (0,))) + dot(low, gather, ((0,), (0,)))
    flat[...] = pooled.astype(BF)
    pooled_square = jnp.sum(jnp.sum(pooled * pooled, axis=1, keepdims=True), axis=0, keepdims=True)
    for k in range(n):
        to = lax.rem(info[ZED] + k, n)
        outs[k][...] = flat[pl.ds(pl.multiple_of(to * g.co, 16), g.co), :]
    send_payload(
        pay, beta_sum, gamma_sum, misc_row(jnp.sum(square, axis=1, keepdims=True), pooled_square)
    )


def pool(g, info, got, table1, pre2, cs):
    n = g.nch
    out = pl.pallas_call(
        functools.partial(pool_kernel, g),
        out_shape=[jax.ShapeDtypeStruct((g.co, 2 * g.seg), BF)] * n
        + [
            jax.ShapeDtypeStruct((MEL, g.win, g.cm), F32),
            jax.ShapeDtypeStruct((TABLE, g.cm), F32),
            jax.ShapeDtypeStruct((g.ndev, 16, 128), F32),
        ],
        in_specs=[SMEM] + [VMEM] * (3 + n),
        out_specs=[VMEM] * (n + 3),
        scratch_shapes=[
            pltpu.VMEM((g.cm, g.cwin * 2), BF),
            pltpu.VMEM((MEL // 2, g.cwin, g.cm), F32),
            pltpu.VMEM((MEL // 2, g.win, g.cm), F32),
            pltpu.VMEM((g.cm, 2 * g.seg), BF),
        ],
        compiler_params=params(40),
        cost_estimate=cost(4e9, 8 * MIB),
        name="pool",
    )(info, got, table1, pre2, *cs)
    return out[:n], out[n], out[n + 1], out[n + 2]


def back_kernel(g, info, got, table, pre2, local2, pre1, w, local1, grad, roots, sums, pay, g3):
    c = g.cm
    beta_sum, gamma_sum = total_of(g, got)
    misc = misc_of(g, got)
    t = table[...]

    def row(i):
        return t[i : i + 1]

    count = row(COUNT)
    sums[...] = jnp.concatenate([beta_sum, gamma_sum] + [jnp.zeros((1, c), F32)] * 6, axis=0)
    one = count[:, :128]
    pairs = t[PAIRS : PAIRS + 1, :128]
    lane = lax.broadcasted_iota(jnp.int32, (1, 128), 1)
    tops = misc_row(pick(t[SQ0 : SQ0 + 1, :128], 0), pick(t[SQ1 : SQ1 + 1, :128], 0))
    tops = jnp.where(lane == 2, pick(misc, 0), jnp.where(lane == 3, pick(misc, 1), tops))
    under = jnp.where(lane == 0, one * g.ci_all, jnp.where(lane == 3, pairs * c, one * c))
    roots[...] = jnp.broadcast_to(jnp.sqrt(tops / under), (8, 128))
    valid, own = row_masks(g, info)
    factor = row(GAMMA2) * row(INV2)
    beta_part, gamma_part = beta_sum / count, gamma_sum / count
    for m in range(MEL):
        scaled = (pre2[m] - row(MEAN2)) * row(INV2)
        value = valid * (factor * (local2[m] - beta_part - scaled * gamma_part))
        low = value.astype(BF)
        before, after = shifted(low.astype(F32))
        g3[m, :, 0:c] = after.astype(BF)
        g3[m, :, c : 2 * c] = low
        g3[m, :, 2 * c : 3 * c] = before.astype(BF)
        grad[m] = (value * own).astype(BF)
    weight = stacked(w)
    beta_sum = gamma_sum = jnp.zeros((1, c), F32)
    for m in range(MEL):
        given = conv_back_rows(m, g3, weight)
        scaled = (pre1[m] - row(MEAN1)) * row(INV1)
        affine = row(GAMMA1) * scaled + row(BETA1)
        sigma = 1.0 / (1.0 + jnp.exp(-affine))
        local = given * valid * sigma * (1.0 + affine * (1.0 - sigma))
        local1[m] = local
        kept = local * own
        beta_sum = beta_sum + jnp.sum(kept, axis=0, keepdims=True)
        gamma_sum = gamma_sum + jnp.sum(kept * scaled, axis=0, keepdims=True)
    send_payload(pay, beta_sum, gamma_sum)


def back(g, info, got, table, pre2, local2, pre1, w):
    return pl.pallas_call(
        functools.partial(back_kernel, g),
        out_shape=[
            jax.ShapeDtypeStruct((MEL, g.win, g.cm), F32),
            jax.ShapeDtypeStruct((MEL, g.win, g.cm), BF),
            jax.ShapeDtypeStruct((8, 128), F32),
            jax.ShapeDtypeStruct((8, g.cm), F32),
            jax.ShapeDtypeStruct((g.ndev, 8, 128), F32),
        ],
        in_specs=[SMEM] + [VMEM] * 6,
        out_specs=[VMEM] * 5,
        scratch_shapes=[pltpu.VMEM((MEL, g.win, 3 * g.cm), BF)],
        compiler_params=params(44),
        cost_estimate=cost(2 * 9 * MEL * g.win * g.cm * g.cm, 20 * MIB),
        name="second_back",
    )(info, got, table, pre2, local2, pre1, w)


def weight_terms(g, info, grad, x3, depth, keep, give):
    core = lax.rem(info[DEE], 2)
    for tap in range(9):
        a, b = tap // 3, tap % 3
        low = max(0, 1 - b)
        high = min(MEL, MEL + 1 - b)
        rows = (high - low) * g.win
        left = grad[low:high].reshape(rows, g.cm)
        right = x3[low + b - 1 : high + b - 1, :, a * depth : (a + 1) * depth].reshape(rows, depth)
        term = dot(left, right, ((0,), (0,))).astype(BF)

        for mine in range(2):

            @pl.when(core == mine)
            def _():
                for z in range(g.nch):
                    for p in range(g.pieces):
                        at = z * g.co + p * g.rows
                        to = keep if p % 2 == mine else give
                        to[p // 2, z, tap] = term[at : at + g.rows]


def pieces_shape(g, depth):
    return jax.ShapeDtypeStruct((g.planes, g.nch, 9, g.rows, depth), BF)


def mid_terms_kernel(g, info, grad, x3, keep, give):
    weight_terms(g, info, grad, x3, g.cm, keep, give)


def mid_terms(g, info, grad, x3):
    return pl.pallas_call(
        functools.partial(mid_terms_kernel, g),
        out_shape=[pieces_shape(g, g.cm)] * 2,
        in_specs=[SMEM, VMEM, VMEM],
        out_specs=[VMEM] * 2,
        compiler_params=params(40),
        cost_estimate=cost(2 * 9 * MEL * g.win * g.cm * g.cm, 12 * MIB),
        name="weight_mid_terms",
    )(info, grad, x3)


def in_terms_kernel(g, info, got, table, pre1, local1, x3, grad, keep, give, sums, own_grad):
    beta_sum, gamma_sum = total_of(g, got)
    t = table[...]
    mean, inverse, gamma = t[MEAN1 : MEAN1 + 1], t[INV1 : INV1 + 1], t[GAMMA1 : GAMMA1 + 1]
    count = t[COUNT : COUNT + 1]
    sums[...] = jnp.concatenate([beta_sum, gamma_sum] + [jnp.zeros((1, g.cm), F32)] * 6, axis=0)
    valid, own = row_masks(g, info)
    factor = gamma * inverse
    beta_part, gamma_part = beta_sum / count, gamma_sum / count
    for m in range(MEL):
        scaled = (pre1[m] - mean) * inverse
        value = valid * (factor * (local1[m] - beta_part - scaled * gamma_part))
        grad[m] = value.astype(BF)
        own_grad[m] = (value * own).astype(BF)
    weight_terms(g, info, own_grad, x3, g.ci_all, keep, give)


def in_terms(g, info, got, table, pre1, local1, x3):
    return pl.pallas_call(
        functools.partial(in_terms_kernel, g),
        out_shape=[
            jax.ShapeDtypeStruct((MEL, g.win, g.cm), BF),
            pieces_shape(g, g.ci_all),
            pieces_shape(g, g.ci_all),
            jax.ShapeDtypeStruct((8, g.cm), F32),
        ],
        in_specs=[SMEM] + [VMEM] * 5,
        out_specs=[VMEM] * 4,
        scratch_shapes=[pltpu.VMEM((MEL, g.win, g.cm), BF)],
        compiler_params=params(40),
        cost_estimate=cost(2 * 9 * MEL * g.win * g.cm * g.ci_all, 14 * MIB),
        name="weight_in_terms",
    )(info, got, table, pre1, local1, x3)


def spectra_kernel(g, info, grad, w, *rest):
    n, c = g.nch, g.cm
    outs, g3, rows, flat = rest[:n], rest[n], rest[n + 1], rest[n + 2]
    for m in range(MEL):
        low = grad[m]
        before, after = shifted(low.astype(F32))
        g3[m, :, 0:c] = after.astype(BF)
        g3[m, :, c : 2 * c] = low
        g3[m, :, 2 * c : 3 * c] = before.astype(BF)
    valid, own = row_masks(g, info)
    weight = stacked(w)
    for m in range(MEL):
        rows[m] = (conv_back_rows(m, g3, weight) * own).astype(BF)
    order = grid_order()
    for j in range(g.seg // 16):
        at = pl.ds(pl.multiple_of(info[OFF] + 16 * j, 16), 16)
        block = jnp.concatenate([rows[m, at, :] for m in range(MEL)], axis=0)
        flat[:, 128 * j : 128 * (j + 1)] = dot(block, order, ((0,), (0,))).astype(BF)
    for k in range(n):
        to = lax.rem(info[ZED] + k, n)
        outs[k][...] = flat[pl.ds(pl.multiple_of(to * g.ci, 16), g.ci), :]


def spectra_back(g, info, grad, w):
    n = g.nch
    return pl.pallas_call(
        functools.partial(spectra_kernel, g),
        out_shape=[jax.ShapeDtypeStruct((g.ci, g.seg * MEL), BF)] * n,
        in_specs=[SMEM, VMEM, VMEM],
        out_specs=[VMEM] * n,
        scratch_shapes=[
            pltpu.VMEM((MEL, g.win, 3 * g.cm), BF),
            pltpu.VMEM((MEL, g.win, g.ci_all), BF),
            pltpu.VMEM((g.ci_all, g.seg * MEL), BF),
        ],
        compiler_params=params(40),
        cost_estimate=cost(2 * 9 * MEL * g.win * g.cm * g.ci_all, 5 * MIB),
        name="spectra_back",
    )(info, grad, w)


def place_kernel(g, width, info, *rest):
    n = g.nch
    parts, out = rest[:n], rest[n]
    for k in range(n):
        source = lax.rem(info[ZED] + n - k, n)
        for zz in range(n):

            @pl.when(source == zz)
            def _():
                seg = zz % g.segs
                out[zz // g.segs, :, seg * width : (seg + 1) * width] = parts[k][...].astype(
                    out.dtype
                )


def place(g, info, parts, dtype, name):
    channels, width = parts[0].shape
    return pl.pallas_call(
        functools.partial(place_kernel, g, width),
        out_shape=jax.ShapeDtypeStruct((g.clips, channels, g.segs * width), dtype),
        in_specs=[SMEM] + [VMEM] * g.nch,
        out_specs=VMEM,
        compiler_params=params(16),
        name=name,
    )(info, *parts)


def core_sum_kernel(g, info, keep, got, *outs):
    plane = lax.rem(info[DEE], g.pieces) // 2
    for j in range(g.planes):
        at = plane ^ j
        outs[j][...] = (keep[at].astype(F32) + got[at].astype(F32)).astype(BF)


def core_sum(g, info, keep, got, name):
    shape = keep.shape[1:]
    return pl.pallas_call(
        functools.partial(core_sum_kernel, g),
        out_shape=[jax.ShapeDtypeStruct(shape, BF)] * g.planes,
        in_specs=[SMEM, VMEM, VMEM],
        out_specs=[VMEM] * g.planes,
        compiler_params=params(16),
        name=name,
    )(info, keep, got)


def plane_sum_kernel(g, info, *rest):
    parts, outs = rest[: g.planes], rest[g.planes :]
    for k in range(g.nch):
        to = lax.rem(info[ZED] + k, g.nch)
        total = parts[0][to].astype(F32)
        for p in parts[1:]:
            total = total + p[to].astype(F32)
        outs[k][...] = total.astype(BF)


def plane_sum(g, info, parts, name):
    shape = parts[0].shape[1:]
    return pl.pallas_call(
        functools.partial(plane_sum_kernel, g),
        out_shape=[jax.ShapeDtypeStruct(shape, BF)] * g.nch,
        in_specs=[SMEM] + [VMEM] * g.planes,
        out_specs=[VMEM] * g.nch,
        compiler_params=params(16),
        name=name,
    )(info, *parts)


def chan_sum_kernel(*refs):
    total = refs[0][...].astype(F32)
    for r in refs[1:-1]:
        total = total + r[...].astype(F32)
    refs[-1][...] = total.astype(BF)


def chan_sum(g, parts, name):
    return pl.pallas_call(
        chan_sum_kernel,
        out_shape=jax.ShapeDtypeStruct(parts[0].shape, BF),
        in_specs=[VMEM] * len(parts),
        out_specs=VMEM,
        compiler_params=params(16),
        name=name,
    )(*parts)


def spread_kernel(g, info, *rest):
    parts, out = rest[:-1], rest[-1]
    for q in range(g.pieces):
        piece = lax.rem(info[DEE], g.pieces) ^ q
        at = pl.multiple_of(piece * g.rows, 16)
        out[:, pl.ds(at, g.rows), :] = parts[q][...].astype(F32)


def spread_out(g, info, parts, depth, name):
    return pl.pallas_call(
        functools.partial(spread_kernel, g),
        out_shape=jax.ShapeDtypeStruct((9, g.co, depth), F32),
        in_specs=[SMEM] + [VMEM] * g.pieces,
        out_specs=VMEM,
        compiler_params=params(16),
        name=name,
    )(info, *parts)


class Links:
    def __init__(self, g):
        self.g = g

    def swap(self, x, bits):
        return lax.ppermute(x, "dp", [(i, i ^ bits) for i in range(self.g.ndp)])

    def along(self, x, k):
        n = self.g.nch
        return lax.ppermute(x, "chan", [(i, (i + k) % n) for i in range(n)])

    def exchange(self, parts):
        return [parts[0]] + [self.along(parts[k], k) for k in range(1, self.g.nch)]

    def gather_pieces(self, x):
        have = [x] + [None] * (self.g.pieces - 1)
        for q in range(2, self.g.pieces, 2):
            have[q] = self.swap(x, q)
        for q in range(1, self.g.pieces, 2):
            have[q] = self.swap(have[q - 1], 1)
        return have

    def whole_weight(self, info, own, piece, depth, name):
        parts = jnp.stack([self.along(piece, k) for k in range(1, self.g.nch)])
        return join(self.g, info, own, self.gather_pieces(parts), depth, name)

    def weight_sum(self, info, keep, give, depth, name):
        g = self.g
        parts = core_sum(g, info, keep, self.swap(give, 1), name + "_core_sum")
        parts = [parts[0]] + [self.swap(parts[j], 2 * j) for j in range(1, g.planes)]
        bit = g.pieces
        parts = plane_sum(g, info, parts, name + "_plane_sum")
        parts = self.exchange(parts)
        mine = chan_sum(g, parts, name + "_chan_sum")
        while bit < g.ndp:
            mine = chan_sum(g, [mine, self.swap(mine, bit)], name + "_rest_sum")
            bit *= 2
        return spread_out(g, info, self.gather_pieces(mine), depth, name + "_out")


def everyone(x):
    return lax.all_to_all(x, ("dp", "chan"), 0, 0)


def make_body(ndp, nch):
    def body(
        spectra, lengths, weight_in, gamma_in, beta_in, weight_mid, gamma_mid, beta_mid, cotangent
    ):
        g = Geometry(
            ndp,
            nch,
            spectra.shape[0],
            spectra.shape[2] // MEL,
            weight_in.shape[2],
            weight_mid.shape[2],
        )
        links = Links(g)
        z = lax.axis_index("chan")
        d = lax.axis_index("dp")
        seg = z % g.segs
        start = jnp.clip(seg * g.seg - HALO, 0, g.frames - g.win)
        cstart = jnp.minimum(start // 64 * 64, g.frames - g.cwin)
        length = lax.dynamic_index_in_dim(lengths, z // g.segs, keepdims=False)
        info = jnp.stack(
            [length, start, seg * g.seg - start, start - cstart, z, d, z * 0, z * 0]
        ).astype(jnp.int32)
        gains = jnp.stack([gamma_in, beta_in, gamma_mid, beta_mid])
        gains = jnp.pad(gains, ((0, 0), (0, 128 - g.co)))

        xs, cs, piece_in, piece_mid = cut(g, info, spectra, cotangent, weight_in, weight_mid)
        w_in = links.whole_weight(info, weight_in, piece_in, g.ci_all, "join_in")
        xs = links.exchange(xs)
        w_mid = links.whole_weight(info, weight_mid, piece_mid, g.cm, "join_mid")
        cs = links.exchange(cs)

        pre1, x3_in, pay = first(g, info, lengths, gains, xs, w_in)
        got = everyone(pay)
        pre2, x3_mid, table, pay = second(g, info, got, pre1, w_mid)
        got = everyone(pay)
        pooled, local2, table, pay = pool(g, info, got, table, pre2, cs)
        pooled = links.exchange(pooled)
        got = everyone(pay)
        local1, grad2, roots, sums2, pay = back(g, info, got, table, pre2, local2, pre1, w_mid)
        got = everyone(pay)
        keep_mid, give_mid = mid_terms(g, info, grad2, x3_mid)
        grad1, keep_in, give_in, sums1 = in_terms(g, info, got, table, pre1, local1, x3_in)
        parts = spectra_back(g, info, grad1, w_in)
        weight_mid_grad = links.weight_sum(info, keep_mid, give_mid, g.cm, "mid")
        weight_in_grad = links.weight_sum(info, keep_in, give_in, g.ci_all, "in")
        parts = links.exchange(parts)
        spectra_grad = place(g, info, parts, F32, "place_spectra")
        block_out = place(g, info, pooled, BF, "place_pooled")

        def share(sums, i):
            return lax.dynamic_slice_in_dim(sums[i], z * g.co, g.co)

        return (
            block_out,
            spectra_grad,
            weight_in_grad,
            share(sums1, 1),
            share(sums1, 0),
            weight_mid_grad,
            share(sums2, 1),
            share(sums2, 0),
            roots[0, :4],
        )

    return body


def solution(mesh):
    placed = (
        P("dp", "chan", None),
        P("dp"),
        P(None, "chan", None),
        P("chan"),
        P("chan"),
        P(None, "chan", None),
        P("chan"),
        P("chan"),
        P("dp", "chan", None),
    )
    return jax.shard_map(
        make_body(mesh.shape["dp"], mesh.shape["chan"]),
        mesh=mesh,
        in_specs=placed,
        out_specs=(
            P("dp", "chan", None),
            P("dp", "chan", None),
            P(None, "chan", None),
            P("chan"),
            P("chan"),
            P(None, "chan", None),
            P("chan"),
            P("chan"),
            P(),
        ),
        check_vma=False,
    )
```

```python
import functools

import jax
import jax.numpy as jnp
from jax import lax
from jax.experimental import pallas as pl
from jax.experimental.pallas import tpu as pltpu
from jax.sharding import PartitionSpec as P

MEL = 8
HALO = 16
BF = jnp.bfloat16
F32 = jnp.float32
MIB = 1024 * 1024

VMEM = pl.BlockSpec(memory_space=pltpu.VMEM)
SMEM = pl.BlockSpec(memory_space=pltpu.SMEM)
ANY = pl.BlockSpec(memory_space=pl.ANY)
HBM = pl.BlockSpec(memory_space=pltpu.HBM)


def bits_of(n):
    return n.bit_length() - 1


class Geometry:
    def __init__(self, ndp, nch, clips, frames, c_in, c_mid):
        self.ndp, self.nch, self.ndev = ndp, nch, ndp * nch
        self.clips, self.frames = clips, frames
        self.ci_all, self.cm = c_in, c_mid
        self.ci, self.co = c_in // nch, c_mid // nch
        self.segs = nch // clips
        self.seg = frames // self.segs
        self.win = self.seg + HALO * min(self.segs - 1, 2)
        starts = [min(max(s * self.seg - HALO, 0), frames - self.win) for s in range(self.segs)]
        self.cwin = min(frames, (self.win + 48 + 63) // 64 * 64)
        assert all(min(s // 64 * 64, frames - self.cwin) + self.cwin >= s + self.win for s in starts)
        self.rows = max(16, self.co // ndp)
        self.pieces = self.co // self.rows
        self.planes = self.pieces // 2
        self.turns = bits_of(self.planes)
        self.zturns = bits_of(nch)

    def mask(self, core, turn):
        low, high = 1 << turn, 1 << (self.turns - 1 - turn)
        return low + core * (high - low)

    def plane_of(self, core, e):
        rel = 0
        for t in range(self.turns):
            if (e >> (self.turns - 1 - t)) & 1:
                rel = rel ^ self.mask(core, t)
        return rel

    def row_of(self, core, plane):
        return core * (self.co // 2) + plane * self.rows

    def zed_of(self, e):
        return sum(1 << t for t in range(self.zturns) if (e >> (self.zturns - 1 - t)) & 1)


class Here:
    def __init__(self, g, lens):
        self.z = lax.axis_index("chan")
        self.d = lax.axis_index("dp")
        self.core = lax.rem(self.d, 2)
        self.plane = lax.rem(self.d, g.pieces) // 2
        clip, seg = self.z // g.segs, lax.rem(self.z, g.segs)
        self.length = lens[clip]
        self.start, self.cstart = g_starts(g, seg)
        self.off = seg * g.seg - self.start
        self.qoff = self.start - self.cstart


def g_starts(g, seg):
    start = jnp.clip(seg * g.seg - HALO, 0, g.frames - g.win)
    return start, jnp.minimum(start // 64 * 64, g.frames - g.cwin)


def aligned(x, n=16):
    return pl.multiple_of(x, n)


def dot(a, b, contract):
    return lax.dot_general(a, b, ((contract[0], contract[1]), ((), ())), preferred_element_type=F32)


def call(body, out, ins, args, scratch, limit, flops, nbytes, name, aliases=None):
    return pl.pallas_call(
        body,
        out_shape=[pltpu.VMEM(o.shape, o.dtype) if isinstance(o, jax.ShapeDtypeStruct) else o for o in out],
        in_specs=ins,
        out_specs=[VMEM if isinstance(o, jax.ShapeDtypeStruct) else ANY for o in out],
        scratch_shapes=scratch,
        input_output_aliases=aliases or {},
        compiler_params=pltpu.CompilerParams(vmem_limit_bytes=limit * MIB),
        cost_estimate=pl.CostEstimate(
            flops=int(flops), bytes_accessed=int(nbytes), transcendentals=0
        ),
        name=name,
    )(*args)


def arr(shape, dtype):
    return jax.ShapeDtypeStruct(shape, dtype)


def keep_near(*xs):
    return [pltpu.with_memory_space_constraint(x, pltpu.VMEM) for x in xs]


class Copies:
    def __init__(self, sems):
        self.sems, self.n, self.open = sems, 0, []

    def start(self, src, dst):
        c = pltpu.make_async_copy(src, dst, self.sems.at[self.n])
        self.n += 1
        c.start()
        self.open.append(c)
        return c

    def wait(self, c):
        self.open = [o for o in self.open if o is not c]
        c.wait()

    def wait_all(self, some=None):
        for c in list(self.open if some is None else some):
            self.wait(c)


def sems(n):
    return pltpu.SemaphoreType.DMA((n,))


def row_masks(g, here, width):
    r = lax.broadcasted_iota(jnp.int32, (g.win, 128), 0)
    valid = (r + here.start) < here.length
    own = valid & (r >= here.off) & (r < here.off + g.seg)
    return widen(valid.astype(F32), width), widen(own.astype(F32), width)


def widen(x, width):
    return jnp.concatenate([x] * (width // 128), axis=1)


def shifted(x):
    n = x.shape[0]
    r = lax.broadcasted_iota(jnp.int32, (8, 1), 0)
    before, after = pltpu.roll(x, 1, 0), pltpu.roll(x, n - 1, 0)
    before = jnp.concatenate([jnp.where(r == 0, 0.0, before[:8]), before[8:]], axis=0)
    after = jnp.concatenate([after[:-8], jnp.where(r == 7, 0.0, after[-8:])], axis=0)
    return before, after


def grid_order(rows=16):
    n = MEL * rows
    r = lax.broadcasted_iota(jnp.int32, (n, n), 0)
    c = lax.broadcasted_iota(jnp.int32, (n, n), 1)
    return (c == (r % rows) * MEL + r // rows).astype(BF)


def lanes(vector):
    n = vector.shape[1] // 128
    return jnp.concatenate([vector[:, 128 * i : 128 * (i + 1)] for i in range(n)], axis=0)


def unlanes(rows):
    return jnp.concatenate([rows[i : i + 1] for i in range(rows.shape[0])], axis=1)


def misc_row(*scalars):
    lane = lax.broadcasted_iota(jnp.int32, (1, 128), 1)
    row = jnp.zeros((1, 128), F32)
    for i, s in enumerate(scalars):
        row = jnp.where(lane == i, s, row)
    return row


def pick(row, i):
    lane = lax.broadcasted_iota(jnp.int32, (1, 128), 1)
    return jnp.sum(jnp.where(lane == i, row, 0.0), axis=1, keepdims=True)


def sum_rows(x):
    return jnp.sum(x, axis=0, keepdims=True)


def payload(rows, *parts):
    have = sum(r.shape[0] for r in parts)
    if have < rows:
        parts = (*parts, jnp.zeros((rows - have, 128), F32))
    return jnp.concatenate(parts, axis=0)


def fan_kernel(pay, *rest):
    out = rest[-1]
    out[...] = jnp.broadcast_to(pay[...][None], out.shape)


def fan(g, pay, *after):
    out = [arr((g.ndev, *pay.shape), F32)]
    ins = [VMEM] + [ANY] * len(after)
    return call(fan_kernel, out, ins, [pay, *after], [], 4, 0, 1e5, "fan")[0]


def total_of(g, ref):
    n = g.cm // 128
    block = jnp.sum(ref[:, : 2 * n, :], axis=0)
    return unlanes(block[:n]), unlanes(block[n:])


def misc_of(g, ref):
    return jnp.sum(ref[:, 2 * (g.cm // 128), :], axis=0, keepdims=True)


def side_by_side(x3, m, low, c, first, last):
    x3[m, :, 0:c] = first.astype(BF)
    x3[m, :, c : 2 * c] = low
    x3[m, :, 2 * c : 3 * c] = last.astype(BF)


def cut_weights_kernel(g, w_in, w_mid, out, sem):
    d = lax.axis_index("dp")
    core, plane = lax.rem(d, 2), lax.rem(d, g.pieces) // 2
    rows = pl.ds(aligned(g.row_of(core, plane)), g.rows)
    copies = Copies(sem)
    copies.start(w_in.at[:, rows, :], out.at[:, :, : g.ci_all])
    copies.start(w_mid.at[:, rows, :], out.at[:, :, g.ci_all :])
    copies.wait_all()


def cut_weights(g, w_in, w_mid):
    out = [arr((9, g.rows, g.ci_all + g.cm), BF)]
    args = [in_hbm(w_in), in_hbm(w_mid)]
    body = functools.partial(cut_weights_kernel, g)
    return call(body, out, [ANY] * 2, args, [sems(2)], 4, 0, 4e5, "cut_weights")[0]


def sort_kernel(g, *rest):
    n = g.nch - 1
    parts, first, second = rest[:n], rest[n], rest[n + 1]
    for k in range(n):
        first[k] = parts[k][:, :, : g.ci_all]
        second[k] = parts[k][:, :, g.ci_all :]


def sort_pieces(g, parts):
    n = g.nch - 1
    out = [arr((n, 9, g.rows, g.ci_all), BF), arr((n, 9, g.rows, g.cm), BF)]
    body = functools.partial(sort_kernel, g)
    return call(body, out, [VMEM] * n, parts, [], 4, 0, 1e6, "sort_pieces")


def cut_maps_kernel(g, spec, after, out, sem):
    copies = Copies(sem)
    for z in range(g.nch):
        start = static_start(g, z % g.segs) * MEL
        copies.start(spec.at[z // g.segs, :, start : start + g.win * MEL], out.at[z])
    copies.wait_all()


def cut_maps(g, spec, after):
    out = [arr((g.nch, g.ci, g.win * MEL), BF)]
    body = functools.partial(cut_maps_kernel, g)
    args = [in_hbm(spec), after]
    return call(body, out, [ANY] * 2, args, [sems(g.nch)], 4, 0, 2e6, "cut_maps")[0]


def static_start(g, seg):
    return min(max(seg * g.seg - HALO, 0), g.frames - g.win)


def cut_cot_kernel(g, cot, after, *rest):
    n = g.nch
    cs, sem = rest[:n], rest[n]
    z = lax.axis_index("chan")
    copies = Copies(sem)
    for k in range(n):
        to = z ^ k
        clip, seg = to // g.segs, lax.rem(to, g.segs)
        _, cstart = g_starts(g, seg)
        copies.start(cot.at[clip, :, pl.ds(aligned(cstart * 2, 128), g.cwin * 2)], cs[k])
    copies.wait_all()


def cut_cot(g, cot, after):
    n = g.nch
    out = [arr((g.co, g.cwin * 2), BF)] * n
    body = functools.partial(cut_cot_kernel, g)
    return call(body, out, [ANY] * 2, [in_hbm(cot), after], [sems(n)], 4, 0, 1e6, "cut_cotangent")


def in_hbm(x):
    return pltpu.with_memory_space_constraint(x, pltpu.HBM)


def join_kernel(g, own, *rest):
    parts, w = rest[:-1], rest[-1]
    z, d = lax.axis_index("chan"), lax.axis_index("dp")
    mine, plane = lax.rem(d, 2), lax.rem(d, g.pieces) // 2
    w[:, pl.ds(aligned(z * g.co), g.co), :] = own[...]
    for side in range(2):
        core = mine if side == 0 else 1 - mine
        for e in range(g.planes):
            row = g.row_of(core, plane ^ g.plane_of(core, e))
            for k in range(1, g.nch):
                at = aligned((z ^ k) * g.co + row)
                w[:, pl.ds(at, g.rows), :] = parts[side * g.planes + e][k - 1]


def join(g, own, parts, depth, name):
    body = functools.partial(join_kernel, g)
    args = [own, *parts]
    ins = [VMEM] * len(args)
    return call(body, [arr((9, g.cm, depth), BF)], ins, args, [], 8, 0, 4 * MIB, name)[0]


GROUP = 4


def conv_group(g, v3, low, high, taps, contract, back):
    total = [None] * (high - low)
    for b in (1, 0, 2):
        move = 1 - b if back else b - 1
        first, last = max(low, -move), min(high, MEL - move)
        rows = v3[first + move : last + move].reshape((last - first) * g.win, v3.shape[2])
        term = dot(rows, taps(b), contract)
        for m in range(first, last):
            part = term[(m - first) * g.win : (m - first + 1) * g.win]
            total[m - low] = part if total[m - low] is None else total[m - low] + part
    return total


def conv_rows(g, x3, w, low, high):
    def taps(b):
        return jnp.concatenate([w[b], w[3 + b], w[6 + b]], axis=1)

    return conv_group(g, x3, low, high, taps, ((1,), (1,)), False)


def conv_back_rows(g, g3, w, low, high):
    def taps(b):
        return jnp.concatenate([w[b], w[3 + b], w[6 + b]], axis=0)

    return conv_group(g, g3, low, high, taps, ((1,), (0,)), True)


def first_kernel(g, lens, gains, maps, w, after, pre_out, x3_out, pay, pre, x3, sem):
    here = Here(g, lens)
    copies = Copies(sem)
    c = g.ci_all
    valid, own = row_masks(g, here, c)
    order = grid_order()
    square = jnp.zeros((1, c), F32)
    for j in range(g.win // 16):
        cells = maps[:, :, 128 * j : 128 * (j + 1)].reshape(c, 128)
        block = dot(order, cells, ((1,), (1,)))
        v = valid[16 * j : 16 * (j + 1)]
        o = own[16 * j : 16 * (j + 1)]
        for m in range(MEL):
            part = block[16 * m : 16 * (m + 1)] * v
            square = square + sum_rows(part * part * o)
            x3[m, 16 * j : 16 * (j + 1), c : 2 * c] = part.astype(BF)
    for m in range(MEL):
        before, after_ = shifted(x3[m, :, c : 2 * c].astype(F32))
        x3[m, :, 0:c] = before.astype(BF)
        x3[m, :, 2 * c : 3 * c] = after_.astype(BF)
        copies.start(x3.at[m], x3_out.at[m])
    _, own = row_masks(g, here, g.cm)
    one = two = jnp.zeros((1, g.cm), F32)
    for low in range(0, MEL, GROUP):
        for m, total in enumerate(conv_rows(g, x3, w, low, low + GROUP), low):
            pre[m] = total
            copies.start(pre.at[m], pre_out.at[m])
            kept = total * own
            one = one + sum_rows(kept)
            two = two + sum_rows(kept * total)
    frame_total = 0
    pair_total = 0
    for i in range(g.clips):
        frame_total = frame_total + lens[i]
        pair_total = pair_total + (lens[i] + 1) // 2
    row = misc_row(
        frame_total.astype(F32), pair_total.astype(F32), jnp.sum(square, axis=1, keepdims=True)
    )
    block = payload(16, lanes(one), lanes(two), row, gains[...])
    pay[...] = jnp.broadcast_to(block[None], pay.shape)
    copies.wait_all()


def first(g, lens, gains, maps, w, after):
    body = functools.partial(first_kernel, g)
    out = [
        pltpu.HBM((MEL, g.win, g.cm), F32),
        pltpu.HBM((MEL, g.win, 3 * g.ci_all), BF),
        arr((g.ndev, 16, 128), F32),
    ]
    scratch = [
        pltpu.VMEM((MEL, g.win, g.cm), F32),
        pltpu.VMEM((MEL, g.win, 3 * g.ci_all), BF),
        sems(2 * MEL),
    ]
    args = [lens, gains, *keep_near(maps, w), after]
    ins = [SMEM, VMEM, VMEM, VMEM, ANY]
    flops = 2 * 9 * MEL * g.win * g.ci_all * g.cm
    return call(body, out, ins, args, scratch, 20, flops, 10 * MIB, "first_conv")


MEAN1, INV1, GAMMA1, BETA1, GAMMA2, BETA2, COUNT, PAIRS, SQ0, MEAN2, INV2 = range(11)
TABLE = 16


def half_affine(mean, inverse, gamma, beta):
    scale = 0.5 * gamma * inverse
    return scale, 0.5 * beta - mean * scale


def second_kernel(g, lens, got, pre1_in, w, pre, x3, table, pay, misc_out, pre1, sem):
    here = Here(g, lens)
    copies = Copies(sem)
    arrive = [copies.start(pre1_in.at[m], pre1.at[m]) for m in range(MEL)]
    c = g.cm
    valid, own = row_masks(g, here, c)
    one, two = total_of(g, got)
    misc = misc_of(g, got)
    count = MEL * pick(misc, 0) / g.nch
    pairs = (MEL // 2) * pick(misc, 1) / g.nch
    at = 2 * (c // 128) + 1
    vectors = [
        jnp.concatenate([got[zz, at + i : at + i + 1, : g.co] for zz in range(g.nch)], axis=1)
        for i in range(4)
    ]
    mean = one / count
    inverse = lax.rsqrt(two / count - mean * mean + 1e-05)
    wide = jnp.zeros((1, c), F32)
    table[...] = jnp.concatenate(
        [mean, inverse, *vectors, wide + count, wide + pairs, wide + pick(misc, 2)]
        + [wide] * (TABLE - 9),
        axis=0,
    )
    scale, shift = half_affine(mean, inverse, vectors[0], vectors[1])

    square = jnp.zeros((1, c), F32)
    for m in range(MEL):
        copies.wait(arrive[m])
        half = pre1[m] * scale + shift
        act = half * (1.0 + jnp.tanh(half)) * valid
        low = act.astype(BF)
        before, after = shifted(low.astype(F32))
        side_by_side(x3, m, low, c, before, after)
        square = square + sum_rows(act * act * own)
    one = two = jnp.zeros((1, c), F32)
    for low in range(0, MEL, GROUP):
        for m, total in enumerate(conv_rows(g, x3, w, low, low + GROUP), low):
            pre[m] = total
            kept = total * own
            one = one + sum_rows(kept)
            two = two + sum_rows(kept * total)
    pay[...] = payload(8, lanes(one), lanes(two))
    misc_out[...] = payload(8, misc_row(jnp.sum(square, axis=1, keepdims=True)))


def second(g, lens, got, pre1, w):
    body = functools.partial(second_kernel, g)
    out = [
        arr((MEL, g.win, g.cm), F32),
        arr((MEL, g.win, 3 * g.cm), BF),
        arr((TABLE, g.cm), F32),
        arr((8, 128), F32),
        arr((8, 128), F32),
    ]
    scratch = [
        pltpu.VMEM((MEL, g.win, g.cm), F32),
        sems(MEL),
    ]
    near = keep_near(got, w)
    args = [lens, near[0], pre1, near[1]]
    flops = 2 * 9 * MEL * g.win * g.cm * g.cm
    ins = [SMEM, VMEM, ANY, VMEM]
    return call(body, out, ins, args, scratch, 22, flops, 17 * MIB, "second_conv")


def pool_kernel(g, lens, got, old_ref, pre2, *rest):
    n, c = g.nch, g.cm
    cs, outs = rest[:n], rest[n : 2 * n]
    local_ref, table, pay, misc_out, held, grads, pooled_ref, flat = rest[2 * n :]
    here = Here(g, lens)
    for k in range(n):
        held[pl.ds(aligned((here.z ^ k) * g.co), g.co), :] = cs[k][...]
    r = lax.broadcasted_iota(jnp.int32, (256, 128), 0)
    l = lax.broadcasted_iota(jnp.int32, (256, 128), 1)
    spread = (l == (r % 64) // 2 * 4 + r // 64).astype(BF)
    for j in range(g.cwin // 64):
        block = dot(spread, held[:, 128 * j : 128 * (j + 1)], ((1,), (1,)))
        for k in range(MEL // 2):
            grads[k, 64 * j : 64 * (j + 1), :] = block[64 * k : 64 * (k + 1)]
    one, two = total_of(g, got)
    old = old_ref[...]
    count = old[COUNT : COUNT + 1]
    mean = one / count
    inverse = lax.rsqrt(two / count - mean * mean + 1e-05)
    wide = jnp.zeros((1, c), F32)
    table[...] = jnp.concatenate([old[:MEAN2], mean, inverse] + [wide] * (TABLE - 11), axis=0)
    half_gamma, half_beta = 0.5 * old[GAMMA2 : GAMMA2 + 1], 0.5 * old[BETA2 : BETA2 + 1]
    less = -mean * inverse
    valid, own = row_masks(g, here, c)
    r = lax.broadcasted_iota(jnp.int32, (g.win, 128), 0) + here.start
    share = widen(jnp.where(here.length - r // 2 * 2 >= 2, 0.25, 0.5), c)
    half_share = 0.5 * share * valid
    window = pl.ds(aligned(here.qoff), g.win)
    segment = pl.ds(aligned(here.off), g.seg)
    beta_sum = gamma_sum = square = jnp.zeros((1, c), F32)
    for k in range(MEL // 2):
        given = grads[k, window, :] * half_share
        pair = None
        for m in (2 * k, 2 * k + 1):
            scaled = pre2[m] * inverse + less
            half = scaled * half_gamma + half_beta
            bend = jnp.tanh(half)
            twice = 1.0 + bend
            act = half * twice * own
            square = square + sum_rows(act * act)
            local = given * (twice * (1.0 + half * (1.0 - bend)))
            local_ref[m] = local
            kept = local * own
            beta_sum = beta_sum + sum_rows(kept)
            gamma_sum = gamma_sum + sum_rows(kept * scaled)
            pair = act if pair is None else pair + act
        pooled_ref[k] = pair * share
    wide_rows = (MEL // 2) * g.seg
    values = jnp.concatenate([pooled_ref[k, segment, :] for k in range(MEL // 2)], axis=0)
    high = values.astype(BF)
    low = (values - high.astype(F32)).astype(BF)
    r = lax.broadcasted_iota(jnp.int32, (wide_rows, 2 * g.seg), 0)
    l = lax.broadcasted_iota(jnp.int32, (wide_rows, 2 * g.seg), 1)
    gather = (l == (r % g.seg) // 2 * 4 + r // g.seg).astype(BF)
    pooled = dot(high, gather, ((0,), (0,))) + dot(low, gather, ((0,), (0,)))
    flat[...] = pooled.astype(BF)
    for k in range(n):
        outs[k][...] = flat[pl.ds(aligned((here.z ^ k) * g.co), g.co), :]
    pooled_square = sum_rows(jnp.sum(pooled * pooled, axis=1, keepdims=True))
    block = payload(8, lanes(beta_sum), lanes(gamma_sum))
    pay[...] = jnp.broadcast_to(block[None], pay.shape)
    misc_out[...] = payload(8, misc_row(jnp.sum(square, axis=1, keepdims=True), pooled_square))


def pool(g, lens, got, table, pre2, cs):
    n = g.nch
    body = functools.partial(pool_kernel, g)
    out = [arr((g.co, 2 * g.seg), BF)] * n + [
        arr((MEL, g.win, g.cm), F32),
        arr((TABLE, g.cm), F32),
        arr((g.ndev, 8, 128), F32),
        arr((8, 128), F32),
    ]
    scratch = [
        pltpu.VMEM((g.cm, g.cwin * 2), BF),
        pltpu.VMEM((MEL // 2, g.cwin, g.cm), F32),
        pltpu.VMEM((MEL // 2, g.win, g.cm), F32),
        pltpu.VMEM((g.cm, 2 * g.seg), BF),
    ]
    args = [lens, *keep_near(got, table, pre2, *cs)]
    ins = [SMEM] + [VMEM] * (len(args) - 1)
    out = call(body, out, ins, args, scratch, 16, 4e9, 8 * MIB, "pool")
    return out[:n], *out[n:]


def terms_kernel(g, depth, norm, near, lens, got, table, pre_in, local, x3_in, after, *rest):
    grad, sums, roots, terms, give = rest[:5]
    here = Here(g, lens)
    if near:
        pre, x3, own_grad = pre_in, x3_in, rest[5]
        copies, arrive, side = None, None, None
    else:
        own_grad, pre, x3, sem = rest[5:]
        copies = Copies(sem)
        arrive = [copies.start(pre_in.at[m], pre.at[m]) for m in range(MEL)]
        side = copies.start(x3_in, x3)
    c = g.cm
    valid, own = row_masks(g, here, c)
    beta_sum, gamma_sum = total_of(g, got)
    t = table[...]
    mean, inverse, gamma = (t[i : i + 1] for i in norm)
    count = t[COUNT : COUNT + 1]
    sums[...] = jnp.concatenate([beta_sum, gamma_sum] + [jnp.zeros((1, c), F32)] * 6, axis=0)
    if got.shape[1] > 8:
        at = 2 * (c // 128)
        square1 = pick(jnp.sum(got[:, at, :], axis=0, keepdims=True), 0)
        later = jnp.sum(got[:, at + 1, :], axis=0, keepdims=True)
        tops = misc_row(pick(t[SQ0 : SQ0 + 1, :128], 0), square1, pick(later, 0), pick(later, 1))
        lane = lax.broadcasted_iota(jnp.int32, (1, 128), 1)
        cells, pairs = count[:, :128], t[PAIRS : PAIRS + 1, :128]
        under = jnp.where(lane == 0, cells * g.ci_all, jnp.where(lane == 3, pairs * c, cells * c))
        roots[...] = jnp.broadcast_to(jnp.sqrt(tops / under), (8, 128))
    factor = gamma * inverse
    slope = factor * inverse * gamma_sum / count
    level = factor * beta_sum / count - mean * slope
    for m in range(MEL):
        if copies:
            copies.wait(arrive[m])
        value = valid * (local[m] * factor - pre[m] * slope - level)
        grad[m] = value.astype(BF)
        own_grad[m] = (value * own).astype(BF)
    if copies:
        copies.wait(side)
    for tap in (1, 4, 7, 0, 3, 6, 2, 5, 8):
        a, b = tap // 3, tap % 3
        low = max(0, 1 - b)
        high = min(MEL, MEL + 1 - b)
        rows = (high - low) * g.win
        left = own_grad[low:high].reshape(rows, c)
        right = x3[low + b - 1 : high + b - 1, :, a * depth : (a + 1) * depth].reshape(rows, depth)
        term = dot(left, right, ((0,), (0,))).astype(BF)
        for z in range(g.nch):
            for s in range(2):
                for p in range(g.planes):
                    at = z * g.co + g.row_of(s, p)
                    terms[s, z, p, tap] = term[at : at + g.rows]
    give[...] = terms[1 - here.core]


def terms_of(g, lens, got, table, pre, local, x3, after, depth, norm, near, name):
    body = functools.partial(terms_kernel, g, depth, norm, near)
    shape = (g.nch, g.planes, 9, g.rows, depth)
    out = [
        arr((MEL, g.win, g.cm), BF),
        arr((8, g.cm), F32),
        arr((8, 128), F32),
        arr((2, *shape), BF),
        arr(shape, BF),
    ]
    scratch = [pltpu.VMEM((MEL, g.win, g.cm), BF)]
    got, table, local = keep_near(got, table, local)
    if near:
        pre, x3 = keep_near(pre, x3)
    else:
        scratch += [
            pltpu.VMEM((MEL, g.win, g.cm), F32),
            pltpu.VMEM((MEL, g.win, 3 * depth), BF),
            sems(MEL + 1),
        ]
    far = VMEM if near else ANY
    args = [lens, got, table, pre, local, x3, after]
    ins = [SMEM, VMEM, VMEM, far, VMEM, far, ANY]
    flops = 2 * 9 * MEL * g.win * g.cm * depth
    return call(body, out, ins, args, scratch, 20, flops, 15 * MIB, name)


def back_kernel(g, lens, table, grad, pre1_in, w, misc2, misc3, local1, pay, g3, pre1, sem):
    here = Here(g, lens)
    copies = Copies(sem)
    arrive = [copies.start(pre1_in.at[m], pre1.at[m]) for m in range(MEL)]
    c = g.cm
    valid, own = row_masks(g, here, c)
    t = table[...]

    def row(i):
        return t[i : i + 1]

    for m in range(MEL):
        low = grad[m]
        before, after = shifted(low.astype(F32))
        side_by_side(g3, m, low, c, after, before)
    inverse, less = row(INV1), -row(MEAN1) * row(INV1)
    half_gamma, half_beta = 0.5 * row(GAMMA1), 0.5 * row(BETA1)
    half_valid = 0.5 * valid
    beta_sum = gamma_sum = jnp.zeros((1, c), F32)
    for low in range(0, MEL, GROUP):
        for m, given in enumerate(conv_back_rows(g, g3, w, low, low + GROUP), low):
            copies.wait(arrive[m])
            scaled = pre1[m] * inverse + less
            half = scaled * half_gamma + half_beta
            bend = jnp.tanh(half)
            local = given * half_valid * ((1.0 + bend) * (1.0 + half * (1.0 - bend)))
            local1[m] = local
            kept = local * own
            beta_sum = beta_sum + sum_rows(kept)
            gamma_sum = gamma_sum + sum_rows(kept * scaled)
    squares = jnp.concatenate([misc2[0:1], misc3[0:1]], axis=0)
    pay[...] = payload(16, lanes(beta_sum), lanes(gamma_sum), squares)


def back(g, lens, table, grad, pre1, w, misc2, misc3):
    body = functools.partial(back_kernel, g)
    out = [arr((MEL, g.win, g.cm), F32), arr((16, 128), F32)]
    scratch = [
        pltpu.VMEM((MEL, g.win, 3 * g.cm), BF),
        pltpu.VMEM((MEL, g.win, g.cm), F32),
        sems(MEL),
    ]
    near = keep_near(table, grad, w, misc2, misc3)
    args = [lens, near[0], near[1], pre1, *near[2:]]
    flops = 2 * 9 * MEL * g.win * g.cm * g.cm
    ins = [SMEM, VMEM, VMEM, ANY, VMEM, VMEM, VMEM]
    return call(body, out, ins, args, scratch, 24, flops, 20 * MIB, "second_back")


def release_kernel(*refs):
    pass


def release(got, arrays):
    out = [arr(x.shape, x.dtype) for x in arrays]
    ins = [ANY] + [VMEM] * len(arrays)
    aliases = {i + 1: i for i in range(len(arrays))}
    args = [got, *keep_near(*arrays)]
    return call(release_kernel, out, ins, args, [], 2, 0, 1, "release", aliases)


def spectra_kernel(g, lens, grad, after, w, *rest):
    n, c = g.nch, g.cm
    outs, g3, rows, flat = rest[:n], rest[n], rest[n + 1], rest[n + 2]
    here = Here(g, lens)
    for m in range(MEL):
        low = grad[m]
        before, after_ = shifted(low.astype(F32))
        side_by_side(g3, m, low, c, after_, before)
    _, own = row_masks(g, here, g.ci_all)
    for low in range(0, MEL, GROUP):
        for m, total in enumerate(conv_back_rows(g, g3, w, low, low + GROUP), low):
            rows[m] = (total * own).astype(BF)
    order = grid_order()
    for j in range(g.seg // 16):
        at = pl.ds(aligned(here.off + 16 * j), 16)
        block = jnp.concatenate([rows[m, at, :] for m in range(MEL)], axis=0)
        flat[:, 128 * j : 128 * (j + 1)] = dot(block, order, ((0,), (0,))).astype(BF)
    for k in range(n):
        outs[k][...] = flat[pl.ds(aligned((here.z ^ k) * g.ci), g.ci), :]


def spectra_back(g, lens, grad, after, w):
    n = g.nch
    body = functools.partial(spectra_kernel, g)
    out = [arr((g.ci, g.seg * MEL), BF)] * n
    scratch = [
        pltpu.VMEM((MEL, g.win, 3 * g.cm), BF),
        pltpu.VMEM((MEL, g.win, g.ci_all), BF),
        pltpu.VMEM((g.ci_all, g.seg * MEL), BF),
    ]
    grad, w = keep_near(grad, w)
    args = [lens, grad, after, w]
    flops = 2 * 9 * MEL * g.win * g.cm * g.ci_all
    ins = [SMEM, VMEM, ANY, VMEM]
    return call(body, out, ins, args, scratch, 16, flops, 5 * MIB, "spectra_back")


def place_kernel(g, width, *rest):
    n = g.nch
    parts, out = rest[:n], rest[n]
    z = lax.axis_index("chan")
    for k in range(n):
        source = z ^ k
        for zz in range(n):

            @pl.when(source == zz)
            def _():
                at = zz % g.segs * width
                out[zz // g.segs, :, at : at + width] = parts[k][...].astype(out.dtype)


def place(g, parts, dtype, name):
    channels, width = parts[0].shape
    return pl.pallas_call(
        functools.partial(place_kernel, g, width),
        out_shape=jax.ShapeDtypeStruct((g.clips, channels, g.segs * width), dtype),
        in_specs=[VMEM] * g.nch,
        out_specs=VMEM,
        compiler_params=pltpu.CompilerParams(vmem_limit_bytes=8 * MIB),
        name=name,
    )(*parts)


def core_sum_kernel(g, terms, got, after, stay, go):
    d, z = lax.axis_index("dp"), lax.axis_index("chan")
    core, plane = lax.rem(d, 2), lax.rem(d, g.pieces) // 2
    half = g.planes // 2
    for e in range(g.planes):
        at = plane ^ g.plane_of(core, e)
        for k in range(g.nch):
            source = z ^ g.zed_of(k)
            value = terms[core, source, at].astype(F32) + got[source, at].astype(F32)
            to = stay if e < half else go
            to[(e % half) * g.nch + k] = value.astype(BF)


def core_sum(g, terms, got, after, name):
    shape = (g.planes // 2 * g.nch, *got.shape[2:])
    return pl.pallas_call(
        functools.partial(core_sum_kernel, g),
        out_shape=[pltpu.VMEM(shape, BF)] * 2,
        in_specs=[VMEM, VMEM, ANY],
        out_specs=[VMEM] * 2,
        compiler_params=pltpu.CompilerParams(vmem_limit_bytes=16 * MIB),
        name=name,
    )(keep_near(terms)[0], got, after)


def halve_kernel(stay, got, after, *outs):
    n = stay.shape[0]
    for i in range(n):
        value = stay[i].astype(F32) + got[i].astype(F32)
        if n == 1:
            outs[0][...] = value.astype(BF)
        else:
            outs[i // (n // 2)][i % (n // 2)] = value.astype(BF)


def halve(stay, got, after, name):
    n = stay.shape[0]
    if n == 1:
        out = [jax.ShapeDtypeStruct(stay.shape[1:], BF)]
    else:
        out = [jax.ShapeDtypeStruct((n // 2, *stay.shape[1:]), BF)] * 2
    return pl.pallas_call(
        halve_kernel,
        out_shape=out,
        in_specs=[VMEM, VMEM, ANY],
        out_specs=[VMEM] * len(out),
        compiler_params=pltpu.CompilerParams(vmem_limit_bytes=8 * MIB),
        name=name,
    )(stay, got, after)


def spread_kernel(g, *rest):
    parts, out = rest[:-1], rest[-1]
    d = lax.axis_index("dp")
    core, plane = lax.rem(d, 2), lax.rem(d, g.pieces) // 2
    for side in range(2):
        c = core if side == 0 else 1 - core
        for e in range(g.planes):
            at = aligned(g.row_of(c, plane ^ g.plane_of(c, e)))
            out[:, pl.ds(at, g.rows), :] = parts[side * g.planes + e][...].astype(F32)


def spread_out(g, parts, depth, name):
    return pl.pallas_call(
        functools.partial(spread_kernel, g),
        out_shape=jax.ShapeDtypeStruct((9, g.co, depth), F32),
        in_specs=[VMEM] * g.pieces,
        out_specs=VMEM,
        compiler_params=pltpu.CompilerParams(vmem_limit_bytes=12 * MIB),
        name=name,
    )(*parts)


class Links:
    def __init__(self, g):
        self.g = g

    def core(self, x):
        return lax.ppermute(x, "dp", [(i, i ^ 1) for i in range(self.g.ndp)])

    def dp(self, x, bit):
        return lax.ppermute(x, "dp", [(i, i ^ bit) for i in range(self.g.ndp)])

    def plane(self, x, turn):
        g = self.g
        return lax.ppermute(x, "dp", [(i, i ^ (2 * g.mask(i & 1, turn))) for i in range(g.ndp)])

    def chan(self, x, k):
        return lax.ppermute(x, "chan", [(i, i ^ k) for i in range(self.g.nch)])

    def exchange(self, parts):
        return [parts[0]] + [self.chan(parts[k], k) for k in range(1, self.g.nch)]

    def gather_planes(self, x):
        have = [x]
        for turn in reversed(range(self.g.turns)):
            have = have + [self.plane(h, turn) for h in have]
        return have

    def gather_cores(self, have):
        return have + [self.core(h) for h in have]

    def gather_plane(self, x):
        return self.gather_cores(self.gather_planes(x))


def everyone(x):
    return lax.all_to_all(x, ("dp", "chan"), 0, 0)


def make_body(ndp, nch):
    def body(
        spectra, lengths, weight_in, gamma_in, beta_in, weight_mid, gamma_mid, beta_mid, cotangent
    ):
        g = Geometry(
            ndp,
            nch,
            spectra.shape[0],
            spectra.shape[2] // MEL,
            weight_in.shape[2],
            weight_mid.shape[2],
        )
        links = Links(g)
        gains = jnp.stack([gamma_in, beta_in, gamma_mid, beta_mid])
        gains = jnp.pad(gains, ((0, 0), (0, 128 - g.co)))

        piece = cut_weights(g, weight_in, weight_mid)
        pieces_in, pieces_mid = sort_pieces(g, [links.chan(piece, k) for k in range(1, nch)])
        maps = lax.all_to_all(cut_maps(g, spectra, pieces_in), "chan", 0, 0)
        w_in = join(g, weight_in, links.gather_plane(pieces_in), g.ci_all, "join_in")
        planes_mid = links.gather_planes(pieces_mid)

        pre1, x3_in, pay = first(g, lengths, gains, maps, w_in, planes_mid[-1])
        got = everyone(pay)
        w_mid = join(g, weight_mid, links.gather_cores(planes_mid), g.cm, "join_mid")
        cs = links.exchange(cut_cot(g, cotangent, got))
        pre2, x3_mid, table, pay, misc2 = second(g, lengths, got, pre1, w_mid)
        got = everyone(fan(g, pay, *cs[1:]))
        pooled, local2, table, pay, misc3 = pool(g, lengths, got, table, pre2, cs)
        got = everyone(pay)
        pooled = links.exchange(release(got, pooled))
        grad2, sums2, _, terms_mid, give_mid = terms_of(
            g, lengths, got, table, pre2, local2, x3_mid, got, g.cm, (MEAN2, INV2, GAMMA2), True, "weight_mid_terms"
        )
        got_mid = links.core(give_mid)
        local1, pay = back(g, lengths, table, grad2, pre1, w_mid, misc2, misc3)
        stay_mid, go_mid = core_sum(g, terms_mid, got_mid, pay, "mid_core_sum")
        block_out = place(g, pooled, BF, "place_pooled")
        got = everyone(fan(g, pay, stay_mid, block_out))
        grad1, sums1, roots, terms_in, give_in = terms_of(
            g, lengths, got, table, pre1, local1, x3_in, got, g.ci_all, (MEAN1, INV1, GAMMA1), False, "weight_in_terms"
        )
        got_in = links.core(give_in)

        class Chain:
            def __init__(self, stay, go, depth, name):
                self.stay, self.go, self.depth, self.name = stay, go, depth, name
                self.turns = [functools.partial(links.plane, turn=t) for t in range(g.turns)]
                self.turns += [functools.partial(links.chan, k=1 << t) for t in range(g.zturns)]

            def turn(self, i, after):
                got = self.turns[i](self.go)
                done = halve(self.stay, got, after, f"{self.name}_sum_{i}")
                self.stay, self.go = done if len(done) == 2 else (done[0], None)
                return self.stay

            def out(self):
                bit = g.pieces
                while bit < ndp:
                    got = links.dp(self.stay, bit)
                    self.stay = halve(self.stay[None], got[None], got, self.name + "_rest")[0]
                    bit *= 2
                return spread_out(g, links.gather_plane(self.stay), self.depth, self.name + "_out")

        turns = g.turns + g.zturns
        mid = Chain(stay_mid, go_mid, g.cm, "mid")
        at = mid.turn(0, grad1)
        parts = spectra_back(g, lengths, grad1, at, w_in)
        stay_in, go_in = core_sum(g, terms_in, got_in, parts[0], "in_core_sum")
        inner = Chain(stay_in, go_in, g.ci_all, "in")
        parts = links.exchange(parts)
        spectra_grad = place(g, parts, F32, "place_spectra")
        at = stay_in
        for i in range(turns):
            if i + 1 < turns:
                at = mid.turn(i + 1, at)
            at = inner.turn(i, spectra_grad if i == turns - 1 else at)
        weight_mid_grad = mid.out()
        weight_in_grad = inner.out()
        z = lax.axis_index("chan")

        def share(sums, i):
            return lax.dynamic_slice_in_dim(sums[i], z * g.co, g.co)

        return (
            block_out,
            spectra_grad,
            weight_in_grad,
            share(sums1, 1),
            share(sums1, 0),
            weight_mid_grad,
            share(sums2, 1),
            share(sums2, 0),
            roots[0, :4],
        )

    return body


def solution(mesh):
    placed = (
        P("dp", "chan", None),
        P("dp"),
        P(None, "chan", None),
        P("chan"),
        P("chan"),
        P(None, "chan", None),
        P("chan"),
        P("chan"),
        P("dp", "chan", None),
    )
    return jax.shard_map(
        make_body(mesh.shape["dp"], mesh.shape["chan"]),
        mesh=mesh,
        in_specs=placed,
        out_specs=(
            P("dp", "chan", None),
            P("dp", "chan", None),
            P(None, "chan", None),
            P("chan"),
            P("chan"),
            P(None, "chan", None),
            P("chan"),
            P("chan"),
            P(),
        ),
        check_vma=False,
    )
```

```python
import functools

import jax
import jax.numpy as jnp
from jax import lax
from jax.experimental import pallas as pl
from jax.experimental.pallas import tpu as pltpu
from jax.sharding import PartitionSpec as P

MEL = 8
HALO = 16
BF = jnp.bfloat16
F32 = jnp.float32
MIB = 1024 * 1024

VMEM = pl.BlockSpec(memory_space=pltpu.VMEM)
SMEM = pl.BlockSpec(memory_space=pltpu.SMEM)
ANY = pl.BlockSpec(memory_space=pl.ANY)
HBM = pl.BlockSpec(memory_space=pltpu.HBM)


def bits_of(n):
    return n.bit_length() - 1


class Geometry:
    def __init__(self, ndp, nch, clips, frames, c_in, c_mid):
        self.ndp, self.nch, self.ndev = ndp, nch, ndp * nch
        self.clips, self.frames = clips, frames
        self.ci_all, self.cm = c_in, c_mid
        self.ci, self.co = c_in // nch, c_mid // nch
        self.segs = nch // clips
        self.seg = frames // self.segs
        self.win = self.seg + HALO * min(self.segs - 1, 2)
        starts = [min(max(s * self.seg - HALO, 0), frames - self.win) for s in range(self.segs)]
        self.cwin = min(frames, (self.win + 48 + 63) // 64 * 64)
        assert all(min(s // 64 * 64, frames - self.cwin) + self.cwin >= s + self.win for s in starts)
        self.rows = max(16, self.co // ndp)
        self.pieces = self.co // self.rows
        self.planes = self.pieces // 2
        self.turns = bits_of(self.planes)
        self.zturns = bits_of(nch)

    def mask(self, core, turn):
        low, high = 1 << turn, 1 << (self.turns - 1 - turn)
        return low + core * (high - low)

    def plane_of(self, core, e):
        rel = 0
        for t in range(self.turns):
            if (e >> (self.turns - 1 - t)) & 1:
                rel = rel ^ self.mask(core, t)
        return rel

    def row_of(self, core, plane):
        return core * (self.co // 2) + plane * self.rows

    def zed_of(self, e):
        return sum(1 << t for t in range(self.zturns) if (e >> (self.zturns - 1 - t)) & 1)


class Here:
    def __init__(self, g, lens):
        self.z = lax.axis_index("chan")
        self.d = lax.axis_index("dp")
        self.core = lax.rem(self.d, 2)
        self.plane = lax.rem(self.d, g.pieces) // 2
        clip, seg = self.z // g.segs, lax.rem(self.z, g.segs)
        self.length = lens[clip]
        self.start, self.cstart = g_starts(g, seg)
        self.off = seg * g.seg - self.start
        self.qoff = self.start - self.cstart


def g_starts(g, seg):
    start = jnp.clip(seg * g.seg - HALO, 0, g.frames - g.win)
    return start, jnp.minimum(start // 64 * 64, g.frames - g.cwin)


def aligned(x, n=16):
    return pl.multiple_of(x, n)


def dot(a, b, contract):
    return lax.dot_general(a, b, ((contract[0], contract[1]), ((), ())), preferred_element_type=F32)


def call(body, out, ins, args, scratch, limit, flops, nbytes, name, aliases=None):
    return pl.pallas_call(
        body,
        out_shape=[pltpu.VMEM(o.shape, o.dtype) if isinstance(o, jax.ShapeDtypeStruct) else o for o in out],
        in_specs=ins,
        out_specs=[VMEM if isinstance(o, jax.ShapeDtypeStruct) else ANY for o in out],
        scratch_shapes=scratch,
        input_output_aliases=aliases or {},
        compiler_params=pltpu.CompilerParams(vmem_limit_bytes=limit * MIB),
        cost_estimate=pl.CostEstimate(
            flops=int(flops), bytes_accessed=int(nbytes), transcendentals=0
        ),
        name=name,
    )(*args)


def arr(shape, dtype):
    return jax.ShapeDtypeStruct(shape, dtype)


def keep_near(*xs):
    return [pltpu.with_memory_space_constraint(x, pltpu.VMEM) for x in xs]


class Copies:
    def __init__(self, sems):
        self.sems, self.n, self.open = sems, 0, []

    def start(self, src, dst):
        c = pltpu.make_async_copy(src, dst, self.sems.at[self.n])
        self.n += 1
        c.start()
        self.open.append(c)
        return c

    def wait(self, c):
        self.open = [o for o in self.open if o is not c]
        c.wait()

    def wait_all(self, some=None):
        for c in list(self.open if some is None else some):
            self.wait(c)


def sems(n):
    return pltpu.SemaphoreType.DMA((n,))


def row_masks(g, here, width):
    r = lax.broadcasted_iota(jnp.int32, (g.win, 128), 0)
    valid = (r + here.start) < here.length
    own = valid & (r >= here.off) & (r < here.off + g.seg)
    return widen(valid.astype(F32), width), widen(own.astype(F32), width)


def widen(x, width):
    return jnp.concatenate([x] * (width // 128), axis=1)


def shifted(x):
    n = x.shape[0]
    r = lax.broadcasted_iota(jnp.int32, (8, 1), 0)
    before, after = pltpu.roll(x, 1, 0), pltpu.roll(x, n - 1, 0)
    before = jnp.concatenate([jnp.where(r == 0, 0.0, before[:8]), before[8:]], axis=0)
    after = jnp.concatenate([after[:-8], jnp.where(r == 7, 0.0, after[-8:])], axis=0)
    return before, after


def grid_order(rows=16):
    n = MEL * rows
    r = lax.broadcasted_iota(jnp.int32, (n, n), 0)
    c = lax.broadcasted_iota(jnp.int32, (n, n), 1)
    return (c == (r % rows) * MEL + r // rows).astype(BF)


def lanes(vector):
    n = vector.shape[1] // 128
    return jnp.concatenate([vector[:, 128 * i : 128 * (i + 1)] for i in range(n)], axis=0)


def unlanes(rows):
    return jnp.concatenate([rows[i : i + 1] for i in range(rows.shape[0])], axis=1)


def misc_row(*scalars):
    lane = lax.broadcasted_iota(jnp.int32, (1, 128), 1)
    row = jnp.zeros((1, 128), F32)
    for i, s in enumerate(scalars):
        row = jnp.where(lane == i, s, row)
    return row


def pick(row, i):
    lane = lax.broadcasted_iota(jnp.int32, (1, 128), 1)
    return jnp.sum(jnp.where(lane == i, row, 0.0), axis=1, keepdims=True)


def sum_rows(x):
    return jnp.sum(x, axis=0, keepdims=True)


def payload(rows, *parts):
    have = sum(r.shape[0] for r in parts)
    if have < rows:
        parts = (*parts, jnp.zeros((rows - have, 128), F32))
    return jnp.concatenate(parts, axis=0)


def fan_kernel(pay, *rest):
    out = rest[-1]
    out[...] = jnp.broadcast_to(pay[...][None], out.shape)


def fan(g, pay, *after):
    out = [arr((g.ndev, *pay.shape), F32)]
    ins = [VMEM] + [ANY] * len(after)
    return call(fan_kernel, out, ins, [pay, *after], [], 4, 0, 1e5, "fan")[0]


def total_of(g, ref):
    n = g.cm // 128
    block = jnp.sum(ref[:, : 2 * n, :], axis=0)
    return unlanes(block[:n]), unlanes(block[n:])


def misc_of(g, ref):
    return jnp.sum(ref[:, 2 * (g.cm // 128), :], axis=0, keepdims=True)


def side_by_side(x3, m, low, c, first, last):
    x3[m, :, 0:c] = first.astype(BF)
    x3[m, :, c : 2 * c] = low
    x3[m, :, 2 * c : 3 * c] = last.astype(BF)


def cut_weights_kernel(g, w_in, w_mid, out, sem):
    d = lax.axis_index("dp")
    core, plane = lax.rem(d, 2), lax.rem(d, g.pieces) // 2
    rows = pl.ds(aligned(g.row_of(core, plane)), g.rows)
    copies = Copies(sem)
    copies.start(w_in.at[:, rows, :], out.at[:, :, : g.ci_all])
    copies.start(w_mid.at[:, rows, :], out.at[:, :, g.ci_all :])
    copies.wait_all()


def cut_weights(g, w_in, w_mid):
    out = [arr((9, g.rows, g.ci_all + g.cm), BF)]
    args = [in_hbm(w_in), in_hbm(w_mid)]
    body = functools.partial(cut_weights_kernel, g)
    return call(body, out, [ANY] * 2, args, [sems(2)], 4, 0, 4e5, "cut_weights")[0]


def stack_kernel(*refs):
    for k, r in enumerate(refs[:-1]):
        refs[-1][k] = r[...]


def stack(parts, name):
    out = [arr((len(parts), *parts[0].shape), parts[0].dtype)]
    return call(stack_kernel, out, [VMEM] * len(parts), parts, [], 4, 0, 1e6, name)[0]


def cut_maps_kernel(g, spec, after, *rest):
    n = g.nch
    xs, sem = rest[:n], rest[n]
    z = lax.axis_index("chan")
    copies = Copies(sem)
    for k in range(n):
        to = z ^ k
        clip, seg = to // g.segs, lax.rem(to, g.segs)
        start, _ = g_starts(g, seg)
        copies.start(spec.at[clip, :, pl.ds(aligned(start * MEL, 128), g.win * MEL)], xs[k])
    copies.wait_all()


def cut_maps(g, spec, after):
    n = g.nch
    out = [arr((g.ci, g.win * MEL), BF)] * n
    body = functools.partial(cut_maps_kernel, g)
    return call(body, out, [ANY] * 2, [in_hbm(spec), after], [sems(n)], 4, 0, 2e6, "cut_maps")


def cut_cot_kernel(g, cot, after, *rest):
    n = g.nch
    cs, sem = rest[:n], rest[n]
    z = lax.axis_index("chan")
    copies = Copies(sem)
    for k in range(n):
        to = z ^ k
        clip, seg = to // g.segs, lax.rem(to, g.segs)
        _, cstart = g_starts(g, seg)
        copies.start(cot.at[clip, :, pl.ds(aligned(cstart * 2, 128), g.cwin * 2)], cs[k])
    copies.wait_all()


def cut_cot(g, cot, after):
    n = g.nch
    out = [arr((g.co, g.cwin * 2), BF)] * n
    body = functools.partial(cut_cot_kernel, g)
    return call(body, out, [ANY] * 2, [in_hbm(cot), after], [sems(n)], 4, 0, 1e6, "cut_cotangent")


def in_hbm(x):
    return pltpu.with_memory_space_constraint(x, pltpu.HBM)


def join_kernel(g, own_in, own_mid, *rest):
    parts, w_in, w_mid = rest[:-2], rest[-2], rest[-1]
    z, d = lax.axis_index("chan"), lax.axis_index("dp")
    mine, plane = lax.rem(d, 2), lax.rem(d, g.pieces) // 2
    w_in[:, pl.ds(aligned(z * g.co), g.co), :] = own_in[...]
    w_mid[:, pl.ds(aligned(z * g.co), g.co), :] = own_mid[...]
    for side in range(2):
        core = mine if side == 0 else 1 - mine
        for e in range(g.planes):
            row = g.row_of(core, plane ^ g.plane_of(core, e))
            for k in range(1, g.nch):
                at = pl.ds(aligned((z ^ k) * g.co + row), g.rows)
                part = parts[side * g.planes + e]
                w_in[:, at, :] = part[k - 1, :, :, : g.ci_all]
                w_mid[:, at, :] = part[k - 1, :, :, g.ci_all :]


def join(g, own_in, own_mid, parts):
    body = functools.partial(join_kernel, g)
    args = [own_in, own_mid, *parts]
    ins = [VMEM] * len(args)
    out = [arr((9, g.cm, g.ci_all), BF), arr((9, g.cm, g.cm), BF)]
    return call(body, out, ins, args, [], 8, 0, 4 * MIB, "join")


def convolve(g, v3, w, part, back, finish, carry):
    def taps(t):
        b = 2 - t if back else t
        return jnp.concatenate([w[b], w[3 + b], w[6 + b]], axis=0 if back else 1)

    contract = ((1,), (0,)) if back else ((1,), (1,))
    depth = v3.shape[2]

    def times(first, n, t):
        return dot(v3[pl.ds(first, n)].reshape(n * g.win, depth), taps(t), contract)

    def step(i, carry):
        part[pl.ds(3 * i + 1, 3)] = times(5 * i, 3, 2 * i).reshape(3, g.win, part.shape[2])
        part[7 * i] = jnp.zeros(part.shape[1:], F32)
        total = times(4 * i, 4, 1) + times(1 + 2 * i, 4, 2 - 2 * i)
        for k in range(4):
            m = 4 * i + k
            carry = finish(m, part[m] + total[k * g.win : (k + 1) * g.win], carry)
        return carry

    return lax.fori_loop(0, 2, step, carry)


def convolve_sums(g, here, x3, w, pre):
    _, own = row_masks(g, here, g.cm)

    def finish(m, total, sums):
        pre[m] = total
        kept = total * own
        return sums[0] + sum_rows(kept), sums[1] + sum_rows(kept * total)

    zero = jnp.zeros((1, g.cm), F32)
    return convolve(g, x3, w, pre, False, finish, (zero, zero))


def first_kernel(g, lens, gains, w, *rest):
    xs, (pre, x3, pay, maps) = rest[: g.nch], rest[g.nch :]
    here = Here(g, lens)
    c = g.ci_all
    for k in range(g.nch):
        maps[pl.ds(aligned((here.z ^ k) * g.ci), g.ci), :] = xs[k][...]
    order = grid_order()
    row = lax.broadcasted_iota(jnp.int32, (MEL * 16, 128), 0) % 16

    def place_cells(j, square):
        cells = maps[:, 128 * j : 128 * (j + 1)]
        frame = row + 16 * j
        valid = (frame + here.start) < here.length
        own = (frame >= here.off) & (frame < here.off + g.seg)
        block = dot(order, cells, ((1,), (1,))) * widen(valid.astype(F32), c)
        x3[:, 16 * j : 16 * (j + 1), c : 2 * c] = block.astype(BF).reshape(MEL, 16, c)
        return square + sum_rows(block * block * widen(own.astype(F32), c))

    square = jnp.zeros((1, c), F32)
    for j in range(g.win // 16):
        square = place_cells(j, square)
    for m in range(MEL):
        before, after_ = shifted(x3[m, :, c : 2 * c].astype(F32))
        x3[m, :, 0:c] = before.astype(BF)
        x3[m, :, 2 * c : 3 * c] = after_.astype(BF)

    one, two = convolve_sums(g, here, x3, w, pre)
    frame_total = 0
    pair_total = 0
    for i in range(g.clips):
        frame_total = frame_total + lens[i]
        pair_total = pair_total + (lens[i] + 1) // 2
    row = misc_row(
        frame_total.astype(F32), pair_total.astype(F32), jnp.sum(square, axis=1, keepdims=True)
    )
    pay[...] = payload(16, lanes(one), lanes(two), row, gains[...])


def first(g, lens, gains, maps, w):
    body = functools.partial(first_kernel, g)
    out = [
        arr((MEL, g.win, g.cm), F32),
        arr((MEL, g.win, 3 * g.ci_all), BF),
        arr((16, 128), F32),
    ]
    args = [lens, gains, *keep_near(w, *maps)]
    ins = [SMEM] + [VMEM] * (2 + g.nch)
    flops = 2 * 9 * MEL * g.win * g.ci_all * g.cm
    scratch = [pltpu.VMEM((g.ci_all, g.win * MEL), BF)]
    return call(body, out, ins, args, scratch, 10, flops, 10 * MIB, "first_conv")


MEAN1, INV1, GAMMA1, BETA1, GAMMA2, BETA2, COUNT, PAIRS, SQ0, MEAN2, INV2 = range(11)
TABLE = 16


def half_affine(mean, inverse, gamma, beta):
    scale = 0.5 * gamma * inverse
    return scale, 0.5 * beta - mean * scale


def second_kernel(g, lens, got, pre1, w, pre, x3, table, pay, misc_out):
    here = Here(g, lens)
    c = g.cm
    valid, own = row_masks(g, here, c)
    one, two = total_of(g, got)
    misc = misc_of(g, got)
    count = MEL * pick(misc, 0) / g.nch
    pairs = (MEL // 2) * pick(misc, 1) / g.nch
    at = 2 * (c // 128) + 1
    vectors = [
        jnp.concatenate([got[zz, at + i : at + i + 1, : g.co] for zz in range(g.nch)], axis=1)
        for i in range(4)
    ]
    mean = one / count
    inverse = lax.rsqrt(two / count - mean * mean + 1e-05)
    wide = jnp.zeros((1, c), F32)
    table[...] = jnp.concatenate(
        [mean, inverse, *vectors, wide + count, wide + pairs, wide + pick(misc, 2)]
        + [wide] * (TABLE - 9),
        axis=0,
    )
    scale, shift = half_affine(mean, inverse, vectors[0], vectors[1])


    def activate(m, square):
        half = pre1[m] * scale + shift
        act = half * (1.0 + jnp.tanh(half)) * valid
        low = act.astype(BF)
        before, after = shifted(low.astype(F32))
        side_by_side(x3, m, low, c, before, after)
        return square + sum_rows(act * act * own)

    square = lax.fori_loop(0, MEL, activate, jnp.zeros((1, c), F32))
    one, two = convolve_sums(g, here, x3, w, pre)
    pay[...] = payload(8, lanes(one), lanes(two))
    misc_out[...] = payload(8, misc_row(jnp.sum(square, axis=1, keepdims=True)))


def second(g, lens, got, pre1, w):
    body = functools.partial(second_kernel, g)
    out = [
        arr((MEL, g.win, g.cm), F32),
        arr((MEL, g.win, 3 * g.cm), BF),
        arr((TABLE, g.cm), F32),
        arr((8, 128), F32),
        arr((8, 128), F32),
    ]
    args = [lens, *keep_near(got, pre1, w)]
    flops = 2 * 9 * MEL * g.win * g.cm * g.cm
    ins = [SMEM, VMEM, VMEM, VMEM]
    return call(body, out, ins, args, [], 10, flops, 17 * MIB, "second_conv")


def pool_kernel(g, lens, got, old_ref, pre2, *rest):
    n, c = g.nch, g.cm
    cs, outs = rest[:n], rest[n : 2 * n]
    local_ref, table, pay, misc_out, held, grads, pooled_ref, flat = rest[2 * n :]
    here = Here(g, lens)
    for k in range(n):
        held[pl.ds(aligned((here.z ^ k) * g.co), g.co), :] = cs[k][...]
    r = lax.broadcasted_iota(jnp.int32, (256, 128), 0)
    l = lax.broadcasted_iota(jnp.int32, (256, 128), 1)
    spread = (l == (r % 64) // 2 * 4 + r // 64).astype(BF)

    @pl.loop(0, g.cwin // 64)
    def _(j):
        cells = held[:, pl.ds(aligned(128 * j, 128), 128)]
        block = dot(spread, cells, ((1,), (1,)))
        grads[:, pl.ds(aligned(64 * j), 64), :] = block.reshape(MEL // 2, 64, c)

    one, two = total_of(g, got)
    old = old_ref[...]
    count = old[COUNT : COUNT + 1]
    mean = one / count
    inverse = lax.rsqrt(two / count - mean * mean + 1e-05)
    wide = jnp.zeros((1, c), F32)
    table[...] = jnp.concatenate([old[:MEAN2], mean, inverse] + [wide] * (TABLE - 11), axis=0)
    half_gamma, half_beta = 0.5 * old[GAMMA2 : GAMMA2 + 1], 0.5 * old[BETA2 : BETA2 + 1]
    less = -mean * inverse
    valid, own = row_masks(g, here, c)
    r = lax.broadcasted_iota(jnp.int32, (g.win, 128), 0) + here.start
    share = widen(jnp.where(here.length - r // 2 * 2 >= 2, 0.25, 0.5), c)
    half_share = 0.5 * share * valid
    window = pl.ds(aligned(here.qoff), g.win)
    segment = pl.ds(aligned(here.off), g.seg)

    def step(k, sums):
        beta_sum, gamma_sum, square = sums
        given = grads[k, window, :] * half_share
        pair = None
        for i in range(2):
            m = 2 * k + i
            scaled = pre2[m] * inverse + less
            half = scaled * half_gamma + half_beta
            bend = jnp.tanh(half)
            twice = 1.0 + bend
            act = half * twice * own
            square = square + sum_rows(act * act)
            local = given * (twice * (1.0 + half * (1.0 - bend)))
            local_ref[m] = local
            kept = local * own
            beta_sum = beta_sum + sum_rows(kept)
            gamma_sum = gamma_sum + sum_rows(kept * scaled)
            pair = act if pair is None else pair + act
        pooled_ref[k] = pair * share
        return beta_sum, gamma_sum, square

    zero = jnp.zeros((1, c), F32)
    beta_sum, gamma_sum, square = lax.fori_loop(0, MEL // 2, step, (zero, zero, zero))
    wide_rows = (MEL // 2) * g.seg
    values = jnp.concatenate([pooled_ref[k, segment, :] for k in range(MEL // 2)], axis=0)
    high = values.astype(BF)
    low = (values - high.astype(F32)).astype(BF)
    r = lax.broadcasted_iota(jnp.int32, (wide_rows, 2 * g.seg), 0)
    l = lax.broadcasted_iota(jnp.int32, (wide_rows, 2 * g.seg), 1)
    gather = (l == (r % g.seg) // 2 * 4 + r // g.seg).astype(BF)
    pooled = dot(high, gather, ((0,), (0,))) + dot(low, gather, ((0,), (0,)))
    flat[...] = pooled.astype(BF)
    for k in range(n):
        outs[k][...] = flat[pl.ds(aligned((here.z ^ k) * g.co), g.co), :]
    pooled_square = sum_rows(jnp.sum(pooled * pooled, axis=1, keepdims=True))
    block = payload(8, lanes(beta_sum), lanes(gamma_sum))
    pay[...] = jnp.broadcast_to(block[None], pay.shape)
    misc_out[...] = payload(8, misc_row(jnp.sum(square, axis=1, keepdims=True), pooled_square))


def pool(g, lens, got, table, pre2, cs):
    n = g.nch
    body = functools.partial(pool_kernel, g)
    out = [arr((g.co, 2 * g.seg), BF)] * n + [
        arr((MEL, g.win, g.cm), F32),
        arr((TABLE, g.cm), F32),
        arr((g.ndev, 8, 128), F32),
        arr((8, 128), F32),
    ]
    scratch = [
        pltpu.VMEM((g.cm, g.cwin * 2), BF),
        pltpu.VMEM((MEL // 2, g.cwin, g.cm), F32),
        pltpu.VMEM((MEL // 2, g.win, g.cm), F32),
        pltpu.VMEM((g.cm, 2 * g.seg), BF),
    ]
    args = [lens, *keep_near(got, table, pre2, *cs)]
    ins = [SMEM] + [VMEM] * (len(args) - 1)
    out = call(body, out, ins, args, scratch, 12, 4e9, 8 * MIB, "pool")
    return out[:n], *out[n:]


def terms_kernel(g, depth, norm, lens, got, table, pre, local, x3, after, *rest):
    grad, sums, roots, terms, give, own_grad = rest
    here = Here(g, lens)
    c = g.cm
    valid, own = row_masks(g, here, c)
    beta_sum, gamma_sum = total_of(g, got)
    t = table[...]
    mean, inverse, gamma = (t[i : i + 1] for i in norm)
    count = t[COUNT : COUNT + 1]
    sums[...] = jnp.concatenate([beta_sum, gamma_sum] + [jnp.zeros((1, c), F32)] * 6, axis=0)
    if got.shape[1] > 8:
        at = 2 * (c // 128)
        square1 = pick(jnp.sum(got[:, at, :], axis=0, keepdims=True), 0)
        later = jnp.sum(got[:, at + 1, :], axis=0, keepdims=True)
        tops = misc_row(pick(t[SQ0 : SQ0 + 1, :128], 0), square1, pick(later, 0), pick(later, 1))
        lane = lax.broadcasted_iota(jnp.int32, (1, 128), 1)
        cells, pairs = count[:, :128], t[PAIRS : PAIRS + 1, :128]
        under = jnp.where(lane == 0, cells * g.ci_all, jnp.where(lane == 3, pairs * c, cells * c))
        roots[...] = jnp.broadcast_to(jnp.sqrt(tops / under), (8, 128))
    factor = gamma * inverse
    slope = factor * inverse * gamma_sum / count
    level = factor * beta_sum / count - mean * slope

    @pl.loop(0, MEL)
    def _(m):
        value = valid * (local[m] * factor - pre[m] * slope - level)
        grad[m] = value.astype(BF)
        own_grad[m] = (value * own).astype(BF)

    @pl.loop(0, 3)
    def _(a):
        lanes_of = pl.ds(aligned(a * depth, 128), depth)
        for b in (1, 0, 2):
            low = max(0, 1 - b)
            high = min(MEL, MEL + 1 - b)
            rows = (high - low) * g.win
            left = own_grad[low:high].reshape(rows, c)
            right = x3[low + b - 1 : high + b - 1, :, lanes_of].reshape(rows, depth)
            term = dot(left, right, ((0,), (0,))).astype(BF)
            for z in range(g.nch):
                for s in range(2):
                    for p in range(g.planes):
                        at = z * g.co + g.row_of(s, p)
                        terms[s, z, p, 3 * a + b] = term[at : at + g.rows]

    give[...] = terms[1 - here.core]


def terms_of(g, lens, got, table, pre, local, x3, after, depth, norm, name):
    body = functools.partial(terms_kernel, g, depth, norm)
    shape = (g.nch, g.planes, 9, g.rows, depth)
    out = [
        arr((MEL, g.win, g.cm), BF),
        arr((8, g.cm), F32),
        arr((8, 128), F32),
        arr((2, *shape), BF),
        arr(shape, BF),
    ]
    scratch = [pltpu.VMEM((MEL, g.win, g.cm), BF)]
    args = [lens, *keep_near(got, table, pre, local, x3), after]
    ins = [SMEM] + [VMEM] * 5 + [ANY]
    flops = 2 * 9 * MEL * g.win * g.cm * depth
    return call(body, out, ins, args, scratch, 10, flops, 15 * MIB, name)


def back_kernel(g, lens, table, grad, pre1, w, misc2, misc3, local1, pay, g3):
    here = Here(g, lens)
    c = g.cm
    valid, own = row_masks(g, here, c)
    t = table[...]

    def row(i):
        return t[i : i + 1]


    @pl.loop(0, MEL)
    def _(m):
        low = grad[m]
        before, after = shifted(low.astype(F32))
        side_by_side(g3, m, low, c, after, before)

    inverse, less = row(INV1), -row(MEAN1) * row(INV1)
    half_gamma, half_beta = 0.5 * row(GAMMA1), 0.5 * row(BETA1)
    half_valid = 0.5 * valid

    def finish(m, given, sums):
        scaled = pre1[m] * inverse + less
        half = scaled * half_gamma + half_beta
        bend = jnp.tanh(half)
        local = given * half_valid * ((1.0 + bend) * (1.0 + half * (1.0 - bend)))
        local1[m] = local
        kept = local * own
        return sums[0] + sum_rows(kept), sums[1] + sum_rows(kept * scaled)

    zero = jnp.zeros((1, c), F32)
    beta_sum, gamma_sum = convolve(g, g3, w, local1, True, finish, (zero, zero))
    squares = jnp.concatenate([misc2[0:1], misc3[0:1]], axis=0)
    pay[...] = payload(16, lanes(beta_sum), lanes(gamma_sum), squares)


def back(g, lens, table, grad, pre1, w, misc2, misc3):
    body = functools.partial(back_kernel, g)
    out = [arr((MEL, g.win, g.cm), F32), arr((16, 128), F32)]
    scratch = [pltpu.VMEM((MEL, g.win, 3 * g.cm), BF)]
    args = [lens, *keep_near(table, grad, pre1, w, misc2, misc3)]
    flops = 2 * 9 * MEL * g.win * g.cm * g.cm
    ins = [SMEM] + [VMEM] * 6
    return call(body, out, ins, args, scratch, 14, flops, 20 * MIB, "second_back")


def release_kernel(*refs):
    pass


def release(gates, arrays):
    out = [arr(x.shape, x.dtype) for x in arrays]
    n = len(gates)
    ins = [ANY] * n + [VMEM] * len(arrays)
    aliases = {i + n: i for i in range(len(arrays))}
    args = [*gates, *keep_near(*arrays)]
    return call(release_kernel, out, ins, args, [], 2, 0, 1, "release", aliases)


def spectra_kernel(g, lens, grad, after, w, *rest):
    n, c = g.nch, g.cm
    outs, (g3, rows, flat, part) = rest[:n], rest[n:]
    here = Here(g, lens)

    @pl.loop(0, MEL)
    def _(m):
        low = grad[m]
        before, after_ = shifted(low.astype(F32))
        side_by_side(g3, m, low, c, after_, before)

    _, own = row_masks(g, here, g.ci_all)

    def finish(m, total, carry):
        rows[m] = (total * own).astype(BF)
        return carry

    convolve(g, g3, w, part, True, finish, 0)
    order = grid_order()

    for j in range(g.seg // 16):
        block = rows[:, pl.ds(aligned(here.off + 16 * j), 16), :].reshape(MEL * 16, g.ci_all)
        flat[:, 128 * j : 128 * (j + 1)] = dot(block, order, ((0,), (0,))).astype(BF)

    for k in range(n):
        outs[k][...] = flat[pl.ds(aligned((here.z ^ k) * g.ci), g.ci), :]


def spectra_back(g, lens, grad, after, w):
    n = g.nch
    body = functools.partial(spectra_kernel, g)
    out = [arr((g.ci, g.seg * MEL), BF)] * n
    scratch = [
        pltpu.VMEM((MEL, g.win, 3 * g.cm), BF),
        pltpu.VMEM((MEL, g.win, g.ci_all), BF),
        pltpu.VMEM((g.ci_all, g.seg * MEL), BF),
        pltpu.VMEM((MEL, g.win, g.ci_all), F32),
    ]
    grad, w = keep_near(grad, w)
    args = [lens, grad, after, w]
    flops = 2 * 9 * MEL * g.win * g.cm * g.ci_all
    ins = [SMEM, VMEM, ANY, VMEM]
    return call(body, out, ins, args, scratch, 14, flops, 5 * MIB, "spectra_back")


def place_kernel(g, width, *rest):
    n = g.nch
    parts, out = rest[:n], rest[n]
    z = lax.axis_index("chan")
    for k in range(n):
        source = z ^ k
        for zz in range(n):

            @pl.when(source == zz)
            def _():
                at = zz % g.segs * width
                out[zz // g.segs, :, at : at + width] = parts[k][...].astype(out.dtype)


def place(g, parts, dtype, name):
    channels, width = parts[0].shape
    return pl.pallas_call(
        functools.partial(place_kernel, g, width),
        out_shape=jax.ShapeDtypeStruct((g.clips, channels, g.segs * width), dtype),
        in_specs=[VMEM] * g.nch,
        out_specs=VMEM,
        compiler_params=pltpu.CompilerParams(vmem_limit_bytes=8 * MIB),
        name=name,
    )(*parts)


def core_sum_kernel(g, terms, got, after, stay, go):
    d, z = lax.axis_index("dp"), lax.axis_index("chan")
    core, plane = lax.rem(d, 2), lax.rem(d, g.pieces) // 2
    half = g.planes // 2
    for e in range(g.planes):
        at = plane ^ g.plane_of(core, e)
        for k in range(g.nch):
            source = z ^ g.zed_of(k)
            value = terms[core, source, at].astype(F32) + got[source, at].astype(F32)
            to = stay if e < half else go
            to[(e % half) * g.nch + k] = value.astype(BF)


def core_sum(g, terms, got, after, name):
    shape = (g.planes // 2 * g.nch, *got.shape[2:])
    return pl.pallas_call(
        functools.partial(core_sum_kernel, g),
        out_shape=[pltpu.VMEM(shape, BF)] * 2,
        in_specs=[VMEM, VMEM, ANY],
        out_specs=[VMEM] * 2,
        compiler_params=pltpu.CompilerParams(vmem_limit_bytes=16 * MIB),
        name=name,
    )(keep_near(terms)[0], got, after)


def halve_kernel(stay, got, *rest):
    n = stay.shape[0]
    outs = rest[-2:] if n > 1 else rest[-1:]
    for i in range(n):
        value = stay[i].astype(F32) + got[i].astype(F32)
        if n == 1:
            outs[0][...] = value.astype(BF)
        else:
            outs[i // (n // 2)][i % (n // 2)] = value.astype(BF)


def halve(stay, got, gates, name):
    n = stay.shape[0]
    if n == 1:
        out = [jax.ShapeDtypeStruct(stay.shape[1:], BF)]
    else:
        out = [jax.ShapeDtypeStruct((n // 2, *stay.shape[1:]), BF)] * 2
    return pl.pallas_call(
        halve_kernel,
        out_shape=out,
        in_specs=[VMEM, VMEM] + [ANY] * len(gates),
        out_specs=[VMEM] * len(out),
        compiler_params=pltpu.CompilerParams(vmem_limit_bytes=8 * MIB),
        name=name,
    )(stay, got, *gates)


def spread_kernel(g, *rest):
    parts, out = rest[:-1], rest[-1]
    d = lax.axis_index("dp")
    core, plane = lax.rem(d, 2), lax.rem(d, g.pieces) // 2
    for side in range(2):
        c = core if side == 0 else 1 - core
        for e in range(g.planes):
            at = aligned(g.row_of(c, plane ^ g.plane_of(c, e)))
            out[:, pl.ds(at, g.rows), :] = parts[side * g.planes + e][...].astype(F32)


def spread_out(g, parts, depth, name):
    return pl.pallas_call(
        functools.partial(spread_kernel, g),
        out_shape=jax.ShapeDtypeStruct((9, g.co, depth), F32),
        in_specs=[VMEM] * g.pieces,
        out_specs=VMEM,
        compiler_params=pltpu.CompilerParams(vmem_limit_bytes=12 * MIB),
        name=name,
    )(*parts)


class Links:
    def __init__(self, g):
        self.g = g

    def core(self, x):
        return lax.ppermute(x, "dp", [(i, i ^ 1) for i in range(self.g.ndp)])

    def dp(self, x, bit):
        return lax.ppermute(x, "dp", [(i, i ^ bit) for i in range(self.g.ndp)])

    def plane(self, x, turn):
        g = self.g
        return lax.ppermute(x, "dp", [(i, i ^ (2 * g.mask(i & 1, turn))) for i in range(g.ndp)])

    def chan(self, x, k):
        return lax.ppermute(x, "chan", [(i, i ^ k) for i in range(self.g.nch)])

    def exchange(self, parts):
        return [parts[0]] + [self.chan(parts[k], k) for k in range(1, self.g.nch)]

    def gather_plane(self, x, gates=()):
        have = [x]
        for turn in reversed(range(self.g.turns)):
            last = have[-1]
            if gates and turn == 0 and len(have) > 1:
                (last,) = release(gates, [last])
            have = have + [self.plane(h, turn) for h in (*have[:-1], last)]
        return have + [self.core(h) for h in have]


def everyone(x):
    return lax.all_to_all(x, ("dp", "chan"), 0, 0)


def make_body(ndp, nch):
    def body(
        spectra, lengths, weight_in, gamma_in, beta_in, weight_mid, gamma_mid, beta_mid, cotangent
    ):
        g = Geometry(
            ndp,
            nch,
            spectra.shape[0],
            spectra.shape[2] // MEL,
            weight_in.shape[2],
            weight_mid.shape[2],
        )
        links = Links(g)
        gains = jnp.stack([gamma_in, beta_in, gamma_mid, beta_mid])
        gains = jnp.pad(gains, ((0, 0), (0, 128 - g.co)))

        piece = cut_weights(g, weight_in, weight_mid)
        pieces = stack([links.chan(piece, k) for k in range(1, nch)], "stack_pieces")
        maps = links.exchange(cut_maps(g, spectra, piece))
        cots = cut_cot(g, cotangent, pieces)
        w_in, w_mid = join(g, weight_in, weight_mid, links.gather_plane(pieces, maps[1:]))

        pre1, x3_in, pay = first(g, lengths, gains, maps, w_in)
        got = everyone(fan(g, pay, cots[0]))
        cs = links.exchange(release([got], cots))
        pre2, x3_mid, table, pay, misc2 = second(g, lengths, got, pre1, w_mid)
        got = everyone(fan(g, pay, *cs[1:]))
        pooled, local2, table, pay, misc3 = pool(g, lengths, got, table, pre2, cs)
        got = everyone(pay)
        pooled = links.exchange(release([got], pooled))
        grad2, sums2, _, terms_mid, give_mid = terms_of(
            g, lengths, got, table, pre2, local2, x3_mid, got, g.cm, (MEAN2, INV2, GAMMA2), "weight_mid_terms"
        )
        got_mid = links.core(give_mid)
        local1, pay = back(g, lengths, table, grad2, pre1, w_mid, misc2, misc3)
        stay_mid, go_mid = core_sum(g, terms_mid, got_mid, pay, "mid_core_sum")
        block_out = place(g, pooled, BF, "place_pooled")
        got = everyone(fan(g, pay, stay_mid, block_out))
        (go_mid,) = release([got], [go_mid])
        grad1, sums1, roots, terms_in, give_in = terms_of(
            g, lengths, got, table, pre1, local1, x3_in, got, g.ci_all, (MEAN1, INV1, GAMMA1), "weight_in_terms"
        )
        got_in = links.core(give_in)

        class Chain:
            def __init__(self, stay, go, depth, name):
                self.stay, self.go, self.depth, self.name = stay, go, depth, name
                self.turns = [functools.partial(links.plane, turn=t) for t in range(g.turns)]
                self.turns += [functools.partial(links.chan, k=1 << t) for t in range(g.zturns)]

            def turn(self, i, *gates):
                got = self.turns[i](self.go)
                done = halve(self.stay, got, gates, f"{self.name}_sum_{i}")
                self.stay, self.go = done if len(done) == 2 else (done[0], None)
                return self.stay

            def out(self):
                bit = g.pieces
                while bit < ndp:
                    got = links.dp(self.stay, bit)
                    self.stay = halve(self.stay[None], got[None], [], self.name + "_rest")[0]
                    bit *= 2
                return spread_out(g, links.gather_plane(self.stay), self.depth, self.name + "_out")

        turns = g.turns + g.zturns
        mid = Chain(stay_mid, go_mid, g.cm, "mid")
        parts = spectra_back(g, lengths, grad1, grad1, w_in)
        at = mid.turn(0, parts[0])
        stay_in, go_in = core_sum(g, terms_in, got_in, parts[0], "in_core_sum")
        inner = Chain(stay_in, go_in, g.ci_all, "in")
        parts = links.exchange(parts)
        spectra_grad = place(g, parts, F32, "place_spectra")
        arrivals = [parts[1 : nch - 1], parts[nch - 1 :]]
        for i in range(turns):
            if i + 1 < turns:
                at = mid.turn(i + 1, at, *(arrivals.pop(0) if arrivals else []))
            at = inner.turn(i, at)
        weight_mid_grad = mid.out()
        weight_in_grad = inner.out()
        z = lax.axis_index("chan")

        def share(sums, i):
            return lax.dynamic_slice_in_dim(sums[i], z * g.co, g.co)

        return (
            block_out,
            spectra_grad,
            weight_in_grad,
            share(sums1, 1),
            share(sums1, 0),
            weight_mid_grad,
            share(sums2, 1),
            share(sums2, 0),
            roots[0, :4],
        )

    return body


def solution(mesh):
    placed = (
        P("dp", "chan", None),
        P("dp"),
        P(None, "chan", None),
        P("chan"),
        P("chan"),
        P(None, "chan", None),
        P("chan"),
        P("chan"),
        P("dp", "chan", None),
    )
    return jax.shard_map(
        make_body(mesh.shape["dp"], mesh.shape["chan"]),
        mesh=mesh,
        in_specs=placed,
        out_specs=(
            P("dp", "chan", None),
            P("dp", "chan", None),
            P(None, "chan", None),
            P("chan"),
            P("chan"),
            P(None, "chan", None),
            P("chan"),
            P("chan"),
            P(),
        ),
        check_vma=False,
    )
```

```python
import functools

import jax
import jax.numpy as jnp
from jax import lax
from jax.experimental import pallas as pl
from jax.experimental.pallas import tpu as pltpu
from jax.sharding import PartitionSpec as P

MEL = 8
HALO = 16
BF = jnp.bfloat16
F32 = jnp.float32
MIB = 1024 * 1024
TINY = pl.CostEstimate(flops=1, bytes_accessed=1, transcendentals=0)

VMEM = pl.BlockSpec(memory_space=pltpu.VMEM)
SMEM = pl.BlockSpec(memory_space=pltpu.SMEM)
ANY = pl.BlockSpec(memory_space=pl.ANY)
HBM = pl.BlockSpec(memory_space=pltpu.HBM)


def bits_of(n):
    return n.bit_length() - 1


class Geometry:
    def __init__(self, ndp, nch, clips, frames, c_in, c_mid):
        self.ndp, self.nch, self.ndev = ndp, nch, ndp * nch
        self.clips, self.frames = clips, frames
        self.ci_all, self.cm = c_in, c_mid
        self.ci, self.co = c_in // nch, c_mid // nch
        self.segs = nch // clips
        self.seg = frames // self.segs
        self.win = self.seg + HALO * min(self.segs - 1, 2)
        starts = [min(max(s * self.seg - HALO, 0), frames - self.win) for s in range(self.segs)]
        self.cwin = min(frames, (self.win + 48 + 63) // 64 * 64)
        assert all(min(s // 64 * 64, frames - self.cwin) + self.cwin >= s + self.win for s in starts)
        self.rows = max(16, self.co // ndp)
        self.pieces = self.co // self.rows
        self.planes = self.pieces // 2
        self.turns = bits_of(self.planes)
        self.zturns = bits_of(nch)

    def mask(self, core, turn):
        low, high = 1 << turn, 1 << (self.turns - 1 - turn)
        return low + core * (high - low)

    def plane_of(self, core, e):
        rel = 0
        for t in range(self.turns):
            if (e >> (self.turns - 1 - t)) & 1:
                rel = rel ^ self.mask(core, t)
        return rel

    def row_of(self, core, plane):
        return core * (self.co // 2) + plane * self.rows

    def zed_of(self, e):
        return sum(1 << t for t in range(self.zturns) if (e >> (self.zturns - 1 - t)) & 1)


class Here:
    def __init__(self, g, lens):
        self.z = lax.axis_index("chan")
        self.d = lax.axis_index("dp")
        self.core = lax.rem(self.d, 2)
        self.plane = lax.rem(self.d, g.pieces) // 2
        clip, seg = self.z // g.segs, lax.rem(self.z, g.segs)
        self.length = lens[clip]
        self.start, self.cstart = g_starts(g, seg)
        self.off = seg * g.seg - self.start
        self.qoff = self.start - self.cstart


def g_starts(g, seg):
    start = jnp.clip(seg * g.seg - HALO, 0, g.frames - g.win)
    return start, jnp.minimum(start // 64 * 64, g.frames - g.cwin)


def aligned(x, n=16):
    return pl.multiple_of(x, n)


def dot(a, b, contract):
    return lax.dot_general(a, b, ((contract[0], contract[1]), ((), ())), preferred_element_type=F32)


def call(body, out, ins, args, scratch, limit, flops, nbytes, name, aliases=None):
    return pl.pallas_call(
        body,
        out_shape=[pltpu.VMEM(o.shape, o.dtype) if isinstance(o, jax.ShapeDtypeStruct) else o for o in out],
        in_specs=ins,
        out_specs=[VMEM if isinstance(o, jax.ShapeDtypeStruct) else ANY for o in out],
        scratch_shapes=scratch,
        input_output_aliases=aliases or {},
        compiler_params=pltpu.CompilerParams(vmem_limit_bytes=limit * MIB),
        cost_estimate=pl.CostEstimate(
            flops=int(flops), bytes_accessed=int(nbytes), transcendentals=0
        ),
        name=name,
    )(*args)


def arr(shape, dtype):
    return jax.ShapeDtypeStruct(shape, dtype)


def keep_near(*xs):
    return [pltpu.with_memory_space_constraint(x, pltpu.VMEM) for x in xs]


class Copies:
    def __init__(self, sems):
        self.sems, self.n, self.open = sems, 0, []

    def start(self, src, dst):
        c = pltpu.make_async_copy(src, dst, self.sems.at[self.n])
        self.n += 1
        c.start()
        self.open.append(c)
        return c

    def wait(self, c):
        self.open = [o for o in self.open if o is not c]
        c.wait()

    def wait_all(self, some=None):
        for c in list(self.open if some is None else some):
            self.wait(c)


def sems(n):
    return pltpu.SemaphoreType.DMA((n,))


def row_masks(g, here, width):
    r = lax.broadcasted_iota(jnp.int32, (g.win, 128), 0)
    valid = (r + here.start) < here.length
    own = valid & (r >= here.off) & (r < here.off + g.seg)
    return widen(valid.astype(F32), width), widen(own.astype(F32), width)


def widen(x, width):
    return jnp.concatenate([x] * (width // 128), axis=1)


def shifted(x):
    n = x.shape[0]
    r = lax.broadcasted_iota(jnp.int32, (8, 1), 0)
    before, after = pltpu.roll(x, 1, 0), pltpu.roll(x, n - 1, 0)
    before = jnp.concatenate([jnp.where(r == 0, 0.0, before[:8]), before[8:]], axis=0)
    after = jnp.concatenate([after[:-8], jnp.where(r == 7, 0.0, after[-8:])], axis=0)
    return before, after


def grid_order(rows=16):
    n = MEL * rows
    r = lax.broadcasted_iota(jnp.int32, (n, n), 0)
    c = lax.broadcasted_iota(jnp.int32, (n, n), 1)
    return (c == (r % rows) * MEL + r // rows).astype(BF)


def lanes(vector):
    n = vector.shape[1] // 128
    return jnp.concatenate([vector[:, 128 * i : 128 * (i + 1)] for i in range(n)], axis=0)


def unlanes(rows):
    return jnp.concatenate([rows[i : i + 1] for i in range(rows.shape[0])], axis=1)


def misc_row(*scalars):
    lane = lax.broadcasted_iota(jnp.int32, (1, 128), 1)
    row = jnp.zeros((1, 128), F32)
    for i, s in enumerate(scalars):
        row = jnp.where(lane == i, s, row)
    return row


def pick(row, i):
    lane = lax.broadcasted_iota(jnp.int32, (1, 128), 1)
    return jnp.sum(jnp.where(lane == i, row, 0.0), axis=1, keepdims=True)


def sum_rows(x):
    return jnp.sum(x, axis=0, keepdims=True)


def payload(rows, *parts):
    have = sum(r.shape[0] for r in parts)
    if have < rows:
        parts = (*parts, jnp.zeros((rows - have, 128), F32))
    return jnp.concatenate(parts, axis=0)


def fan_kernel(pay, *rest):
    out = rest[-1]
    out[...] = jnp.broadcast_to(pay[...][None], out.shape)


def fan(g, pay, *after):
    out = [arr((g.ndev, *pay.shape), F32)]
    ins = [VMEM] + [ANY] * len(after)
    return call(fan_kernel, out, ins, [pay, *after], [], 4, 0, 1e5, "fan")[0]


def total_of(g, ref):
    n = g.cm // 128
    block = jnp.sum(ref[:, : 2 * n, :], axis=0)
    return unlanes(block[:n]), unlanes(block[n:])


def misc_of(g, ref):
    return jnp.sum(ref[:, 2 * (g.cm // 128), :], axis=0, keepdims=True)


def side_by_side(x3, m, low, c, first, last):
    x3[m, :, 0:c] = first.astype(BF)
    x3[m, :, c : 2 * c] = low
    x3[m, :, 2 * c : 3 * c] = last.astype(BF)


def cut_weights_kernel(g, w_in, w_mid, out, sem):
    d = lax.axis_index("dp")
    core, plane = lax.rem(d, 2), lax.rem(d, g.pieces) // 2
    rows = pl.ds(aligned(g.row_of(core, plane)), g.rows)
    copies = Copies(sem)
    copies.start(w_in.at[:, rows, :], out.at[:, :, : g.ci_all])
    copies.start(w_mid.at[:, rows, :], out.at[:, :, g.ci_all :])
    copies.wait_all()


def cut_weights(g, w_in, w_mid):
    out = [arr((9, g.rows, g.ci_all + g.cm), BF)]
    args = [in_hbm(w_in), in_hbm(w_mid)]
    body = functools.partial(cut_weights_kernel, g)
    return call(body, out, [ANY] * 2, args, [sems(2)], 4, 0, 4e5, "cut_weights")[0]


def sort_kernel(g, *rest):
    n = g.nch - 1
    parts, first, second = rest[:n], rest[-2], rest[-1]
    for k in range(n):
        first[k] = parts[k][:, :, : g.ci_all]
        second[k] = parts[k][:, :, g.ci_all :]


def sort_pieces(g, parts, gates):
    n = g.nch - 1
    out = [arr((n, 9, g.rows, g.ci_all), BF), arr((n, 9, g.rows, g.cm), BF)]
    body = functools.partial(sort_kernel, g)
    ins = [VMEM] * n + [ANY] * len(gates)
    return call(body, out, ins, [*parts, *gates], [], 4, 0, 1e6, "sort_pieces")


def cut_maps_kernel(g, spec, after, out, held, sem):
    copies = Copies(sem)
    first = []
    for z in range(g.nch):
        start = static_start(g, z % g.segs) * MEL
        first.append(copies.start(spec.at[z // g.segs, :, start : start + g.win * MEL], held.at[z]))
    for z in range(g.nch):
        copies.wait(first[z])
        copies.start(held.at[z], out.at[z])
    copies.wait_all()


def cut_maps(g, spec, after):
    shape = (g.nch, g.ci, g.win * MEL)
    body = functools.partial(cut_maps_kernel, g)
    args = [in_hbm(spec), after]
    scratch = [pltpu.VMEM(shape, BF), sems(2 * g.nch)]
    return call(body, [pltpu.HBM(shape, BF)], [ANY] * 2, args, scratch, 4, 0, 2e6, "cut_maps")[0]


def static_start(g, seg):
    return min(max(seg * g.seg - HALO, 0), g.frames - g.win)


def cut_cot_kernel(g, cot, after, *rest):
    n = g.nch
    cs, sem = rest[:n], rest[n]
    z = lax.axis_index("chan")
    copies = Copies(sem)
    for k in range(n):
        to = z ^ k
        clip, seg = to // g.segs, lax.rem(to, g.segs)
        _, cstart = g_starts(g, seg)
        copies.start(cot.at[clip, :, pl.ds(aligned(cstart * 2, 128), g.cwin * 2)], cs[k])
    copies.wait_all()


def cut_cot(g, cot, after):
    n = g.nch
    out = [arr((g.co, g.cwin * 2), BF)] * n
    body = functools.partial(cut_cot_kernel, g)
    return call(body, out, [ANY] * 2, [in_hbm(cot), after], [sems(n)], 4, 0, 1e6, "cut_cotangent")


def in_hbm(x):
    return pltpu.with_memory_space_constraint(x, pltpu.HBM)


def join_kernel(g, own, *rest):
    parts, w = rest[:-1], rest[-1]
    z, d = lax.axis_index("chan"), lax.axis_index("dp")
    mine, plane = lax.rem(d, 2), lax.rem(d, g.pieces) // 2
    w[:, pl.ds(aligned(z * g.co), g.co), :] = own[...]
    for side in range(2):
        core = mine if side == 0 else 1 - mine
        for e in range(g.planes):
            row = g.row_of(core, plane ^ g.plane_of(core, e))
            for k in range(1, g.nch):
                at = aligned((z ^ k) * g.co + row)
                w[:, pl.ds(at, g.rows), :] = parts[side * g.planes + e][k - 1]


def join(g, own, parts, depth, name):
    body = functools.partial(join_kernel, g)
    args = [*keep_near(own), *parts]
    ins = [VMEM] * len(args)
    return call(body, [arr((9, g.cm, depth), BF)], ins, args, [], 8, 0, 4 * MIB, name)[0]


def convolve(v3, w, part, back, finish, carry, unrolled=False, window=None):
    def taps(t):
        b = 2 - t if back else t
        return jnp.concatenate([w[b], w[3 + b], w[6 + b]], axis=0 if back else 1)

    contract = ((1,), (0,)) if back else ((1,), (1,))
    depth = v3.shape[2]

    size = part.shape[1]
    window = pl.ds(0, size) if window is None else window

    def times(first, n, t):
        return dot(v3[pl.ds(first, n), window, :].reshape(n * size, depth), taps(t), contract)

    def rows_of(term, n):
        return [term[k * size : (k + 1) * size] for k in range(n)]

    if unrolled:
        for i in range(2):
            total = rows_of(times(4 * i, 4, 1), 4)
            side = rows_of(times(1 + 2 * i, 4, 2 - 2 * i), 4)
            edge = rows_of(times(5 * i, 3, 2 * i), 3)
            for k in range(4):
                value = total[k] + side[k]
                if 0 <= k + i - 1 < 3:
                    value = value + edge[k + i - 1]
                carry = finish(4 * i + k, value, carry)
        return carry

    def step(i, carry):
        part[pl.ds(3 * i + 1, 3)] = times(5 * i, 3, 2 * i).reshape(3, size, part.shape[2])
        part[7 * i] = jnp.zeros(part.shape[1:], F32)
        total = times(4 * i, 4, 1) + times(1 + 2 * i, 4, 2 - 2 * i)
        for k in range(4):
            m = 4 * i + k
            carry = finish(m, part[m] + total[k * size : (k + 1) * size], carry)
        return carry

    return lax.fori_loop(0, 2, step, carry)


def convolve_sums(g, here, x3, w, pre, unrolled):
    _, own = row_masks(g, here, g.cm)

    def finish(m, total, sums):
        pre[m] = total
        kept = total * own
        return sums[0] + sum_rows(kept), sums[1] + sum_rows(kept * total)

    zero = jnp.zeros((1, g.cm), F32)
    return convolve(x3, w, pre, False, finish, (zero, zero), unrolled)


def first_kernel(g, lens, gains, w, maps, pre, x3, pay):
    here = Here(g, lens)
    c = g.ci_all
    order = grid_order()
    row = lax.broadcasted_iota(jnp.int32, (MEL * 16, 128), 0) % 16

    def place_cells(j, square):
        cells = maps[:, :, 128 * j : 128 * (j + 1)].reshape(c, 128)
        frame = row + 16 * j
        valid = (frame + here.start) < here.length
        own = (frame >= here.off) & (frame < here.off + g.seg)
        block = dot(order, cells, ((1,), (1,))) * widen(valid.astype(F32), c)
        x3[:, 16 * j : 16 * (j + 1), c : 2 * c] = block.astype(BF).reshape(MEL, 16, c)
        return square + sum_rows(block * block * widen(own.astype(F32), c))

    square = jnp.zeros((1, c), F32)
    for j in range(g.win // 16):
        square = place_cells(j, square)
    for m in range(MEL):
        before, after_ = shifted(x3[m, :, c : 2 * c].astype(F32))
        x3[m, :, 0:c] = before.astype(BF)
        x3[m, :, 2 * c : 3 * c] = after_.astype(BF)

    one, two = convolve_sums(g, here, x3, w, pre, True)
    frame_total = 0
    pair_total = 0
    for i in range(g.clips):
        frame_total = frame_total + lens[i]
        pair_total = pair_total + (lens[i] + 1) // 2
    row = misc_row(
        frame_total.astype(F32), pair_total.astype(F32), jnp.sum(square, axis=1, keepdims=True)
    )
    pay[...] = payload(16, lanes(one), lanes(two), row, gains[...])


def first(g, lens, gains, maps, w):
    body = functools.partial(first_kernel, g)
    out = [
        arr((MEL, g.win, g.cm), F32),
        arr((MEL, g.win, 3 * g.ci_all), BF),
        arr((16, 128), F32),
    ]
    args = [lens, gains, *keep_near(w, maps)]
    ins = [SMEM] + [VMEM] * 3
    flops = 2 * 9 * MEL * g.win * g.ci_all * g.cm
    return call(body, out, ins, args, [], 10, flops, 10 * MIB, "first_conv")


MEAN1, INV1, GAMMA1, BETA1, GAMMA2, BETA2, COUNT, PAIRS, SQ0, MEAN2, INV2 = range(11)
TABLE = 16


def half_affine(mean, inverse, gamma, beta):
    scale = 0.5 * gamma * inverse
    return scale, 0.5 * beta - mean * scale


def second_kernel(g, lens, got, pre1, w, pre, x3, table, pay, misc_out):
    here = Here(g, lens)
    c = g.cm
    valid, own = row_masks(g, here, c)
    one, two = total_of(g, got)
    misc = misc_of(g, got)
    count = MEL * pick(misc, 0) / g.nch
    pairs = (MEL // 2) * pick(misc, 1) / g.nch
    at = 2 * (c // 128) + 1
    vectors = [
        jnp.concatenate([got[zz, at + i : at + i + 1, : g.co] for zz in range(g.nch)], axis=1)
        for i in range(4)
    ]
    mean = one / count
    inverse = lax.rsqrt(two / count - mean * mean + 1e-05)
    wide = jnp.zeros((1, c), F32)
    table[...] = jnp.concatenate(
        [mean, inverse, *vectors, wide + count, wide + pairs, wide + pick(misc, 2)]
        + [wide] * (TABLE - 9),
        axis=0,
    )
    scale, shift = half_affine(mean, inverse, vectors[0], vectors[1])


    def activate(m, square):
        half = pre1[m] * scale + shift
        act = half * (1.0 + jnp.tanh(half)) * valid
        low = act.astype(BF)
        before, after = shifted(low.astype(F32))
        side_by_side(x3, m, low, c, before, after)
        return square + sum_rows(act * act * own)

    square = jnp.zeros((1, c), F32)
    for m in range(MEL):
        square = activate(m, square)
    one, two = convolve_sums(g, here, x3, w, pre, True)
    pay[...] = payload(8, lanes(one), lanes(two))
    misc_out[...] = payload(8, misc_row(jnp.sum(square, axis=1, keepdims=True)))


def second(g, lens, got, pre1, w):
    body = functools.partial(second_kernel, g)
    out = [
        arr((MEL, g.win, g.cm), F32),
        arr((MEL, g.win, 3 * g.cm), BF),
        arr((TABLE, g.cm), F32),
        arr((8, 128), F32),
        arr((8, 128), F32),
    ]
    args = [lens, *keep_near(got, pre1, w)]
    flops = 2 * 9 * MEL * g.win * g.cm * g.cm
    ins = [SMEM, VMEM, VMEM, VMEM]
    return call(body, out, ins, args, [], 10, flops, 17 * MIB, "second_conv")


def pool_kernel(g, lens, got, old_ref, pre2, *rest):
    n, c = g.nch, g.cm
    cs, outs = rest[:n], rest[n : 2 * n]
    local_ref, table, pay, misc_out, held, grads, total, flat = rest[2 * n :]
    here = Here(g, lens)
    for k in range(n):
        held[pl.ds(aligned((here.z ^ k) * g.co), g.co), :] = cs[k][...]
    r = lax.broadcasted_iota(jnp.int32, (256, 128), 0)
    l = lax.broadcasted_iota(jnp.int32, (256, 128), 1)
    spread = (l == (r % 64) // 2 * 4 + r // 64).astype(BF)

    @pl.loop(0, g.cwin // 64)
    def _(j):
        cells = held[:, pl.ds(aligned(128 * j, 128), 128)]
        block = dot(spread, cells, ((1,), (1,)))
        grads[:, pl.ds(aligned(64 * j), 64), :] = block.reshape(MEL // 2, 64, c)

    one, two = total_of(g, got)
    old = old_ref[...]
    count = old[COUNT : COUNT + 1]
    mean = one / count
    inverse = lax.rsqrt(two / count - mean * mean + 1e-05)
    wide = jnp.zeros((1, c), F32)
    table[...] = jnp.concatenate([old[:MEAN2], mean, inverse] + [wide] * (TABLE - 11), axis=0)
    half_gamma, half_beta = 0.5 * old[GAMMA2 : GAMMA2 + 1], 0.5 * old[BETA2 : BETA2 + 1]
    less = -mean * inverse
    valid, own = row_masks(g, here, c)
    r = lax.broadcasted_iota(jnp.int32, (g.win, 128), 0) + here.start
    share = widen(jnp.where(here.length - r // 2 * 2 >= 2, 0.25, 0.5), c)
    half_share = 0.5 * share * valid
    window = pl.ds(aligned(here.qoff), g.win)
    out_row = lax.broadcasted_iota(jnp.int32, (g.win, 2 * g.seg), 0) - here.off
    out_cell = lax.broadcasted_iota(jnp.int32, (g.win, 2 * g.seg), 1)
    first_cell = jnp.where(out_row >= 0, out_row // 2 * 4, -MEL)
    total[...] = jnp.zeros(total.shape, F32)

    def step(k, sums):
        beta_sum, gamma_sum, square = sums
        given = grads[k, window, :] * half_share
        pair = None
        for i in range(2):
            m = 2 * k + i
            scaled = pre2[m] * inverse + less
            half = scaled * half_gamma + half_beta
            bend = jnp.tanh(half)
            twice = 1.0 + bend
            whole = half * twice
            act = whole * own
            square = square + sum_rows(act * act)
            local = given * (twice + whole * (1.0 - bend))
            local_ref[m] = local
            kept = local * own
            beta_sum = beta_sum + sum_rows(kept)
            gamma_sum = gamma_sum + sum_rows(kept * scaled)
            pair = act if pair is None else pair + act
        pair = pair * share
        high = pair.astype(BF)
        low = (pair - high.astype(F32)).astype(BF)
        gather = (out_cell == first_cell + k).astype(BF)
        total[...] += dot(high, gather, ((0,), (0,))) + dot(low, gather, ((0,), (0,)))
        return beta_sum, gamma_sum, square

    zero = jnp.zeros((1, c), F32)
    beta_sum, gamma_sum, square = lax.fori_loop(0, MEL // 2, step, (zero, zero, zero))
    pooled = total[...]
    flat[...] = pooled.astype(BF)
    for k in range(n):
        outs[k][...] = flat[pl.ds(aligned((here.z ^ k) * g.co), g.co), :]
    pooled_square = sum_rows(jnp.sum(pooled * pooled, axis=1, keepdims=True))
    block = payload(8, lanes(beta_sum), lanes(gamma_sum))
    pay[...] = jnp.broadcast_to(block[None], pay.shape)
    misc_out[...] = payload(8, misc_row(jnp.sum(square, axis=1, keepdims=True), pooled_square))


def pool(g, lens, got, table, pre2, cs):
    n = g.nch
    body = functools.partial(pool_kernel, g)
    out = [arr((g.co, 2 * g.seg), BF)] * n + [
        arr((MEL, g.win, g.cm), F32),
        arr((TABLE, g.cm), F32),
        arr((g.ndev, 8, 128), F32),
        arr((8, 128), F32),
    ]
    scratch = [
        pltpu.VMEM((g.cm, g.cwin * 2), BF),
        pltpu.VMEM((MEL // 2, g.cwin, g.cm), F32),
        pltpu.VMEM((g.cm, 2 * g.seg), F32),
        pltpu.VMEM((g.cm, 2 * g.seg), BF),
    ]
    args = [lens, *keep_near(got, table, pre2, *cs)]
    ins = [SMEM] + [VMEM] * (len(args) - 1)
    out = call(body, out, ins, args, scratch, 12, 4e9, 8 * MIB, "pool")
    return out[:n], *out[n:]


def terms_kernel(g, depth, norm, lens, got, table, pre, local, x3, after, *rest):
    grad, sums, roots, terms, give = rest
    here = Here(g, lens)
    c = g.cm
    valid, _ = row_masks(g, here, c)
    beta_sum, gamma_sum = total_of(g, got)
    t = table[...]
    mean, inverse, gamma = (t[i : i + 1] for i in norm)
    count = t[COUNT : COUNT + 1]
    sums[...] = jnp.concatenate([beta_sum, gamma_sum] + [jnp.zeros((1, c), F32)] * 6, axis=0)
    if got.shape[1] > 8:
        at = 2 * (c // 128)
        square1 = pick(jnp.sum(got[:, at, :], axis=0, keepdims=True), 0)
        later = jnp.sum(got[:, at + 1, :], axis=0, keepdims=True)
        tops = misc_row(pick(t[SQ0 : SQ0 + 1, :128], 0), square1, pick(later, 0), pick(later, 1))
        lane = lax.broadcasted_iota(jnp.int32, (1, 128), 1)
        cells, pairs = count[:, :128], t[PAIRS : PAIRS + 1, :128]
        under = jnp.where(lane == 0, cells * g.ci_all, jnp.where(lane == 3, pairs * c, cells * c))
        roots[...] = jnp.broadcast_to(jnp.sqrt(tops / under), (8, 128))
    factor = gamma * inverse
    slope = factor * inverse * gamma_sum / count
    level = factor * beta_sum / count - mean * slope

    @pl.loop(0, MEL)
    def _(m):
        value = valid * (local[m] * factor - pre[m] * slope - level)
        grad[m] = value.astype(BF)

    segment = pl.ds(aligned(here.off), g.seg)

    @pl.loop(0, 3)
    def _(a):
        lanes_of = pl.ds(aligned(a * depth, 128), depth)
        for b in (1, 0, 2):
            low = max(0, 1 - b)
            high = min(MEL, MEL + 1 - b)
            rows = (high - low) * g.seg
            left = grad[low:high, segment, :].reshape(rows, c)
            right = x3[low + b - 1 : high + b - 1, segment, lanes_of].reshape(rows, depth)
            term = dot(left, right, ((0,), (0,))).astype(BF)
            for z in range(g.nch):
                for s in range(2):
                    for p in range(g.planes):
                        at = z * g.co + g.row_of(s, p)
                        terms[s, z, p, 3 * a + b] = term[at : at + g.rows]

    give[...] = terms[1 - here.core]


def terms_of(g, lens, got, table, pre, local, x3, after, depth, norm, name):
    body = functools.partial(terms_kernel, g, depth, norm)
    shape = (g.nch, g.planes, 9, g.rows, depth)
    out = [
        arr((MEL, g.win, g.cm), BF),
        arr((8, g.cm), F32),
        arr((8, 128), F32),
        arr((2, *shape), BF),
        arr(shape, BF),
    ]
    args = [lens, *keep_near(got, table, pre, local, x3), after]
    ins = [SMEM] + [VMEM] * 5 + [ANY]
    flops = 2 * 9 * MEL * g.win * g.cm * depth
    return call(body, out, ins, args, [], 10, flops, 15 * MIB, name)


def back_kernel(g, lens, table, grad, pre1, w, misc2, misc3, after, local1, pay, g3):
    here = Here(g, lens)
    c = g.cm
    valid, own = row_masks(g, here, c)
    t = table[...]

    def row(i):
        return t[i : i + 1]


    for m in range(MEL):
        low = grad[m]
        before, after = shifted(low.astype(F32))
        side_by_side(g3, m, low, c, after, before)

    inverse, less = row(INV1), -row(MEAN1) * row(INV1)
    half_gamma, half_beta = 0.5 * row(GAMMA1), 0.5 * row(BETA1)
    half_valid = 0.5 * valid

    def finish(m, given, sums):
        scaled = pre1[m] * inverse + less
        half = scaled * half_gamma + half_beta
        bend = jnp.tanh(half)
        twice = 1.0 + bend
        local = given * half_valid * (twice + half * twice * (1.0 - bend))
        local1[m] = local
        kept = local * own
        return sums[0] + sum_rows(kept), sums[1] + sum_rows(kept * scaled)

    zero = jnp.zeros((1, c), F32)
    beta_sum, gamma_sum = convolve(g3, w, local1, True, finish, (zero, zero), True)
    squares = jnp.concatenate([misc2[0:1], misc3[0:1]], axis=0)
    pay[...] = payload(16, lanes(beta_sum), lanes(gamma_sum), squares)


def back(g, lens, table, grad, pre1, w, misc2, misc3, after):
    body = functools.partial(back_kernel, g)
    out = [arr((MEL, g.win, g.cm), F32), arr((16, 128), F32)]
    scratch = [pltpu.VMEM((MEL, g.win, 3 * g.cm), BF)]
    args = [lens, *keep_near(table, grad, pre1, w, misc2, misc3), after]
    flops = 2 * 9 * MEL * g.win * g.cm * g.cm
    ins = [SMEM] + [VMEM] * 6 + [ANY]
    return call(body, out, ins, args, scratch, 14, flops, 20 * MIB, "second_back")


def release_kernel(*refs):
    pass


def release_far(gates, x):
    n = len(gates)
    return pl.pallas_call(
        release_kernel,
        out_shape=pltpu.HBM(x.shape, x.dtype),
        in_specs=[ANY] * (n + 1),
        out_specs=ANY,
        input_output_aliases={n: 0},
        compiler_params=pltpu.CompilerParams(vmem_limit_bytes=2 * MIB),
        name="release_far",
    )(*gates, in_hbm(x))


def release(gates, arrays):
    out = [arr(x.shape, x.dtype) for x in arrays]
    n = len(gates)
    ins = [ANY] * n + [VMEM] * len(arrays)
    aliases = {i + n: i for i in range(len(arrays))}
    args = [*gates, *keep_near(*arrays)]
    return call(release_kernel, out, ins, args, [], 2, 0, 1, "release", aliases)


def spectra_kernel(g, lens, grad, after, w, *rest):
    n, c = g.nch, g.cm
    outs, (g3, rows, flat, part) = rest[:n], rest[n:]
    here = Here(g, lens)

    @pl.loop(0, MEL)
    def _(m):
        low = grad[m]
        before, after_ = shifted(low.astype(F32))
        side_by_side(g3, m, low, c, after_, before)

    r = lax.broadcasted_iota(jnp.int32, (g.seg, 128), 0) + here.off + here.start
    valid = widen((r < here.length).astype(F32), g.ci_all)

    def finish(m, total, carry):
        rows[m] = (total * valid).astype(BF)
        return carry

    convolve(g3, w, part, True, finish, 0, False, pl.ds(aligned(here.off), g.seg))
    order = grid_order()

    for j in range(g.seg // 16):
        block = rows[:, 16 * j : 16 * (j + 1), :].reshape(MEL * 16, g.ci_all)
        flat[:, 128 * j : 128 * (j + 1)] = dot(block, order, ((0,), (0,))).astype(BF)

    for k in range(n):
        outs[k][...] = flat[pl.ds(aligned((here.z ^ k) * g.ci), g.ci), :]


def spectra_back(g, lens, grad, after, w):
    n = g.nch
    body = functools.partial(spectra_kernel, g)
    out = [arr((g.ci, g.seg * MEL), BF)] * n
    scratch = [
        pltpu.VMEM((MEL, g.win, 3 * g.cm), BF),
        pltpu.VMEM((MEL, g.seg, g.ci_all), BF),
        pltpu.VMEM((g.ci_all, g.seg * MEL), BF),
        pltpu.VMEM((MEL, g.seg, g.ci_all), F32),
    ]
    grad, w = keep_near(grad, w)
    args = [lens, grad, after, w]
    flops = 2 * 9 * MEL * g.win * g.cm * g.ci_all
    ins = [SMEM, VMEM, ANY, VMEM]
    return call(body, out, ins, args, scratch, 14, flops, 5 * MIB, "spectra_back")


def place_kernel(g, width, *rest):
    n = g.nch
    parts, out, done = rest[:n], rest[n], rest[n + 1]
    z = lax.axis_index("chan")
    done[...] = jnp.zeros(done.shape, F32)
    for k in range(n):
        source = z ^ k
        for zz in range(n):

            @pl.when(source == zz)
            def _():
                at = zz % g.segs * width
                out[zz // g.segs, :, at : at + width] = parts[k][...].astype(out.dtype)


def place(g, parts, dtype, name):
    channels, width = parts[0].shape
    return pl.pallas_call(
        functools.partial(place_kernel, g, width),
        out_shape=[
            jax.ShapeDtypeStruct((g.clips, channels, g.segs * width), dtype),
            jax.ShapeDtypeStruct((8, 128), F32),
        ],
        in_specs=[VMEM] * g.nch,
        out_specs=[VMEM] * 2,
        compiler_params=pltpu.CompilerParams(vmem_limit_bytes=8 * MIB),
        cost_estimate=TINY,
        name=name,
    )(*parts)


def core_sum_kernel(g, terms, got, after, stay, go):
    d, z = lax.axis_index("dp"), lax.axis_index("chan")
    core, plane = lax.rem(d, 2), lax.rem(d, g.pieces) // 2
    half = g.planes // 2
    for e in range(g.planes):
        at = plane ^ g.plane_of(core, e)
        for k in range(g.nch):
            source = z ^ g.zed_of(k)
            value = terms[core, source, at].astype(F32) + got[source, at].astype(F32)
            to = stay if e < half else go
            to[(e % half) * g.nch + k] = value.astype(BF)


def core_sum(g, terms, got, after, name):
    shape = (g.planes // 2 * g.nch, *got.shape[2:])
    return pl.pallas_call(
        functools.partial(core_sum_kernel, g),
        out_shape=[pltpu.VMEM(shape, BF)] * 2,
        in_specs=[VMEM, VMEM, ANY],
        out_specs=[VMEM] * 2,
        compiler_params=pltpu.CompilerParams(vmem_limit_bytes=16 * MIB),
        name=name,
    )(keep_near(terms)[0], got, after)


def quarter_kernel(g, terms, got, *outs):
    d, z = lax.axis_index("dp"), lax.axis_index("chan")
    core, plane = lax.rem(d, 2), lax.rem(d, g.pieces) // 2
    for e in range(g.planes):
        at = plane ^ g.plane_of(core, e)
        for k in range(g.nch):
            source = z ^ g.zed_of(k)
            value = terms[core, source, at].astype(F32) + got[source, at].astype(F32)
            outs[e][k] = value.astype(BF)


def quarters(g, terms, got, name):
    shape = (g.nch, *got.shape[2:])
    return pl.pallas_call(
        functools.partial(quarter_kernel, g),
        out_shape=[pltpu.VMEM(shape, BF)] * g.planes,
        in_specs=[VMEM, VMEM],
        out_specs=[VMEM] * g.planes,
        compiler_params=pltpu.CompilerParams(vmem_limit_bytes=16 * MIB),
        name=name,
    )(keep_near(terms)[0], got)


def add_kernel(n, halves, *rest):
    first = rest[0]
    outs = rest[len(rest) - halves :]
    count = first.shape[0] // halves
    for i in range(first.shape[0]):
        total = first[i].astype(F32)
        for r in rest[1:n]:
            total = total + r[i].astype(F32)
        outs[i // count][i % count] = total.astype(BF)


def add_up(parts, halves, gates, name):
    n = len(parts)
    shape = (parts[0].shape[0] // halves, *parts[0].shape[1:])
    return pl.pallas_call(
        functools.partial(add_kernel, n, halves),
        out_shape=[pltpu.VMEM(shape, BF)] * halves,
        in_specs=[VMEM] * n + [ANY] * len(gates),
        out_specs=[VMEM] * halves,
        compiler_params=pltpu.CompilerParams(vmem_limit_bytes=8 * MIB),
        name=name,
    )(*parts, *gates)


def halve_kernel(stay, got, *rest):
    n = stay.shape[0]
    outs = rest[-2:] if n > 1 else rest[-1:]
    for i in range(n):
        value = stay[i].astype(F32) + got[i].astype(F32)
        if n == 1:
            outs[0][...] = value.astype(BF)
        else:
            outs[i // (n // 2)][i % (n // 2)] = value.astype(BF)


def halve(stay, got, gates, name):
    n = stay.shape[0]
    if n == 1:
        out = [jax.ShapeDtypeStruct(stay.shape[1:], BF)]
    else:
        out = [jax.ShapeDtypeStruct((n // 2, *stay.shape[1:]), BF)] * 2
    return pl.pallas_call(
        halve_kernel,
        out_shape=out,
        in_specs=[VMEM, VMEM] + [ANY] * len(gates),
        out_specs=[VMEM] * len(out),
        compiler_params=pltpu.CompilerParams(vmem_limit_bytes=8 * MIB),
        name=name,
    )(stay, got, *gates)


def spread_kernel(g, mine, other, out):
    d = lax.axis_index("dp")
    core, plane = lax.rem(d, 2), lax.rem(d, g.pieces) // 2
    for side, part in enumerate((mine, other)):
        c = core if side == 0 else 1 - core
        for e in range(g.planes):
            at = aligned(g.row_of(c, plane ^ g.plane_of(c, e)))
            out[:, pl.ds(at, g.rows), :] = part[e].astype(F32)


def spread_out(g, mine, other, depth, name):
    return pl.pallas_call(
        functools.partial(spread_kernel, g),
        out_shape=jax.ShapeDtypeStruct((9, g.co, depth), F32),
        in_specs=[VMEM] * 2,
        out_specs=VMEM,
        compiler_params=pltpu.CompilerParams(vmem_limit_bytes=12 * MIB),
        name=name,
    )(mine, other)


def stack_kernel(n, *refs):
    for k, r in enumerate(refs[:n]):
        refs[-1][k] = r[...]


def stack(parts, gates, name):
    n = len(parts)
    out = [arr((n, *parts[0].shape), parts[0].dtype)]
    ins = [VMEM] * n + [ANY] * len(gates)
    body = functools.partial(stack_kernel, n)
    return call(body, out, ins, [*parts, *gates], [], 6, 0, 1e6, name)[0]


class Links:
    def __init__(self, g):
        self.g = g

    def core(self, x):
        return lax.ppermute(x, "dp", [(i, i ^ 1) for i in range(self.g.ndp)])

    def dp(self, x, bit):
        return lax.ppermute(x, "dp", [(i, i ^ bit) for i in range(self.g.ndp)])

    def plane(self, x, turn):
        g = self.g
        return lax.ppermute(x, "dp", [(i, i ^ (2 * g.mask(i & 1, turn))) for i in range(g.ndp)])

    def chan(self, x, k):
        return lax.ppermute(x, "chan", [(i, i ^ k) for i in range(self.g.nch)])

    def exchange(self, parts):
        return [parts[0]] + [self.chan(parts[k], k) for k in range(1, self.g.nch)]

    def gather_planes(self, x, gates=()):
        have = [x]
        for turn in reversed(range(self.g.turns)):
            more = [self.plane(h, turn) for h in have[:1]]
            rest = have[1:]
            if gates and turn == 0 and rest:
                rest = release([*gates, *more], rest)
            have = have + more + [self.plane(h, turn) for h in rest]
        return have

    def gather_cores(self, have):
        return [*have, *[self.core(h) for h in have]]

    def gather_direct(self, x):
        g = self.g
        pairs = [[(i, i ^ (2 * g.plane_of(i & 1, e))) for i in range(g.ndp)] for e in range(g.planes)]
        return [x] + [lax.ppermute(x, "dp", p) for p in pairs[1:]]


def everyone(x):
    return lax.all_to_all(x, ("dp", "chan"), 0, 0)


def make_body(ndp, nch):
    def body(
        spectra, lengths, weight_in, gamma_in, beta_in, weight_mid, gamma_mid, beta_mid, cotangent
    ):
        g = Geometry(
            ndp,
            nch,
            spectra.shape[0],
            spectra.shape[2] // MEL,
            weight_in.shape[2],
            weight_mid.shape[2],
        )
        links = Links(g)
        gains = jnp.stack([gamma_in, beta_in, gamma_mid, beta_mid])
        gains = jnp.pad(gains, ((0, 0), (0, 128 - g.co)))

        piece = cut_weights(g, weight_in, weight_mid)
        cells = cut_maps(g, spectra, piece)
        cots = cut_cot(g, cotangent, cells)
        pieces_in, pieces_mid = sort_pieces(
            g, [links.chan(piece, k) for k in range(1, nch)], [cots[0]]
        )
        maps = lax.all_to_all(release_far([pieces_in], cells), "chan", 0, 0)
        planes_in = links.gather_planes(pieces_in)
        w_in = join(g, weight_in, links.gather_cores(planes_in), g.ci_all, "join_in")
        planes_mid = links.gather_planes(pieces_mid, [maps])

        pre1, x3_in, pay = first(g, lengths, gains, maps, w_in)
        got = everyone(fan(g, pay, cots[0], *planes_mid[1:]))
        planes_mid = release([got], planes_mid)
        w_mid = join(g, weight_mid, links.gather_cores(planes_mid), g.cm, "join_mid")
        cs = links.exchange(release([got], cots))
        pre2, x3_mid, table, pay, misc2 = second(g, lengths, got, pre1, w_mid)
        got = everyone(fan(g, pay, *cs[1:]))
        pooled, local2, table, pay, misc3 = pool(g, lengths, got, table, pre2, cs)
        got = everyone(pay)
        pooled = links.exchange(release([got], pooled))
        grad2, sums2, _, terms_mid, give_mid = terms_of(
            g, lengths, got, table, pre2, local2, x3_mid, got, g.cm, (MEAN2, INV2, GAMMA2), "weight_mid_terms"
        )
        got_mid = links.core(give_mid)
        split = g.turns == 2
        if split:
            stay_a, stay_b, go_a, go_b = quarters(g, terms_mid, got_mid, "mid_core_sum")
            got_b = links.plane(go_b, 0)
        else:
            stay_mid, go_b = core_sum(g, terms_mid, got_mid, got_mid, "mid_core_sum")
            got_b = go_b
        local1, pay = back(g, lengths, table, grad2, pre1, w_mid, misc2, misc3, go_b)
        got = everyone(fan(g, pay, got_b, *pooled[1:]))
        block_out, pooled_done = place(g, pooled, BF, "place_pooled")
        if split:
            (go_1,) = add_up([stay_b, got_b], 1, [got], "mid_sum_b")
            got_1 = links.plane(go_1, 1)
            got_a = links.plane(release([got], [go_a])[0], 0)
        else:
            (go_mid,) = release([got], [go_b])
        grad1, sums1, roots, terms_in, give_in = terms_of(
            g, lengths, got, table, pre1, local1, x3_in, got, g.ci_all, (MEAN1, INV1, GAMMA1), "weight_in_terms"
        )
        got_in = links.core(give_in)

        class Chain:
            def __init__(self, stay, go, depth, name):
                self.stay, self.go, self.depth, self.name = stay, go, depth, name
                self.turns = [functools.partial(links.plane, turn=t) for t in range(g.turns)]
                self.turns += [functools.partial(links.chan, k=1 << t) for t in range(g.zturns)]

            def turn(self, i, *gates):
                got = self.turns[i](self.go)
                done = halve(self.stay, got, gates, f"{self.name}_sum_{i}")
                self.stay, self.go = done if len(done) == 2 else (done[0], None)
                return self.stay

            def rest(self):
                bit = g.pieces
                while bit < ndp:
                    got = links.dp(self.stay, bit)
                    self.stay = halve(self.stay[None], got[None], [], self.name + "_rest")[0]
                    bit *= 2

            def out(self, planes, *gates):
                mine = stack(planes, gates, self.name + "_stack")
                return spread_out(g, mine, links.core(mine), self.depth, self.name + "_out")

        turns = g.turns + g.zturns
        parts = spectra_back(g, lengths, grad1, grad1, w_in)
        stay_in, go_in = core_sum(g, terms_in, got_in, parts[0], "in_core_sum")
        inner = Chain(stay_in, go_in, g.ci_all, "in")
        parts = links.exchange(parts)
        spectra_grad, spectra_done = place(g, parts, F32, "place_spectra")
        if split:
            halves = add_up([stay_a, got_a, got_1], 2, [stay_in], "mid_sum_1")
            mid = Chain(*halves, g.cm, "mid")
        else:
            mid = Chain(stay_mid, go_mid, g.cm, "mid")
            for i in range(g.turns):
                mid.turn(i, stay_in)
        gates = [parts[1 : nch - 1], [*parts[nch - 1 :], pooled_done]]
        at = mid.stay
        for i in range(g.turns):
            at = inner.turn(i, at, *(gates[i] if i < 2 else []))
            if i == 0:
                at = mid.turn(g.turns, at)
        for i in range(g.turns, turns):
            at = inner.turn(i, at, *([spectra_done] if i == g.turns else []))
            if i + 1 < turns:
                at = mid.turn(i + 1, at)
        inner.rest()
        mid.rest()
        planes_in = links.gather_planes(inner.stay)
        weight_mid_grad = mid.out(links.gather_planes(mid.stay), *planes_in[1:3])
        weight_in_grad = inner.out(planes_in)
        z = lax.axis_index("chan")

        def share(sums, i):
            return lax.dynamic_slice_in_dim(sums[i], z * g.co, g.co)

        return (
            block_out,
            spectra_grad,
            weight_in_grad,
            share(sums1, 1),
            share(sums1, 0),
            weight_mid_grad,
            share(sums2, 1),
            share(sums2, 0),
            roots[0, :4],
        )

    return body


def solution(mesh):
    placed = (
        P("dp", "chan", None),
        P("dp"),
        P(None, "chan", None),
        P("chan"),
        P("chan"),
        P(None, "chan", None),
        P("chan"),
        P("chan"),
        P("dp", "chan", None),
    )
    return jax.shard_map(
        make_body(mesh.shape["dp"], mesh.shape["chan"]),
        mesh=mesh,
        in_specs=placed,
        out_specs=(
            P("dp", "chan", None),
            P("dp", "chan", None),
            P(None, "chan", None),
            P("chan"),
            P("chan"),
            P(None, "chan", None),
            P("chan"),
            P("chan"),
            P(),
        ),
        check_vma=False,
    )
```

```python
import functools

import jax
import jax.numpy as jnp
from jax import lax
from jax.experimental import pallas as pl
from jax.experimental.pallas import tpu as pltpu
from jax.sharding import PartitionSpec as P

MEL = 8
HALO = 16
BF = jnp.bfloat16
F32 = jnp.float32
MIB = 1024 * 1024
TINY = pl.CostEstimate(flops=1, bytes_accessed=1, transcendentals=0)

VMEM = pl.BlockSpec(memory_space=pltpu.VMEM)
SMEM = pl.BlockSpec(memory_space=pltpu.SMEM)
ANY = pl.BlockSpec(memory_space=pl.ANY)
HBM = pl.BlockSpec(memory_space=pltpu.HBM)


def bits_of(n):
    return n.bit_length() - 1


class Geometry:
    def __init__(self, ndp, nch, clips, frames, c_in, c_mid):
        self.ndp, self.nch, self.ndev = ndp, nch, ndp * nch
        self.clips, self.frames = clips, frames
        self.ci_all, self.cm = c_in, c_mid
        self.ci, self.co = c_in // nch, c_mid // nch
        self.segs = nch // clips
        self.seg = frames // self.segs
        self.win = self.seg + HALO * min(self.segs - 1, 2)
        starts = [min(max(s * self.seg - HALO, 0), frames - self.win) for s in range(self.segs)]
        self.cwin = min(frames, (self.win + 48 + 63) // 64 * 64)
        assert all(min(s // 64 * 64, frames - self.cwin) + self.cwin >= s + self.win for s in starts)
        self.rows = max(16, self.co // ndp)
        self.pieces = self.co // self.rows
        self.planes = self.pieces // 2
        self.turns = bits_of(self.planes)
        self.zturns = bits_of(nch)

    def mask(self, core, turn):
        low, high = 1 << turn, 1 << (self.turns - 1 - turn)
        return low + core * (high - low)

    def plane_of(self, core, e):
        rel = 0
        for t in range(self.turns):
            if (e >> (self.turns - 1 - t)) & 1:
                rel = rel ^ self.mask(core, t)
        return rel

    def row_of(self, core, plane):
        return core * (self.co // 2) + plane * self.rows

    def zed_of(self, e):
        return sum(1 << t for t in range(self.zturns) if (e >> (self.zturns - 1 - t)) & 1)


class Here:
    def __init__(self, g, lens):
        self.z = lax.axis_index("chan")
        self.d = lax.axis_index("dp")
        self.core = lax.rem(self.d, 2)
        self.plane = lax.rem(self.d, g.pieces) // 2
        clip, seg = self.z // g.segs, lax.rem(self.z, g.segs)
        self.length = lens[clip]
        self.start, self.cstart = g_starts(g, seg)
        self.off = seg * g.seg - self.start
        self.qoff = self.start - self.cstart


def g_starts(g, seg):
    start = jnp.clip(seg * g.seg - HALO, 0, g.frames - g.win)
    return start, jnp.minimum(start // 64 * 64, g.frames - g.cwin)


def aligned(x, n=16):
    return pl.multiple_of(x, n)


def dot(a, b, contract):
    return lax.dot_general(a, b, ((contract[0], contract[1]), ((), ())), preferred_element_type=F32)


def call(body, out, ins, args, scratch, limit, flops, nbytes, name, aliases=None):
    return pl.pallas_call(
        body,
        out_shape=[pltpu.VMEM(o.shape, o.dtype) if isinstance(o, jax.ShapeDtypeStruct) else o for o in out],
        in_specs=ins,
        out_specs=[VMEM if isinstance(o, jax.ShapeDtypeStruct) else ANY for o in out],
        scratch_shapes=scratch,
        input_output_aliases=aliases or {},
        compiler_params=pltpu.CompilerParams(vmem_limit_bytes=limit * MIB),
        cost_estimate=pl.CostEstimate(
            flops=int(flops), bytes_accessed=int(nbytes), transcendentals=0
        ),
        name=name,
    )(*args)


def arr(shape, dtype):
    return jax.ShapeDtypeStruct(shape, dtype)


def keep_near(*xs):
    return [pltpu.with_memory_space_constraint(x, pltpu.VMEM) for x in xs]


class Copies:
    def __init__(self, sems):
        self.sems, self.n, self.open = sems, 0, []

    def start(self, src, dst):
        c = pltpu.make_async_copy(src, dst, self.sems.at[self.n])
        self.n += 1
        c.start()
        self.open.append(c)
        return c

    def wait(self, c):
        self.open = [o for o in self.open if o is not c]
        c.wait()

    def wait_all(self, some=None):
        for c in list(self.open if some is None else some):
            self.wait(c)


def sems(n):
    return pltpu.SemaphoreType.DMA((n,))


def row_masks(g, here, width):
    r = lax.broadcasted_iota(jnp.int32, (g.win, 128), 0)
    valid = (r + here.start) < here.length
    own = valid & (r >= here.off) & (r < here.off + g.seg)
    return widen(valid.astype(F32), width), widen(own.astype(F32), width)


def widen(x, width):
    return jnp.concatenate([x] * (width // 128), axis=1)


def shifted(x):
    n = x.shape[0]
    r = lax.broadcasted_iota(jnp.int32, (8, 1), 0)
    before, after = pltpu.roll(x, 1, 0), pltpu.roll(x, n - 1, 0)
    before = jnp.concatenate([jnp.where(r == 0, 0.0, before[:8]), before[8:]], axis=0)
    after = jnp.concatenate([after[:-8], jnp.where(r == 7, 0.0, after[-8:])], axis=0)
    return before, after


def grid_order(rows=16):
    n = MEL * rows
    r = lax.broadcasted_iota(jnp.int32, (n, n), 0)
    c = lax.broadcasted_iota(jnp.int32, (n, n), 1)
    return (c == (r % rows) * MEL + r // rows).astype(BF)


def misc_row(*scalars):
    lane = lax.broadcasted_iota(jnp.int32, (1, 128), 1)
    row = jnp.zeros((1, 128), F32)
    for i, s in enumerate(scalars):
        row = jnp.where(lane == i, s, row)
    return row


def pick(row, i):
    lane = lax.broadcasted_iota(jnp.int32, (1, 128), 1)
    return jnp.sum(jnp.where(lane == i, row, 0.0), axis=1, keepdims=True)


def sum_rows(x):
    return jnp.sum(x, axis=0, keepdims=True)


def payload(*parts):
    return jnp.concatenate(parts, axis=1)


def fan_kernel(pay, *rest):
    out = rest[-1]
    out[...] = jnp.broadcast_to(pay[...][None], out.shape)


def fan(g, pay, *after):
    out = [arr((g.ndev, *pay.shape), F32)]
    ins = [VMEM] + [ANY] * len(after)
    return call(fan_kernel, out, ins, [pay, *after], [], 4, 0, 1e5, "fan")[0]


def total_of(g, ref):
    row = jnp.sum(ref[...], axis=0)
    return row[:, : g.cm], row[:, g.cm : 2 * g.cm], row[:, 2 * g.cm :]


def side_by_side(x3, m, low, c, first, last):
    x3[m, :, 0:c] = first.astype(BF)
    x3[m, :, c : 2 * c] = low
    x3[m, :, 2 * c : 3 * c] = last.astype(BF)


def cut_weights_kernel(g, w_in, w_mid, out, sem):
    d = lax.axis_index("dp")
    core, plane = lax.rem(d, 2), lax.rem(d, g.pieces) // 2
    rows = pl.ds(aligned(g.row_of(core, plane)), g.rows)
    copies = Copies(sem)
    copies.start(w_in.at[:, rows, :], out.at[:, :, : g.ci_all])
    copies.start(w_mid.at[:, rows, :], out.at[:, :, g.ci_all :])
    copies.wait_all()


def cut_weights(g, w_in, w_mid):
    out = [arr((9, g.rows, g.ci_all + g.cm), BF)]
    args = [in_hbm(w_in), in_hbm(w_mid)]
    body = functools.partial(cut_weights_kernel, g)
    return call(body, out, [ANY] * 2, args, [sems(2)], 4, 0, 4e5, "cut_weights")[0]


def sort_kernel(g, *rest):
    n = g.nch - 1
    parts, first, second = rest[:n], rest[-2], rest[-1]
    for k in range(n):
        first[k] = parts[k][:, :, : g.ci_all]
        second[k] = parts[k][:, :, g.ci_all :]


def sort_pieces(g, parts, gates):
    n = g.nch - 1
    out = [arr((n, 9, g.rows, g.ci_all), BF), arr((n, 9, g.rows, g.cm), BF)]
    body = functools.partial(sort_kernel, g)
    ins = [VMEM] * n + [ANY] * len(gates)
    return call(body, out, ins, [*parts, *gates], [], 4, 0, 1e6, "sort_pieces")


def cut_maps_kernel(g, spec, after, out, held, sem):
    copies = Copies(sem)
    first = []
    for z in range(g.nch):
        start = static_start(g, z % g.segs) * MEL
        first.append(copies.start(spec.at[z // g.segs, :, start : start + g.win * MEL], held.at[z]))
    for z in range(g.nch):
        copies.wait(first[z])
        copies.start(held.at[z], out.at[z])
    copies.wait_all()


def cut_maps(g, spec, after):
    shape = (g.nch, g.ci, g.win * MEL)
    body = functools.partial(cut_maps_kernel, g)
    args = [in_hbm(spec), after]
    scratch = [pltpu.VMEM(shape, BF), sems(2 * g.nch)]
    return call(body, [pltpu.HBM(shape, BF)], [ANY] * 2, args, scratch, 4, 0, 2e6, "cut_maps")[0]


def static_start(g, seg):
    return min(max(seg * g.seg - HALO, 0), g.frames - g.win)


def cut_cot_kernel(g, cot, after, *rest):
    n = g.nch
    cs, sem = rest[:n], rest[n]
    z = lax.axis_index("chan")
    copies = Copies(sem)
    for k in range(n):
        to = z ^ k
        clip, seg = to // g.segs, lax.rem(to, g.segs)
        _, cstart = g_starts(g, seg)
        copies.start(cot.at[clip, :, pl.ds(aligned(cstart * 2, 128), g.cwin * 2)], cs[k])
    copies.wait_all()


def cut_cot(g, cot, after):
    n = g.nch
    out = [arr((g.co, g.cwin * 2), BF)] * n
    body = functools.partial(cut_cot_kernel, g)
    return call(body, out, [ANY] * 2, [in_hbm(cot), after], [sems(n)], 4, 0, 1e6, "cut_cotangent")


def in_hbm(x):
    return pltpu.with_memory_space_constraint(x, pltpu.HBM)


def join_kernel(g, own, *rest):
    parts, w = rest[:-1], rest[-1]
    z, d = lax.axis_index("chan"), lax.axis_index("dp")
    mine, plane = lax.rem(d, 2), lax.rem(d, g.pieces) // 2
    w[:, pl.ds(aligned(z * g.co), g.co), :] = own[...]
    for side in range(2):
        core = mine if side == 0 else 1 - mine
        for e in range(g.planes):
            row = g.row_of(core, plane ^ g.plane_of(core, e))
            for k in range(1, g.nch):
                at = aligned((z ^ k) * g.co + row)
                w[:, pl.ds(at, g.rows), :] = parts[side * g.planes + e][k - 1]


def join(g, own, parts, depth, name):
    body = functools.partial(join_kernel, g)
    args = [*keep_near(own), *parts]
    ins = [VMEM] * len(args)
    return call(body, [arr((9, g.cm, depth), BF)], ins, args, [], 8, 0, 4 * MIB, name)[0]


def convolve(v3, w, part, back, finish, carry, unrolled=False, window=None):
    def taps(t):
        b = 2 - t if back else t
        return jnp.concatenate([w[b], w[3 + b], w[6 + b]], axis=0 if back else 1)

    contract = ((1,), (0,)) if back else ((1,), (1,))
    depth = v3.shape[2]

    size = part.shape[1]
    window = pl.ds(0, size) if window is None else window

    def times(first, n, t):
        return dot(v3[pl.ds(first, n), window, :].reshape(n * size, depth), taps(t), contract)

    def rows_of(term, n):
        return [term[k * size : (k + 1) * size] for k in range(n)]

    if unrolled:
        for i in range(2):
            total = rows_of(times(4 * i, 4, 1), 4)
            side = rows_of(times(1 + 2 * i, 4, 2 - 2 * i), 4)
            edge = rows_of(times(5 * i, 3, 2 * i), 3)
            for k in range(4):
                value = total[k] + side[k]
                if 0 <= k + i - 1 < 3:
                    value = value + edge[k + i - 1]
                carry = finish(4 * i + k, value, carry)
        return carry

    def step(i, carry):
        part[pl.ds(3 * i + 1, 3)] = times(5 * i, 3, 2 * i).reshape(3, size, part.shape[2])
        part[7 * i] = jnp.zeros(part.shape[1:], F32)
        total = times(4 * i, 4, 1) + times(1 + 2 * i, 4, 2 - 2 * i)
        for k in range(4):
            m = 4 * i + k
            carry = finish(m, part[m] + total[k * size : (k + 1) * size], carry)
        return carry

    return lax.fori_loop(0, 2, step, carry)


def convolve_sums(g, here, x3, w, pre, unrolled):
    _, own = row_masks(g, here, g.cm)

    def finish(m, total, sums):
        pre[m] = total
        kept = total * own
        return sums[0] + sum_rows(kept), sums[1] + sum_rows(kept * total)

    zero = jnp.zeros((1, g.cm), F32)
    return convolve(x3, w, pre, False, finish, (zero, zero), unrolled)


def first_kernel(g, lens, gains, w, maps, pre, x3, pay):
    here = Here(g, lens)
    c = g.ci_all
    order = grid_order()
    row = lax.broadcasted_iota(jnp.int32, (MEL * 16, 128), 0) % 16

    def place_cells(j, square):
        cells = maps[:, :, 128 * j : 128 * (j + 1)].reshape(c, 128)
        frame = row + 16 * j
        valid = (frame + here.start) < here.length
        own = (frame >= here.off) & (frame < here.off + g.seg)
        block = dot(order, cells, ((1,), (1,))) * widen(valid.astype(F32), c)
        x3[:, 16 * j : 16 * (j + 1), c : 2 * c] = block.astype(BF).reshape(MEL, 16, c)
        return square + sum_rows(block * block * widen(own.astype(F32), c))

    square = jnp.zeros((1, c), F32)
    for j in range(g.win // 16):
        square = place_cells(j, square)
    for m in range(MEL):
        before, after_ = shifted(x3[m, :, c : 2 * c].astype(F32))
        x3[m, :, 0:c] = before.astype(BF)
        x3[m, :, 2 * c : 3 * c] = after_.astype(BF)

    one, two = convolve_sums(g, here, x3, w, pre, True)
    frame_total = 0
    pair_total = 0
    for i in range(g.clips):
        frame_total = frame_total + lens[i]
        pair_total = pair_total + (lens[i] + 1) // 2
    row = misc_row(
        frame_total.astype(F32), pair_total.astype(F32), jnp.sum(square, axis=1, keepdims=True)
    )
    pay[...] = payload(one, two, row, *[gains[i : i + 1] for i in range(4)])


def first(g, lens, gains, maps, w):
    body = functools.partial(first_kernel, g)
    out = [
        arr((MEL, g.win, g.cm), F32),
        arr((MEL, g.win, 3 * g.ci_all), BF),
        arr((1, 2 * g.cm + 5 * 128), F32),
    ]
    args = [lens, gains, *keep_near(w, maps)]
    ins = [SMEM] + [VMEM] * 3
    flops = 2 * 9 * MEL * g.win * g.ci_all * g.cm
    return call(body, out, ins, args, [], 10, flops, 10 * MIB, "first_conv")


MEAN1, INV1, GAMMA1, BETA1, GAMMA2, BETA2, COUNT, PAIRS, SQ0, MEAN2, INV2 = range(11)
TABLE = 16


def half_affine(mean, inverse, gamma, beta):
    scale = 0.5 * gamma * inverse
    return scale, 0.5 * beta - mean * scale


def second_kernel(g, lens, got, pre1, w, pre, x3, table, pay, misc_out):
    here = Here(g, lens)
    c = g.cm
    valid, own = row_masks(g, here, c)
    one, two, rest = total_of(g, got)
    misc = rest[:, :128]
    count = MEL * pick(misc, 0) / g.nch
    pairs = (MEL // 2) * pick(misc, 1) / g.nch
    at = [2 * c + 128 * (1 + i) for i in range(4)]
    vectors = [
        jnp.concatenate([got[zz, :, i : i + g.co] for zz in range(g.nch)], axis=1) for i in at
    ]
    mean = one / count
    inverse = lax.rsqrt(two / count - mean * mean + 1e-05)
    wide = jnp.zeros((1, c), F32)
    table[...] = jnp.concatenate(
        [mean, inverse, *vectors, wide + count, wide + pairs, wide + pick(misc, 2)]
        + [wide] * (TABLE - 9),
        axis=0,
    )
    scale, shift = half_affine(mean, inverse, vectors[0], vectors[1])


    def activate(m, square):
        half = pre1[m] * scale + shift
        act = half * (1.0 + jnp.tanh(half)) * valid
        low = act.astype(BF)
        before, after = shifted(low.astype(F32))
        side_by_side(x3, m, low, c, before, after)
        return square + sum_rows(act * act * own)

    square = jnp.zeros((1, c), F32)
    for m in range(MEL):
        square = activate(m, square)
    one, two = convolve_sums(g, here, x3, w, pre, True)
    pay[...] = payload(one, two)
    misc_out[...] = misc_row(jnp.sum(square, axis=1, keepdims=True))


def second(g, lens, got, pre1, w):
    body = functools.partial(second_kernel, g)
    out = [
        arr((MEL, g.win, g.cm), F32),
        arr((MEL, g.win, 3 * g.cm), BF),
        arr((TABLE, g.cm), F32),
        arr((1, 2 * g.cm), F32),
        arr((1, 128), F32),
    ]
    args = [lens, *keep_near(got, pre1, w)]
    flops = 2 * 9 * MEL * g.win * g.cm * g.cm
    ins = [SMEM, VMEM, VMEM, VMEM]
    return call(body, out, ins, args, [], 10, flops, 17 * MIB, "second_conv")


def pool_kernel(g, lens, got, old_ref, pre2, *rest):
    n, c = g.nch, g.cm
    cs, outs = rest[:n], rest[n : 2 * n]
    local_ref, table, pay, misc_out, held, grads, total, flat = rest[2 * n :]
    here = Here(g, lens)
    for k in range(n):
        held[pl.ds(aligned((here.z ^ k) * g.co), g.co), :] = cs[k][...]
    r = lax.broadcasted_iota(jnp.int32, (256, 128), 0)
    l = lax.broadcasted_iota(jnp.int32, (256, 128), 1)
    spread = (l == (r % 64) // 2 * 4 + r // 64).astype(BF)

    @pl.loop(0, g.cwin // 64)
    def _(j):
        cells = held[:, pl.ds(aligned(128 * j, 128), 128)]
        block = dot(spread, cells, ((1,), (1,)))
        grads[:, pl.ds(aligned(64 * j), 64), :] = block.reshape(MEL // 2, 64, c)

    one, two, _ = total_of(g, got)
    old = old_ref[...]
    count = old[COUNT : COUNT + 1]
    mean = one / count
    inverse = lax.rsqrt(two / count - mean * mean + 1e-05)
    wide = jnp.zeros((1, c), F32)
    table[...] = jnp.concatenate([old[:MEAN2], mean, inverse] + [wide] * (TABLE - 11), axis=0)
    half_gamma, half_beta = 0.5 * old[GAMMA2 : GAMMA2 + 1], 0.5 * old[BETA2 : BETA2 + 1]
    less = -mean * inverse
    side = g.win - g.seg
    segment = pl.ds(aligned(here.off), g.seg)
    sides = [
        aligned(jnp.where(16 * j < here.off, 16 * j, 16 * j + g.seg)) for j in range(side // 16)
    ]

    def weights(rows, start, width):
        frame = lax.broadcasted_iota(jnp.int32, (rows, 128), 0) + (here.start + start)
        valid = (frame < here.length).astype(F32)
        share = jnp.where(here.length - frame // 2 * 2 >= 2, 0.25, 0.5)
        return widen(0.5 * share * valid, width), widen(valid, width)

    half_share, valid = weights(g.seg, here.off, c)
    side_shares = [weights(16, start, c)[0] for start in sides]
    out_row = lax.broadcasted_iota(jnp.int32, (g.seg, 2 * g.seg), 0)
    out_cell = lax.broadcasted_iota(jnp.int32, (g.seg, 2 * g.seg), 1)
    first_cell = out_row // 2 * 4
    frame = out_row + (here.start + here.off)
    out_share = jnp.where(here.length - frame // 2 * 2 >= 2, 0.25, 0.5)
    total[...] = jnp.zeros(total.shape, F32)

    def bent(pre):
        scaled = pre * inverse + less
        half = scaled * half_gamma + half_beta
        bend = jnp.tanh(half)
        twice = 1.0 + bend
        whole = half * twice
        return scaled, whole, twice + whole * (1.0 - bend)

    def step(k, sums):
        beta_sum, gamma_sum, square = sums
        given = grads[k, pl.ds(aligned(here.qoff + here.off), g.seg), :] * half_share
        pair = None
        for i in range(2):
            m = 2 * k + i
            scaled, whole, slope = bent(pre2[m, segment, :])
            act = whole * valid
            square = square + sum_rows(act * act)
            local = given * slope
            local_ref[m, segment, :] = local
            beta_sum = beta_sum + sum_rows(local)
            gamma_sum = gamma_sum + sum_rows(local * scaled)
            pair = act if pair is None else pair + act
            for start, side_share in zip(sides, side_shares, strict=True):
                rows = pl.ds(start, 16)
                _, _, slope = bent(pre2[m, rows, :])
                given_side = grads[k, pl.ds(aligned(here.qoff + start), 16), :] * side_share
                local_ref[m, rows, :] = given_side * slope
        gather = jnp.where(out_cell == first_cell + k, out_share, 0.0).astype(BF)
        total[...] += dot(pair.astype(BF), gather, ((0,), (0,)))
        return beta_sum, gamma_sum, square

    zero = jnp.zeros((1, c), F32)
    beta_sum, gamma_sum, square = lax.fori_loop(0, MEL // 2, step, (zero, zero, zero))
    pooled = total[...]
    flat[...] = pooled.astype(BF)
    for k in range(n):
        outs[k][...] = flat[pl.ds(aligned((here.z ^ k) * g.co), g.co), :]
    pooled_square = sum_rows(jnp.sum(pooled * pooled, axis=1, keepdims=True))
    pay[...] = jnp.broadcast_to(payload(beta_sum, gamma_sum)[None], pay.shape)
    misc_out[...] = misc_row(jnp.sum(square, axis=1, keepdims=True), pooled_square)


def pool(g, lens, got, table, pre2, cs):
    n = g.nch
    body = functools.partial(pool_kernel, g)
    out = [arr((g.co, 2 * g.seg), BF)] * n + [
        arr((MEL, g.win, g.cm), F32),
        arr((TABLE, g.cm), F32),
        arr((g.ndev, 1, 2 * g.cm), F32),
        arr((1, 128), F32),
    ]
    scratch = [
        pltpu.VMEM((g.cm, g.cwin * 2), BF),
        pltpu.VMEM((MEL // 2, g.cwin, g.cm), F32),
        pltpu.VMEM((g.cm, 2 * g.seg), F32),
        pltpu.VMEM((g.cm, 2 * g.seg), BF),
    ]
    args = [lens, *keep_near(got, table, pre2, *cs)]
    ins = [SMEM] + [VMEM] * (len(args) - 1)
    out = call(body, out, ins, args, scratch, 12, 4e9, 8 * MIB, "pool")
    return out[:n], *out[n:]


def terms_kernel(g, depth, norm, lens, got, table, pre, local, x3, after, *refs):
    grad, sums, roots, terms, give = refs
    here = Here(g, lens)
    c = g.cm
    valid, _ = row_masks(g, here, c)
    beta_sum, gamma_sum, rest = total_of(g, got)
    t = table[...]
    mean, inverse, gamma = (t[i : i + 1] for i in norm)
    count = t[COUNT : COUNT + 1]
    sums[...] = jnp.concatenate([beta_sum, gamma_sum] + [jnp.zeros((1, c), F32)] * 6, axis=0)
    if rest.shape[1]:
        second, third = rest[:, :128], rest[:, 128:]
        tops = misc_row(
            pick(t[SQ0 : SQ0 + 1, :128], 0), pick(second, 0), pick(third, 0), pick(third, 1)
        )
        lane = lax.broadcasted_iota(jnp.int32, (1, 128), 1)
        cells, pairs = count[:, :128], t[PAIRS : PAIRS + 1, :128]
        under = jnp.where(lane == 0, cells * g.ci_all, jnp.where(lane == 3, pairs * c, cells * c))
        roots[...] = jnp.broadcast_to(jnp.sqrt(tops / under), (8, 128))
    factor = gamma * inverse
    slope = factor * inverse * gamma_sum / count
    level = factor * beta_sum / count - mean * slope

    @pl.loop(0, MEL)
    def _(m):
        value = valid * (local[m] * factor - pre[m] * slope - level)
        grad[m] = value.astype(BF)

    segment = pl.ds(aligned(here.off), g.seg)

    @pl.loop(0, 3)
    def _(a):
        lanes_of = pl.ds(aligned(a * depth, 128), depth)
        for b in (1, 0, 2):
            low = max(0, 1 - b)
            high = min(MEL, MEL + 1 - b)
            rows = (high - low) * g.seg
            left = grad[low:high, segment, :].reshape(rows, c)
            right = x3[low + b - 1 : high + b - 1, segment, lanes_of].reshape(rows, depth)
            term = dot(left, right, ((0,), (0,))).astype(BF)
            for z in range(g.nch):
                for s in range(2):
                    for p in range(g.planes):
                        at = z * g.co + g.row_of(s, p)
                        terms[s, z, p, 3 * a + b] = term[at : at + g.rows]

    give[...] = terms[1 - here.core]


def terms_of(g, lens, got, table, pre, local, x3, after, depth, norm, name):
    body = functools.partial(terms_kernel, g, depth, norm)
    shape = (g.nch, g.planes, 9, g.rows, depth)
    out = [
        arr((MEL, g.win, g.cm), BF),
        arr((8, g.cm), F32),
        arr((8, 128), F32),
        arr((2, *shape), BF),
        arr(shape, BF),
    ]
    args = [lens, *keep_near(got, table, pre, local, x3), after]
    ins = [SMEM] + [VMEM] * 5 + [ANY]
    flops = 2 * 9 * MEL * g.win * g.cm * depth
    return call(body, out, ins, args, [], 10, flops, 15 * MIB, name)


def back_kernel(g, lens, table, grad, pre1, w, misc2, misc3, after, local1, pay, g3):
    here = Here(g, lens)
    c = g.cm
    valid, own = row_masks(g, here, c)
    t = table[...]

    def row(i):
        return t[i : i + 1]


    for m in range(MEL):
        low = grad[m]
        before, after = shifted(low.astype(F32))
        side_by_side(g3, m, low, c, after, before)

    inverse, less = row(INV1), -row(MEAN1) * row(INV1)
    half_gamma, half_beta = 0.5 * row(GAMMA1), 0.5 * row(BETA1)
    half_valid = 0.5 * valid

    def finish(m, given, sums):
        scaled = pre1[m] * inverse + less
        half = scaled * half_gamma + half_beta
        bend = jnp.tanh(half)
        twice = 1.0 + bend
        local = given * half_valid * (twice + half * twice * (1.0 - bend))
        local1[m] = local
        kept = local * own
        return sums[0] + sum_rows(kept), sums[1] + sum_rows(kept * scaled)

    zero = jnp.zeros((1, c), F32)
    beta_sum, gamma_sum = convolve(g3, w, local1, True, finish, (zero, zero), True)
    pay[...] = payload(beta_sum, gamma_sum, misc2[...], misc3[...])


def back(g, lens, table, grad, pre1, w, misc2, misc3, after):
    body = functools.partial(back_kernel, g)
    out = [arr((MEL, g.win, g.cm), F32), arr((1, 2 * g.cm + 2 * 128), F32)]
    scratch = [pltpu.VMEM((MEL, g.win, 3 * g.cm), BF)]
    args = [lens, *keep_near(table, grad, pre1, w, misc2, misc3), after]
    flops = 2 * 9 * MEL * g.win * g.cm * g.cm
    ins = [SMEM] + [VMEM] * 6 + [ANY]
    return call(body, out, ins, args, scratch, 14, flops, 20 * MIB, "second_back")


def release_kernel(*refs):
    pass


def release_far(gates, x):
    n = len(gates)
    return pl.pallas_call(
        release_kernel,
        out_shape=pltpu.HBM(x.shape, x.dtype),
        in_specs=[ANY] * (n + 1),
        out_specs=ANY,
        input_output_aliases={n: 0},
        compiler_params=pltpu.CompilerParams(vmem_limit_bytes=2 * MIB),
        name="release_far",
    )(*gates, in_hbm(x))


def release(gates, arrays):
    out = [arr(x.shape, x.dtype) for x in arrays]
    n = len(gates)
    ins = [ANY] * n + [VMEM] * len(arrays)
    aliases = {i + n: i for i in range(len(arrays))}
    args = [*gates, *keep_near(*arrays)]
    return call(release_kernel, out, ins, args, [], 2, 0, 1, "release", aliases)


def spectra_kernel(g, lens, grad, after, w, *rest):
    n, c = g.nch, g.cm
    outs, (g3, rows, flat, part) = rest[:n], rest[n:]
    here = Here(g, lens)

    @pl.loop(0, MEL)
    def _(m):
        low = grad[m]
        before, after_ = shifted(low.astype(F32))
        side_by_side(g3, m, low, c, after_, before)

    r = lax.broadcasted_iota(jnp.int32, (g.seg, 128), 0) + here.off + here.start
    valid = widen((r < here.length).astype(F32), g.ci_all)

    def finish(m, total, carry):
        rows[m] = (total * valid).astype(BF)
        return carry

    convolve(g3, w, part, True, finish, 0, False, pl.ds(aligned(here.off), g.seg))
    order = grid_order()

    for j in range(g.seg // 16):
        block = rows[:, 16 * j : 16 * (j + 1), :].reshape(MEL * 16, g.ci_all)
        flat[:, 128 * j : 128 * (j + 1)] = dot(block, order, ((0,), (0,))).astype(BF)

    for k in range(n):
        outs[k][...] = flat[pl.ds(aligned((here.z ^ k) * g.ci), g.ci), :]


def spectra_back(g, lens, grad, after, w):
    n = g.nch
    body = functools.partial(spectra_kernel, g)
    out = [arr((g.ci, g.seg * MEL), BF)] * n
    scratch = [
        pltpu.VMEM((MEL, g.win, 3 * g.cm), BF),
        pltpu.VMEM((MEL, g.seg, g.ci_all), BF),
        pltpu.VMEM((g.ci_all, g.seg * MEL), BF),
        pltpu.VMEM((MEL, g.seg, g.ci_all), F32),
    ]
    grad, w = keep_near(grad, w)
    args = [lens, grad, after, w]
    flops = 2 * 9 * MEL * g.win * g.cm * g.ci_all
    ins = [SMEM, VMEM, ANY, VMEM]
    return call(body, out, ins, args, scratch, 14, flops, 5 * MIB, "spectra_back")


def place_kernel(g, width, *rest):
    n = g.nch
    parts, out, done = rest[:n], rest[n], rest[n + 1]
    z = lax.axis_index("chan")
    done[...] = jnp.zeros(done.shape, F32)
    for k in range(n):
        source = z ^ k
        for zz in range(n):

            @pl.when(source == zz)
            def _():
                at = zz % g.segs * width
                out[zz // g.segs, :, at : at + width] = parts[k][...].astype(out.dtype)


def place(g, parts, dtype, name):
    channels, width = parts[0].shape
    return pl.pallas_call(
        functools.partial(place_kernel, g, width),
        out_shape=[
            jax.ShapeDtypeStruct((g.clips, channels, g.segs * width), dtype),
            jax.ShapeDtypeStruct((8, 128), F32),
        ],
        in_specs=[VMEM] * g.nch,
        out_specs=[VMEM] * 2,
        compiler_params=pltpu.CompilerParams(vmem_limit_bytes=8 * MIB),
        cost_estimate=TINY,
        name=name,
    )(*parts)


def core_sum_kernel(g, terms, got, after, stay, go):
    d, z = lax.axis_index("dp"), lax.axis_index("chan")
    core, plane = lax.rem(d, 2), lax.rem(d, g.pieces) // 2
    half = g.planes // 2
    for e in range(g.planes):
        at = plane ^ g.plane_of(core, e)
        for k in range(g.nch):
            source = z ^ g.zed_of(k)
            value = terms[core, source, at].astype(F32) + got[source, at].astype(F32)
            to = stay if e < half else go
            to[(e % half) * g.nch + k] = value.astype(BF)


def core_sum(g, terms, got, after, name):
    shape = (g.planes // 2 * g.nch, *got.shape[2:])
    return pl.pallas_call(
        functools.partial(core_sum_kernel, g),
        out_shape=[pltpu.VMEM(shape, BF)] * 2,
        in_specs=[VMEM, VMEM, ANY],
        out_specs=[VMEM] * 2,
        compiler_params=pltpu.CompilerParams(vmem_limit_bytes=16 * MIB),
        name=name,
    )(keep_near(terms)[0], got, after)


def quarter_kernel(g, terms, got, *outs):
    d, z = lax.axis_index("dp"), lax.axis_index("chan")
    core, plane = lax.rem(d, 2), lax.rem(d, g.pieces) // 2
    for e in range(g.planes):
        at = plane ^ g.plane_of(core, e)
        for k in range(g.nch):
            source = z ^ g.zed_of(k)
            value = terms[core, source, at].astype(F32) + got[source, at].astype(F32)
            outs[e][k] = value.astype(BF)


def quarters(g, terms, got, name):
    shape = (g.nch, *got.shape[2:])
    return pl.pallas_call(
        functools.partial(quarter_kernel, g),
        out_shape=[pltpu.VMEM(shape, BF)] * g.planes,
        in_specs=[VMEM, VMEM],
        out_specs=[VMEM] * g.planes,
        compiler_params=pltpu.CompilerParams(vmem_limit_bytes=16 * MIB),
        name=name,
    )(keep_near(terms)[0], got)


def add_kernel(n, halves, *rest):
    first = rest[0]
    outs = rest[len(rest) - halves :]
    count = first.shape[0] // halves
    for i in range(first.shape[0]):
        total = first[i].astype(F32)
        for r in rest[1:n]:
            total = total + r[i].astype(F32)
        outs[i // count][i % count] = total.astype(BF)


def add_up(parts, halves, gates, name):
    n = len(parts)
    shape = (parts[0].shape[0] // halves, *parts[0].shape[1:])
    return pl.pallas_call(
        functools.partial(add_kernel, n, halves),
        out_shape=[pltpu.VMEM(shape, BF)] * halves,
        in_specs=[VMEM] * n + [ANY] * len(gates),
        out_specs=[VMEM] * halves,
        compiler_params=pltpu.CompilerParams(vmem_limit_bytes=8 * MIB),
        name=name,
    )(*parts, *gates)


def halve_kernel(stay, got, *rest):
    n = stay.shape[0]
    outs = rest[-2:] if n > 1 else rest[-1:]
    for i in range(n):
        value = stay[i].astype(F32) + got[i].astype(F32)
        if n == 1:
            outs[0][...] = value.astype(BF)
        else:
            outs[i // (n // 2)][i % (n // 2)] = value.astype(BF)


def halve(stay, got, gates, name):
    n = stay.shape[0]
    if n == 1:
        out = [jax.ShapeDtypeStruct(stay.shape[1:], BF)]
    else:
        out = [jax.ShapeDtypeStruct((n // 2, *stay.shape[1:]), BF)] * 2
    return pl.pallas_call(
        halve_kernel,
        out_shape=out,
        in_specs=[VMEM, VMEM] + [ANY] * len(gates),
        out_specs=[VMEM] * len(out),
        compiler_params=pltpu.CompilerParams(vmem_limit_bytes=8 * MIB),
        name=name,
    )(stay, got, *gates)


def spread_kernel(g, mine, other, out):
    d = lax.axis_index("dp")
    core, plane = lax.rem(d, 2), lax.rem(d, g.pieces) // 2
    for side, part in enumerate((mine, other)):
        c = core if side == 0 else 1 - core
        for e in range(g.planes):
            at = aligned(g.row_of(c, plane ^ g.plane_of(c, e)))
            out[:, pl.ds(at, g.rows), :] = part[e].astype(F32)


def spread_out(g, mine, other, depth, name):
    return pl.pallas_call(
        functools.partial(spread_kernel, g),
        out_shape=jax.ShapeDtypeStruct((9, g.co, depth), F32),
        in_specs=[VMEM] * 2,
        out_specs=VMEM,
        compiler_params=pltpu.CompilerParams(vmem_limit_bytes=12 * MIB),
        name=name,
    )(mine, other)


def stack_kernel(n, *refs):
    for k, r in enumerate(refs[:n]):
        refs[-1][k] = r[...]


def stack(parts, gates, name):
    n = len(parts)
    out = [arr((n, *parts[0].shape), parts[0].dtype)]
    ins = [VMEM] * n + [ANY] * len(gates)
    body = functools.partial(stack_kernel, n)
    return call(body, out, ins, [*parts, *gates], [], 6, 0, 1e6, name)[0]


class Links:
    def __init__(self, g):
        self.g = g

    def core(self, x):
        return lax.ppermute(x, "dp", [(i, i ^ 1) for i in range(self.g.ndp)])

    def dp(self, x, bit):
        return lax.ppermute(x, "dp", [(i, i ^ bit) for i in range(self.g.ndp)])

    def plane(self, x, turn):
        g = self.g
        return lax.ppermute(x, "dp", [(i, i ^ (2 * g.mask(i & 1, turn))) for i in range(g.ndp)])

    def chan(self, x, k):
        return lax.ppermute(x, "chan", [(i, i ^ k) for i in range(self.g.nch)])

    def exchange(self, parts):
        return [parts[0]] + [self.chan(parts[k], k) for k in range(1, self.g.nch)]

    def gather_planes(self, x, gates=()):
        have = [x]
        for turn in reversed(range(self.g.turns)):
            more = [self.plane(h, turn) for h in have[:1]]
            rest = have[1:]
            if gates and turn == 0 and rest:
                rest = release([*gates, *more], rest)
            have = have + more + [self.plane(h, turn) for h in rest]
        return have

    def gather_cores(self, have):
        return [*have, *[self.core(h) for h in have]]

    def gather_direct(self, x):
        g = self.g
        pairs = [[(i, i ^ (2 * g.plane_of(i & 1, e))) for i in range(g.ndp)] for e in range(g.planes)]
        return [x] + [lax.ppermute(x, "dp", p) for p in pairs[1:]]


def everyone(x):
    return lax.all_to_all(x, ("dp", "chan"), 0, 0)


def make_body(ndp, nch):
    def body(
        spectra, lengths, weight_in, gamma_in, beta_in, weight_mid, gamma_mid, beta_mid, cotangent
    ):
        g = Geometry(
            ndp,
            nch,
            spectra.shape[0],
            spectra.shape[2] // MEL,
            weight_in.shape[2],
            weight_mid.shape[2],
        )
        links = Links(g)
        gains = jnp.stack([gamma_in, beta_in, gamma_mid, beta_mid])
        gains = jnp.pad(gains, ((0, 0), (0, 128 - g.co)))

        piece = cut_weights(g, weight_in, weight_mid)
        cells = cut_maps(g, spectra, piece)
        cots = cut_cot(g, cotangent, cells)
        pieces_in, pieces_mid = sort_pieces(
            g, [links.chan(piece, k) for k in range(1, nch)], [cots[0]]
        )
        maps = lax.all_to_all(release_far([pieces_in], cells), "chan", 0, 0)
        planes_in = links.gather_planes(pieces_in)
        w_in = join(g, weight_in, links.gather_cores(planes_in), g.ci_all, "join_in")
        planes_mid = links.gather_planes(pieces_mid, [maps])

        pre1, x3_in, pay = first(g, lengths, gains, maps, w_in)
        got = everyone(fan(g, pay, cots[0], *planes_mid[1:]))
        planes_mid = release([got], planes_mid)
        w_mid = join(g, weight_mid, links.gather_cores(planes_mid), g.cm, "join_mid")
        cs = links.exchange(release([got], cots))
        pre2, x3_mid, table, pay, misc2 = second(g, lengths, got, pre1, w_mid)
        got = everyone(fan(g, pay, *cs[1:]))
        pooled, local2, table, pay, misc3 = pool(g, lengths, got, table, pre2, cs)
        got = everyone(pay)
        pooled = links.exchange(release([got], pooled))
        grad2, sums2, _, terms_mid, give_mid = terms_of(
            g, lengths, got, table, pre2, local2, x3_mid, got, g.cm, (MEAN2, INV2, GAMMA2), "weight_mid_terms"
        )
        got_mid = links.core(give_mid)
        split = g.turns == 2
        if split:
            stay_a, stay_b, go_a, go_b = quarters(g, terms_mid, got_mid, "mid_core_sum")
            got_b = links.plane(go_b, 0)
        else:
            stay_mid, go_b = core_sum(g, terms_mid, got_mid, got_mid, "mid_core_sum")
            got_b = go_b
        local1, pay = back(g, lengths, table, grad2, pre1, w_mid, misc2, misc3, go_b)
        got = everyone(fan(g, pay, got_b, *pooled[1:]))
        block_out, pooled_done = place(g, pooled, BF, "place_pooled")
        if split:
            (go_1,) = add_up([stay_b, got_b], 1, [got], "mid_sum_b")
            got_1 = links.plane(go_1, 1)
            got_a = links.plane(release([got], [go_a])[0], 0)
        else:
            (go_mid,) = release([got], [go_b])
        grad1, sums1, roots, terms_in, give_in = terms_of(
            g, lengths, got, table, pre1, local1, x3_in, got, g.ci_all, (MEAN1, INV1, GAMMA1), "weight_in_terms"
        )
        got_in = links.core(give_in)

        class Chain:
            def __init__(self, stay, go, depth, name):
                self.stay, self.go, self.depth, self.name = stay, go, depth, name
                self.turns = [functools.partial(links.plane, turn=t) for t in range(g.turns)]
                self.turns += [functools.partial(links.chan, k=1 << t) for t in range(g.zturns)]

            def turn(self, i, *gates):
                got = self.turns[i](self.go)
                done = halve(self.stay, got, gates, f"{self.name}_sum_{i}")
                self.stay, self.go = done if len(done) == 2 else (done[0], None)
                return self.stay

            def rest(self):
                bit = g.pieces
                while bit < ndp:
                    got = links.dp(self.stay, bit)
                    self.stay = halve(self.stay[None], got[None], [], self.name + "_rest")[0]
                    bit *= 2

            def out(self, planes, *gates):
                mine = stack(planes, gates, self.name + "_stack")
                return spread_out(g, mine, links.core(mine), self.depth, self.name + "_out")

        turns = g.turns + g.zturns
        parts = spectra_back(g, lengths, grad1, grad1, w_in)
        stay_in, go_in = core_sum(g, terms_in, got_in, parts[0], "in_core_sum")
        inner = Chain(stay_in, go_in, g.ci_all, "in")
        parts = links.exchange(parts)
        spectra_grad, spectra_done = place(g, parts, F32, "place_spectra")
        if split:
            halves = add_up([stay_a, got_a, got_1], 2, [stay_in], "mid_sum_1")
            mid = Chain(*halves, g.cm, "mid")
        else:
            mid = Chain(stay_mid, go_mid, g.cm, "mid")
            for i in range(g.turns):
                mid.turn(i, stay_in)
        gates = [parts[1 : nch - 1], [*parts[nch - 1 :], pooled_done]]
        at = mid.stay
        for i in range(g.turns):
            at = inner.turn(i, at, *(gates[i] if i < 2 else []))
            if i == 0:
                at = mid.turn(g.turns, at)
        for i in range(g.turns, turns):
            at = inner.turn(i, at, *([spectra_done] if i == g.turns else []))
            if i + 1 < turns:
                at = mid.turn(i + 1, at)
        inner.rest()
        mid.rest()
        planes_in = links.gather_planes(inner.stay)
        weight_mid_grad = mid.out(links.gather_planes(mid.stay), *planes_in[1:3])
        weight_in_grad = inner.out(planes_in)
        z = lax.axis_index("chan")

        def share(sums, i):
            return lax.dynamic_slice_in_dim(sums[i], z * g.co, g.co)

        return (
            block_out,
            spectra_grad,
            weight_in_grad,
            share(sums1, 1),
            share(sums1, 0),
            weight_mid_grad,
            share(sums2, 1),
            share(sums2, 0),
            roots[0, :4],
        )

    return body


def solution(mesh):
    placed = (
        P("dp", "chan", None),
        P("dp"),
        P(None, "chan", None),
        P("chan"),
        P("chan"),
        P(None, "chan", None),
        P("chan"),
        P("chan"),
        P("dp", "chan", None),
    )
    return jax.shard_map(
        make_body(mesh.shape["dp"], mesh.shape["chan"]),
        mesh=mesh,
        in_specs=placed,
        out_specs=(
            P("dp", "chan", None),
            P("dp", "chan", None),
            P(None, "chan", None),
            P("chan"),
            P("chan"),
            P(None, "chan", None),
            P("chan"),
            P("chan"),
            P(),
        ),
        check_vma=False,
    )
```

```python
import functools

import jax
import jax.numpy as jnp
from jax import lax
from jax.experimental import pallas as pl
from jax.experimental.pallas import tpu as pltpu
from jax.sharding import PartitionSpec as P

MEL = 8
HALO = 16
BF = jnp.bfloat16
F32 = jnp.float32
MIB = 1024 * 1024
TINY = pl.CostEstimate(flops=1, bytes_accessed=1, transcendentals=0)

VMEM = pl.BlockSpec(memory_space=pltpu.VMEM)
SMEM = pl.BlockSpec(memory_space=pltpu.SMEM)
ANY = pl.BlockSpec(memory_space=pl.ANY)
HBM = pl.BlockSpec(memory_space=pltpu.HBM)


def bits_of(n):
    return n.bit_length() - 1


class Geometry:
    def __init__(self, ndp, nch, clips, frames, c_in, c_mid):
        self.ndp, self.nch, self.ndev = ndp, nch, ndp * nch
        self.clips, self.frames = clips, frames
        self.ci_all, self.cm = c_in, c_mid
        self.ci, self.co = c_in // nch, c_mid // nch
        self.segs = nch // clips
        self.seg = frames // self.segs
        self.win = self.seg + HALO * min(self.segs - 1, 2)
        starts = [min(max(s * self.seg - HALO, 0), frames - self.win) for s in range(self.segs)]
        self.cwin = min(frames, (self.win + 48 + 63) // 64 * 64)
        assert all(min(s // 64 * 64, frames - self.cwin) + self.cwin >= s + self.win for s in starts)
        self.rows = max(16, self.co // ndp)
        self.pieces = self.co // self.rows
        self.planes = self.pieces // 2
        self.turns = bits_of(self.planes)
        self.zturns = bits_of(nch)

    def mask(self, core, turn):
        low, high = 1 << turn, 1 << (self.turns - 1 - turn)
        return low + core * (high - low)

    def plane_of(self, core, e):
        rel = 0
        for t in range(self.turns):
            if (e >> (self.turns - 1 - t)) & 1:
                rel = rel ^ self.mask(core, t)
        return rel

    def row_of(self, core, plane):
        return core * (self.co // 2) + plane * self.rows

    def zed_of(self, e):
        return sum(1 << t for t in range(self.zturns) if (e >> (self.zturns - 1 - t)) & 1)


class Here:
    def __init__(self, g, lens):
        self.z = lax.axis_index("chan")
        self.d = lax.axis_index("dp")
        self.core = lax.rem(self.d, 2)
        self.plane = lax.rem(self.d, g.pieces) // 2
        clip, seg = self.z // g.segs, lax.rem(self.z, g.segs)
        self.length = lens[clip]
        self.start, self.cstart = g_starts(g, seg)
        self.off = seg * g.seg - self.start
        self.qoff = self.start - self.cstart


def g_starts(g, seg):
    start = jnp.clip(seg * g.seg - HALO, 0, g.frames - g.win)
    return start, jnp.minimum(start // 64 * 64, g.frames - g.cwin)


def aligned(x, n=16):
    return pl.multiple_of(x, n)


def dot(a, b, contract):
    return lax.dot_general(a, b, ((contract[0], contract[1]), ((), ())), preferred_element_type=F32)


def call(body, out, ins, args, scratch, limit, flops, nbytes, name, aliases=None):
    return pl.pallas_call(
        body,
        out_shape=[pltpu.VMEM(o.shape, o.dtype) if isinstance(o, jax.ShapeDtypeStruct) else o for o in out],
        in_specs=ins,
        out_specs=[VMEM if isinstance(o, jax.ShapeDtypeStruct) else ANY for o in out],
        scratch_shapes=scratch,
        input_output_aliases=aliases or {},
        compiler_params=pltpu.CompilerParams(vmem_limit_bytes=limit * MIB),
        cost_estimate=pl.CostEstimate(
            flops=int(flops), bytes_accessed=int(nbytes), transcendentals=0
        ),
        name=name,
    )(*args)


def arr(shape, dtype):
    return jax.ShapeDtypeStruct(shape, dtype)


def keep_near(*xs):
    return [pltpu.with_memory_space_constraint(x, pltpu.VMEM) for x in xs]


class Copies:
    def __init__(self, sems):
        self.sems, self.n, self.open = sems, 0, []

    def start(self, src, dst):
        c = pltpu.make_async_copy(src, dst, self.sems.at[self.n])
        self.n += 1
        c.start()
        self.open.append(c)
        return c

    def wait(self, c):
        self.open = [o for o in self.open if o is not c]
        c.wait()

    def wait_all(self, some=None):
        for c in list(self.open if some is None else some):
            self.wait(c)


def sems(n):
    return pltpu.SemaphoreType.DMA((n,))


def row_masks(g, here, width):
    r = lax.broadcasted_iota(jnp.int32, (g.win, 128), 0)
    valid = (r + here.start) < here.length
    own = valid & (r >= here.off) & (r < here.off + g.seg)
    return widen(valid.astype(F32), width), widen(own.astype(F32), width)


def widen(x, width):
    return jnp.concatenate([x] * (width // 128), axis=1)


def shifted(x):
    n = x.shape[0]
    r = lax.broadcasted_iota(jnp.int32, (8, 1), 0)
    before, after = pltpu.roll(x, 1, 0), pltpu.roll(x, n - 1, 0)
    before = jnp.concatenate([jnp.where(r == 0, 0.0, before[:8]), before[8:]], axis=0)
    after = jnp.concatenate([after[:-8], jnp.where(r == 7, 0.0, after[-8:])], axis=0)
    return before, after


def grid_order(rows=16):
    n = MEL * rows
    r = lax.broadcasted_iota(jnp.int32, (n, n), 0)
    c = lax.broadcasted_iota(jnp.int32, (n, n), 1)
    return (c == (r % rows) * MEL + r // rows).astype(BF)


def misc_row(*scalars):
    lane = lax.broadcasted_iota(jnp.int32, (1, 128), 1)
    row = jnp.zeros((1, 128), F32)
    for i, s in enumerate(scalars):
        row = jnp.where(lane == i, s, row)
    return row


def pick(row, i):
    lane = lax.broadcasted_iota(jnp.int32, (1, 128), 1)
    return jnp.sum(jnp.where(lane == i, row, 0.0), axis=1, keepdims=True)


def sum_rows(x):
    return jnp.sum(x, axis=0, keepdims=True)


def payload(*parts):
    return jnp.concatenate(parts, axis=1)


def fan_kernel(pay, *rest):
    out = rest[-1]
    out[...] = jnp.broadcast_to(pay[...][None], out.shape)


def fan(g, pay, *after):
    out = [arr((g.ndev, *pay.shape), F32)]
    ins = [VMEM] + [ANY] * len(after)
    return call(fan_kernel, out, ins, [pay, *after], [], 4, 0, 1e5, "fan")[0]


def total_of(g, ref):
    row = jnp.sum(ref[...], axis=0)
    return row[:, : g.cm], row[:, g.cm : 2 * g.cm], row[:, 2 * g.cm :]


def side_by_side(x3, m, low, c, first, last):
    x3[m, :, 0:c] = first.astype(BF)
    x3[m, :, c : 2 * c] = low
    x3[m, :, 2 * c : 3 * c] = last.astype(BF)


def cut_weights_kernel(g, w_in, w_mid, out, sem):
    d = lax.axis_index("dp")
    core, plane = lax.rem(d, 2), lax.rem(d, g.pieces) // 2
    rows = pl.ds(aligned(g.row_of(core, plane)), g.rows)
    copies = Copies(sem)
    copies.start(w_in.at[:, rows, :], out.at[:, :, : g.ci_all])
    copies.start(w_mid.at[:, rows, :], out.at[:, :, g.ci_all :])
    copies.wait_all()


def cut_weights(g, w_in, w_mid):
    out = [arr((9, g.rows, g.ci_all + g.cm), BF)]
    args = [in_hbm(w_in), in_hbm(w_mid)]
    body = functools.partial(cut_weights_kernel, g)
    return call(body, out, [ANY] * 2, args, [sems(2)], 4, 0, 4e5, "cut_weights")[0]


def sort_kernel(g, *rest):
    n = g.nch - 1
    parts, first, second = rest[:n], rest[-2], rest[-1]
    for k in range(n):
        first[k] = parts[k][:, :, : g.ci_all]
        second[k] = parts[k][:, :, g.ci_all :]


def sort_pieces(g, parts, gates):
    n = g.nch - 1
    out = [arr((n, 9, g.rows, g.ci_all), BF), arr((n, 9, g.rows, g.cm), BF)]
    body = functools.partial(sort_kernel, g)
    ins = [VMEM] * n + [ANY] * len(gates)
    return call(body, out, ins, [*parts, *gates], [], 4, 0, 1e6, "sort_pieces")


def cut_maps_kernel(g, spec, after, out, held, sem):
    copies = Copies(sem)
    first = []
    for z in range(g.nch):
        start = static_start(g, z % g.segs) * MEL
        first.append(copies.start(spec.at[z // g.segs, :, start : start + g.win * MEL], held.at[z]))
    for z in range(g.nch):
        copies.wait(first[z])
        copies.start(held.at[z], out.at[z])
    copies.wait_all()


def cut_maps(g, spec, after):
    shape = (g.nch, g.ci, g.win * MEL)
    body = functools.partial(cut_maps_kernel, g)
    args = [in_hbm(spec), after]
    scratch = [pltpu.VMEM(shape, BF), sems(2 * g.nch)]
    return call(body, [pltpu.HBM(shape, BF)], [ANY] * 2, args, scratch, 4, 0, 2e6, "cut_maps")[0]


def static_start(g, seg):
    return min(max(seg * g.seg - HALO, 0), g.frames - g.win)


def cut_cot_kernel(g, cot, after, *rest):
    n = g.nch
    cs, sem = rest[:n], rest[n]
    z = lax.axis_index("chan")
    copies = Copies(sem)
    for k in range(n):
        to = z ^ k
        clip, seg = to // g.segs, lax.rem(to, g.segs)
        _, cstart = g_starts(g, seg)
        copies.start(cot.at[clip, :, pl.ds(aligned(cstart * 2, 128), g.cwin * 2)], cs[k])
    copies.wait_all()


def cut_cot(g, cot, after):
    n = g.nch
    out = [arr((g.co, g.cwin * 2), BF)] * n
    body = functools.partial(cut_cot_kernel, g)
    return call(body, out, [ANY] * 2, [in_hbm(cot), after], [sems(n)], 4, 0, 1e6, "cut_cotangent")


def in_hbm(x):
    return pltpu.with_memory_space_constraint(x, pltpu.HBM)


def join_kernel(g, own, *rest):
    parts, w = rest[:-1], rest[-1]
    z, d = lax.axis_index("chan"), lax.axis_index("dp")
    mine, plane = lax.rem(d, 2), lax.rem(d, g.pieces) // 2
    w[:, pl.ds(aligned(z * g.co), g.co), :] = own[...]
    for side in range(2):
        core = mine if side == 0 else 1 - mine
        for e in range(g.planes):
            row = g.row_of(core, plane ^ g.plane_of(core, e))
            for k in range(1, g.nch):
                at = aligned((z ^ k) * g.co + row)
                w[:, pl.ds(at, g.rows), :] = parts[side * g.planes + e][k - 1]


def join(g, own, parts, depth, name):
    body = functools.partial(join_kernel, g)
    args = [*keep_near(own), *parts]
    ins = [VMEM] * len(args)
    return call(body, [arr((9, g.cm, depth), BF)], ins, args, [], 8, 0, 4 * MIB, name)[0]


def convolve(v3, w, part, back, finish, carry, unrolled=False, window=None):
    def taps(t):
        b = 2 - t if back else t
        return jnp.concatenate([w[b], w[3 + b], w[6 + b]], axis=0 if back else 1)

    contract = ((1,), (0,)) if back else ((1,), (1,))
    depth = v3.shape[2]

    size = part.shape[1]
    window = pl.ds(0, size) if window is None else window

    def times(first, n, t):
        return dot(v3[pl.ds(first, n), window, :].reshape(n * size, depth), taps(t), contract)

    def rows_of(term, n):
        return [term[k * size : (k + 1) * size] for k in range(n)]

    if unrolled:
        for i in range(2):
            total = rows_of(times(4 * i, 4, 1), 4)
            side = rows_of(times(1 + 2 * i, 4, 2 - 2 * i), 4)
            edge = rows_of(times(5 * i, 3, 2 * i), 3)
            for k in range(4):
                value = total[k] + side[k]
                if 0 <= k + i - 1 < 3:
                    value = value + edge[k + i - 1]
                carry = finish(4 * i + k, value, carry)
        return carry

    def step(i, carry):
        part[pl.ds(3 * i + 1, 3)] = times(5 * i, 3, 2 * i).reshape(3, size, part.shape[2])
        part[7 * i] = jnp.zeros(part.shape[1:], F32)
        total = times(4 * i, 4, 1) + times(1 + 2 * i, 4, 2 - 2 * i)
        for k in range(4):
            m = 4 * i + k
            carry = finish(m, part[m] + total[k * size : (k + 1) * size], carry)
        return carry

    return lax.fori_loop(0, 2, step, carry)


def convolve_sums(g, here, x3, w, pre, unrolled):
    _, own = row_masks(g, here, g.cm)

    def finish(m, total, sums):
        pre[m] = total
        kept = total * own
        return sums[0] + sum_rows(kept), sums[1] + sum_rows(kept * total)

    zero = jnp.zeros((1, g.cm), F32)
    return convolve(x3, w, pre, False, finish, (zero, zero), unrolled)


def first_kernel(g, lens, gains, w, maps, pre, x3, pay):
    here = Here(g, lens)
    c = g.ci_all
    order = grid_order()
    row = lax.broadcasted_iota(jnp.int32, (MEL * 16, 128), 0) % 16

    def place_cells(j, square):
        cells = maps[:, :, 128 * j : 128 * (j + 1)].reshape(c, 128)
        frame = row + 16 * j
        valid = (frame + here.start) < here.length
        own = (frame >= here.off) & (frame < here.off + g.seg)
        block = dot(order, cells, ((1,), (1,))) * widen(valid.astype(F32), c)
        x3[:, 16 * j : 16 * (j + 1), c : 2 * c] = block.astype(BF).reshape(MEL, 16, c)
        return square + sum_rows(block * block * widen(own.astype(F32), c))

    square = jnp.zeros((1, c), F32)
    for j in range(g.win // 16):
        square = place_cells(j, square)
    for m in range(MEL):
        before, after_ = shifted(x3[m, :, c : 2 * c].astype(F32))
        x3[m, :, 0:c] = before.astype(BF)
        x3[m, :, 2 * c : 3 * c] = after_.astype(BF)

    one, two = convolve_sums(g, here, x3, w, pre, True)
    frame_total = 0
    pair_total = 0
    for i in range(g.clips):
        frame_total = frame_total + lens[i]
        pair_total = pair_total + (lens[i] + 1) // 2
    row = misc_row(
        frame_total.astype(F32), pair_total.astype(F32), jnp.sum(square, axis=1, keepdims=True)
    )
    pay[...] = payload(one, two, row, *[gains[i : i + 1] for i in range(4)])


def first(g, lens, gains, maps, w):
    body = functools.partial(first_kernel, g)
    out = [
        arr((MEL, g.win, g.cm), F32),
        arr((MEL, g.win, 3 * g.ci_all), BF),
        arr((1, 2 * g.cm + 5 * 128), F32),
    ]
    args = [lens, gains, *keep_near(w, maps)]
    ins = [SMEM] + [VMEM] * 3
    flops = 2 * 9 * MEL * g.win * g.ci_all * g.cm
    return call(body, out, ins, args, [], 10, flops, 10 * MIB, "first_conv")


MEAN1, INV1, GAMMA1, BETA1, GAMMA2, BETA2, COUNT, PAIRS, SQ0, MEAN2, INV2 = range(11)
TABLE = 16


def half_affine(mean, inverse, gamma, beta):
    scale = 0.5 * gamma * inverse
    return scale, 0.5 * beta - mean * scale


def second_kernel(g, lens, got, pre1, w, pre, x3, table, pay, misc_out):
    here = Here(g, lens)
    c = g.cm
    valid, own = row_masks(g, here, c)
    one, two, rest = total_of(g, got)
    misc = rest[:, :128]
    count = MEL * pick(misc, 0) / g.nch
    pairs = (MEL // 2) * pick(misc, 1) / g.nch
    at = [2 * c + 128 * (1 + i) for i in range(4)]
    vectors = [
        jnp.concatenate([got[zz, :, i : i + g.co] for zz in range(g.nch)], axis=1) for i in at
    ]
    mean = one / count
    inverse = lax.rsqrt(two / count - mean * mean + 1e-05)
    wide = jnp.zeros((1, c), F32)
    table[...] = jnp.concatenate(
        [mean, inverse, *vectors, wide + count, wide + pairs, wide + pick(misc, 2)]
        + [wide] * (TABLE - 9),
        axis=0,
    )
    scale, shift = half_affine(mean, inverse, vectors[0], vectors[1])


    def activate(m, square):
        half = pre1[m] * scale + shift
        act = half * (1.0 + jnp.tanh(half)) * valid
        low = act.astype(BF)
        before, after = shifted(low.astype(F32))
        side_by_side(x3, m, low, c, before, after)
        return square + sum_rows(act * act * own)

    square = jnp.zeros((1, c), F32)
    for m in range(MEL):
        square = activate(m, square)
    one, two = convolve_sums(g, here, x3, w, pre, True)
    pay[...] = payload(one, two)
    misc_out[...] = misc_row(jnp.sum(square, axis=1, keepdims=True))


def second(g, lens, got, pre1, w):
    body = functools.partial(second_kernel, g)
    out = [
        arr((MEL, g.win, g.cm), F32),
        arr((MEL, g.win, 3 * g.cm), BF),
        arr((TABLE, g.cm), F32),
        arr((1, 2 * g.cm), F32),
        arr((1, 128), F32),
    ]
    args = [lens, *keep_near(got, pre1, w)]
    flops = 2 * 9 * MEL * g.win * g.cm * g.cm
    ins = [SMEM, VMEM, VMEM, VMEM]
    return call(body, out, ins, args, [], 10, flops, 17 * MIB, "second_conv")


def pool_kernel(g, lens, got, old_ref, pre2, *rest):
    n, c = g.nch, g.cm
    cs, outs = rest[:n], rest[n : 2 * n]
    local_ref, table, pay, misc_out, held, grads, total, flat = rest[2 * n :]
    here = Here(g, lens)
    for k in range(n):
        held[pl.ds(aligned((here.z ^ k) * g.co), g.co), :] = cs[k][...]
    r = lax.broadcasted_iota(jnp.int32, (256, 128), 0)
    l = lax.broadcasted_iota(jnp.int32, (256, 128), 1)
    spread = (l == (r % 64) // 2 * 4 + r // 64).astype(BF)

    @pl.loop(0, g.cwin // 64)
    def _(j):
        cells = held[:, pl.ds(aligned(128 * j, 128), 128)]
        block = dot(spread, cells, ((1,), (1,)))
        grads[:, pl.ds(aligned(64 * j), 64), :] = block.reshape(MEL // 2, 64, c)

    one, two, _ = total_of(g, got)
    old = old_ref[...]
    count = old[COUNT : COUNT + 1]
    mean = one / count
    inverse = lax.rsqrt(two / count - mean * mean + 1e-05)
    wide = jnp.zeros((1, c), F32)
    table[...] = jnp.concatenate([old[:MEAN2], mean, inverse] + [wide] * (TABLE - 11), axis=0)
    half_gamma, half_beta = 0.5 * old[GAMMA2 : GAMMA2 + 1], 0.5 * old[BETA2 : BETA2 + 1]
    less = -mean * inverse
    side = g.win - g.seg
    segment = pl.ds(aligned(here.off), g.seg)
    sides = [
        aligned(jnp.where(16 * j < here.off, 16 * j, 16 * j + g.seg)) for j in range(side // 16)
    ]

    def weights(rows, start, width):
        frame = lax.broadcasted_iota(jnp.int32, (rows, 128), 0) + (here.start + start)
        valid = (frame < here.length).astype(F32)
        share = jnp.where(here.length - frame // 2 * 2 >= 2, 0.25, 0.5)
        return widen(0.5 * share * valid, width), widen(valid, width)

    half_share, valid = weights(g.seg, here.off, c)
    side_shares = [weights(16, start, c)[0] for start in sides]
    out_row = lax.broadcasted_iota(jnp.int32, (g.seg, 2 * g.seg), 0)
    out_cell = lax.broadcasted_iota(jnp.int32, (g.seg, 2 * g.seg), 1)
    first_cell = out_row // 2 * 4
    frame = out_row + (here.start + here.off)
    out_share = jnp.where(here.length - frame // 2 * 2 >= 2, 0.25, 0.5)
    total[...] = jnp.zeros(total.shape, F32)

    def bent(pre):
        scaled = pre * inverse + less
        half = scaled * half_gamma + half_beta
        bend = jnp.tanh(half)
        twice = 1.0 + bend
        whole = half * twice
        return scaled, whole, twice + whole * (1.0 - bend)

    def step(k, sums):
        beta_sum, gamma_sum, square = sums
        given = grads[k, pl.ds(aligned(here.qoff + here.off), g.seg), :] * half_share
        pair = None
        for i in range(2):
            m = 2 * k + i
            scaled, whole, slope = bent(pre2[m, segment, :])
            act = whole * valid
            square = square + sum_rows(act * act)
            local = given * slope
            local_ref[m, segment, :] = local
            beta_sum = beta_sum + sum_rows(local)
            gamma_sum = gamma_sum + sum_rows(local * scaled)
            pair = act if pair is None else pair + act
            for start, side_share in zip(sides, side_shares, strict=True):
                rows = pl.ds(start, 16)
                _, _, slope = bent(pre2[m, rows, :])
                given_side = grads[k, pl.ds(aligned(here.qoff + start), 16), :] * side_share
                local_ref[m, rows, :] = given_side * slope
        gather = jnp.where(out_cell == first_cell + k, out_share, 0.0).astype(BF)
        total[...] += dot(pair.astype(BF), gather, ((0,), (0,)))
        return beta_sum, gamma_sum, square

    zero = jnp.zeros((1, c), F32)
    beta_sum, gamma_sum, square = lax.fori_loop(0, MEL // 2, step, (zero, zero, zero))
    pooled = total[...]
    flat[...] = pooled.astype(BF)
    for k in range(n):
        outs[k][...] = flat[pl.ds(aligned((here.z ^ k) * g.co), g.co), :]
    pooled_square = sum_rows(jnp.sum(pooled * pooled, axis=1, keepdims=True))
    pay[...] = jnp.broadcast_to(payload(beta_sum, gamma_sum)[None], pay.shape)
    misc_out[...] = misc_row(jnp.sum(square, axis=1, keepdims=True), pooled_square)


def pool(g, lens, got, table, pre2, cs):
    n = g.nch
    body = functools.partial(pool_kernel, g)
    out = [arr((g.co, 2 * g.seg), BF)] * n + [
        arr((MEL, g.win, g.cm), F32),
        arr((TABLE, g.cm), F32),
        arr((g.ndev, 1, 2 * g.cm), F32),
        arr((1, 128), F32),
    ]
    scratch = [
        pltpu.VMEM((g.cm, g.cwin * 2), BF),
        pltpu.VMEM((MEL // 2, g.cwin, g.cm), F32),
        pltpu.VMEM((g.cm, 2 * g.seg), F32),
        pltpu.VMEM((g.cm, 2 * g.seg), BF),
    ]
    args = [lens, *keep_near(got, table, pre2, *cs)]
    ins = [SMEM] + [VMEM] * (len(args) - 1)
    out = call(body, out, ins, args, scratch, 12, 4e9, 8 * MIB, "pool")
    return out[:n], *out[n:]


def terms_kernel(g, depth, norm, lens, got, table, pre, local, x3, after, *refs):
    grad, sums, roots, terms, give = refs
    here = Here(g, lens)
    c = g.cm
    valid, _ = row_masks(g, here, c)
    beta_sum, gamma_sum, rest = total_of(g, got)
    t = table[...]
    mean, inverse, gamma = (t[i : i + 1] for i in norm)
    count = t[COUNT : COUNT + 1]
    sums[...] = jnp.concatenate([beta_sum, gamma_sum] + [jnp.zeros((1, c), F32)] * 6, axis=0)
    if rest.shape[1]:
        second, third = rest[:, :128], rest[:, 128:]
        tops = misc_row(
            pick(t[SQ0 : SQ0 + 1, :128], 0), pick(second, 0), pick(third, 0), pick(third, 1)
        )
        lane = lax.broadcasted_iota(jnp.int32, (1, 128), 1)
        cells, pairs = count[:, :128], t[PAIRS : PAIRS + 1, :128]
        under = jnp.where(lane == 0, cells * g.ci_all, jnp.where(lane == 3, pairs * c, cells * c))
        roots[...] = jnp.broadcast_to(jnp.sqrt(tops / under), (8, 128))
    factor = gamma * inverse
    slope = factor * inverse * gamma_sum / count
    level = factor * beta_sum / count - mean * slope

    @pl.loop(0, MEL)
    def _(m):
        value = valid * (local[m] * factor - pre[m] * slope - level)
        grad[m] = value.astype(BF)

    segment = pl.ds(aligned(here.off), g.seg)

    @pl.loop(0, 3)
    def _(a):
        lanes_of = pl.ds(aligned(a * depth, 128), depth)
        for b in (1, 0, 2):
            low = max(0, 1 - b)
            high = min(MEL, MEL + 1 - b)
            rows = (high - low) * g.seg
            left = grad[low:high, segment, :].reshape(rows, c)
            right = x3[low + b - 1 : high + b - 1, segment, lanes_of].reshape(rows, depth)
            term = dot(left, right, ((0,), (0,))).astype(BF)
            for z in range(g.nch):
                for s in range(2):
                    for p in range(g.planes):
                        at = z * g.co + g.row_of(s, p)
                        terms[s, z, p, 3 * a + b] = term[at : at + g.rows]

    give[...] = terms[1 - here.core]


def terms_of(g, lens, got, table, pre, local, x3, after, depth, norm, name):
    body = functools.partial(terms_kernel, g, depth, norm)
    shape = (g.nch, g.planes, 9, g.rows, depth)
    out = [
        arr((MEL, g.win, g.cm), BF),
        arr((8, g.cm), F32),
        arr((8, 128), F32),
        arr((2, *shape), BF),
        arr(shape, BF),
    ]
    args = [lens, *keep_near(got, table, pre, local, x3), after]
    ins = [SMEM] + [VMEM] * 5 + [ANY]
    flops = 2 * 9 * MEL * g.win * g.cm * depth
    return call(body, out, ins, args, [], 10, flops, 15 * MIB, name)


def back_kernel(g, lens, table, grad, pre1, w, misc2, misc3, after, local1, pay, g3):
    here = Here(g, lens)
    c = g.cm
    valid, own = row_masks(g, here, c)
    t = table[...]

    def row(i):
        return t[i : i + 1]


    for m in range(MEL):
        low = grad[m]
        before, after = shifted(low.astype(F32))
        side_by_side(g3, m, low, c, after, before)

    inverse, less = row(INV1), -row(MEAN1) * row(INV1)
    half_gamma, half_beta = 0.5 * row(GAMMA1), 0.5 * row(BETA1)
    half_valid = 0.5 * valid

    def finish(m, given, sums):
        scaled = pre1[m] * inverse + less
        half = scaled * half_gamma + half_beta
        bend = jnp.tanh(half)
        twice = 1.0 + bend
        local = given * half_valid * (twice + half * twice * (1.0 - bend))
        local1[m] = local
        kept = local * own
        return sums[0] + sum_rows(kept), sums[1] + sum_rows(kept * scaled)

    zero = jnp.zeros((1, c), F32)
    beta_sum, gamma_sum = convolve(g3, w, local1, True, finish, (zero, zero), True)
    pay[...] = payload(beta_sum, gamma_sum, misc2[...], misc3[...])


def back(g, lens, table, grad, pre1, w, misc2, misc3, after):
    body = functools.partial(back_kernel, g)
    out = [arr((MEL, g.win, g.cm), F32), arr((1, 2 * g.cm + 2 * 128), F32)]
    scratch = [pltpu.VMEM((MEL, g.win, 3 * g.cm), BF)]
    args = [lens, *keep_near(table, grad, pre1, w, misc2, misc3), after]
    flops = 2 * 9 * MEL * g.win * g.cm * g.cm
    ins = [SMEM] + [VMEM] * 6 + [ANY]
    return call(body, out, ins, args, scratch, 14, flops, 20 * MIB, "second_back")


def release_kernel(*refs):
    pass


def release_far(gates, x):
    n = len(gates)
    return pl.pallas_call(
        release_kernel,
        out_shape=pltpu.HBM(x.shape, x.dtype),
        in_specs=[ANY] * (n + 1),
        out_specs=ANY,
        input_output_aliases={n: 0},
        compiler_params=pltpu.CompilerParams(vmem_limit_bytes=2 * MIB),
        name="release_far",
    )(*gates, in_hbm(x))


def release(gates, arrays):
    out = [arr(x.shape, x.dtype) for x in arrays]
    n = len(gates)
    ins = [ANY] * n + [VMEM] * len(arrays)
    aliases = {i + n: i for i in range(len(arrays))}
    args = [*gates, *keep_near(*arrays)]
    return call(release_kernel, out, ins, args, [], 2, 0, 1, "release", aliases)


def spectra_kernel(g, lens, grad, after, w, *rest):
    n, c = g.nch, g.cm
    outs, (g3, rows, flat, part) = rest[:n], rest[n:]
    here = Here(g, lens)

    @pl.loop(0, MEL)
    def _(m):
        low = grad[m]
        before, after_ = shifted(low.astype(F32))
        side_by_side(g3, m, low, c, after_, before)

    r = lax.broadcasted_iota(jnp.int32, (g.seg, 128), 0) + here.off + here.start
    valid = widen((r < here.length).astype(F32), g.ci_all)

    def finish(m, total, carry):
        rows[m] = (total * valid).astype(BF)
        return carry

    convolve(g3, w, part, True, finish, 0, False, pl.ds(aligned(here.off), g.seg))
    order = grid_order()

    for j in range(g.seg // 16):
        block = rows[:, 16 * j : 16 * (j + 1), :].reshape(MEL * 16, g.ci_all)
        flat[:, 128 * j : 128 * (j + 1)] = dot(block, order, ((0,), (0,))).astype(BF)

    for k in range(n):
        outs[k][...] = flat[pl.ds(aligned((here.z ^ k) * g.ci), g.ci), :]


def spectra_back(g, lens, grad, after, w):
    n = g.nch
    body = functools.partial(spectra_kernel, g)
    out = [arr((g.ci, g.seg * MEL), BF)] * n
    scratch = [
        pltpu.VMEM((MEL, g.win, 3 * g.cm), BF),
        pltpu.VMEM((MEL, g.seg, g.ci_all), BF),
        pltpu.VMEM((g.ci_all, g.seg * MEL), BF),
        pltpu.VMEM((MEL, g.seg, g.ci_all), F32),
    ]
    grad, w = keep_near(grad, w)
    args = [lens, grad, after, w]
    flops = 2 * 9 * MEL * g.win * g.cm * g.ci_all
    ins = [SMEM, VMEM, ANY, VMEM]
    return call(body, out, ins, args, scratch, 14, flops, 5 * MIB, "spectra_back")


def place_kernel(g, width, *rest):
    n = g.nch
    parts, out, done = rest[:n], rest[n], rest[n + 1]
    z = lax.axis_index("chan")
    done[...] = jnp.zeros(done.shape, F32)
    for k in range(n):
        source = z ^ k
        for zz in range(n):

            @pl.when(source == zz)
            def _():
                at = zz % g.segs * width
                out[zz // g.segs, :, at : at + width] = parts[k][...].astype(out.dtype)


def place(g, parts, dtype, name):
    channels, width = parts[0].shape
    return pl.pallas_call(
        functools.partial(place_kernel, g, width),
        out_shape=[
            jax.ShapeDtypeStruct((g.clips, channels, g.segs * width), dtype),
            jax.ShapeDtypeStruct((8, 128), F32),
        ],
        in_specs=[VMEM] * g.nch,
        out_specs=[VMEM] * 2,
        compiler_params=pltpu.CompilerParams(vmem_limit_bytes=8 * MIB),
        cost_estimate=TINY,
        name=name,
    )(*parts)


def core_sum_kernel(g, terms, got, after, stay, go):
    d, z = lax.axis_index("dp"), lax.axis_index("chan")
    core, plane = lax.rem(d, 2), lax.rem(d, g.pieces) // 2
    half = g.planes // 2
    for e in range(g.planes):
        at = plane ^ g.plane_of(core, e)
        for k in range(g.nch):
            source = z ^ g.zed_of(k)
            value = terms[core, source, at].astype(F32) + got[source, at].astype(F32)
            to = stay if e < half else go
            to[(e % half) * g.nch + k] = value.astype(BF)


def core_sum(g, terms, got, after, name):
    shape = (g.planes // 2 * g.nch, *got.shape[2:])
    return pl.pallas_call(
        functools.partial(core_sum_kernel, g),
        out_shape=[pltpu.VMEM(shape, BF)] * 2,
        in_specs=[VMEM, VMEM, ANY],
        out_specs=[VMEM] * 2,
        compiler_params=pltpu.CompilerParams(vmem_limit_bytes=16 * MIB),
        name=name,
    )(keep_near(terms)[0], got, after)


def quarter_kernel(g, terms, got, *outs):
    d, z = lax.axis_index("dp"), lax.axis_index("chan")
    core, plane = lax.rem(d, 2), lax.rem(d, g.pieces) // 2
    for e in range(g.planes):
        at = plane ^ g.plane_of(core, e)
        for k in range(g.nch):
            source = z ^ g.zed_of(k)
            value = terms[core, source, at].astype(F32) + got[source, at].astype(F32)
            outs[e][k] = value.astype(BF)


def quarters(g, terms, got, name):
    shape = (g.nch, *got.shape[2:])
    return pl.pallas_call(
        functools.partial(quarter_kernel, g),
        out_shape=[pltpu.VMEM(shape, BF)] * g.planes,
        in_specs=[VMEM, VMEM],
        out_specs=[VMEM] * g.planes,
        compiler_params=pltpu.CompilerParams(vmem_limit_bytes=16 * MIB),
        name=name,
    )(keep_near(terms)[0], got)


def add_kernel(n, halves, *rest):
    first = rest[0]
    outs = rest[len(rest) - halves :]
    count = first.shape[0] // halves
    for i in range(first.shape[0]):
        total = first[i].astype(F32)
        for r in rest[1:n]:
            total = total + r[i].astype(F32)
        outs[i // count][i % count] = total.astype(BF)


def add_up(parts, halves, gates, name):
    n = len(parts)
    shape = (parts[0].shape[0] // halves, *parts[0].shape[1:])
    return pl.pallas_call(
        functools.partial(add_kernel, n, halves),
        out_shape=[pltpu.VMEM(shape, BF)] * halves,
        in_specs=[VMEM] * n + [ANY] * len(gates),
        out_specs=[VMEM] * halves,
        compiler_params=pltpu.CompilerParams(vmem_limit_bytes=8 * MIB),
        name=name,
    )(*parts, *gates)


def halve_kernel(stay, got, *rest):
    n = stay.shape[0]
    outs = rest[-2:] if n > 1 else rest[-1:]
    for i in range(n):
        value = stay[i].astype(F32) + got[i].astype(F32)
        if n == 1:
            outs[0][...] = value.astype(BF)
        else:
            outs[i // (n // 2)][i % (n // 2)] = value.astype(BF)


def halve(stay, got, gates, name):
    n = stay.shape[0]
    if n == 1:
        out = [jax.ShapeDtypeStruct(stay.shape[1:], BF)]
    else:
        out = [jax.ShapeDtypeStruct((n // 2, *stay.shape[1:]), BF)] * 2
    return pl.pallas_call(
        halve_kernel,
        out_shape=out,
        in_specs=[VMEM, VMEM] + [ANY] * len(gates),
        out_specs=[VMEM] * len(out),
        compiler_params=pltpu.CompilerParams(vmem_limit_bytes=8 * MIB),
        name=name,
    )(stay, got, *gates)


def spread_kernel(g, mine, other, out, done):
    done[...] = jnp.zeros(done.shape, F32)
    d = lax.axis_index("dp")
    core, plane = lax.rem(d, 2), lax.rem(d, g.pieces) // 2
    for side, part in enumerate((mine, other)):
        c = core if side == 0 else 1 - core
        for e in range(g.planes):
            at = aligned(g.row_of(c, plane ^ g.plane_of(c, e)))
            out[:, pl.ds(at, g.rows), :] = part[e].astype(F32)


def spread_out(g, mine, other, depth, name):
    return pl.pallas_call(
        functools.partial(spread_kernel, g),
        out_shape=[
            jax.ShapeDtypeStruct((9, g.co, depth), F32),
            jax.ShapeDtypeStruct((8, 128), F32),
        ],
        in_specs=[VMEM] * 2,
        out_specs=[VMEM] * 2,
        compiler_params=pltpu.CompilerParams(vmem_limit_bytes=12 * MIB),
        name=name,
    )(mine, other)


def stack_kernel(n, *refs):
    for k, r in enumerate(refs[:n]):
        refs[-1][k] = r[...]


def stack(parts, gates, name):
    n = len(parts)
    out = [arr((n, *parts[0].shape), parts[0].dtype)]
    ins = [VMEM] * n + [ANY] * len(gates)
    body = functools.partial(stack_kernel, n)
    return call(body, out, ins, [*parts, *gates], [], 6, 0, 1e6, name)[0]


class Links:
    def __init__(self, g):
        self.g = g

    def core(self, x):
        return lax.ppermute(x, "dp", [(i, i ^ 1) for i in range(self.g.ndp)])

    def dp(self, x, bit):
        return lax.ppermute(x, "dp", [(i, i ^ bit) for i in range(self.g.ndp)])

    def plane(self, x, turn):
        g = self.g
        return lax.ppermute(x, "dp", [(i, i ^ (2 * g.mask(i & 1, turn))) for i in range(g.ndp)])

    def chan(self, x, k):
        return lax.ppermute(x, "chan", [(i, i ^ k) for i in range(self.g.nch)])

    def exchange(self, parts):
        return [parts[0]] + [self.chan(parts[k], k) for k in range(1, self.g.nch)]

    def gather_planes(self, x, gates=()):
        have = [x]
        for turn in reversed(range(self.g.turns)):
            more = [self.plane(h, turn) for h in have[:1]]
            rest = have[1:]
            if gates and turn == 0 and rest:
                rest = release([*gates, *more], rest)
            have = have + more + [self.plane(h, turn) for h in rest]
        return have

    def gather_cores(self, have):
        return [*have, *[self.core(h) for h in have]]

    def gather_direct(self, x):
        g = self.g
        pairs = [[(i, i ^ (2 * g.plane_of(i & 1, e))) for i in range(g.ndp)] for e in range(g.planes)]
        return [x] + [lax.ppermute(x, "dp", p) for p in pairs[1:]]


def everyone(x):
    return lax.all_to_all(x, ("dp", "chan"), 0, 0)


def make_body(ndp, nch):
    def body(
        spectra, lengths, weight_in, gamma_in, beta_in, weight_mid, gamma_mid, beta_mid, cotangent
    ):
        g = Geometry(
            ndp,
            nch,
            spectra.shape[0],
            spectra.shape[2] // MEL,
            weight_in.shape[2],
            weight_mid.shape[2],
        )
        links = Links(g)
        gains = jnp.stack([gamma_in, beta_in, gamma_mid, beta_mid])
        gains = jnp.pad(gains, ((0, 0), (0, 128 - g.co)))

        piece = cut_weights(g, weight_in, weight_mid)
        cells = cut_maps(g, spectra, piece)
        cots = cut_cot(g, cotangent, cells)
        pieces_in, pieces_mid = sort_pieces(
            g, [links.chan(piece, k) for k in range(1, nch)], [cots[0]]
        )
        maps = lax.all_to_all(release_far([pieces_in], cells), "chan", 0, 0)
        planes_in = links.gather_planes(pieces_in)
        w_in = join(g, weight_in, links.gather_cores(planes_in), g.ci_all, "join_in")
        planes_mid = links.gather_planes(pieces_mid, [maps])

        pre1, x3_in, pay = first(g, lengths, gains, maps, w_in)
        got = everyone(fan(g, pay, cots[0], *planes_mid[1:]))
        planes_mid = release([got], planes_mid)
        w_mid = join(g, weight_mid, links.gather_cores(planes_mid), g.cm, "join_mid")
        cs = links.exchange(release([got], cots))
        pre2, x3_mid, table, pay, misc2 = second(g, lengths, got, pre1, w_mid)
        got = everyone(fan(g, pay, *cs[1:]))
        pooled, local2, table, pay, misc3 = pool(g, lengths, got, table, pre2, cs)
        got = everyone(pay)
        pooled = links.exchange(release([got], pooled))
        grad2, sums2, _, terms_mid, give_mid = terms_of(
            g, lengths, got, table, pre2, local2, x3_mid, got, g.cm, (MEAN2, INV2, GAMMA2), "weight_mid_terms"
        )
        got_mid = links.core(give_mid)
        split = g.turns == 2
        if split:
            stay_a, stay_b, go_a, go_b = quarters(g, terms_mid, got_mid, "mid_core_sum")
            got_b = links.plane(go_b, 0)
        else:
            stay_mid, go_b = core_sum(g, terms_mid, got_mid, got_mid, "mid_core_sum")
            got_b = go_b
        local1, pay = back(g, lengths, table, grad2, pre1, w_mid, misc2, misc3, go_b)
        got = everyone(fan(g, pay, got_b, *pooled[1:]))
        block_out, pooled_done = place(g, pooled, BF, "place_pooled")
        if split:
            (go_1,) = add_up([stay_b, got_b], 1, [got], "mid_sum_b")
            got_1 = links.plane(go_1, 1)
            got_a = links.plane(release([got], [go_a])[0], 0)
        else:
            (go_mid,) = release([got], [go_b])
        grad1, sums1, roots, terms_in, give_in = terms_of(
            g, lengths, got, table, pre1, local1, x3_in, got, g.ci_all, (MEAN1, INV1, GAMMA1), "weight_in_terms"
        )
        got_in = links.core(give_in)

        class Chain:
            def __init__(self, stay, go, depth, name):
                self.stay, self.go, self.depth, self.name = stay, go, depth, name
                self.turns = [functools.partial(links.plane, turn=t) for t in range(g.turns)]
                self.turns += [functools.partial(links.chan, k=1 << t) for t in range(g.zturns)]

            def turn(self, i, *gates):
                got = self.turns[i](self.go)
                done = halve(self.stay, got, gates, f"{self.name}_sum_{i}")
                self.stay, self.go = done if len(done) == 2 else (done[0], None)
                return self.stay

            def rest(self):
                bit = g.pieces
                while bit < ndp:
                    got = links.dp(self.stay, bit)
                    self.stay = halve(self.stay[None], got[None], [], self.name + "_rest")[0]
                    bit *= 2

            def out(self, planes, *gates):
                mine = stack(planes, gates, self.name + "_stack")
                return spread_out(g, mine, links.core(mine), self.depth, self.name + "_out")

        turns = g.turns + g.zturns
        parts = spectra_back(g, lengths, grad1, grad1, w_in)
        stay_in, go_in = core_sum(g, terms_in, got_in, parts[0], "in_core_sum")
        inner = Chain(stay_in, go_in, g.ci_all, "in")
        parts = links.exchange(parts)
        spectra_grad, spectra_done = place(g, parts, F32, "place_spectra")
        if split:
            halves = add_up([stay_a, got_a, got_1], 2, [stay_in], "mid_sum_1")
            mid = Chain(*halves, g.cm, "mid")
        else:
            mid = Chain(stay_mid, go_mid, g.cm, "mid")
            for i in range(g.turns):
                mid.turn(i, stay_in)
        gates = [parts[1 : nch - 1], [pooled_done]]
        at = mid.stay
        for i in range(g.turns):
            at = inner.turn(i, at, *(gates[i] if i < 2 else []))
            if i == 0:
                at = mid.turn(g.turns, at)
        for i in range(g.turns, turns):
            at = inner.turn(i, at, *(parts[nch - 1 :] if i == g.turns else []))
            if i + 1 < turns:
                at = mid.turn(i + 1, at)
        inner.rest()
        mid.rest()
        planes_in = links.gather_planes(inner.stay)
        weight_mid_grad, mid_done = mid.out(links.gather_direct(mid.stay), *planes_in[1:3])
        weight_in_grad, _ = inner.out(planes_in, mid_done, spectra_done)
        z = lax.axis_index("chan")

        def share(sums, i):
            return lax.dynamic_slice_in_dim(sums[i], z * g.co, g.co)

        return (
            block_out,
            spectra_grad,
            weight_in_grad,
            share(sums1, 1),
            share(sums1, 0),
            weight_mid_grad,
            share(sums2, 1),
            share(sums2, 0),
            roots[0, :4],
        )

    return body


def solution(mesh):
    placed = (
        P("dp", "chan", None),
        P("dp"),
        P(None, "chan", None),
        P("chan"),
        P("chan"),
        P(None, "chan", None),
        P("chan"),
        P("chan"),
        P("dp", "chan", None),
    )
    return jax.shard_map(
        make_body(mesh.shape["dp"], mesh.shape["chan"]),
        mesh=mesh,
        in_specs=placed,
        out_specs=(
            P("dp", "chan", None),
            P("dp", "chan", None),
            P(None, "chan", None),
            P("chan"),
            P("chan"),
            P(None, "chan", None),
            P("chan"),
            P("chan"),
            P(),
        ),
        check_vma=False,
    )
```

```python
import functools

import jax
import jax.numpy as jnp
from jax import lax
from jax.experimental import pallas as pl
from jax.experimental.pallas import tpu as pltpu
from jax.sharding import PartitionSpec as P

MEL = 8
HALO = 16
BF = jnp.bfloat16
F32 = jnp.float32
MIB = 1024 * 1024
TINY = pl.CostEstimate(flops=1, bytes_accessed=1, transcendentals=0)

VMEM = pl.BlockSpec(memory_space=pltpu.VMEM)
SMEM = pl.BlockSpec(memory_space=pltpu.SMEM)
ANY = pl.BlockSpec(memory_space=pl.ANY)
HBM = pl.BlockSpec(memory_space=pltpu.HBM)


def bits_of(n):
    return n.bit_length() - 1


class Geometry:
    def __init__(self, ndp, nch, clips, frames, c_in, c_mid):
        self.ndp, self.nch, self.ndev = ndp, nch, ndp * nch
        self.clips, self.frames = clips, frames
        self.ci_all, self.cm = c_in, c_mid
        self.ci, self.co = c_in // nch, c_mid // nch
        self.segs = nch // clips
        self.seg = frames // self.segs
        self.win = self.seg + HALO * min(self.segs - 1, 2)
        starts = [min(max(s * self.seg - HALO, 0), frames - self.win) for s in range(self.segs)]
        self.cwin = min(frames, (self.win + 48 + 63) // 64 * 64)
        assert all(min(s // 64 * 64, frames - self.cwin) + self.cwin >= s + self.win for s in starts)
        self.rows = max(16, self.co // ndp)
        self.pieces = self.co // self.rows
        self.planes = self.pieces // 2
        self.turns = bits_of(self.planes)
        self.zturns = bits_of(nch)

    def mask(self, core, turn):
        low, high = 1 << turn, 1 << (self.turns - 1 - turn)
        return low + core * (high - low)

    def plane_of(self, core, e):
        rel = 0
        for t in range(self.turns):
            if (e >> (self.turns - 1 - t)) & 1:
                rel = rel ^ self.mask(core, t)
        return rel

    def row_of(self, core, plane):
        return core * (self.co // 2) + plane * self.rows

    def zed_of(self, e):
        return sum(1 << t for t in range(self.zturns) if (e >> (self.zturns - 1 - t)) & 1)


class Here:
    def __init__(self, g, lens):
        self.z = lax.axis_index("chan")
        self.d = lax.axis_index("dp")
        self.core = lax.rem(self.d, 2)
        self.plane = lax.rem(self.d, g.pieces) // 2
        clip, seg = self.z // g.segs, lax.rem(self.z, g.segs)
        self.length = lens[clip]
        self.start, self.cstart = g_starts(g, seg)
        self.off = seg * g.seg - self.start
        self.qoff = self.start - self.cstart


def g_starts(g, seg):
    start = jnp.clip(seg * g.seg - HALO, 0, g.frames - g.win)
    return start, jnp.minimum(start // 64 * 64, g.frames - g.cwin)


def aligned(x, n=16):
    return pl.multiple_of(x, n)


def dot(a, b, contract):
    return lax.dot_general(a, b, ((contract[0], contract[1]), ((), ())), preferred_element_type=F32)


def call(body, out, ins, args, scratch, limit, flops, nbytes, name, aliases=None):
    return pl.pallas_call(
        body,
        out_shape=[pltpu.VMEM(o.shape, o.dtype) if isinstance(o, jax.ShapeDtypeStruct) else o for o in out],
        in_specs=ins,
        out_specs=[VMEM if isinstance(o, jax.ShapeDtypeStruct) else ANY for o in out],
        scratch_shapes=scratch,
        input_output_aliases=aliases or {},
        compiler_params=pltpu.CompilerParams(vmem_limit_bytes=limit * MIB),
        cost_estimate=pl.CostEstimate(
            flops=int(flops), bytes_accessed=int(nbytes), transcendentals=0
        ),
        name=name,
    )(*args)


def arr(shape, dtype):
    return jax.ShapeDtypeStruct(shape, dtype)


def keep_near(*xs):
    return [pltpu.with_memory_space_constraint(x, pltpu.VMEM) for x in xs]


class Copies:
    def __init__(self, sems):
        self.sems, self.n, self.open = sems, 0, []

    def start(self, src, dst):
        c = pltpu.make_async_copy(src, dst, self.sems.at[self.n])
        self.n += 1
        c.start()
        self.open.append(c)
        return c

    def wait(self, c):
        self.open = [o for o in self.open if o is not c]
        c.wait()

    def wait_all(self, some=None):
        for c in list(self.open if some is None else some):
            self.wait(c)


def sems(n):
    return pltpu.SemaphoreType.DMA((n,))


def row_masks(g, here, width):
    r = lax.broadcasted_iota(jnp.int32, (g.win, 128), 0)
    valid = (r + here.start) < here.length
    own = valid & (r >= here.off) & (r < here.off + g.seg)
    return widen(valid.astype(F32), width), widen(own.astype(F32), width)


def widen(x, width):
    return jnp.concatenate([x] * (width // 128), axis=1)


def shifted(x):
    n = x.shape[0]
    r = lax.broadcasted_iota(jnp.int32, (8, 1), 0)
    before, after = pltpu.roll(x, 1, 0), pltpu.roll(x, n - 1, 0)
    before = jnp.concatenate([jnp.where(r == 0, 0.0, before[:8]), before[8:]], axis=0)
    after = jnp.concatenate([after[:-8], jnp.where(r == 7, 0.0, after[-8:])], axis=0)
    return before, after


def grid_order(rows=16):
    n = MEL * rows
    r = lax.broadcasted_iota(jnp.int32, (n, n), 0)
    c = lax.broadcasted_iota(jnp.int32, (n, n), 1)
    return (c == (r % rows) * MEL + r // rows).astype(BF)


def misc_row(*scalars):
    lane = lax.broadcasted_iota(jnp.int32, (1, 128), 1)
    row = jnp.zeros((1, 128), F32)
    for i, s in enumerate(scalars):
        row = jnp.where(lane == i, s, row)
    return row


def pick(row, i):
    lane = lax.broadcasted_iota(jnp.int32, (1, 128), 1)
    return jnp.sum(jnp.where(lane == i, row, 0.0), axis=1, keepdims=True)


def sum_rows(x):
    return jnp.sum(x, axis=0, keepdims=True)


def payload(*parts):
    return jnp.concatenate(parts, axis=1)


def fan_kernel(pay, *rest):
    out = rest[-1]
    out[...] = jnp.broadcast_to(pay[...][None], out.shape)


def fan(g, pay, *after):
    out = [arr((g.ndev, *pay.shape), F32)]
    ins = [VMEM] + [ANY] * len(after)
    return call(fan_kernel, out, ins, [pay, *after], [], 4, 0, 1e5, "fan")[0]


def total_of(g, ref):
    row = jnp.sum(ref[...], axis=0)
    return row[:, : g.cm], row[:, g.cm : 2 * g.cm], row[:, 2 * g.cm :]


def side_by_side(x3, m, low, c, first, last):
    x3[m, :, 0:c] = first.astype(BF)
    x3[m, :, c : 2 * c] = low
    x3[m, :, 2 * c : 3 * c] = last.astype(BF)


def cut_weights_kernel(g, w_in, w_mid, out, sem):
    d = lax.axis_index("dp")
    core, plane = lax.rem(d, 2), lax.rem(d, g.pieces) // 2
    rows = pl.ds(aligned(g.row_of(core, plane)), g.rows)
    copies = Copies(sem)
    copies.start(w_in.at[:, rows, :], out.at[:, :, : g.ci_all])
    copies.start(w_mid.at[:, rows, :], out.at[:, :, g.ci_all :])
    copies.wait_all()


def cut_weights(g, w_in, w_mid):
    out = [arr((9, g.rows, g.ci_all + g.cm), BF)]
    args = [in_hbm(w_in), in_hbm(w_mid)]
    body = functools.partial(cut_weights_kernel, g)
    return call(body, out, [ANY] * 2, args, [sems(2)], 4, 0, 4e5, "cut_weights")[0]


def sort_kernel(g, *rest):
    n = g.nch - 1
    parts, first, second = rest[:n], rest[-2], rest[-1]
    for k in range(n):
        first[k] = parts[k][:, :, : g.ci_all]
        second[k] = parts[k][:, :, g.ci_all :]


def sort_pieces(g, parts, gates):
    n = g.nch - 1
    out = [arr((n, 9, g.rows, g.ci_all), BF), arr((n, 9, g.rows, g.cm), BF)]
    body = functools.partial(sort_kernel, g)
    ins = [VMEM] * n + [ANY] * len(gates)
    return call(body, out, ins, [*parts, *gates], [], 4, 0, 1e6, "sort_pieces")


def cut_maps_kernel(g, spec, after, out, held, sem):
    copies = Copies(sem)
    first = []
    for z in range(g.nch):
        start = static_start(g, z % g.segs) * MEL
        first.append(copies.start(spec.at[z // g.segs, :, start : start + g.win * MEL], held.at[z]))
    for z in range(g.nch):
        copies.wait(first[z])
        copies.start(held.at[z], out.at[z])
    copies.wait_all()


def cut_maps(g, spec, after):
    shape = (g.nch, g.ci, g.win * MEL)
    body = functools.partial(cut_maps_kernel, g)
    args = [in_hbm(spec), after]
    scratch = [pltpu.VMEM(shape, BF), sems(2 * g.nch)]
    return call(body, [pltpu.HBM(shape, BF)], [ANY] * 2, args, scratch, 4, 0, 2e6, "cut_maps")[0]


def static_start(g, seg):
    return min(max(seg * g.seg - HALO, 0), g.frames - g.win)


def cut_cot_kernel(g, cot, after, *rest):
    n = g.nch
    cs, sem = rest[:n], rest[n]
    z = lax.axis_index("chan")
    copies = Copies(sem)
    for k in range(n):
        to = z ^ k
        clip, seg = to // g.segs, lax.rem(to, g.segs)
        _, cstart = g_starts(g, seg)
        copies.start(cot.at[clip, :, pl.ds(aligned(cstart * 2, 128), g.cwin * 2)], cs[k])
    copies.wait_all()


def cut_cot(g, cot, after):
    n = g.nch
    out = [arr((g.co, g.cwin * 2), BF)] * n
    body = functools.partial(cut_cot_kernel, g)
    return call(body, out, [ANY] * 2, [in_hbm(cot), after], [sems(n)], 4, 0, 1e6, "cut_cotangent")


def in_hbm(x):
    return pltpu.with_memory_space_constraint(x, pltpu.HBM)


def join_kernel(g, own, *rest):
    parts, w = rest[:-1], rest[-1]
    z, d = lax.axis_index("chan"), lax.axis_index("dp")
    mine, plane = lax.rem(d, 2), lax.rem(d, g.pieces) // 2
    w[:, pl.ds(aligned(z * g.co), g.co), :] = own[...]
    for side in range(2):
        core = mine if side == 0 else 1 - mine
        for e in range(g.planes):
            row = g.row_of(core, plane ^ g.plane_of(core, e))
            for k in range(1, g.nch):
                at = aligned((z ^ k) * g.co + row)
                w[:, pl.ds(at, g.rows), :] = parts[side * g.planes + e][k - 1]


def join(g, own, parts, depth, name):
    body = functools.partial(join_kernel, g)
    args = [*keep_near(own), *parts]
    ins = [VMEM] * len(args)
    return call(body, [arr((9, g.cm, depth), BF)], ins, args, [], 8, 0, 4 * MIB, name)[0]


def convolve(v3, w, part, back, finish, carry, unrolled=False, window=None):
    def taps(t):
        b = 2 - t if back else t
        return jnp.concatenate([w[b], w[3 + b], w[6 + b]], axis=0 if back else 1)

    contract = ((1,), (0,)) if back else ((1,), (1,))
    depth = v3.shape[2]

    size = part.shape[1]
    window = pl.ds(0, size) if window is None else window

    def times(first, n, t):
        return dot(v3[pl.ds(first, n), window, :].reshape(n * size, depth), taps(t), contract)

    def rows_of(term, n):
        return [term[k * size : (k + 1) * size] for k in range(n)]

    if unrolled:
        for i in range(2):
            total = rows_of(times(4 * i, 4, 1), 4)
            side = rows_of(times(1 + 2 * i, 4, 2 - 2 * i), 4)
            edge = rows_of(times(5 * i, 3, 2 * i), 3)
            for k in range(4):
                value = total[k] + side[k]
                if 0 <= k + i - 1 < 3:
                    value = value + edge[k + i - 1]
                carry = finish(4 * i + k, value, carry)
        return carry

    def step(i, carry):
        part[pl.ds(3 * i + 1, 3)] = times(5 * i, 3, 2 * i).reshape(3, size, part.shape[2])
        part[7 * i] = jnp.zeros(part.shape[1:], F32)
        total = times(4 * i, 4, 1) + times(1 + 2 * i, 4, 2 - 2 * i)
        for k in range(4):
            m = 4 * i + k
            carry = finish(m, part[m] + total[k * size : (k + 1) * size], carry)
        return carry

    return lax.fori_loop(0, 2, step, carry)


def convolve_sums(g, here, x3, w, pre, unrolled):
    _, own = row_masks(g, here, g.cm)

    def finish(m, total, sums):
        pre[m] = total
        kept = total * own
        return sums[0] + sum_rows(kept), sums[1] + sum_rows(kept * total)

    zero = jnp.zeros((1, g.cm), F32)
    return convolve(x3, w, pre, False, finish, (zero, zero), unrolled)


def first_kernel(g, lens, gains, w, maps, pre, x3, pay):
    here = Here(g, lens)
    c = g.ci_all
    order = grid_order()
    row = lax.broadcasted_iota(jnp.int32, (MEL * 16, 128), 0) % 16

    def place_cells(j, square):
        cells = maps[:, :, 128 * j : 128 * (j + 1)].reshape(c, 128)
        frame = row + 16 * j
        valid = (frame + here.start) < here.length
        own = (frame >= here.off) & (frame < here.off + g.seg)
        block = dot(order, cells, ((1,), (1,))) * widen(valid.astype(F32), c)
        x3[:, 16 * j : 16 * (j + 1), c : 2 * c] = block.astype(BF).reshape(MEL, 16, c)
        return square + sum_rows(block * block * widen(own.astype(F32), c))

    square = jnp.zeros((1, c), F32)
    for j in range(g.win // 16):
        square = place_cells(j, square)
    for m in range(MEL):
        before, after_ = shifted(x3[m, :, c : 2 * c].astype(F32))
        x3[m, :, 0:c] = before.astype(BF)
        x3[m, :, 2 * c : 3 * c] = after_.astype(BF)

    one, two = convolve_sums(g, here, x3, w, pre, True)
    frame_total = 0
    pair_total = 0
    for i in range(g.clips):
        frame_total = frame_total + lens[i]
        pair_total = pair_total + (lens[i] + 1) // 2
    row = misc_row(
        frame_total.astype(F32), pair_total.astype(F32), jnp.sum(square, axis=1, keepdims=True)
    )
    pay[...] = payload(one, two, row, *[gains[i : i + 1] for i in range(4)])


def first(g, lens, gains, maps, w):
    body = functools.partial(first_kernel, g)
    out = [
        arr((MEL, g.win, g.cm), F32),
        arr((MEL, g.win, 3 * g.ci_all), BF),
        arr((1, 2 * g.cm + 5 * 128), F32),
    ]
    args = [lens, gains, *keep_near(w, maps)]
    ins = [SMEM] + [VMEM] * 3
    flops = 2 * 9 * MEL * g.win * g.ci_all * g.cm
    return call(body, out, ins, args, [], 10, flops, 10 * MIB, "first_conv")


MEAN1, INV1, GAMMA1, BETA1, GAMMA2, BETA2, COUNT, PAIRS, SQ0, MEAN2, INV2 = range(11)
TABLE = 16


def half_affine(mean, inverse, gamma, beta):
    scale = 0.5 * gamma * inverse
    return scale, 0.5 * beta - mean * scale


def second_kernel(g, lens, got, pre1, w, pre, x3, table, pay, misc_out):
    here = Here(g, lens)
    c = g.cm
    valid, own = row_masks(g, here, c)
    one, two, rest = total_of(g, got)
    misc = rest[:, :128]
    count = MEL * pick(misc, 0) / g.nch
    pairs = (MEL // 2) * pick(misc, 1) / g.nch
    at = [2 * c + 128 * (1 + i) for i in range(4)]
    vectors = [
        jnp.concatenate([got[zz, :, i : i + g.co] for zz in range(g.nch)], axis=1) for i in at
    ]
    mean = one / count
    inverse = lax.rsqrt(two / count - mean * mean + 1e-05)
    wide = jnp.zeros((1, c), F32)
    table[...] = jnp.concatenate(
        [mean, inverse, *vectors, wide + count, wide + pairs, wide + pick(misc, 2)]
        + [wide] * (TABLE - 9),
        axis=0,
    )
    scale, shift = half_affine(mean, inverse, vectors[0], vectors[1])


    def activate(m, square):
        half = pre1[m] * scale + shift
        act = half * (1.0 + jnp.tanh(half)) * valid
        low = act.astype(BF)
        before, after = shifted(low.astype(F32))
        side_by_side(x3, m, low, c, before, after)
        return square + sum_rows(act * act * own)

    square = jnp.zeros((1, c), F32)
    for m in range(MEL):
        square = activate(m, square)
    one, two = convolve_sums(g, here, x3, w, pre, True)
    pay[...] = payload(one, two)
    misc_out[...] = misc_row(jnp.sum(square, axis=1, keepdims=True))


def second(g, lens, got, pre1, w):
    body = functools.partial(second_kernel, g)
    out = [
        arr((MEL, g.win, g.cm), F32),
        arr((MEL, g.win, 3 * g.cm), BF),
        arr((TABLE, g.cm), F32),
        arr((1, 2 * g.cm), F32),
        arr((1, 128), F32),
    ]
    args = [lens, *keep_near(got, pre1, w)]
    flops = 2 * 9 * MEL * g.win * g.cm * g.cm
    ins = [SMEM, VMEM, VMEM, VMEM]
    return call(body, out, ins, args, [], 10, flops, 17 * MIB, "second_conv")


def pool_kernel(g, lens, got, old_ref, pre2, *rest):
    n, c = g.nch, g.cm
    cs, outs = rest[:n], rest[n : 2 * n]
    local_ref, table, pay, misc_out, held, grads, total, flat = rest[2 * n :]
    here = Here(g, lens)
    for k in range(n):
        held[pl.ds(aligned((here.z ^ k) * g.co), g.co), :] = cs[k][...]
    r = lax.broadcasted_iota(jnp.int32, (256, 128), 0)
    l = lax.broadcasted_iota(jnp.int32, (256, 128), 1)
    spread = (l == (r % 64) // 2 * 4 + r // 64).astype(BF)

    @pl.loop(0, g.cwin // 64)
    def _(j):
        cells = held[:, pl.ds(aligned(128 * j, 128), 128)]
        block = dot(spread, cells, ((1,), (1,)))
        grads[:, pl.ds(aligned(64 * j), 64), :] = block.reshape(MEL // 2, 64, c)

    one, two, _ = total_of(g, got)
    old = old_ref[...]
    count = old[COUNT : COUNT + 1]
    mean = one / count
    inverse = lax.rsqrt(two / count - mean * mean + 1e-05)
    wide = jnp.zeros((1, c), F32)
    table[...] = jnp.concatenate([old[:MEAN2], mean, inverse] + [wide] * (TABLE - 11), axis=0)
    half_gamma, half_beta = 0.5 * old[GAMMA2 : GAMMA2 + 1], 0.5 * old[BETA2 : BETA2 + 1]
    less = -mean * inverse
    side = g.win - g.seg
    segment = pl.ds(aligned(here.off), g.seg)
    sides = [
        aligned(jnp.where(16 * j < here.off, 16 * j, 16 * j + g.seg)) for j in range(side // 16)
    ]

    def weights(rows, start, width):
        frame = lax.broadcasted_iota(jnp.int32, (rows, 128), 0) + (here.start + start)
        valid = (frame < here.length).astype(F32)
        share = jnp.where(here.length - frame // 2 * 2 >= 2, 0.25, 0.5)
        return widen(0.5 * share * valid, width), widen(valid, width)

    half_share, valid = weights(g.seg, here.off, c)
    side_shares = [weights(16, start, c)[0] for start in sides]
    out_row = lax.broadcasted_iota(jnp.int32, (g.seg, 2 * g.seg), 0)
    out_cell = lax.broadcasted_iota(jnp.int32, (g.seg, 2 * g.seg), 1)
    first_cell = out_row // 2 * 4
    frame = out_row + (here.start + here.off)
    out_share = jnp.where(here.length - frame // 2 * 2 >= 2, 0.25, 0.5)
    total[...] = jnp.zeros(total.shape, F32)

    def bent(pre):
        scaled = pre * inverse + less
        half = scaled * half_gamma + half_beta
        bend = jnp.tanh(half)
        twice = 1.0 + bend
        whole = half * twice
        return scaled, whole, twice + whole * (1.0 - bend)

    def step(k, sums):
        beta_sum, gamma_sum, square = sums
        given = grads[k, pl.ds(aligned(here.qoff + here.off), g.seg), :] * half_share
        pair = None
        for i in range(2):
            m = 2 * k + i
            scaled, whole, slope = bent(pre2[m, segment, :])
            act = whole * valid
            square = square + sum_rows(act * act)
            local = given * slope
            local_ref[m, segment, :] = local
            beta_sum = beta_sum + sum_rows(local)
            gamma_sum = gamma_sum + sum_rows(local * scaled)
            pair = act if pair is None else pair + act
            for start, side_share in zip(sides, side_shares, strict=True):
                rows = pl.ds(start, 16)
                _, _, slope = bent(pre2[m, rows, :])
                given_side = grads[k, pl.ds(aligned(here.qoff + start), 16), :] * side_share
                local_ref[m, rows, :] = given_side * slope
        gather = jnp.where(out_cell == first_cell + k, out_share, 0.0).astype(BF)
        total[...] += dot(pair.astype(BF), gather, ((0,), (0,)))
        return beta_sum, gamma_sum, square

    zero = jnp.zeros((1, c), F32)
    beta_sum, gamma_sum, square = lax.fori_loop(0, MEL // 2, step, (zero, zero, zero))
    pooled = total[...]
    flat[...] = pooled.astype(BF)
    for k in range(n):
        outs[k][...] = flat[pl.ds(aligned((here.z ^ k) * g.co), g.co), :]
    pooled_square = sum_rows(jnp.sum(pooled * pooled, axis=1, keepdims=True))
    pay[...] = jnp.broadcast_to(payload(beta_sum, gamma_sum)[None], pay.shape)
    misc_out[...] = misc_row(jnp.sum(square, axis=1, keepdims=True), pooled_square)


def pool(g, lens, got, table, pre2, cs):
    n = g.nch
    body = functools.partial(pool_kernel, g)
    out = [arr((g.co, 2 * g.seg), BF)] * n + [
        arr((MEL, g.win, g.cm), F32),
        arr((TABLE, g.cm), F32),
        arr((g.ndev, 1, 2 * g.cm), F32),
        arr((1, 128), F32),
    ]
    scratch = [
        pltpu.VMEM((g.cm, g.cwin * 2), BF),
        pltpu.VMEM((MEL // 2, g.cwin, g.cm), F32),
        pltpu.VMEM((g.cm, 2 * g.seg), F32),
        pltpu.VMEM((g.cm, 2 * g.seg), BF),
    ]
    args = [lens, *keep_near(got, table, pre2, *cs)]
    ins = [SMEM] + [VMEM] * (len(args) - 1)
    out = call(body, out, ins, args, scratch, 12, 4e9, 8 * MIB, "pool")
    return out[:n], *out[n:]


def terms_kernel(g, depth, norm, lens, got, table, pre, local, x3, after, *refs):
    grad, sums, roots, terms, give = refs
    here = Here(g, lens)
    c = g.cm
    valid, _ = row_masks(g, here, c)
    beta_sum, gamma_sum, rest = total_of(g, got)
    t = table[...]
    mean, inverse, gamma = (t[i : i + 1] for i in norm)
    count = t[COUNT : COUNT + 1]
    sums[...] = jnp.concatenate([beta_sum, gamma_sum] + [jnp.zeros((1, c), F32)] * 6, axis=0)
    if rest.shape[1]:
        second, third = rest[:, :128], rest[:, 128:]
        tops = misc_row(
            pick(t[SQ0 : SQ0 + 1, :128], 0), pick(second, 0), pick(third, 0), pick(third, 1)
        )
        lane = lax.broadcasted_iota(jnp.int32, (1, 128), 1)
        cells, pairs = count[:, :128], t[PAIRS : PAIRS + 1, :128]
        under = jnp.where(lane == 0, cells * g.ci_all, jnp.where(lane == 3, pairs * c, cells * c))
        roots[...] = jnp.broadcast_to(jnp.sqrt(tops / under), (8, 128))
    factor = gamma * inverse
    slope = factor * inverse * gamma_sum / count
    level = factor * beta_sum / count - mean * slope

    for m in range(MEL):
        value = valid * (local[m] * factor - pre[m] * slope - level)
        grad[m] = value.astype(BF)

    segment = pl.ds(aligned(here.off), g.seg)

    for a in range(3):
        lanes_of = slice(a * depth, (a + 1) * depth)
        for b in (1, 0, 2):
            low = max(0, 1 - b)
            high = min(MEL, MEL + 1 - b)
            rows = (high - low) * g.seg
            left = grad[low:high, segment, :].reshape(rows, c)
            right = x3[low + b - 1 : high + b - 1, segment, lanes_of].reshape(rows, depth)
            term = dot(left, right, ((0,), (0,))).astype(BF)
            for z in range(g.nch):
                for s in range(2):
                    for p in range(g.planes):
                        at = z * g.co + g.row_of(s, p)
                        terms[s, z, p, 3 * a + b] = term[at : at + g.rows]

    give[...] = terms[1 - here.core]


def terms_of(g, lens, got, table, pre, local, x3, after, depth, norm, name):
    body = functools.partial(terms_kernel, g, depth, norm)
    shape = (g.nch, g.planes, 9, g.rows, depth)
    out = [
        arr((MEL, g.win, g.cm), BF),
        arr((8, g.cm), F32),
        arr((8, 128), F32),
        arr((2, *shape), BF),
        arr(shape, BF),
    ]
    args = [lens, *keep_near(got, table, pre, local, x3), after]
    ins = [SMEM] + [VMEM] * 5 + [ANY]
    flops = 2 * 9 * MEL * g.win * g.cm * depth
    return call(body, out, ins, args, [], 10, flops, 15 * MIB, name)


def back_kernel(g, lens, table, grad, pre1, w, misc2, misc3, after, local1, pay, g3):
    here = Here(g, lens)
    c = g.cm
    valid, own = row_masks(g, here, c)
    t = table[...]

    def row(i):
        return t[i : i + 1]


    for m in range(MEL):
        low = grad[m]
        before, after = shifted(low.astype(F32))
        side_by_side(g3, m, low, c, after, before)

    inverse, less = row(INV1), -row(MEAN1) * row(INV1)
    half_gamma, half_beta = 0.5 * row(GAMMA1), 0.5 * row(BETA1)
    half_valid = 0.5 * valid

    def finish(m, given, sums):
        scaled = pre1[m] * inverse + less
        half = scaled * half_gamma + half_beta
        bend = jnp.tanh(half)
        twice = 1.0 + bend
        local = given * half_valid * (twice + half * twice * (1.0 - bend))
        local1[m] = local
        kept = local * own
        return sums[0] + sum_rows(kept), sums[1] + sum_rows(kept * scaled)

    zero = jnp.zeros((1, c), F32)
    beta_sum, gamma_sum = convolve(g3, w, local1, True, finish, (zero, zero), True)
    pay[...] = payload(beta_sum, gamma_sum, misc2[...], misc3[...])


def back(g, lens, table, grad, pre1, w, misc2, misc3, after):
    body = functools.partial(back_kernel, g)
    out = [arr((MEL, g.win, g.cm), F32), arr((1, 2 * g.cm + 2 * 128), F32)]
    scratch = [pltpu.VMEM((MEL, g.win, 3 * g.cm), BF)]
    args = [lens, *keep_near(table, grad, pre1, w, misc2, misc3), after]
    flops = 2 * 9 * MEL * g.win * g.cm * g.cm
    ins = [SMEM] + [VMEM] * 6 + [ANY]
    return call(body, out, ins, args, scratch, 14, flops, 20 * MIB, "second_back")


def release_kernel(*refs):
    pass


def release_far(gates, x):
    n = len(gates)
    return pl.pallas_call(
        release_kernel,
        out_shape=pltpu.HBM(x.shape, x.dtype),
        in_specs=[ANY] * (n + 1),
        out_specs=ANY,
        input_output_aliases={n: 0},
        compiler_params=pltpu.CompilerParams(vmem_limit_bytes=2 * MIB),
        name="release_far",
    )(*gates, in_hbm(x))


def release(gates, arrays):
    out = [arr(x.shape, x.dtype) for x in arrays]
    n = len(gates)
    ins = [ANY] * n + [VMEM] * len(arrays)
    aliases = {i + n: i for i in range(len(arrays))}
    args = [*gates, *keep_near(*arrays)]
    return call(release_kernel, out, ins, args, [], 2, 0, 1, "release", aliases)


def spectra_kernel(g, lens, grad, after, w, *rest):
    n, c = g.nch, g.cm
    outs, (g3, rows, flat, part) = rest[:n], rest[n:]
    here = Here(g, lens)

    @pl.loop(0, MEL)
    def _(m):
        low = grad[m]
        before, after_ = shifted(low.astype(F32))
        side_by_side(g3, m, low, c, after_, before)

    r = lax.broadcasted_iota(jnp.int32, (g.seg, 128), 0) + here.off + here.start
    valid = widen((r < here.length).astype(F32), g.ci_all)

    def finish(m, total, carry):
        rows[m] = (total * valid).astype(BF)
        return carry

    convolve(g3, w, part, True, finish, 0, False, pl.ds(aligned(here.off), g.seg))
    order = grid_order()

    for j in range(g.seg // 16):
        block = rows[:, 16 * j : 16 * (j + 1), :].reshape(MEL * 16, g.ci_all)
        flat[:, 128 * j : 128 * (j + 1)] = dot(block, order, ((0,), (0,))).astype(BF)

    for k in range(n):
        outs[k][...] = flat[pl.ds(aligned((here.z ^ k) * g.ci), g.ci), :]


def spectra_back(g, lens, grad, after, w):
    n = g.nch
    body = functools.partial(spectra_kernel, g)
    out = [arr((g.ci, g.seg * MEL), BF)] * n
    scratch = [
        pltpu.VMEM((MEL, g.win, 3 * g.cm), BF),
        pltpu.VMEM((MEL, g.seg, g.ci_all), BF),
        pltpu.VMEM((g.ci_all, g.seg * MEL), BF),
        pltpu.VMEM((MEL, g.seg, g.ci_all), F32),
    ]
    grad, w = keep_near(grad, w)
    args = [lens, grad, after, w]
    flops = 2 * 9 * MEL * g.win * g.cm * g.ci_all
    ins = [SMEM, VMEM, ANY, VMEM]
    return call(body, out, ins, args, scratch, 14, flops, 5 * MIB, "spectra_back")


def place_kernel(g, width, *rest):
    n = g.nch
    parts, out, done = rest[:n], rest[n], rest[n + 1]
    z = lax.axis_index("chan")
    done[...] = jnp.zeros(done.shape, F32)
    for k in range(n):
        source = z ^ k
        for zz in range(n):

            @pl.when(source == zz)
            def _():
                at = zz % g.segs * width
                out[zz // g.segs, :, at : at + width] = parts[k][...].astype(out.dtype)


def place(g, parts, dtype, name):
    channels, width = parts[0].shape
    return pl.pallas_call(
        functools.partial(place_kernel, g, width),
        out_shape=[
            jax.ShapeDtypeStruct((g.clips, channels, g.segs * width), dtype),
            jax.ShapeDtypeStruct((8, 128), F32),
        ],
        in_specs=[VMEM] * g.nch,
        out_specs=[VMEM] * 2,
        compiler_params=pltpu.CompilerParams(vmem_limit_bytes=8 * MIB),
        cost_estimate=TINY,
        name=name,
    )(*parts)


def core_sum_kernel(g, terms, got, after, stay, go):
    d, z = lax.axis_index("dp"), lax.axis_index("chan")
    core, plane = lax.rem(d, 2), lax.rem(d, g.pieces) // 2
    half = g.planes // 2
    for e in range(g.planes):
        at = plane ^ g.plane_of(core, e)
        for k in range(g.nch):
            source = z ^ g.zed_of(k)
            value = terms[core, source, at].astype(F32) + got[source, at].astype(F32)
            to = stay if e < half else go
            to[(e % half) * g.nch + k] = value.astype(BF)


def core_sum(g, terms, got, after, name):
    shape = (g.planes // 2 * g.nch, *got.shape[2:])
    return pl.pallas_call(
        functools.partial(core_sum_kernel, g),
        out_shape=[pltpu.VMEM(shape, BF)] * 2,
        in_specs=[VMEM, VMEM, ANY],
        out_specs=[VMEM] * 2,
        compiler_params=pltpu.CompilerParams(vmem_limit_bytes=16 * MIB),
        name=name,
    )(keep_near(terms)[0], got, after)


def quarter_kernel(g, terms, got, *outs):
    d, z = lax.axis_index("dp"), lax.axis_index("chan")
    core, plane = lax.rem(d, 2), lax.rem(d, g.pieces) // 2
    for e in range(g.planes):
        at = plane ^ g.plane_of(core, e)
        for k in range(g.nch):
            source = z ^ g.zed_of(k)
            value = terms[core, source, at].astype(F32) + got[source, at].astype(F32)
            outs[e][k] = value.astype(BF)


def quarters(g, terms, got, name):
    shape = (g.nch, *got.shape[2:])
    return pl.pallas_call(
        functools.partial(quarter_kernel, g),
        out_shape=[pltpu.VMEM(shape, BF)] * g.planes,
        in_specs=[VMEM, VMEM],
        out_specs=[VMEM] * g.planes,
        compiler_params=pltpu.CompilerParams(vmem_limit_bytes=16 * MIB),
        name=name,
    )(keep_near(terms)[0], got)


def add_kernel(n, halves, *rest):
    first = rest[0]
    outs = rest[len(rest) - halves :]
    count = first.shape[0] // halves
    for i in range(first.shape[0]):
        total = first[i].astype(F32)
        for r in rest[1:n]:
            total = total + r[i].astype(F32)
        outs[i // count][i % count] = total.astype(BF)


def add_up(parts, halves, gates, name):
    n = len(parts)
    shape = (parts[0].shape[0] // halves, *parts[0].shape[1:])
    return pl.pallas_call(
        functools.partial(add_kernel, n, halves),
        out_shape=[pltpu.VMEM(shape, BF)] * halves,
        in_specs=[VMEM] * n + [ANY] * len(gates),
        out_specs=[VMEM] * halves,
        compiler_params=pltpu.CompilerParams(vmem_limit_bytes=8 * MIB),
        name=name,
    )(*parts, *gates)


def halve_kernel(stay, got, *rest):
    n = stay.shape[0]
    outs = rest[-2:] if n > 1 else rest[-1:]
    for i in range(n):
        value = stay[i].astype(F32) + got[i].astype(F32)
        if n == 1:
            outs[0][...] = value.astype(BF)
        else:
            outs[i // (n // 2)][i % (n // 2)] = value.astype(BF)


def halve(stay, got, gates, name):
    n = stay.shape[0]
    if n == 1:
        out = [jax.ShapeDtypeStruct(stay.shape[1:], BF)]
    else:
        out = [jax.ShapeDtypeStruct((n // 2, *stay.shape[1:]), BF)] * 2
    return pl.pallas_call(
        halve_kernel,
        out_shape=out,
        in_specs=[VMEM, VMEM] + [ANY] * len(gates),
        out_specs=[VMEM] * len(out),
        compiler_params=pltpu.CompilerParams(vmem_limit_bytes=8 * MIB),
        name=name,
    )(stay, got, *gates)


def spread_kernel(g, mine, other, out, done):
    done[...] = jnp.zeros(done.shape, F32)
    d = lax.axis_index("dp")
    core, plane = lax.rem(d, 2), lax.rem(d, g.pieces) // 2
    for side, part in enumerate((mine, other)):
        c = core if side == 0 else 1 - core
        for e in range(g.planes):
            at = aligned(g.row_of(c, plane ^ g.plane_of(c, e)))
            out[:, pl.ds(at, g.rows), :] = part[e].astype(F32)


def spread_out(g, mine, other, depth, name):
    return pl.pallas_call(
        functools.partial(spread_kernel, g),
        out_shape=[
            jax.ShapeDtypeStruct((9, g.co, depth), F32),
            jax.ShapeDtypeStruct((8, 128), F32),
        ],
        in_specs=[VMEM] * 2,
        out_specs=[VMEM] * 2,
        compiler_params=pltpu.CompilerParams(vmem_limit_bytes=12 * MIB),
        name=name,
    )(mine, other)


def stack_kernel(n, *refs):
    for k, r in enumerate(refs[:n]):
        refs[-1][k] = r[...]


def stack(parts, gates, name):
    n = len(parts)
    out = [arr((n, *parts[0].shape), parts[0].dtype)]
    ins = [VMEM] * n + [ANY] * len(gates)
    body = functools.partial(stack_kernel, n)
    return call(body, out, ins, [*parts, *gates], [], 6, 0, 1e6, name)[0]


class Links:
    def __init__(self, g):
        self.g = g

    def core(self, x):
        return lax.ppermute(x, "dp", [(i, i ^ 1) for i in range(self.g.ndp)])

    def dp(self, x, bit):
        return lax.ppermute(x, "dp", [(i, i ^ bit) for i in range(self.g.ndp)])

    def plane(self, x, turn):
        g = self.g
        return lax.ppermute(x, "dp", [(i, i ^ (2 * g.mask(i & 1, turn))) for i in range(g.ndp)])

    def chan(self, x, k):
        return lax.ppermute(x, "chan", [(i, i ^ k) for i in range(self.g.nch)])

    def exchange(self, parts):
        return [parts[0]] + [self.chan(parts[k], k) for k in range(1, self.g.nch)]

    def gather_planes(self, x, gates=()):
        have = [x]
        for turn in reversed(range(self.g.turns)):
            more = [self.plane(h, turn) for h in have[:1]]
            rest = have[1:]
            if gates and turn == 0 and rest:
                rest = release([*gates, *more], rest)
            have = have + more + [self.plane(h, turn) for h in rest]
        return have

    def gather_cores(self, have):
        return [*have, *[self.core(h) for h in have]]

    def gather_direct(self, x):
        g = self.g
        pairs = [[(i, i ^ (2 * g.plane_of(i & 1, e))) for i in range(g.ndp)] for e in range(g.planes)]
        return [x] + [lax.ppermute(x, "dp", p) for p in pairs[1:]]


def everyone(x):
    return lax.all_to_all(x, ("dp", "chan"), 0, 0)


def make_body(ndp, nch):
    def body(
        spectra, lengths, weight_in, gamma_in, beta_in, weight_mid, gamma_mid, beta_mid, cotangent
    ):
        g = Geometry(
            ndp,
            nch,
            spectra.shape[0],
            spectra.shape[2] // MEL,
            weight_in.shape[2],
            weight_mid.shape[2],
        )
        links = Links(g)
        gains = jnp.stack([gamma_in, beta_in, gamma_mid, beta_mid])
        gains = jnp.pad(gains, ((0, 0), (0, 128 - g.co)))

        piece = cut_weights(g, weight_in, weight_mid)
        cells = cut_maps(g, spectra, piece)
        cots = cut_cot(g, cotangent, cells)
        pieces_in, pieces_mid = sort_pieces(
            g, [links.chan(piece, k) for k in range(1, nch)], [cots[0]]
        )
        maps = lax.all_to_all(release_far([pieces_in], cells), "chan", 0, 0)
        planes_in = links.gather_planes(pieces_in)
        w_in = join(g, weight_in, links.gather_cores(planes_in), g.ci_all, "join_in")
        planes_mid = links.gather_planes(pieces_mid, [maps])

        pre1, x3_in, pay = first(g, lengths, gains, maps, w_in)
        got = everyone(fan(g, pay, cots[0], *planes_mid[1:]))
        planes_mid = release([got], planes_mid)
        w_mid = join(g, weight_mid, links.gather_cores(planes_mid), g.cm, "join_mid")
        cs = links.exchange(release([got], cots))
        pre2, x3_mid, table, pay, misc2 = second(g, lengths, got, pre1, w_mid)
        got = everyone(fan(g, pay, *cs[1:]))
        pooled, local2, table, pay, misc3 = pool(g, lengths, got, table, pre2, cs)
        got = everyone(pay)
        pooled = links.exchange(release([got], pooled))
        grad2, sums2, _, terms_mid, give_mid = terms_of(
            g, lengths, got, table, pre2, local2, x3_mid, got, g.cm, (MEAN2, INV2, GAMMA2), "weight_mid_terms"
        )
        got_mid = links.core(give_mid)
        split = g.turns == 2
        if split:
            stay_a, stay_b, go_a, go_b = quarters(g, terms_mid, got_mid, "mid_core_sum")
            got_b = links.plane(go_b, 0)
        else:
            stay_mid, go_b = core_sum(g, terms_mid, got_mid, got_mid, "mid_core_sum")
            got_b = go_b
        local1, pay = back(g, lengths, table, grad2, pre1, w_mid, misc2, misc3, go_b)
        got = everyone(fan(g, pay, got_b, *pooled[1:]))
        block_out, pooled_done = place(g, pooled, BF, "place_pooled")
        if split:
            (go_1,) = add_up([stay_b, got_b], 1, [got], "mid_sum_b")
            got_1 = links.plane(go_1, 1)
            got_a = links.plane(release([got], [go_a])[0], 0)
        else:
            (go_mid,) = release([got], [go_b])
        grad1, sums1, roots, terms_in, give_in = terms_of(
            g, lengths, got, table, pre1, local1, x3_in, got, g.ci_all, (MEAN1, INV1, GAMMA1), "weight_in_terms"
        )
        got_in = links.core(give_in)

        class Chain:
            def __init__(self, stay, go, depth, name):
                self.stay, self.go, self.depth, self.name = stay, go, depth, name
                self.turns = [functools.partial(links.plane, turn=t) for t in range(g.turns)]
                self.turns += [functools.partial(links.chan, k=1 << t) for t in range(g.zturns)]

            def turn(self, i, *gates):
                got = self.turns[i](self.go)
                done = halve(self.stay, got, gates, f"{self.name}_sum_{i}")
                self.stay, self.go = done if len(done) == 2 else (done[0], None)
                return self.stay

            def rest(self):
                bit = g.pieces
                while bit < ndp:
                    got = links.dp(self.stay, bit)
                    self.stay = halve(self.stay[None], got[None], [], self.name + "_rest")[0]
                    bit *= 2

            def out(self, planes, *gates):
                mine = stack(planes, gates, self.name + "_stack")
                return spread_out(g, mine, links.core(mine), self.depth, self.name + "_out")

        turns = g.turns + g.zturns
        parts = spectra_back(g, lengths, grad1, grad1, w_in)
        stay_in, go_in = core_sum(g, terms_in, got_in, parts[0], "in_core_sum")
        inner = Chain(stay_in, go_in, g.ci_all, "in")
        parts = links.exchange(parts)
        spectra_grad, spectra_done = place(g, parts, F32, "place_spectra")
        if split:
            halves = add_up([stay_a, got_a, got_1], 2, [stay_in], "mid_sum_1")
            mid = Chain(*halves, g.cm, "mid")
        else:
            mid = Chain(stay_mid, go_mid, g.cm, "mid")
            for i in range(g.turns):
                mid.turn(i, stay_in)
        gates = [parts[2 : nch - 1], [pooled_done]]
        at = mid.stay
        for i in range(g.turns):
            at = inner.turn(i, at, *(gates[i] if i < 2 else []))
            if i == 0:
                at = mid.turn(g.turns, at)
        for i in range(g.turns, turns):
            at = inner.turn(i, at, *(parts[nch - 1 :] if i == g.turns else []))
            if i + 1 < turns:
                at = mid.turn(i + 1, at)
        inner.rest()
        mid.rest()
        planes_in = links.gather_planes(inner.stay)
        weight_mid_grad, mid_done = mid.out(links.gather_direct(mid.stay), *planes_in[1:3], parts[1])
        weight_in_grad, _ = inner.out(planes_in, mid_done, spectra_done)
        z = lax.axis_index("chan")

        def share(sums, i):
            return lax.dynamic_slice_in_dim(sums[i], z * g.co, g.co)

        return (
            block_out,
            spectra_grad,
            weight_in_grad,
            share(sums1, 1),
            share(sums1, 0),
            weight_mid_grad,
            share(sums2, 1),
            share(sums2, 0),
            roots[0, :4],
        )

    return body


def solution(mesh):
    placed = (
        P("dp", "chan", None),
        P("dp"),
        P(None, "chan", None),
        P("chan"),
        P("chan"),
        P(None, "chan", None),
        P("chan"),
        P("chan"),
        P("dp", "chan", None),
    )
    return jax.shard_map(
        make_body(mesh.shape["dp"], mesh.shape["chan"]),
        mesh=mesh,
        in_specs=placed,
        out_specs=(
            P("dp", "chan", None),
            P("dp", "chan", None),
            P(None, "chan", None),
            P("chan"),
            P("chan"),
            P(None, "chan", None),
            P("chan"),
            P("chan"),
            P(),
        ),
        check_vma=False,
    )
```

```python
import functools

import jax
import jax.numpy as jnp
from jax import lax
from jax.experimental import pallas as pl
from jax.experimental.pallas import tpu as pltpu
from jax.sharding import PartitionSpec as P

MEL = 8
HALO = 16
BF = jnp.bfloat16
F32 = jnp.float32
MIB = 1024 * 1024
TINY = pl.CostEstimate(flops=1, bytes_accessed=1, transcendentals=0)

VMEM = pl.BlockSpec(memory_space=pltpu.VMEM)
SMEM = pl.BlockSpec(memory_space=pltpu.SMEM)
ANY = pl.BlockSpec(memory_space=pl.ANY)
HBM = pl.BlockSpec(memory_space=pltpu.HBM)


def bits_of(n):
    return n.bit_length() - 1


class Geometry:
    def __init__(self, ndp, nch, clips, frames, c_in, c_mid):
        self.ndp, self.nch, self.ndev = ndp, nch, ndp * nch
        self.clips, self.frames = clips, frames
        self.ci_all, self.cm = c_in, c_mid
        self.ci, self.co = c_in // nch, c_mid // nch
        self.segs = nch // clips
        self.seg = frames // self.segs
        self.win = self.seg + HALO * min(self.segs - 1, 2)
        starts = [min(max(s * self.seg - HALO, 0), frames - self.win) for s in range(self.segs)]
        self.cwin = min(frames, (self.win + 48 + 63) // 64 * 64)
        assert all(min(s // 64 * 64, frames - self.cwin) + self.cwin >= s + self.win for s in starts)
        self.rows = max(16, self.co // ndp)
        self.pieces = self.co // self.rows
        self.planes = self.pieces // 2
        self.turns = bits_of(self.planes)
        self.zturns = bits_of(nch)

    def mask(self, core, turn):
        low, high = 1 << turn, 1 << (self.turns - 1 - turn)
        return low + core * (high - low)

    def plane_of(self, core, e):
        rel = 0
        for t in range(self.turns):
            if (e >> (self.turns - 1 - t)) & 1:
                rel = rel ^ self.mask(core, t)
        return rel

    def row_of(self, core, plane):
        return core * (self.co // 2) + plane * self.rows

    def zed_of(self, e):
        return sum(1 << t for t in range(self.zturns) if (e >> (self.zturns - 1 - t)) & 1)


class Here:
    def __init__(self, g, lens):
        self.z = lax.axis_index("chan")
        self.d = lax.axis_index("dp")
        self.core = lax.rem(self.d, 2)
        self.plane = lax.rem(self.d, g.pieces) // 2
        clip, seg = self.z // g.segs, lax.rem(self.z, g.segs)
        self.length = lens[clip]
        self.start, self.cstart = g_starts(g, seg)
        self.off = seg * g.seg - self.start
        self.qoff = self.start - self.cstart


def g_starts(g, seg):
    start = jnp.clip(seg * g.seg - HALO, 0, g.frames - g.win)
    return start, jnp.minimum(start // 64 * 64, g.frames - g.cwin)


def aligned(x, n=16):
    return pl.multiple_of(x, n)


def dot(a, b, contract):
    return lax.dot_general(a, b, ((contract[0], contract[1]), ((), ())), preferred_element_type=F32)


def call(body, out, ins, args, scratch, limit, flops, nbytes, name, aliases=None):
    return pl.pallas_call(
        body,
        out_shape=[pltpu.VMEM(o.shape, o.dtype) if isinstance(o, jax.ShapeDtypeStruct) else o for o in out],
        in_specs=ins,
        out_specs=[VMEM if isinstance(o, jax.ShapeDtypeStruct) else ANY for o in out],
        scratch_shapes=scratch,
        input_output_aliases=aliases or {},
        compiler_params=pltpu.CompilerParams(vmem_limit_bytes=limit * MIB),
        cost_estimate=pl.CostEstimate(
            flops=int(flops), bytes_accessed=int(nbytes), transcendentals=0
        ),
        name=name,
    )(*args)


def arr(shape, dtype):
    return jax.ShapeDtypeStruct(shape, dtype)


def keep_near(*xs):
    return [pltpu.with_memory_space_constraint(x, pltpu.VMEM) for x in xs]


class Copies:
    def __init__(self, sems):
        self.sems, self.n, self.open = sems, 0, []

    def start(self, src, dst):
        c = pltpu.make_async_copy(src, dst, self.sems.at[self.n])
        self.n += 1
        c.start()
        self.open.append(c)
        return c

    def wait(self, c):
        self.open = [o for o in self.open if o is not c]
        c.wait()

    def wait_all(self, some=None):
        for c in list(self.open if some is None else some):
            self.wait(c)


def sems(n):
    return pltpu.SemaphoreType.DMA((n,))


def row_masks(g, here, width):
    r = lax.broadcasted_iota(jnp.int32, (g.win, 128), 0)
    valid = (r + here.start) < here.length
    own = valid & (r >= here.off) & (r < here.off + g.seg)
    return widen(valid.astype(F32), width), widen(own.astype(F32), width)


def widen(x, width):
    return jnp.concatenate([x] * (width // 128), axis=1)


def shifted(x):
    n = x.shape[0]
    r = lax.broadcasted_iota(jnp.int32, (8, 1), 0)
    before, after = pltpu.roll(x, 1, 0), pltpu.roll(x, n - 1, 0)
    before = jnp.concatenate([jnp.where(r == 0, 0.0, before[:8]), before[8:]], axis=0)
    after = jnp.concatenate([after[:-8], jnp.where(r == 7, 0.0, after[-8:])], axis=0)
    return before, after


def grid_order(rows=16):
    n = MEL * rows
    r = lax.broadcasted_iota(jnp.int32, (n, n), 0)
    c = lax.broadcasted_iota(jnp.int32, (n, n), 1)
    return (c == (r % rows) * MEL + r // rows).astype(BF)


def misc_row(*scalars):
    lane = lax.broadcasted_iota(jnp.int32, (1, 128), 1)
    row = jnp.zeros((1, 128), F32)
    for i, s in enumerate(scalars):
        row = jnp.where(lane == i, s, row)
    return row


def pick(row, i):
    lane = lax.broadcasted_iota(jnp.int32, (1, 128), 1)
    return jnp.sum(jnp.where(lane == i, row, 0.0), axis=1, keepdims=True)


def sum_rows(x):
    return jnp.sum(x, axis=0, keepdims=True)


def payload(*parts):
    return jnp.concatenate(parts, axis=1)


def fan_kernel(pay, *rest):
    out = rest[-1]
    out[...] = jnp.broadcast_to(pay[...][None], out.shape)


def fan(g, pay, *after):
    out = [arr((g.ndev, *pay.shape), F32)]
    ins = [VMEM] + [ANY] * len(after)
    return call(fan_kernel, out, ins, [pay, *after], [], 4, 0, 1e5, "fan")[0]


def total_of(g, ref):
    row = jnp.sum(ref[...], axis=0)
    return row[:, : g.cm], row[:, g.cm : 2 * g.cm], row[:, 2 * g.cm :]


def side_by_side(x3, m, low, c, first, last):
    x3[m, :, 0:c] = first.astype(BF)
    x3[m, :, c : 2 * c] = low
    x3[m, :, 2 * c : 3 * c] = last.astype(BF)


def cut_weights_kernel(g, w_in, w_mid, out, sem):
    d = lax.axis_index("dp")
    core, plane = lax.rem(d, 2), lax.rem(d, g.pieces) // 2
    rows = pl.ds(aligned(g.row_of(core, plane)), g.rows)
    copies = Copies(sem)
    copies.start(w_in.at[:, rows, :], out.at[:, :, : g.ci_all])
    copies.start(w_mid.at[:, rows, :], out.at[:, :, g.ci_all :])
    copies.wait_all()


def cut_weights(g, w_in, w_mid):
    out = [arr((9, g.rows, g.ci_all + g.cm), BF)]
    args = [in_hbm(w_in), in_hbm(w_mid)]
    body = functools.partial(cut_weights_kernel, g)
    return call(body, out, [ANY] * 2, args, [sems(2)], 4, 0, 4e5, "cut_weights")[0]


def sort_kernel(g, *rest):
    n = g.nch - 1
    parts, first, second = rest[:n], rest[-2], rest[-1]
    for k in range(n):
        first[k] = parts[k][:, :, : g.ci_all]
        second[k] = parts[k][:, :, g.ci_all :]


def sort_pieces(g, parts, gates):
    n = g.nch - 1
    out = [arr((n, 9, g.rows, g.ci_all), BF), arr((n, 9, g.rows, g.cm), BF)]
    body = functools.partial(sort_kernel, g)
    ins = [VMEM] * n + [ANY] * len(gates)
    return call(body, out, ins, [*parts, *gates], [], 4, 0, 1e6, "sort_pieces")


def cut_maps_kernel(g, spec, after, out, held, sem):
    copies = Copies(sem)
    first = []
    for z in range(g.nch):
        start = static_start(g, z % g.segs) * MEL
        first.append(copies.start(spec.at[z // g.segs, :, start : start + g.win * MEL], held.at[z]))
    for z in range(g.nch):
        copies.wait(first[z])
        copies.start(held.at[z], out.at[z])
    copies.wait_all()


def cut_maps(g, spec, after):
    shape = (g.nch, g.ci, g.win * MEL)
    body = functools.partial(cut_maps_kernel, g)
    args = [in_hbm(spec), after]
    scratch = [pltpu.VMEM(shape, BF), sems(2 * g.nch)]
    return call(body, [pltpu.HBM(shape, BF)], [ANY] * 2, args, scratch, 4, 0, 2e6, "cut_maps")[0]


def static_start(g, seg):
    return min(max(seg * g.seg - HALO, 0), g.frames - g.win)


def cut_cot_kernel(g, cot, after, *rest):
    n = g.nch
    cs, sem = rest[:n], rest[n]
    z = lax.axis_index("chan")
    copies = Copies(sem)
    for k in range(n):
        to = z ^ k
        clip, seg = to // g.segs, lax.rem(to, g.segs)
        _, cstart = g_starts(g, seg)
        copies.start(cot.at[clip, :, pl.ds(aligned(cstart * 2, 128), g.cwin * 2)], cs[k])
    copies.wait_all()


def cut_cot(g, cot, after):
    n = g.nch
    out = [arr((g.co, g.cwin * 2), BF)] * n
    body = functools.partial(cut_cot_kernel, g)
    return call(body, out, [ANY] * 2, [in_hbm(cot), after], [sems(n)], 4, 0, 1e6, "cut_cotangent")


def in_hbm(x):
    return pltpu.with_memory_space_constraint(x, pltpu.HBM)


def join_kernel(g, own, *rest):
    parts, w = rest[:-1], rest[-1]
    z, d = lax.axis_index("chan"), lax.axis_index("dp")
    mine, plane = lax.rem(d, 2), lax.rem(d, g.pieces) // 2
    w[:, pl.ds(aligned(z * g.co), g.co), :] = own[...]
    for side in range(2):
        core = mine if side == 0 else 1 - mine
        for e in range(g.planes):
            row = g.row_of(core, plane ^ g.plane_of(core, e))
            for k in range(1, g.nch):
                at = aligned((z ^ k) * g.co + row)
                w[:, pl.ds(at, g.rows), :] = parts[side * g.planes + e][k - 1]


def join(g, own, parts, depth, name):
    body = functools.partial(join_kernel, g)
    args = [*keep_near(own), *parts]
    ins = [VMEM] * len(args)
    return call(body, [arr((9, g.cm, depth), BF)], ins, args, [], 8, 0, 4 * MIB, name)[0]


def convolve(v3, w, part, back, finish, carry, unrolled=False, window=None):
    def taps(t):
        b = 2 - t if back else t
        return jnp.concatenate([w[b], w[3 + b], w[6 + b]], axis=0 if back else 1)

    contract = ((1,), (0,)) if back else ((1,), (1,))
    depth = v3.shape[2]

    size = part.shape[1]
    window = pl.ds(0, size) if window is None else window

    def times(first, n, t):
        return dot(v3[pl.ds(first, n), window, :].reshape(n * size, depth), taps(t), contract)

    def rows_of(term, n):
        return [term[k * size : (k + 1) * size] for k in range(n)]

    if unrolled:
        for i in range(2):
            total = rows_of(times(4 * i, 4, 1), 4)
            side = rows_of(times(1 + 2 * i, 4, 2 - 2 * i), 4)
            edge = rows_of(times(5 * i, 3, 2 * i), 3)
            for k in range(4):
                value = total[k] + side[k]
                if 0 <= k + i - 1 < 3:
                    value = value + edge[k + i - 1]
                carry = finish(4 * i + k, value, carry)
        return carry

    def step(i, carry):
        part[pl.ds(3 * i + 1, 3)] = times(5 * i, 3, 2 * i).reshape(3, size, part.shape[2])
        part[7 * i] = jnp.zeros(part.shape[1:], F32)
        total = times(4 * i, 4, 1) + times(1 + 2 * i, 4, 2 - 2 * i)
        for k in range(4):
            m = 4 * i + k
            carry = finish(m, part[m] + total[k * size : (k + 1) * size], carry)
        return carry

    return lax.fori_loop(0, 2, step, carry)


def convolve_sums(g, here, x3, w, pre, unrolled):
    _, own = row_masks(g, here, g.cm)

    def finish(m, total, sums):
        pre[m] = total
        kept = total * own
        return sums[0] + sum_rows(kept), sums[1] + sum_rows(kept * total)

    zero = jnp.zeros((1, g.cm), F32)
    return convolve(x3, w, pre, False, finish, (zero, zero), unrolled)


def first_kernel(g, lens, gains, w, maps, pre, x3, pay):
    here = Here(g, lens)
    c = g.ci_all
    order = grid_order()
    row = lax.broadcasted_iota(jnp.int32, (MEL * 16, 128), 0) % 16

    def place_cells(j, square):
        cells = maps[:, :, 128 * j : 128 * (j + 1)].reshape(c, 128)
        frame = row + 16 * j
        valid = (frame + here.start) < here.length
        own = (frame >= here.off) & (frame < here.off + g.seg)
        block = dot(order, cells, ((1,), (1,))) * widen(valid.astype(F32), c)
        x3[:, 16 * j : 16 * (j + 1), c : 2 * c] = block.astype(BF).reshape(MEL, 16, c)
        return square + sum_rows(block * block * widen(own.astype(F32), c))

    square = jnp.zeros((1, c), F32)
    for j in range(g.win // 16):
        square = place_cells(j, square)
    for m in range(MEL):
        before, after_ = shifted(x3[m, :, c : 2 * c].astype(F32))
        x3[m, :, 0:c] = before.astype(BF)
        x3[m, :, 2 * c : 3 * c] = after_.astype(BF)

    one, two = convolve_sums(g, here, x3, w, pre, True)
    frame_total = 0
    pair_total = 0
    for i in range(g.clips):
        frame_total = frame_total + lens[i]
        pair_total = pair_total + (lens[i] + 1) // 2
    row = misc_row(
        frame_total.astype(F32), pair_total.astype(F32), jnp.sum(square, axis=1, keepdims=True)
    )
    pay[...] = payload(one, two, row, *[gains[i : i + 1] for i in range(4)])


def first(g, lens, gains, maps, w):
    body = functools.partial(first_kernel, g)
    out = [
        arr((MEL, g.win, g.cm), F32),
        arr((MEL, g.win, 3 * g.ci_all), BF),
        arr((1, 2 * g.cm + 5 * 128), F32),
    ]
    args = [lens, gains, *keep_near(w, maps)]
    ins = [SMEM] + [VMEM] * 3
    flops = 2 * 9 * MEL * g.win * g.ci_all * g.cm
    return call(body, out, ins, args, [], 10, flops, 10 * MIB, "first_conv")


MEAN1, INV1, GAMMA1, BETA1, GAMMA2, BETA2, COUNT, PAIRS, SQ0, MEAN2, INV2 = range(11)
TABLE = 16


def half_affine(mean, inverse, gamma, beta):
    scale = 0.5 * gamma * inverse
    return scale, 0.5 * beta - mean * scale


def second_kernel(g, lens, got, pre1, w, pre, x3, table, pay, misc_out):
    here = Here(g, lens)
    c = g.cm
    valid, own = row_masks(g, here, c)
    one, two, rest = total_of(g, got)
    misc = rest[:, :128]
    count = MEL * pick(misc, 0) / g.nch
    pairs = (MEL // 2) * pick(misc, 1) / g.nch
    at = [2 * c + 128 * (1 + i) for i in range(4)]
    vectors = [
        jnp.concatenate([got[zz, :, i : i + g.co] for zz in range(g.nch)], axis=1) for i in at
    ]
    mean = one / count
    inverse = lax.rsqrt(two / count - mean * mean + 1e-05)
    wide = jnp.zeros((1, c), F32)
    table[...] = jnp.concatenate(
        [mean, inverse, *vectors, wide + count, wide + pairs, wide + pick(misc, 2)]
        + [wide] * (TABLE - 9),
        axis=0,
    )
    scale, shift = half_affine(mean, inverse, vectors[0], vectors[1])


    def activate(m, square):
        half = pre1[m] * scale + shift
        act = half * (1.0 + jnp.tanh(half)) * valid
        low = act.astype(BF)
        before, after = shifted(low.astype(F32))
        side_by_side(x3, m, low, c, before, after)
        return square + sum_rows(act * act * own)

    square = jnp.zeros((1, c), F32)
    for m in range(MEL):
        square = activate(m, square)
    one, two = convolve_sums(g, here, x3, w, pre, True)
    pay[...] = payload(one, two)
    misc_out[...] = misc_row(jnp.sum(square, axis=1, keepdims=True))


def second(g, lens, got, pre1, w):
    body = functools.partial(second_kernel, g)
    out = [
        arr((MEL, g.win, g.cm), F32),
        arr((MEL, g.win, 3 * g.cm), BF),
        arr((TABLE, g.cm), F32),
        arr((1, 2 * g.cm), F32),
        arr((1, 128), F32),
    ]
    args = [lens, *keep_near(got, pre1, w)]
    flops = 2 * 9 * MEL * g.win * g.cm * g.cm
    ins = [SMEM, VMEM, VMEM, VMEM]
    return call(body, out, ins, args, [], 10, flops, 17 * MIB, "second_conv")


def pool_kernel(g, lens, got, old_ref, pre2, *rest):
    n, c = g.nch, g.cm
    cs, outs = rest[:n], rest[n : 2 * n]
    local_ref, table, pay, misc_out, held, grads, total, flat = rest[2 * n :]
    here = Here(g, lens)
    for k in range(n):
        held[pl.ds(aligned((here.z ^ k) * g.co), g.co), :] = cs[k][...]
    r = lax.broadcasted_iota(jnp.int32, (256, 128), 0)
    l = lax.broadcasted_iota(jnp.int32, (256, 128), 1)
    spread = (l == (r % 64) // 2 * 4 + r // 64).astype(BF)

    @pl.loop(0, g.cwin // 64)
    def _(j):
        cells = held[:, pl.ds(aligned(128 * j, 128), 128)]
        block = dot(spread, cells, ((1,), (1,)))
        grads[:, pl.ds(aligned(64 * j), 64), :] = block.reshape(MEL // 2, 64, c)

    one, two, _ = total_of(g, got)
    old = old_ref[...]
    count = old[COUNT : COUNT + 1]
    mean = one / count
    inverse = lax.rsqrt(two / count - mean * mean + 1e-05)
    wide = jnp.zeros((1, c), F32)
    table[...] = jnp.concatenate([old[:MEAN2], mean, inverse] + [wide] * (TABLE - 11), axis=0)
    half_gamma, half_beta = 0.5 * old[GAMMA2 : GAMMA2 + 1], 0.5 * old[BETA2 : BETA2 + 1]
    less = -mean * inverse
    side = g.win - g.seg
    segment = pl.ds(aligned(here.off), g.seg)
    sides = [
        aligned(jnp.where(16 * j < here.off, 16 * j, 16 * j + g.seg)) for j in range(side // 16)
    ]

    def weights(rows, start, width):
        frame = lax.broadcasted_iota(jnp.int32, (rows, 128), 0) + (here.start + start)
        valid = (frame < here.length).astype(F32)
        share = jnp.where(here.length - frame // 2 * 2 >= 2, 0.25, 0.5)
        return widen(0.5 * share * valid, width), widen(valid, width)

    half_share, valid = weights(g.seg, here.off, c)
    side_shares = [weights(16, start, c)[0] for start in sides]
    out_row = lax.broadcasted_iota(jnp.int32, (g.seg, 2 * g.seg), 0)
    out_cell = lax.broadcasted_iota(jnp.int32, (g.seg, 2 * g.seg), 1)
    first_cell = out_row // 2 * 4
    frame = out_row + (here.start + here.off)
    out_share = jnp.where(here.length - frame // 2 * 2 >= 2, 0.25, 0.5)
    total[...] = jnp.zeros(total.shape, F32)

    def bent(pre):
        scaled = pre * inverse + less
        half = scaled * half_gamma + half_beta
        bend = jnp.tanh(half)
        twice = 1.0 + bend
        whole = half * twice
        return scaled, whole, twice + whole * (1.0 - bend)

    def step(k, sums):
        beta_sum, gamma_sum, square = sums
        given = grads[k, pl.ds(aligned(here.qoff + here.off), g.seg), :] * half_share
        pair = None
        for i in range(2):
            m = 2 * k + i
            scaled, whole, slope = bent(pre2[m, segment, :])
            act = whole * valid
            square = square + sum_rows(act * act)
            local = given * slope
            local_ref[m, segment, :] = local
            beta_sum = beta_sum + sum_rows(local)
            gamma_sum = gamma_sum + sum_rows(local * scaled)
            pair = act if pair is None else pair + act
            for start, side_share in zip(sides, side_shares, strict=True):
                rows = pl.ds(start, 16)
                _, _, slope = bent(pre2[m, rows, :])
                given_side = grads[k, pl.ds(aligned(here.qoff + start), 16), :] * side_share
                local_ref[m, rows, :] = given_side * slope
        gather = jnp.where(out_cell == first_cell + k, out_share, 0.0).astype(BF)
        total[...] += dot(pair.astype(BF), gather, ((0,), (0,)))
        return beta_sum, gamma_sum, square

    zero = jnp.zeros((1, c), F32)
    beta_sum, gamma_sum, square = lax.fori_loop(0, MEL // 2, step, (zero, zero, zero))
    pooled = total[...]
    flat[...] = pooled.astype(BF)
    for k in range(n):
        outs[k][...] = flat[pl.ds(aligned((here.z ^ k) * g.co), g.co), :]
    pooled_square = sum_rows(jnp.sum(pooled * pooled, axis=1, keepdims=True))
    pay[...] = jnp.broadcast_to(payload(beta_sum, gamma_sum)[None], pay.shape)
    misc_out[...] = misc_row(jnp.sum(square, axis=1, keepdims=True), pooled_square)


def pool(g, lens, got, table, pre2, cs):
    n = g.nch
    body = functools.partial(pool_kernel, g)
    out = [arr((g.co, 2 * g.seg), BF)] * n + [
        arr((MEL, g.win, g.cm), F32),
        arr((TABLE, g.cm), F32),
        arr((g.ndev, 1, 2 * g.cm), F32),
        arr((1, 128), F32),
    ]
    scratch = [
        pltpu.VMEM((g.cm, g.cwin * 2), BF),
        pltpu.VMEM((MEL // 2, g.cwin, g.cm), F32),
        pltpu.VMEM((g.cm, 2 * g.seg), F32),
        pltpu.VMEM((g.cm, 2 * g.seg), BF),
    ]
    args = [lens, *keep_near(got, table, pre2, *cs)]
    ins = [SMEM] + [VMEM] * (len(args) - 1)
    out = call(body, out, ins, args, scratch, 12, 4e9, 8 * MIB, "pool")
    return out[:n], *out[n:]


def terms_kernel(g, depth, norm, lens, got, table, pre, local, x3, after, *refs):
    grad, sums, roots, terms, give = refs
    here = Here(g, lens)
    c = g.cm
    valid, _ = row_masks(g, here, c)
    beta_sum, gamma_sum, rest = total_of(g, got)
    t = table[...]
    mean, inverse, gamma = (t[i : i + 1] for i in norm)
    count = t[COUNT : COUNT + 1]
    sums[...] = jnp.concatenate([beta_sum, gamma_sum] + [jnp.zeros((1, c), F32)] * 6, axis=0)
    if rest.shape[1]:
        second, third = rest[:, :128], rest[:, 128:]
        tops = misc_row(
            pick(t[SQ0 : SQ0 + 1, :128], 0), pick(second, 0), pick(third, 0), pick(third, 1)
        )
        lane = lax.broadcasted_iota(jnp.int32, (1, 128), 1)
        cells, pairs = count[:, :128], t[PAIRS : PAIRS + 1, :128]
        under = jnp.where(lane == 0, cells * g.ci_all, jnp.where(lane == 3, pairs * c, cells * c))
        roots[...] = jnp.broadcast_to(jnp.sqrt(tops / under), (8, 128))
    factor = gamma * inverse
    slope = factor * inverse * gamma_sum / count
    level = factor * beta_sum / count - mean * slope

    @pl.loop(0, MEL)
    def _(m):
        value = valid * (local[m] * factor - pre[m] * slope - level)
        grad[m] = value.astype(BF)

    segment = pl.ds(aligned(here.off), g.seg)

    @pl.loop(0, 3)
    def _(a):
        lanes_of = pl.ds(aligned(a * depth, 128), depth)
        for b in (1, 0, 2):
            low = max(0, 1 - b)
            high = min(MEL, MEL + 1 - b)
            rows = (high - low) * g.seg
            left = grad[low:high, segment, :].reshape(rows, c)
            right = x3[low + b - 1 : high + b - 1, segment, lanes_of].reshape(rows, depth)
            term = dot(left, right, ((0,), (0,))).astype(BF)
            for z in range(g.nch):
                for s in range(2):
                    for p in range(g.planes):
                        at = z * g.co + g.row_of(s, p)
                        terms[s, z, p, 3 * a + b] = term[at : at + g.rows]

    give[...] = terms[1 - here.core]


def terms_of(g, lens, got, table, pre, local, x3, after, depth, norm, name):
    body = functools.partial(terms_kernel, g, depth, norm)
    shape = (g.nch, g.planes, 9, g.rows, depth)
    out = [
        arr((MEL, g.win, g.cm), BF),
        arr((8, g.cm), F32),
        arr((8, 128), F32),
        arr((2, *shape), BF),
        arr(shape, BF),
    ]
    args = [lens, *keep_near(got, table, pre, local, x3), after]
    ins = [SMEM] + [VMEM] * 5 + [ANY]
    flops = 2 * 9 * MEL * g.win * g.cm * depth
    return call(body, out, ins, args, [], 10, flops, 15 * MIB, name)


def back_kernel(g, lens, table, grad, pre1, w, misc2, misc3, after, local1, pay, g3):
    here = Here(g, lens)
    c = g.cm
    valid, own = row_masks(g, here, c)
    t = table[...]

    def row(i):
        return t[i : i + 1]


    for m in range(MEL):
        low = grad[m]
        before, after = shifted(low.astype(F32))
        side_by_side(g3, m, low, c, after, before)

    inverse, less = row(INV1), -row(MEAN1) * row(INV1)
    half_gamma, half_beta = 0.5 * row(GAMMA1), 0.5 * row(BETA1)
    half_valid = 0.5 * valid

    def finish(m, given, sums):
        scaled = pre1[m] * inverse + less
        half = scaled * half_gamma + half_beta
        bend = jnp.tanh(half)
        twice = 1.0 + bend
        local = given * half_valid * (twice + half * twice * (1.0 - bend))
        local1[m] = local
        kept = local * own
        return sums[0] + sum_rows(kept), sums[1] + sum_rows(kept * scaled)

    zero = jnp.zeros((1, c), F32)
    beta_sum, gamma_sum = convolve(g3, w, local1, True, finish, (zero, zero), True)
    pay[...] = payload(beta_sum, gamma_sum, misc2[...], misc3[...])


def back(g, lens, table, grad, pre1, w, misc2, misc3, after):
    body = functools.partial(back_kernel, g)
    out = [arr((MEL, g.win, g.cm), F32), arr((1, 2 * g.cm + 2 * 128), F32)]
    scratch = [pltpu.VMEM((MEL, g.win, 3 * g.cm), BF)]
    args = [lens, *keep_near(table, grad, pre1, w, misc2, misc3), after]
    flops = 2 * 9 * MEL * g.win * g.cm * g.cm
    ins = [SMEM] + [VMEM] * 6 + [ANY]
    return call(body, out, ins, args, scratch, 14, flops, 20 * MIB, "second_back")


def release_kernel(*refs):
    pass


def release_far(gates, x):
    n = len(gates)
    return pl.pallas_call(
        release_kernel,
        out_shape=pltpu.HBM(x.shape, x.dtype),
        in_specs=[ANY] * (n + 1),
        out_specs=ANY,
        input_output_aliases={n: 0},
        compiler_params=pltpu.CompilerParams(vmem_limit_bytes=2 * MIB),
        name="release_far",
    )(*gates, in_hbm(x))


def release(gates, arrays):
    out = [arr(x.shape, x.dtype) for x in arrays]
    n = len(gates)
    ins = [ANY] * n + [VMEM] * len(arrays)
    aliases = {i + n: i for i in range(len(arrays))}
    args = [*gates, *keep_near(*arrays)]
    return call(release_kernel, out, ins, args, [], 2, 0, 1, "release", aliases)


def spectra_kernel(g, lens, grad, after, w, *rest):
    n, c = g.nch, g.cm
    outs, (g3, rows, flat, part) = rest[:n], rest[n:]
    here = Here(g, lens)

    @pl.loop(0, MEL)
    def _(m):
        low = grad[m]
        before, after_ = shifted(low.astype(F32))
        side_by_side(g3, m, low, c, after_, before)

    r = lax.broadcasted_iota(jnp.int32, (g.seg, 128), 0) + here.off + here.start
    valid = widen((r < here.length).astype(F32), g.ci_all)

    def finish(m, total, carry):
        rows[m] = (total * valid).astype(BF)
        return carry

    convolve(g3, w, part, True, finish, 0, False, pl.ds(aligned(here.off), g.seg))
    order = grid_order()

    for j in range(g.seg // 16):
        block = rows[:, 16 * j : 16 * (j + 1), :].reshape(MEL * 16, g.ci_all)
        flat[:, 128 * j : 128 * (j + 1)] = dot(block, order, ((0,), (0,))).astype(BF)

    for k in range(n):
        outs[k][...] = flat[pl.ds(aligned((here.z ^ k) * g.ci), g.ci), :]


def spectra_back(g, lens, grad, after, w):
    n = g.nch
    body = functools.partial(spectra_kernel, g)
    out = [arr((g.ci, g.seg * MEL), BF)] * n
    scratch = [
        pltpu.VMEM((MEL, g.win, 3 * g.cm), BF),
        pltpu.VMEM((MEL, g.seg, g.ci_all), BF),
        pltpu.VMEM((g.ci_all, g.seg * MEL), BF),
        pltpu.VMEM((MEL, g.seg, g.ci_all), F32),
    ]
    grad, w = keep_near(grad, w)
    args = [lens, grad, after, w]
    flops = 2 * 9 * MEL * g.win * g.cm * g.ci_all
    ins = [SMEM, VMEM, ANY, VMEM]
    return call(body, out, ins, args, scratch, 14, flops, 5 * MIB, "spectra_back")


def place_kernel(g, width, *rest):
    n = g.nch
    parts, out, done = rest[:n], rest[n], rest[n + 1]
    z = lax.axis_index("chan")
    done[...] = jnp.zeros(done.shape, F32)
    for k in range(n):
        source = z ^ k
        for zz in range(n):

            @pl.when(source == zz)
            def _():
                at = zz % g.segs * width
                out[zz // g.segs, :, at : at + width] = parts[k][...].astype(out.dtype)


def place(g, parts, dtype, name):
    channels, width = parts[0].shape
    return pl.pallas_call(
        functools.partial(place_kernel, g, width),
        out_shape=[
            jax.ShapeDtypeStruct((g.clips, channels, g.segs * width), dtype),
            jax.ShapeDtypeStruct((8, 128), F32),
        ],
        in_specs=[VMEM] * g.nch,
        out_specs=[VMEM] * 2,
        compiler_params=pltpu.CompilerParams(vmem_limit_bytes=8 * MIB),
        cost_estimate=TINY,
        name=name,
    )(*parts)


def core_sum_kernel(g, terms, got, after, stay, go):
    d, z = lax.axis_index("dp"), lax.axis_index("chan")
    core, plane = lax.rem(d, 2), lax.rem(d, g.pieces) // 2
    half = g.planes // 2
    for e in range(g.planes):
        at = plane ^ g.plane_of(core, e)
        for k in range(g.nch):
            source = z ^ g.zed_of(k)
            value = terms[core, source, at].astype(F32) + got[source, at].astype(F32)
            to = stay if e < half else go
            to[(e % half) * g.nch + k] = value.astype(BF)


def core_sum(g, terms, got, after, name):
    shape = (g.planes // 2 * g.nch, *got.shape[2:])
    return pl.pallas_call(
        functools.partial(core_sum_kernel, g),
        out_shape=[pltpu.VMEM(shape, BF)] * 2,
        in_specs=[VMEM, VMEM, ANY],
        out_specs=[VMEM] * 2,
        compiler_params=pltpu.CompilerParams(vmem_limit_bytes=16 * MIB),
        name=name,
    )(keep_near(terms)[0], got, after)


def quarter_kernel(g, terms, got, *outs):
    d, z = lax.axis_index("dp"), lax.axis_index("chan")
    core, plane = lax.rem(d, 2), lax.rem(d, g.pieces) // 2
    for e in range(g.planes):
        at = plane ^ g.plane_of(core, e)
        for k in range(g.nch):
            source = z ^ g.zed_of(k)
            value = terms[core, source, at].astype(F32) + got[source, at].astype(F32)
            outs[e][k] = value.astype(BF)


def quarters(g, terms, got, name):
    shape = (g.nch, *got.shape[2:])
    return pl.pallas_call(
        functools.partial(quarter_kernel, g),
        out_shape=[pltpu.VMEM(shape, BF)] * g.planes,
        in_specs=[VMEM, VMEM],
        out_specs=[VMEM] * g.planes,
        compiler_params=pltpu.CompilerParams(vmem_limit_bytes=16 * MIB),
        name=name,
    )(keep_near(terms)[0], got)


def add_kernel(n, halves, *rest):
    first = rest[0]
    outs = rest[len(rest) - halves :]
    count = first.shape[0] // halves
    for i in range(first.shape[0]):
        total = first[i].astype(F32)
        for r in rest[1:n]:
            total = total + r[i].astype(F32)
        outs[i // count][i % count] = total.astype(BF)


def add_up(parts, halves, gates, name):
    n = len(parts)
    shape = (parts[0].shape[0] // halves, *parts[0].shape[1:])
    return pl.pallas_call(
        functools.partial(add_kernel, n, halves),
        out_shape=[pltpu.VMEM(shape, BF)] * halves,
        in_specs=[VMEM] * n + [ANY] * len(gates),
        out_specs=[VMEM] * halves,
        compiler_params=pltpu.CompilerParams(vmem_limit_bytes=8 * MIB),
        name=name,
    )(*parts, *gates)


def halve_kernel(stay, got, *rest):
    n = stay.shape[0]
    outs = rest[-2:] if n > 1 else rest[-1:]
    for i in range(n):
        value = stay[i].astype(F32) + got[i].astype(F32)
        if n == 1:
            outs[0][...] = value.astype(BF)
        else:
            outs[i // (n // 2)][i % (n // 2)] = value.astype(BF)


def halve(stay, got, gates, name):
    n = stay.shape[0]
    if n == 1:
        out = [jax.ShapeDtypeStruct(stay.shape[1:], BF)]
    else:
        out = [jax.ShapeDtypeStruct((n // 2, *stay.shape[1:]), BF)] * 2
    return pl.pallas_call(
        halve_kernel,
        out_shape=out,
        in_specs=[VMEM, VMEM] + [ANY] * len(gates),
        out_specs=[VMEM] * len(out),
        compiler_params=pltpu.CompilerParams(vmem_limit_bytes=8 * MIB),
        name=name,
    )(stay, got, *gates)


def spread_kernel(g, mine, other, out, done):
    done[...] = jnp.zeros(done.shape, F32)
    d = lax.axis_index("dp")
    core, plane = lax.rem(d, 2), lax.rem(d, g.pieces) // 2
    for side, part in enumerate((mine, other)):
        c = core if side == 0 else 1 - core
        for e in range(g.planes):
            at = aligned(g.row_of(c, plane ^ g.plane_of(c, e)))
            out[:, pl.ds(at, g.rows), :] = part[e].astype(F32)


def spread_out(g, mine, other, depth, name):
    return pl.pallas_call(
        functools.partial(spread_kernel, g),
        out_shape=[
            jax.ShapeDtypeStruct((9, g.co, depth), F32),
            jax.ShapeDtypeStruct((8, 128), F32),
        ],
        in_specs=[VMEM] * 2,
        out_specs=[VMEM] * 2,
        compiler_params=pltpu.CompilerParams(vmem_limit_bytes=12 * MIB),
        name=name,
    )(mine, other)


def stack_kernel(n, *refs):
    for k, r in enumerate(refs[:n]):
        refs[-1][k] = r[...]


def stack(parts, gates, name):
    n = len(parts)
    out = [arr((n, *parts[0].shape), parts[0].dtype)]
    ins = [VMEM] * n + [ANY] * len(gates)
    body = functools.partial(stack_kernel, n)
    return call(body, out, ins, [*parts, *gates], [], 6, 0, 1e6, name)[0]


class Links:
    def __init__(self, g):
        self.g = g

    def core(self, x):
        return lax.ppermute(x, "dp", [(i, i ^ 1) for i in range(self.g.ndp)])

    def dp(self, x, bit):
        return lax.ppermute(x, "dp", [(i, i ^ bit) for i in range(self.g.ndp)])

    def plane(self, x, turn):
        g = self.g
        return lax.ppermute(x, "dp", [(i, i ^ (2 * g.mask(i & 1, turn))) for i in range(g.ndp)])

    def chan(self, x, k):
        return lax.ppermute(x, "chan", [(i, i ^ k) for i in range(self.g.nch)])

    def exchange(self, parts):
        return [parts[0]] + [self.chan(parts[k], k) for k in range(1, self.g.nch)]

    def gather_planes(self, x, gates=()):
        have = [x]
        for turn in reversed(range(self.g.turns)):
            more = [self.plane(h, turn) for h in have[:1]]
            rest = have[1:]
            if gates and turn == 0 and rest:
                rest = release([*gates, *more], rest)
            have = have + more + [self.plane(h, turn) for h in rest]
        return have

    def gather_cores(self, have):
        return [*have, *[self.core(h) for h in have]]

    def gather_direct(self, x):
        g = self.g
        pairs = [[(i, i ^ (2 * g.plane_of(i & 1, e))) for i in range(g.ndp)] for e in range(g.planes)]
        return [x] + [lax.ppermute(x, "dp", p) for p in pairs[1:]]


def everyone(x):
    return lax.all_to_all(x, ("dp", "chan"), 0, 0)


def make_body(ndp, nch):
    def body(
        spectra, lengths, weight_in, gamma_in, beta_in, weight_mid, gamma_mid, beta_mid, cotangent
    ):
        g = Geometry(
            ndp,
            nch,
            spectra.shape[0],
            spectra.shape[2] // MEL,
            weight_in.shape[2],
            weight_mid.shape[2],
        )
        links = Links(g)
        gains = jnp.stack([gamma_in, beta_in, gamma_mid, beta_mid])
        gains = jnp.pad(gains, ((0, 0), (0, 128 - g.co)))

        piece = cut_weights(g, weight_in, weight_mid)
        cells = cut_maps(g, spectra, piece)
        cots = cut_cot(g, cotangent, cells)
        pieces_in, pieces_mid = sort_pieces(
            g, [links.chan(piece, k) for k in range(1, nch)], [cots[0]]
        )
        maps = lax.all_to_all(release_far([pieces_in], cells), "chan", 0, 0)
        planes_in = links.gather_planes(pieces_in)
        w_in = join(g, weight_in, links.gather_cores(planes_in), g.ci_all, "join_in")
        planes_mid = links.gather_planes(pieces_mid, [maps])

        pre1, x3_in, pay = first(g, lengths, gains, maps, w_in)
        got = everyone(fan(g, pay, cots[0], *planes_mid[1:]))
        planes_mid = release([got], planes_mid)
        w_mid = join(g, weight_mid, links.gather_cores(planes_mid), g.cm, "join_mid")
        cs = links.exchange(release([got], cots))
        pre2, x3_mid, table, pay, misc2 = second(g, lengths, got, pre1, w_mid)
        got = everyone(fan(g, pay, *cs[1:]))
        pooled, local2, table, pay, misc3 = pool(g, lengths, got, table, pre2, cs)
        got = everyone(pay)
        pooled = links.exchange(release([got], pooled))
        grad2, sums2, _, terms_mid, give_mid = terms_of(
            g, lengths, got, table, pre2, local2, x3_mid, got, g.cm, (MEAN2, INV2, GAMMA2), "weight_mid_terms"
        )
        got_mid = links.core(give_mid)
        split = g.turns == 2
        if split:
            stay_a, stay_b, go_a, go_b = quarters(g, terms_mid, got_mid, "mid_core_sum")
            got_b = links.plane(go_b, 0)
        else:
            stay_mid, go_b = core_sum(g, terms_mid, got_mid, got_mid, "mid_core_sum")
            got_b = go_b
        local1, pay = back(g, lengths, table, grad2, pre1, w_mid, misc2, misc3, go_b)
        got = everyone(fan(g, pay, got_b, *pooled[1:]))
        block_out, pooled_done = place(g, pooled, BF, "place_pooled")
        if split:
            (go_1,) = add_up([stay_b, got_b], 1, [got], "mid_sum_b")
            got_1 = links.plane(go_1, 1)
            got_a = links.plane(release([got], [go_a])[0], 0)
        else:
            (go_mid,) = release([got], [go_b])
        grad1, sums1, roots, terms_in, give_in = terms_of(
            g, lengths, got, table, pre1, local1, x3_in, got, g.ci_all, (MEAN1, INV1, GAMMA1), "weight_in_terms"
        )
        got_in = links.core(give_in)

        class Chain:
            def __init__(self, stay, go, depth, name):
                self.stay, self.go, self.depth, self.name = stay, go, depth, name
                self.turns = [functools.partial(links.plane, turn=t) for t in range(g.turns)]
                self.turns += [functools.partial(links.chan, k=1 << t) for t in range(g.zturns)]

            def turn(self, i, *gates):
                got = self.turns[i](self.go)
                done = halve(self.stay, got, gates, f"{self.name}_sum_{i}")
                self.stay, self.go = done if len(done) == 2 else (done[0], None)
                return self.stay

            def rest(self):
                bit = g.pieces
                while bit < ndp:
                    got = links.dp(self.stay, bit)
                    self.stay = halve(self.stay[None], got[None], [], self.name + "_rest")[0]
                    bit *= 2

            def out(self, planes, *gates):
                mine = stack(planes, gates, self.name + "_stack")
                return spread_out(g, mine, links.core(mine), self.depth, self.name + "_out")

        turns = g.turns + g.zturns
        parts = spectra_back(g, lengths, grad1, grad1, w_in)
        stay_in, go_in = core_sum(g, terms_in, got_in, parts[0], "in_core_sum")
        inner = Chain(stay_in, go_in, g.ci_all, "in")
        parts = links.exchange(parts)
        spectra_grad, spectra_done = place(g, parts, F32, "place_spectra")
        if split:
            halves = add_up([stay_a, got_a, got_1], 2, [stay_in], "mid_sum_1")
            mid = Chain(*halves, g.cm, "mid")
        else:
            mid = Chain(stay_mid, go_mid, g.cm, "mid")
            for i in range(g.turns):
                mid.turn(i, stay_in)
        gates = [parts[2 : nch - 1], [pooled_done]]
        at = mid.stay
        for i in range(g.turns):
            at = inner.turn(i, at, *(gates[i] if i < 2 else []))
            if i == 0:
                at = mid.turn(g.turns, at)
        for i in range(g.turns, turns):
            at = inner.turn(i, at, *(parts[nch - 1 :] if i == g.turns else []))
            if i + 1 < turns:
                at = mid.turn(i + 1, at)
        inner.rest()
        mid.rest()
        planes_in = links.gather_planes(inner.stay)
        weight_mid_grad, mid_done = mid.out(links.gather_direct(mid.stay), *planes_in[1:3], parts[1])
        weight_in_grad, _ = inner.out(planes_in, mid_done, spectra_done)
        z = lax.axis_index("chan")

        def share(sums, i):
            return lax.dynamic_slice_in_dim(sums[i], z * g.co, g.co)

        return (
            block_out,
            spectra_grad,
            weight_in_grad,
            share(sums1, 1),
            share(sums1, 0),
            weight_mid_grad,
            share(sums2, 1),
            share(sums2, 0),
            roots[0, :4],
        )

    return body


def solution(mesh):
    placed = (
        P("dp", "chan", None),
        P("dp"),
        P(None, "chan", None),
        P("chan"),
        P("chan"),
        P(None, "chan", None),
        P("chan"),
        P("chan"),
        P("dp", "chan", None),
    )
    return jax.shard_map(
        make_body(mesh.shape["dp"], mesh.shape["chan"]),
        mesh=mesh,
        in_specs=placed,
        out_specs=(
            P("dp", "chan", None),
            P("dp", "chan", None),
            P(None, "chan", None),
            P("chan"),
            P("chan"),
            P(None, "chan", None),
            P("chan"),
            P("chan"),
            P(),
        ),
        check_vma=False,
    )
```

```python
import functools

import jax
import jax.numpy as jnp
from jax import lax
from jax.experimental import pallas as pl
from jax.experimental.pallas import tpu as pltpu
from jax.sharding import PartitionSpec as P

MEL = 8
HALO = 16
BF = jnp.bfloat16
F32 = jnp.float32
MIB = 1024 * 1024
TINY = pl.CostEstimate(flops=1, bytes_accessed=1, transcendentals=0)

VMEM = pl.BlockSpec(memory_space=pltpu.VMEM)
SMEM = pl.BlockSpec(memory_space=pltpu.SMEM)
ANY = pl.BlockSpec(memory_space=pl.ANY)
HBM = pl.BlockSpec(memory_space=pltpu.HBM)


def bits_of(n):
    return n.bit_length() - 1


class Geometry:
    def __init__(self, ndp, nch, clips, frames, c_in, c_mid):
        self.ndp, self.nch, self.ndev = ndp, nch, ndp * nch
        self.clips, self.frames = clips, frames
        self.ci_all, self.cm = c_in, c_mid
        self.ci, self.co = c_in // nch, c_mid // nch
        self.segs = nch // clips
        self.seg = frames // self.segs
        self.win = self.seg + HALO * min(self.segs - 1, 2)
        starts = [min(max(s * self.seg - HALO, 0), frames - self.win) for s in range(self.segs)]
        self.cwin = min(frames, (self.win + 48 + 63) // 64 * 64)
        assert all(min(s // 64 * 64, frames - self.cwin) + self.cwin >= s + self.win for s in starts)
        self.rows = max(16, self.co // ndp)
        self.pieces = self.co // self.rows
        self.planes = self.pieces // 2
        self.turns = bits_of(self.planes)
        self.zturns = bits_of(nch)

    def mask(self, core, turn):
        low, high = 1 << turn, 1 << (self.turns - 1 - turn)
        return low + core * (high - low)

    def plane_of(self, core, e):
        rel = 0
        for t in range(self.turns):
            if (e >> (self.turns - 1 - t)) & 1:
                rel = rel ^ self.mask(core, t)
        return rel

    def row_of(self, core, plane):
        return core * (self.co // 2) + plane * self.rows

    def zed_of(self, e):
        return sum(1 << t for t in range(self.zturns) if (e >> (self.zturns - 1 - t)) & 1)


class Here:
    def __init__(self, g, lens):
        self.z = lax.axis_index("chan")
        self.d = lax.axis_index("dp")
        self.core = lax.rem(self.d, 2)
        self.plane = lax.rem(self.d, g.pieces) // 2
        clip, seg = self.z // g.segs, lax.rem(self.z, g.segs)
        self.length = lens[clip]
        self.start, self.cstart = g_starts(g, seg)
        self.off = seg * g.seg - self.start
        self.qoff = self.start - self.cstart


def g_starts(g, seg):
    start = jnp.clip(seg * g.seg - HALO, 0, g.frames - g.win)
    return start, jnp.minimum(start // 64 * 64, g.frames - g.cwin)


def aligned(x, n=16):
    return pl.multiple_of(x, n)


def dot(a, b, contract):
    return lax.dot_general(a, b, ((contract[0], contract[1]), ((), ())), preferred_element_type=F32)


def call(body, out, ins, args, scratch, limit, flops, nbytes, name, aliases=None):
    return pl.pallas_call(
        body,
        out_shape=[pltpu.VMEM(o.shape, o.dtype) if isinstance(o, jax.ShapeDtypeStruct) else o for o in out],
        in_specs=ins,
        out_specs=[VMEM if isinstance(o, jax.ShapeDtypeStruct) else ANY for o in out],
        scratch_shapes=scratch,
        input_output_aliases=aliases or {},
        compiler_params=pltpu.CompilerParams(vmem_limit_bytes=limit * MIB),
        cost_estimate=pl.CostEstimate(
            flops=int(flops), bytes_accessed=int(nbytes), transcendentals=0
        ),
        name=name,
    )(*args)


def arr(shape, dtype):
    return jax.ShapeDtypeStruct(shape, dtype)


def keep_near(*xs):
    return [pltpu.with_memory_space_constraint(x, pltpu.VMEM) for x in xs]


class Copies:
    def __init__(self, sems):
        self.sems, self.n, self.open = sems, 0, []

    def start(self, src, dst):
        c = pltpu.make_async_copy(src, dst, self.sems.at[self.n])
        self.n += 1
        c.start()
        self.open.append(c)
        return c

    def wait(self, c):
        self.open = [o for o in self.open if o is not c]
        c.wait()

    def wait_all(self, some=None):
        for c in list(self.open if some is None else some):
            self.wait(c)


def sems(n):
    return pltpu.SemaphoreType.DMA((n,))


def row_masks(g, here, width):
    r = lax.broadcasted_iota(jnp.int32, (g.win, 128), 0)
    valid = (r + here.start) < here.length
    own = valid & (r >= here.off) & (r < here.off + g.seg)
    return widen(valid.astype(F32), width), widen(own.astype(F32), width)


def widen(x, width):
    return jnp.concatenate([x] * (width // 128), axis=1)


def shifted(x):
    n = x.shape[0]
    r = lax.broadcasted_iota(jnp.int32, (8, 1), 0)
    before, after = pltpu.roll(x, 1, 0), pltpu.roll(x, n - 1, 0)
    before = jnp.concatenate([jnp.where(r == 0, 0.0, before[:8]), before[8:]], axis=0)
    after = jnp.concatenate([after[:-8], jnp.where(r == 7, 0.0, after[-8:])], axis=0)
    return before, after


def grid_order(rows=16):
    n = MEL * rows
    r = lax.broadcasted_iota(jnp.int32, (n, n), 0)
    c = lax.broadcasted_iota(jnp.int32, (n, n), 1)
    return (c == (r % rows) * MEL + r // rows).astype(BF)


def misc_row(*scalars):
    lane = lax.broadcasted_iota(jnp.int32, (1, 128), 1)
    row = jnp.zeros((1, 128), F32)
    for i, s in enumerate(scalars):
        row = jnp.where(lane == i, s, row)
    return row


def pick(row, i):
    lane = lax.broadcasted_iota(jnp.int32, (1, 128), 1)
    return jnp.sum(jnp.where(lane == i, row, 0.0), axis=1, keepdims=True)


def sum_rows(x):
    return jnp.sum(x, axis=0, keepdims=True)


def payload(*parts):
    return jnp.concatenate(parts, axis=1)


def fan_kernel(pay, *rest):
    out = rest[-1]
    out[...] = jnp.broadcast_to(pay[...][None], out.shape)


def fan(g, pay, *after):
    out = [arr((g.ndev, *pay.shape), F32)]
    ins = [VMEM] + [ANY] * len(after)
    return call(fan_kernel, out, ins, [pay, *after], [], 4, 0, 1e5, "fan")[0]


def total_of(g, ref):
    row = jnp.sum(ref[...], axis=0)
    return row[:, : g.cm], row[:, g.cm : 2 * g.cm], row[:, 2 * g.cm :]


def side_by_side(x3, m, low, c, first, last):
    x3[m, :, 0:c] = first.astype(BF)
    x3[m, :, c : 2 * c] = low
    x3[m, :, 2 * c : 3 * c] = last.astype(BF)


def cut_weights_kernel(g, w_in, w_mid, out, sem):
    d = lax.axis_index("dp")
    core, plane = lax.rem(d, 2), lax.rem(d, g.pieces) // 2
    rows = pl.ds(aligned(g.row_of(core, plane)), g.rows)
    copies = Copies(sem)
    copies.start(w_in.at[:, rows, :], out.at[:, :, : g.ci_all])
    copies.start(w_mid.at[:, rows, :], out.at[:, :, g.ci_all :])
    copies.wait_all()


def cut_weights(g, w_in, w_mid):
    out = [arr((9, g.rows, g.ci_all + g.cm), BF)]
    args = [in_hbm(w_in), in_hbm(w_mid)]
    body = functools.partial(cut_weights_kernel, g)
    return call(body, out, [ANY] * 2, args, [sems(2)], 4, 0, 4e5, "cut_weights")[0]


def sort_kernel(g, *rest):
    n = g.nch - 1
    parts, first, second = rest[:n], rest[-2], rest[-1]
    for k in range(n):
        first[k] = parts[k][:, :, : g.ci_all]
        second[k] = parts[k][:, :, g.ci_all :]


def sort_pieces(g, parts, gates):
    n = g.nch - 1
    out = [arr((n, 9, g.rows, g.ci_all), BF), arr((n, 9, g.rows, g.cm), BF)]
    body = functools.partial(sort_kernel, g)
    ins = [VMEM] * n + [ANY] * len(gates)
    return call(body, out, ins, [*parts, *gates], [], 4, 0, 1e6, "sort_pieces")


def cut_maps_kernel(g, spec, after, out, held, sem):
    copies = Copies(sem)
    first = []
    for z in range(g.nch):
        start = static_start(g, z % g.segs) * MEL
        first.append(copies.start(spec.at[z // g.segs, :, start : start + g.win * MEL], held.at[z]))
    for z in range(g.nch):
        copies.wait(first[z])
        copies.start(held.at[z], out.at[z])
    copies.wait_all()


def cut_maps(g, spec, after):
    shape = (g.nch, g.ci, g.win * MEL)
    body = functools.partial(cut_maps_kernel, g)
    args = [in_hbm(spec), after]
    scratch = [pltpu.VMEM(shape, BF), sems(2 * g.nch)]
    return call(body, [pltpu.HBM(shape, BF)], [ANY] * 2, args, scratch, 4, 0, 2e6, "cut_maps")[0]


def static_start(g, seg):
    return min(max(seg * g.seg - HALO, 0), g.frames - g.win)


def cut_cot_kernel(g, cot, after, *rest):
    n = g.nch
    cs, sem = rest[:n], rest[n]
    z = lax.axis_index("chan")
    copies = Copies(sem)
    for k in range(n):
        to = z ^ k
        clip, seg = to // g.segs, lax.rem(to, g.segs)
        _, cstart = g_starts(g, seg)
        copies.start(cot.at[clip, :, pl.ds(aligned(cstart * 2, 128), g.cwin * 2)], cs[k])
    copies.wait_all()


def cut_cot(g, cot, after):
    n = g.nch
    out = [arr((g.co, g.cwin * 2), BF)] * n
    body = functools.partial(cut_cot_kernel, g)
    return call(body, out, [ANY] * 2, [in_hbm(cot), after], [sems(n)], 4, 0, 1e6, "cut_cotangent")


def in_hbm(x):
    return pltpu.with_memory_space_constraint(x, pltpu.HBM)


def join_kernel(g, own, *rest):
    parts, w = rest[:-1], rest[-1]
    z, d = lax.axis_index("chan"), lax.axis_index("dp")
    mine, plane = lax.rem(d, 2), lax.rem(d, g.pieces) // 2
    w[:, pl.ds(aligned(z * g.co), g.co), :] = own[...]
    for side in range(2):
        core = mine if side == 0 else 1 - mine
        for e in range(g.planes):
            row = g.row_of(core, plane ^ g.plane_of(core, e))
            for k in range(1, g.nch):
                at = aligned((z ^ k) * g.co + row)
                w[:, pl.ds(at, g.rows), :] = parts[side * g.planes + e][k - 1]


def join(g, own, parts, depth, name):
    body = functools.partial(join_kernel, g)
    args = [*keep_near(own), *parts]
    ins = [VMEM] * len(args)
    return call(body, [arr((9, g.cm, depth), BF)], ins, args, [], 8, 0, 4 * MIB, name)[0]


def convolve(v3, w, part, back, finish, carry, unrolled=False, window=None):
    def taps(t):
        b = 2 - t if back else t
        return jnp.concatenate([w[b], w[3 + b], w[6 + b]], axis=0 if back else 1)

    contract = ((1,), (0,)) if back else ((1,), (1,))
    depth = v3.shape[2]

    size = part.shape[1]
    window = pl.ds(0, size) if window is None else window

    def times(first, n, t):
        return dot(v3[pl.ds(first, n), window, :].reshape(n * size, depth), taps(t), contract)

    def rows_of(term, n):
        return [term[k * size : (k + 1) * size] for k in range(n)]

    if unrolled:
        for i in range(2):
            total = rows_of(times(4 * i, 4, 1), 4)
            side = rows_of(times(1 + 2 * i, 4, 2 - 2 * i), 4)
            edge = rows_of(times(5 * i, 3, 2 * i), 3)
            for k in range(4):
                value = total[k] + side[k]
                if 0 <= k + i - 1 < 3:
                    value = value + edge[k + i - 1]
                carry = finish(4 * i + k, value, carry)
        return carry

    def step(i, carry):
        part[pl.ds(3 * i + 1, 3)] = times(5 * i, 3, 2 * i).reshape(3, size, part.shape[2])
        part[7 * i] = jnp.zeros(part.shape[1:], F32)
        total = times(4 * i, 4, 1) + times(1 + 2 * i, 4, 2 - 2 * i)
        for k in range(4):
            m = 4 * i + k
            carry = finish(m, part[m] + total[k * size : (k + 1) * size], carry)
        return carry

    return lax.fori_loop(0, 2, step, carry)


def convolve_sums(g, here, x3, w, pre, unrolled):
    _, own = row_masks(g, here, g.cm)

    def finish(m, total, sums):
        pre[m] = total
        kept = total * own
        return sums[0] + sum_rows(kept), sums[1] + sum_rows(kept * total)

    zero = jnp.zeros((1, g.cm), F32)
    return convolve(x3, w, pre, False, finish, (zero, zero), unrolled)


def first_kernel(g, lens, gains, w, maps, pre, x3, pay):
    here = Here(g, lens)
    c = g.ci_all
    order = grid_order()
    row = lax.broadcasted_iota(jnp.int32, (MEL * 16, 128), 0) % 16

    def place_cells(j, square):
        cells = maps[:, :, 128 * j : 128 * (j + 1)].reshape(c, 128)
        frame = row + 16 * j
        valid = (frame + here.start) < here.length
        own = (frame >= here.off) & (frame < here.off + g.seg)
        block = dot(order, cells, ((1,), (1,))) * widen(valid.astype(F32), c)
        x3[:, 16 * j : 16 * (j + 1), c : 2 * c] = block.astype(BF).reshape(MEL, 16, c)
        return square + sum_rows(block * block * widen(own.astype(F32), c))

    square = jnp.zeros((1, c), F32)
    for j in range(g.win // 16):
        square = place_cells(j, square)
    for m in range(MEL):
        before, after_ = shifted(x3[m, :, c : 2 * c].astype(F32))
        x3[m, :, 0:c] = before.astype(BF)
        x3[m, :, 2 * c : 3 * c] = after_.astype(BF)

    one, two = convolve_sums(g, here, x3, w, pre, True)
    frame_total = 0
    pair_total = 0
    for i in range(g.clips):
        frame_total = frame_total + lens[i]
        pair_total = pair_total + (lens[i] + 1) // 2
    row = misc_row(
        frame_total.astype(F32), pair_total.astype(F32), jnp.sum(square, axis=1, keepdims=True)
    )
    pay[...] = payload(one, two, row, *[gains[i : i + 1] for i in range(4)])


def first(g, lens, gains, maps, w):
    body = functools.partial(first_kernel, g)
    out = [
        arr((MEL, g.win, g.cm), F32),
        arr((MEL, g.win, 3 * g.ci_all), BF),
        arr((1, 2 * g.cm + 5 * 128), F32),
    ]
    args = [lens, gains, *keep_near(w, maps)]
    ins = [SMEM] + [VMEM] * 3
    flops = 2 * 9 * MEL * g.win * g.ci_all * g.cm
    return call(body, out, ins, args, [], 10, flops, 10 * MIB, "first_conv")


MEAN1, INV1, GAMMA1, BETA1, GAMMA2, BETA2, COUNT, PAIRS, SQ0, MEAN2, INV2 = range(11)
TABLE = 16


def half_affine(mean, inverse, gamma, beta):
    scale = 0.5 * gamma * inverse
    return scale, 0.5 * beta - mean * scale


def second_kernel(g, lens, got, pre1, w, pre, x3, table, pay, misc_out):
    here = Here(g, lens)
    c = g.cm
    valid, own = row_masks(g, here, c)
    one, two, rest = total_of(g, got)
    misc = rest[:, :128]
    count = MEL * pick(misc, 0) / g.nch
    pairs = (MEL // 2) * pick(misc, 1) / g.nch
    at = [2 * c + 128 * (1 + i) for i in range(4)]
    vectors = [
        jnp.concatenate([got[zz, :, i : i + g.co] for zz in range(g.nch)], axis=1) for i in at
    ]
    mean = one / count
    inverse = lax.rsqrt(two / count - mean * mean + 1e-05)
    wide = jnp.zeros((1, c), F32)
    table[...] = jnp.concatenate(
        [mean, inverse, *vectors, wide + count, wide + pairs, wide + pick(misc, 2)]
        + [wide] * (TABLE - 9),
        axis=0,
    )
    scale, shift = half_affine(mean, inverse, vectors[0], vectors[1])


    def activate(m, square):
        half = pre1[m] * scale + shift
        act = half * (1.0 + jnp.tanh(half)) * valid
        low = act.astype(BF)
        before, after = shifted(low.astype(F32))
        side_by_side(x3, m, low, c, before, after)
        return square + sum_rows(act * act * own)

    square = jnp.zeros((1, c), F32)
    for m in range(MEL):
        square = activate(m, square)
    one, two = convolve_sums(g, here, x3, w, pre, True)
    pay[...] = payload(one, two)
    misc_out[...] = misc_row(jnp.sum(square, axis=1, keepdims=True))


def second(g, lens, got, pre1, w):
    body = functools.partial(second_kernel, g)
    out = [
        arr((MEL, g.win, g.cm), F32),
        arr((MEL, g.win, 3 * g.cm), BF),
        arr((TABLE, g.cm), F32),
        arr((1, 2 * g.cm), F32),
        arr((1, 128), F32),
    ]
    args = [lens, *keep_near(got, pre1, w)]
    flops = 2 * 9 * MEL * g.win * g.cm * g.cm
    ins = [SMEM, VMEM, VMEM, VMEM]
    return call(body, out, ins, args, [], 10, flops, 17 * MIB, "second_conv")


def pool_kernel(g, lens, got, old_ref, pre2, *rest):
    n, c = g.nch, g.cm
    cs, outs = rest[:n], rest[n : 2 * n]
    local_ref, table, pay, misc_out, held, grads, total, flat = rest[2 * n :]
    here = Here(g, lens)
    for k in range(n):
        held[pl.ds(aligned((here.z ^ k) * g.co), g.co), :] = cs[k][...]
    r = lax.broadcasted_iota(jnp.int32, (256, 128), 0)
    l = lax.broadcasted_iota(jnp.int32, (256, 128), 1)
    spread = (l == (r % 64) // 2 * 4 + r // 64).astype(BF)

    @pl.loop(0, g.cwin // 64)
    def _(j):
        cells = held[:, pl.ds(aligned(128 * j, 128), 128)]
        block = dot(spread, cells, ((1,), (1,)))
        grads[:, pl.ds(aligned(64 * j), 64), :] = block.reshape(MEL // 2, 64, c)

    one, two, _ = total_of(g, got)
    old = old_ref[...]
    count = old[COUNT : COUNT + 1]
    mean = one / count
    inverse = lax.rsqrt(two / count - mean * mean + 1e-05)
    wide = jnp.zeros((1, c), F32)
    table[...] = jnp.concatenate([old[:MEAN2], mean, inverse] + [wide] * (TABLE - 11), axis=0)
    half_gamma, half_beta = 0.5 * old[GAMMA2 : GAMMA2 + 1], 0.5 * old[BETA2 : BETA2 + 1]
    less = -mean * inverse
    side = g.win - g.seg
    segment = pl.ds(aligned(here.off), g.seg)
    sides = [
        aligned(jnp.where(16 * j < here.off, 16 * j, 16 * j + g.seg)) for j in range(side // 16)
    ]

    def weights(rows, start, width):
        frame = lax.broadcasted_iota(jnp.int32, (rows, 128), 0) + (here.start + start)
        valid = (frame < here.length).astype(F32)
        share = jnp.where(here.length - frame // 2 * 2 >= 2, 0.25, 0.5)
        return widen(0.5 * share * valid, width), widen(valid, width)

    half_share, valid = weights(g.seg, here.off, c)
    side_shares = [weights(16, start, c)[0] for start in sides]
    out_row = lax.broadcasted_iota(jnp.int32, (g.seg, 2 * g.seg), 0)
    out_cell = lax.broadcasted_iota(jnp.int32, (g.seg, 2 * g.seg), 1)
    first_cell = out_row // 2 * 4
    frame = out_row + (here.start + here.off)
    out_share = jnp.where(here.length - frame // 2 * 2 >= 2, 0.25, 0.5)
    total[...] = jnp.zeros(total.shape, F32)

    def bent(pre):
        scaled = pre * inverse + less
        half = scaled * half_gamma + half_beta
        bend = jnp.tanh(half)
        twice = 1.0 + bend
        whole = half * twice
        return scaled, whole, twice + whole * (1.0 - bend)

    def step(k, sums):
        beta_sum, gamma_sum, square = sums
        given = grads[k, pl.ds(aligned(here.qoff + here.off), g.seg), :] * half_share
        pair = None
        for i in range(2):
            m = 2 * k + i
            scaled, whole, slope = bent(pre2[m, segment, :])
            act = whole * valid
            square = square + sum_rows(act * act)
            local = given * slope
            local_ref[m, segment, :] = local
            beta_sum = beta_sum + sum_rows(local)
            gamma_sum = gamma_sum + sum_rows(local * scaled)
            pair = act if pair is None else pair + act
            for start, side_share in zip(sides, side_shares, strict=True):
                rows = pl.ds(start, 16)
                _, _, slope = bent(pre2[m, rows, :])
                given_side = grads[k, pl.ds(aligned(here.qoff + start), 16), :] * side_share
                local_ref[m, rows, :] = given_side * slope
        gather = jnp.where(out_cell == first_cell + k, out_share, 0.0).astype(BF)
        total[...] += dot(pair.astype(BF), gather, ((0,), (0,)))
        return beta_sum, gamma_sum, square

    zero = jnp.zeros((1, c), F32)
    beta_sum, gamma_sum, square = lax.fori_loop(0, MEL // 2, step, (zero, zero, zero))
    pooled = total[...]
    flat[...] = pooled.astype(BF)
    for k in range(n):
        outs[k][...] = flat[pl.ds(aligned((here.z ^ k) * g.co), g.co), :]
    pooled_square = sum_rows(jnp.sum(pooled * pooled, axis=1, keepdims=True))
    pay[...] = jnp.broadcast_to(payload(beta_sum, gamma_sum)[None], pay.shape)
    misc_out[...] = misc_row(jnp.sum(square, axis=1, keepdims=True), pooled_square)


def pool(g, lens, got, table, pre2, cs):
    n = g.nch
    body = functools.partial(pool_kernel, g)
    out = [arr((g.co, 2 * g.seg), BF)] * n + [
        arr((MEL, g.win, g.cm), F32),
        arr((TABLE, g.cm), F32),
        arr((g.ndev, 1, 2 * g.cm), F32),
        arr((1, 128), F32),
    ]
    scratch = [
        pltpu.VMEM((g.cm, g.cwin * 2), BF),
        pltpu.VMEM((MEL // 2, g.cwin, g.cm), F32),
        pltpu.VMEM((g.cm, 2 * g.seg), F32),
        pltpu.VMEM((g.cm, 2 * g.seg), BF),
    ]
    args = [lens, *keep_near(got, table, pre2, *cs)]
    ins = [SMEM] + [VMEM] * (len(args) - 1)
    out = call(body, out, ins, args, scratch, 12, 4e9, 8 * MIB, "pool")
    return out[:n], *out[n:]


def terms_kernel(g, depth, norm, lens, got, table, pre, local, x3, after, *refs):
    grad, sums, roots, terms, give = refs
    here = Here(g, lens)
    c = g.cm
    valid, _ = row_masks(g, here, c)
    beta_sum, gamma_sum, rest = total_of(g, got)
    t = table[...]
    mean, inverse, gamma = (t[i : i + 1] for i in norm)
    count = t[COUNT : COUNT + 1]
    sums[...] = jnp.concatenate([beta_sum, gamma_sum] + [jnp.zeros((1, c), F32)] * 6, axis=0)
    if rest.shape[1]:
        second, third = rest[:, :128], rest[:, 128:]
        tops = misc_row(
            pick(t[SQ0 : SQ0 + 1, :128], 0), pick(second, 0), pick(third, 0), pick(third, 1)
        )
        lane = lax.broadcasted_iota(jnp.int32, (1, 128), 1)
        cells, pairs = count[:, :128], t[PAIRS : PAIRS + 1, :128]
        under = jnp.where(lane == 0, cells * g.ci_all, jnp.where(lane == 3, pairs * c, cells * c))
        roots[...] = jnp.broadcast_to(jnp.sqrt(tops / under), (8, 128))
    factor = gamma * inverse
    slope = factor * inverse * gamma_sum / count
    level = factor * beta_sum / count - mean * slope

    @pl.loop(0, MEL)
    def _(m):
        value = valid * (local[m] * factor - pre[m] * slope - level)
        grad[m] = value.astype(BF)

    segment = pl.ds(aligned(here.off), g.seg)

    @pl.loop(0, 3)
    def _(a):
        lanes_of = pl.ds(aligned(a * depth, 128), depth)
        for b in (1, 0, 2):
            low = max(0, 1 - b)
            high = min(MEL, MEL + 1 - b)
            rows = (high - low) * g.seg
            left = grad[low:high, segment, :].reshape(rows, c)
            right = x3[low + b - 1 : high + b - 1, segment, lanes_of].reshape(rows, depth)
            term = dot(left, right, ((0,), (0,))).astype(BF)
            for z in range(g.nch):
                for s in range(2):
                    for p in range(g.planes):
                        at = z * g.co + g.row_of(s, p)
                        terms[s, z, p, 3 * a + b] = term[at : at + g.rows]

    give[...] = terms[1 - here.core]


def terms_of(g, lens, got, table, pre, local, x3, after, depth, norm, name):
    body = functools.partial(terms_kernel, g, depth, norm)
    shape = (g.nch, g.planes, 9, g.rows, depth)
    out = [
        arr((MEL, g.win, g.cm), BF),
        arr((8, g.cm), F32),
        arr((8, 128), F32),
        arr((2, *shape), BF),
        arr(shape, BF),
    ]
    args = [lens, *keep_near(got, table, pre, local, x3), after]
    ins = [SMEM] + [VMEM] * 5 + [ANY]
    flops = 2 * 9 * MEL * g.win * g.cm * depth
    return call(body, out, ins, args, [], 10, flops, 15 * MIB, name)


def back_kernel(g, lens, table, grad, pre1, w, misc2, misc3, after, local1, pay, g3):
    here = Here(g, lens)
    c = g.cm
    valid, own = row_masks(g, here, c)
    t = table[...]

    def row(i):
        return t[i : i + 1]


    for m in range(MEL):
        low = grad[m]
        before, after = shifted(low.astype(F32))
        side_by_side(g3, m, low, c, after, before)

    inverse, less = row(INV1), -row(MEAN1) * row(INV1)
    half_gamma, half_beta = 0.5 * row(GAMMA1), 0.5 * row(BETA1)
    half_valid = 0.5 * valid

    def finish(m, given, sums):
        scaled = pre1[m] * inverse + less
        half = scaled * half_gamma + half_beta
        bend = jnp.tanh(half)
        twice = 1.0 + bend
        local = given * half_valid * (twice + half * twice * (1.0 - bend))
        local1[m] = local
        kept = local * own
        return sums[0] + sum_rows(kept), sums[1] + sum_rows(kept * scaled)

    zero = jnp.zeros((1, c), F32)
    beta_sum, gamma_sum = convolve(g3, w, local1, True, finish, (zero, zero), True)
    pay[...] = payload(beta_sum, gamma_sum, misc2[...], misc3[...])


def back(g, lens, table, grad, pre1, w, misc2, misc3, after):
    body = functools.partial(back_kernel, g)
    out = [arr((MEL, g.win, g.cm), F32), arr((1, 2 * g.cm + 2 * 128), F32)]
    scratch = [pltpu.VMEM((MEL, g.win, 3 * g.cm), BF)]
    args = [lens, *keep_near(table, grad, pre1, w, misc2, misc3), after]
    flops = 2 * 9 * MEL * g.win * g.cm * g.cm
    ins = [SMEM] + [VMEM] * 6 + [ANY]
    return call(body, out, ins, args, scratch, 14, flops, 20 * MIB, "second_back")


def release_kernel(*refs):
    pass


def release_far(gates, x):
    n = len(gates)
    return pl.pallas_call(
        release_kernel,
        out_shape=pltpu.HBM(x.shape, x.dtype),
        in_specs=[ANY] * (n + 1),
        out_specs=ANY,
        input_output_aliases={n: 0},
        compiler_params=pltpu.CompilerParams(vmem_limit_bytes=2 * MIB),
        name="release_far",
    )(*gates, in_hbm(x))


def release(gates, arrays):
    out = [arr(x.shape, x.dtype) for x in arrays]
    n = len(gates)
    ins = [ANY] * n + [VMEM] * len(arrays)
    aliases = {i + n: i for i in range(len(arrays))}
    args = [*gates, *keep_near(*arrays)]
    return call(release_kernel, out, ins, args, [], 2, 0, 1, "release", aliases)


def spectra_kernel(g, lens, grad, after, w, *rest):
    n, c = g.nch, g.cm
    outs, (g3, rows, flat, part) = rest[:n], rest[n:]
    here = Here(g, lens)

    @pl.loop(0, MEL)
    def _(m):
        low = grad[m]
        before, after_ = shifted(low.astype(F32))
        side_by_side(g3, m, low, c, after_, before)

    r = lax.broadcasted_iota(jnp.int32, (g.seg, 128), 0) + here.off + here.start
    valid = widen((r < here.length).astype(F32), g.ci_all)

    def finish(m, total, carry):
        rows[m] = (total * valid).astype(BF)
        return carry

    convolve(g3, w, part, True, finish, 0, False, pl.ds(aligned(here.off), g.seg))
    order = grid_order()

    for j in range(g.seg // 16):
        block = rows[:, 16 * j : 16 * (j + 1), :].reshape(MEL * 16, g.ci_all)
        flat[:, 128 * j : 128 * (j + 1)] = dot(block, order, ((0,), (0,))).astype(BF)

    for k in range(n):
        outs[k][...] = flat[pl.ds(aligned((here.z ^ k) * g.ci), g.ci), :]


def spectra_back(g, lens, grad, after, w):
    n = g.nch
    body = functools.partial(spectra_kernel, g)
    out = [arr((g.ci, g.seg * MEL), BF)] * n
    scratch = [
        pltpu.VMEM((MEL, g.win, 3 * g.cm), BF),
        pltpu.VMEM((MEL, g.seg, g.ci_all), BF),
        pltpu.VMEM((g.ci_all, g.seg * MEL), BF),
        pltpu.VMEM((MEL, g.seg, g.ci_all), F32),
    ]
    grad, w = keep_near(grad, w)
    args = [lens, grad, after, w]
    flops = 2 * 9 * MEL * g.win * g.cm * g.ci_all
    ins = [SMEM, VMEM, ANY, VMEM]
    return call(body, out, ins, args, scratch, 14, flops, 5 * MIB, "spectra_back")


def place_kernel(g, width, *rest):
    n = g.nch
    parts, out, done = rest[:n], rest[n], rest[n + 1]
    z = lax.axis_index("chan")
    done[...] = jnp.zeros(done.shape, F32)
    for k in range(n):
        source = z ^ k
        for zz in range(n):

            @pl.when(source == zz)
            def _():
                at = zz % g.segs * width
                out[zz // g.segs, :, at : at + width] = parts[k][...].astype(out.dtype)


def place(g, parts, dtype, name):
    channels, width = parts[0].shape
    return pl.pallas_call(
        functools.partial(place_kernel, g, width),
        out_shape=[
            jax.ShapeDtypeStruct((g.clips, channels, g.segs * width), dtype),
            jax.ShapeDtypeStruct((8, 128), F32),
        ],
        in_specs=[VMEM] * g.nch,
        out_specs=[VMEM] * 2,
        compiler_params=pltpu.CompilerParams(vmem_limit_bytes=8 * MIB),
        cost_estimate=TINY,
        name=name,
    )(*parts)


def core_sum_kernel(g, terms, got, after, stay, go):
    d, z = lax.axis_index("dp"), lax.axis_index("chan")
    core, plane = lax.rem(d, 2), lax.rem(d, g.pieces) // 2
    half = g.planes // 2
    for e in range(g.planes):
        at = plane ^ g.plane_of(core, e)
        for k in range(g.nch):
            source = z ^ g.zed_of(k)
            value = terms[core, source, at].astype(F32) + got[source, at].astype(F32)
            to = stay if e < half else go
            to[(e % half) * g.nch + k] = value.astype(BF)


def core_sum(g, terms, got, after, name):
    shape = (g.planes // 2 * g.nch, *got.shape[2:])
    return pl.pallas_call(
        functools.partial(core_sum_kernel, g),
        out_shape=[pltpu.VMEM(shape, BF)] * 2,
        in_specs=[VMEM, VMEM, ANY],
        out_specs=[VMEM] * 2,
        compiler_params=pltpu.CompilerParams(vmem_limit_bytes=16 * MIB),
        name=name,
    )(keep_near(terms)[0], got, after)


def quarter_kernel(g, terms, got, *outs):
    d, z = lax.axis_index("dp"), lax.axis_index("chan")
    core, plane = lax.rem(d, 2), lax.rem(d, g.pieces) // 2
    for e in range(g.planes):
        at = plane ^ g.plane_of(core, e)
        for k in range(g.nch):
            source = z ^ g.zed_of(k)
            value = terms[core, source, at].astype(F32) + got[source, at].astype(F32)
            outs[e][k] = value.astype(BF)


def quarters(g, terms, got, name):
    shape = (g.nch, *got.shape[2:])
    return pl.pallas_call(
        functools.partial(quarter_kernel, g),
        out_shape=[pltpu.VMEM(shape, BF)] * g.planes,
        in_specs=[VMEM, VMEM],
        out_specs=[VMEM] * g.planes,
        compiler_params=pltpu.CompilerParams(vmem_limit_bytes=16 * MIB),
        name=name,
    )(keep_near(terms)[0], got)


def add_kernel(n, halves, *rest):
    first = rest[0]
    outs = rest[len(rest) - halves :]
    count = first.shape[0] // halves
    for i in range(first.shape[0]):
        total = first[i].astype(F32)
        for r in rest[1:n]:
            total = total + r[i].astype(F32)
        outs[i // count][i % count] = total.astype(BF)


def add_up(parts, halves, gates, name):
    n = len(parts)
    shape = (parts[0].shape[0] // halves, *parts[0].shape[1:])
    return pl.pallas_call(
        functools.partial(add_kernel, n, halves),
        out_shape=[pltpu.VMEM(shape, BF)] * halves,
        in_specs=[VMEM] * n + [ANY] * len(gates),
        out_specs=[VMEM] * halves,
        compiler_params=pltpu.CompilerParams(vmem_limit_bytes=8 * MIB),
        name=name,
    )(*parts, *gates)


def halve_kernel(stay, got, *rest):
    n = stay.shape[0]
    outs = rest[-2:] if n > 1 else rest[-1:]
    for i in range(n):
        value = stay[i].astype(F32) + got[i].astype(F32)
        if n == 1:
            outs[0][...] = value.astype(BF)
        else:
            outs[i // (n // 2)][i % (n // 2)] = value.astype(BF)


def halve(stay, got, gates, name):
    n = stay.shape[0]
    if n == 1:
        out = [jax.ShapeDtypeStruct(stay.shape[1:], BF)]
    else:
        out = [jax.ShapeDtypeStruct((n // 2, *stay.shape[1:]), BF)] * 2
    return pl.pallas_call(
        halve_kernel,
        out_shape=out,
        in_specs=[VMEM, VMEM] + [ANY] * len(gates),
        out_specs=[VMEM] * len(out),
        compiler_params=pltpu.CompilerParams(vmem_limit_bytes=8 * MIB),
        name=name,
    )(stay, got, *gates)


def spread_kernel(g, mine, other, out, done):
    done[...] = jnp.zeros(done.shape, F32)
    d = lax.axis_index("dp")
    core, plane = lax.rem(d, 2), lax.rem(d, g.pieces) // 2
    for side, part in enumerate((mine, other)):
        c = core if side == 0 else 1 - core
        for e in range(g.planes):
            at = aligned(g.row_of(c, plane ^ g.plane_of(c, e)))
            out[:, pl.ds(at, g.rows), :] = part[e].astype(F32)


def spread_out(g, mine, other, depth, name):
    return pl.pallas_call(
        functools.partial(spread_kernel, g),
        out_shape=[
            jax.ShapeDtypeStruct((9, g.co, depth), F32),
            jax.ShapeDtypeStruct((8, 128), F32),
        ],
        in_specs=[VMEM] * 2,
        out_specs=[VMEM] * 2,
        compiler_params=pltpu.CompilerParams(vmem_limit_bytes=12 * MIB),
        name=name,
    )(mine, other)


def stack_kernel(n, *refs):
    for k, r in enumerate(refs[:n]):
        refs[-1][k] = r[...]


def stack(parts, gates, name):
    n = len(parts)
    out = [arr((n, *parts[0].shape), parts[0].dtype)]
    ins = [VMEM] * n + [ANY] * len(gates)
    body = functools.partial(stack_kernel, n)
    return call(body, out, ins, [*parts, *gates], [], 6, 0, 1e6, name)[0]


class Links:
    def __init__(self, g):
        self.g = g

    def core(self, x):
        return lax.ppermute(x, "dp", [(i, i ^ 1) for i in range(self.g.ndp)])

    def dp(self, x, bit):
        return lax.ppermute(x, "dp", [(i, i ^ bit) for i in range(self.g.ndp)])

    def plane(self, x, turn):
        g = self.g
        return lax.ppermute(x, "dp", [(i, i ^ (2 * g.mask(i & 1, turn))) for i in range(g.ndp)])

    def chan(self, x, k):
        return lax.ppermute(x, "chan", [(i, i ^ k) for i in range(self.g.nch)])

    def exchange(self, parts):
        return [parts[0]] + [self.chan(parts[k], k) for k in range(1, self.g.nch)]

    def gather_planes(self, x, gates=()):
        have = [x]
        for turn in reversed(range(self.g.turns)):
            more = [self.plane(h, turn) for h in have[:1]]
            rest = have[1:]
            if gates and turn == 0 and rest:
                rest = release([*gates, *more], rest)
            have = have + more + [self.plane(h, turn) for h in rest]
        return have

    def gather_cores(self, have):
        return [*have, *[self.core(h) for h in have]]

    def gather_direct(self, x):
        g = self.g
        pairs = [[(i, i ^ (2 * g.plane_of(i & 1, e))) for i in range(g.ndp)] for e in range(g.planes)]
        return [x] + [lax.ppermute(x, "dp", p) for p in pairs[1:]]


def everyone(x):
    return lax.all_to_all(x, ("dp", "chan"), 0, 0)


def make_body(ndp, nch):
    def body(
        spectra, lengths, weight_in, gamma_in, beta_in, weight_mid, gamma_mid, beta_mid, cotangent
    ):
        g = Geometry(
            ndp,
            nch,
            spectra.shape[0],
            spectra.shape[2] // MEL,
            weight_in.shape[2],
            weight_mid.shape[2],
        )
        links = Links(g)
        gains = jnp.stack([gamma_in, beta_in, gamma_mid, beta_mid])
        gains = jnp.pad(gains, ((0, 0), (0, 128 - g.co)))

        piece = cut_weights(g, weight_in, weight_mid)
        cells = cut_maps(g, spectra, piece)
        cots = cut_cot(g, cotangent, cells)
        pieces_in, pieces_mid = sort_pieces(
            g, [links.chan(piece, k) for k in range(1, nch)], [cots[0]]
        )
        maps = lax.all_to_all(release_far([pieces_in], cells), "chan", 0, 0)
        planes_in = links.gather_planes(pieces_in)
        w_in = join(g, weight_in, links.gather_cores(planes_in), g.ci_all, "join_in")
        planes_mid = links.gather_planes(pieces_mid, [maps])

        pre1, x3_in, pay = first(g, lengths, gains, maps, w_in)
        got = everyone(fan(g, pay, cots[0], *planes_mid[1:]))
        planes_mid = release([got], planes_mid)
        w_mid = join(g, weight_mid, links.gather_cores(planes_mid), g.cm, "join_mid")
        cs = links.exchange(release([got], cots))
        pre2, x3_mid, table, pay, misc2 = second(g, lengths, got, pre1, w_mid)
        got = everyone(fan(g, pay, *cs[1:]))
        pooled, local2, table, pay, misc3 = pool(g, lengths, got, table, pre2, cs)
        got = everyone(pay)
        pooled = links.exchange(release([got], pooled))
        grad2, sums2, _, terms_mid, give_mid = terms_of(
            g, lengths, got, table, pre2, local2, x3_mid, got, g.cm, (MEAN2, INV2, GAMMA2), "weight_mid_terms"
        )
        got_mid = links.core(give_mid)
        split = g.turns == 2
        if split:
            stay_a, stay_b, go_a, go_b = quarters(g, terms_mid, got_mid, "mid_core_sum")
            got_b = links.plane(go_b, 0)
        else:
            stay_mid, go_b = core_sum(g, terms_mid, got_mid, got_mid, "mid_core_sum")
            got_b = go_b
        local1, pay = back(g, lengths, table, grad2, pre1, w_mid, misc2, misc3, go_b)
        got = everyone(fan(g, pay, got_b, *pooled[1:]))
        block_out, pooled_done = place(g, pooled, BF, "place_pooled")
        if split:
            (go_1,) = add_up([stay_b, got_b], 1, [pay, *pooled[1:]], "mid_sum_b")
            got_1 = early = links.plane(go_1, 1)
            got_a = links.plane(release([got], [go_a])[0], 0)
        else:
            (go_mid,) = release([got], [go_b])
            early = got
        grad1, sums1, roots, terms_in, give_in = terms_of(
            g, lengths, got, table, pre1, local1, x3_in, early, g.ci_all, (MEAN1, INV1, GAMMA1), "weight_in_terms"
        )
        got_in = links.core(give_in)

        class Chain:
            def __init__(self, stay, go, depth, name):
                self.stay, self.go, self.depth, self.name = stay, go, depth, name
                self.turns = [functools.partial(links.plane, turn=t) for t in range(g.turns)]
                self.turns += [functools.partial(links.chan, k=1 << t) for t in range(g.zturns)]

            def turn(self, i, *gates):
                got = self.turns[i](self.go)
                done = halve(self.stay, got, gates, f"{self.name}_sum_{i}")
                self.stay, self.go = done if len(done) == 2 else (done[0], None)
                return self.stay

            def rest(self):
                bit = g.pieces
                while bit < ndp:
                    got = links.dp(self.stay, bit)
                    self.stay = halve(self.stay[None], got[None], [], self.name + "_rest")[0]
                    bit *= 2

            def out(self, planes, *gates):
                mine = stack(planes, gates, self.name + "_stack")
                return spread_out(g, mine, links.core(mine), self.depth, self.name + "_out")

        turns = g.turns + g.zturns
        parts = spectra_back(g, lengths, grad1, grad1, w_in)
        stay_in, go_in = core_sum(g, terms_in, got_in, parts[0], "in_core_sum")
        inner = Chain(stay_in, go_in, g.ci_all, "in")
        parts = links.exchange(parts)
        spectra_grad, spectra_done = place(g, parts, F32, "place_spectra")
        if split:
            halves = add_up([stay_a, got_a, got_1], 2, [stay_in], "mid_sum_1")
            mid = Chain(*halves, g.cm, "mid")
        else:
            mid = Chain(stay_mid, go_mid, g.cm, "mid")
            for i in range(g.turns):
                mid.turn(i, stay_in)
        gates = [parts[2 : nch - 1], [pooled_done]]
        at = mid.stay
        for i in range(g.turns):
            at = inner.turn(i, at, *(gates[i] if i < 2 else []))
            if i == 0:
                at = mid.turn(g.turns, at)
        for i in range(g.turns, turns):
            at = inner.turn(i, at, *(parts[nch - 1 :] if i == g.turns else []))
            if i + 1 < turns:
                at = mid.turn(i + 1, at)
        inner.rest()
        mid.rest()
        planes_in = links.gather_planes(inner.stay)
        weight_mid_grad, mid_done = mid.out(links.gather_direct(mid.stay), *planes_in[1:3], parts[1])
        weight_in_grad, _ = inner.out(planes_in, mid_done, spectra_done)
        z = lax.axis_index("chan")

        def share(sums, i):
            return lax.dynamic_slice_in_dim(sums[i], z * g.co, g.co)

        return (
            block_out,
            spectra_grad,
            weight_in_grad,
            share(sums1, 1),
            share(sums1, 0),
            weight_mid_grad,
            share(sums2, 1),
            share(sums2, 0),
            roots[0, :4],
        )

    return body


def solution(mesh):
    placed = (
        P("dp", "chan", None),
        P("dp"),
        P(None, "chan", None),
        P("chan"),
        P("chan"),
        P(None, "chan", None),
        P("chan"),
        P("chan"),
        P("dp", "chan", None),
    )
    return jax.shard_map(
        make_body(mesh.shape["dp"], mesh.shape["chan"]),
        mesh=mesh,
        in_specs=placed,
        out_specs=(
            P("dp", "chan", None),
            P("dp", "chan", None),
            P(None, "chan", None),
            P("chan"),
            P("chan"),
            P(None, "chan", None),
            P("chan"),
            P("chan"),
            P(),
        ),
        check_vma=False,
    )
```

```python
import functools

import jax
import jax.numpy as jnp
from jax import lax
from jax.experimental import pallas as pl
from jax.experimental.pallas import tpu as pltpu
from jax.sharding import PartitionSpec as P

MEL = 8
HALO = 16
BF = jnp.bfloat16
F32 = jnp.float32
MIB = 1024 * 1024
TINY = pl.CostEstimate(flops=1, bytes_accessed=1, transcendentals=0)

VMEM = pl.BlockSpec(memory_space=pltpu.VMEM)
SMEM = pl.BlockSpec(memory_space=pltpu.SMEM)
ANY = pl.BlockSpec(memory_space=pl.ANY)
HBM = pl.BlockSpec(memory_space=pltpu.HBM)


def bits_of(n):
    return n.bit_length() - 1


class Geometry:
    def __init__(self, ndp, nch, clips, frames, c_in, c_mid):
        self.ndp, self.nch, self.ndev = ndp, nch, ndp * nch
        self.clips, self.frames = clips, frames
        self.ci_all, self.cm = c_in, c_mid
        self.ci, self.co = c_in // nch, c_mid // nch
        self.segs = nch // clips
        self.seg = frames // self.segs
        self.win = self.seg + HALO * min(self.segs - 1, 2)
        starts = [min(max(s * self.seg - HALO, 0), frames - self.win) for s in range(self.segs)]
        self.cwin = min(frames, (self.win + 48 + 63) // 64 * 64)
        assert all(min(s // 64 * 64, frames - self.cwin) + self.cwin >= s + self.win for s in starts)
        self.rows = max(16, self.co // ndp)
        self.pieces = self.co // self.rows
        self.planes = self.pieces // 2
        self.turns = bits_of(self.planes)
        self.zturns = bits_of(nch)

    def mask(self, core, turn):
        low, high = 1 << turn, 1 << (self.turns - 1 - turn)
        return low + core * (high - low)

    def plane_of(self, core, e):
        rel = 0
        for t in range(self.turns):
            if (e >> (self.turns - 1 - t)) & 1:
                rel = rel ^ self.mask(core, t)
        return rel

    def row_of(self, core, plane):
        return core * (self.co // 2) + plane * self.rows

    def zed_of(self, e):
        return sum(1 << t for t in range(self.zturns) if (e >> (self.zturns - 1 - t)) & 1)


class Here:
    def __init__(self, g, lens):
        self.z = lax.axis_index("chan")
        self.d = lax.axis_index("dp")
        self.core = lax.rem(self.d, 2)
        self.plane = lax.rem(self.d, g.pieces) // 2
        clip, seg = self.z // g.segs, lax.rem(self.z, g.segs)
        self.length = lens[clip]
        self.start, self.cstart = g_starts(g, seg)
        self.off = seg * g.seg - self.start
        self.qoff = self.start - self.cstart


def g_starts(g, seg):
    start = jnp.clip(seg * g.seg - HALO, 0, g.frames - g.win)
    return start, jnp.minimum(start // 64 * 64, g.frames - g.cwin)


def aligned(x, n=16):
    return pl.multiple_of(x, n)


def dot(a, b, contract):
    return lax.dot_general(a, b, ((contract[0], contract[1]), ((), ())), preferred_element_type=F32)


def call(body, out, ins, args, scratch, limit, flops, nbytes, name, aliases=None):
    return pl.pallas_call(
        body,
        out_shape=[pltpu.VMEM(o.shape, o.dtype) if isinstance(o, jax.ShapeDtypeStruct) else o for o in out],
        in_specs=ins,
        out_specs=[VMEM if isinstance(o, jax.ShapeDtypeStruct) else ANY for o in out],
        scratch_shapes=scratch,
        input_output_aliases=aliases or {},
        compiler_params=pltpu.CompilerParams(vmem_limit_bytes=limit * MIB),
        cost_estimate=pl.CostEstimate(
            flops=int(flops), bytes_accessed=int(nbytes), transcendentals=0
        ),
        name=name,
    )(*args)


def arr(shape, dtype):
    return jax.ShapeDtypeStruct(shape, dtype)


def keep_near(*xs):
    return [pltpu.with_memory_space_constraint(x, pltpu.VMEM) for x in xs]


class Copies:
    def __init__(self, sems):
        self.sems, self.n, self.open = sems, 0, []

    def start(self, src, dst):
        c = pltpu.make_async_copy(src, dst, self.sems.at[self.n])
        self.n += 1
        c.start()
        self.open.append(c)
        return c

    def wait(self, c):
        self.open = [o for o in self.open if o is not c]
        c.wait()

    def wait_all(self, some=None):
        for c in list(self.open if some is None else some):
            self.wait(c)


def sems(n):
    return pltpu.SemaphoreType.DMA((n,))


def row_masks(g, here, width):
    r = lax.broadcasted_iota(jnp.int32, (g.win, 128), 0)
    valid = (r + here.start) < here.length
    own = valid & (r >= here.off) & (r < here.off + g.seg)
    return widen(valid.astype(F32), width), widen(own.astype(F32), width)


def widen(x, width):
    return jnp.concatenate([x] * (width // 128), axis=1)


def shifted(x):
    n = x.shape[0]
    r = lax.broadcasted_iota(jnp.int32, (8, 1), 0)
    before, after = pltpu.roll(x, 1, 0), pltpu.roll(x, n - 1, 0)
    before = jnp.concatenate([jnp.where(r == 0, 0.0, before[:8]), before[8:]], axis=0)
    after = jnp.concatenate([after[:-8], jnp.where(r == 7, 0.0, after[-8:])], axis=0)
    return before, after


def grid_order(rows=16):
    n = MEL * rows
    r = lax.broadcasted_iota(jnp.int32, (n, n), 0)
    c = lax.broadcasted_iota(jnp.int32, (n, n), 1)
    return (c == (r % rows) * MEL + r // rows).astype(BF)


def misc_row(*scalars):
    lane = lax.broadcasted_iota(jnp.int32, (1, 128), 1)
    row = jnp.zeros((1, 128), F32)
    for i, s in enumerate(scalars):
        row = jnp.where(lane == i, s, row)
    return row


def pick(row, i):
    lane = lax.broadcasted_iota(jnp.int32, (1, 128), 1)
    return jnp.sum(jnp.where(lane == i, row, 0.0), axis=1, keepdims=True)


def sum_rows(x):
    return jnp.sum(x, axis=0, keepdims=True)


def payload(*parts):
    return jnp.concatenate(parts, axis=1)


def fan_kernel(pay, *rest):
    out = rest[-1]
    out[...] = jnp.broadcast_to(pay[...][None], out.shape)


def fan(g, pay, *after):
    out = [arr((g.ndev, *pay.shape), F32)]
    ins = [VMEM] + [ANY] * len(after)
    return call(fan_kernel, out, ins, [pay, *after], [], 4, 0, 1e5, "fan")[0]


def total_of(g, ref):
    row = jnp.sum(ref[...], axis=0)
    return row[:, : g.cm], row[:, g.cm : 2 * g.cm], row[:, 2 * g.cm :]


def side_by_side(x3, m, low, c, first, last):
    x3[m, :, 0:c] = first.astype(BF)
    x3[m, :, c : 2 * c] = low
    x3[m, :, 2 * c : 3 * c] = last.astype(BF)


def cut_weights_kernel(g, w_in, w_mid, out, sem):
    d = lax.axis_index("dp")
    core, plane = lax.rem(d, 2), lax.rem(d, g.pieces) // 2
    rows = pl.ds(aligned(g.row_of(core, plane)), g.rows)
    copies = Copies(sem)
    copies.start(w_in.at[:, rows, :], out.at[:, :, : g.ci_all])
    copies.start(w_mid.at[:, rows, :], out.at[:, :, g.ci_all :])
    copies.wait_all()


def cut_weights(g, w_in, w_mid):
    out = [arr((9, g.rows, g.ci_all + g.cm), BF)]
    args = [in_hbm(w_in), in_hbm(w_mid)]
    body = functools.partial(cut_weights_kernel, g)
    return call(body, out, [ANY] * 2, args, [sems(2)], 4, 0, 4e5, "cut_weights")[0]


def sort_kernel(g, *rest):
    n = g.nch - 1
    parts, first, second = rest[:n], rest[-2], rest[-1]
    for k in range(n):
        first[k] = parts[k][:, :, : g.ci_all]
        second[k] = parts[k][:, :, g.ci_all :]


def sort_pieces(g, parts, gates):
    n = g.nch - 1
    out = [arr((n, 9, g.rows, g.ci_all), BF), arr((n, 9, g.rows, g.cm), BF)]
    body = functools.partial(sort_kernel, g)
    ins = [VMEM] * n + [ANY] * len(gates)
    return call(body, out, ins, [*parts, *gates], [], 4, 0, 1e6, "sort_pieces")


def cut_maps_kernel(g, spec, after, out, held, sem):
    copies = Copies(sem)
    first = []
    for z in range(g.nch):
        start = static_start(g, z % g.segs) * MEL
        first.append(copies.start(spec.at[z // g.segs, :, start : start + g.win * MEL], held.at[z]))
    for z in range(g.nch):
        copies.wait(first[z])
        copies.start(held.at[z], out.at[z])
    copies.wait_all()


def cut_maps(g, spec, after):
    shape = (g.nch, g.ci, g.win * MEL)
    body = functools.partial(cut_maps_kernel, g)
    args = [in_hbm(spec), after]
    scratch = [pltpu.VMEM(shape, BF), sems(2 * g.nch)]
    return call(body, [pltpu.HBM(shape, BF)], [ANY] * 2, args, scratch, 4, 0, 2e6, "cut_maps")[0]


def static_start(g, seg):
    return min(max(seg * g.seg - HALO, 0), g.frames - g.win)


def cut_cot_kernel(g, cot, after, *rest):
    n = g.nch
    cs, sem = rest[:n], rest[n]
    z = lax.axis_index("chan")
    copies = Copies(sem)
    for k in range(n):
        to = z ^ k
        clip, seg = to // g.segs, lax.rem(to, g.segs)
        _, cstart = g_starts(g, seg)
        copies.start(cot.at[clip, :, pl.ds(aligned(cstart * 2, 128), g.cwin * 2)], cs[k])
    copies.wait_all()


def cut_cot(g, cot, after):
    n = g.nch
    out = [arr((g.co, g.cwin * 2), BF)] * n
    body = functools.partial(cut_cot_kernel, g)
    return call(body, out, [ANY] * 2, [in_hbm(cot), after], [sems(n)], 4, 0, 1e6, "cut_cotangent")


def in_hbm(x):
    return pltpu.with_memory_space_constraint(x, pltpu.HBM)


def join_kernel(g, own, *rest):
    parts, w = rest[:-1], rest[-1]
    z, d = lax.axis_index("chan"), lax.axis_index("dp")
    mine, plane = lax.rem(d, 2), lax.rem(d, g.pieces) // 2
    w[:, pl.ds(aligned(z * g.co), g.co), :] = own[...]
    for side in range(2):
        core = mine if side == 0 else 1 - mine
        for e in range(g.planes):
            row = g.row_of(core, plane ^ g.plane_of(core, e))
            for k in range(1, g.nch):
                at = aligned((z ^ k) * g.co + row)
                w[:, pl.ds(at, g.rows), :] = parts[side * g.planes + e][k - 1]


def join(g, own, parts, depth, name):
    body = functools.partial(join_kernel, g)
    args = [*keep_near(own), *parts]
    ins = [VMEM] * len(args)
    return call(body, [arr((9, g.cm, depth), BF)], ins, args, [], 8, 0, 4 * MIB, name)[0]


def convolve(v3, w, part, back, finish, carry, unrolled=False, window=None):
    def taps(t):
        b = 2 - t if back else t
        return jnp.concatenate([w[b], w[3 + b], w[6 + b]], axis=0 if back else 1)

    contract = ((1,), (0,)) if back else ((1,), (1,))
    depth = v3.shape[2]

    size = part.shape[1]
    window = pl.ds(0, size) if window is None else window

    def times(first, n, t):
        return dot(v3[pl.ds(first, n), window, :].reshape(n * size, depth), taps(t), contract)

    def rows_of(term, n):
        return [term[k * size : (k + 1) * size] for k in range(n)]

    if unrolled:
        for i in range(2):
            total = rows_of(times(4 * i, 4, 1), 4)
            side = rows_of(times(1 + 2 * i, 4, 2 - 2 * i), 4)
            edge = rows_of(times(5 * i, 3, 2 * i), 3)
            for k in range(4):
                value = total[k] + side[k]
                if 0 <= k + i - 1 < 3:
                    value = value + edge[k + i - 1]
                carry = finish(4 * i + k, value, carry)
        return carry

    def step(i, carry):
        part[pl.ds(3 * i + 1, 3)] = times(5 * i, 3, 2 * i).reshape(3, size, part.shape[2])
        part[7 * i] = jnp.zeros(part.shape[1:], F32)
        total = times(4 * i, 4, 1) + times(1 + 2 * i, 4, 2 - 2 * i)
        for k in range(4):
            m = 4 * i + k
            carry = finish(m, part[m] + total[k * size : (k + 1) * size], carry)
        return carry

    return lax.fori_loop(0, 2, step, carry)


def convolve_sums(g, here, x3, w, pre, unrolled):
    _, own = row_masks(g, here, g.cm)

    def finish(m, total, sums):
        pre[m] = total
        kept = total * own
        return sums[0] + sum_rows(kept), sums[1] + sum_rows(kept * total)

    zero = jnp.zeros((1, g.cm), F32)
    return convolve(x3, w, pre, False, finish, (zero, zero), unrolled)


def first_kernel(g, lens, gains, w, maps, pre, x3, pay):
    here = Here(g, lens)
    c = g.ci_all
    order = grid_order()
    row = lax.broadcasted_iota(jnp.int32, (MEL * 16, 128), 0) % 16

    def place_cells(j, square):
        cells = maps[:, :, 128 * j : 128 * (j + 1)].reshape(c, 128)
        frame = row + 16 * j
        valid = (frame + here.start) < here.length
        own = (frame >= here.off) & (frame < here.off + g.seg)
        block = dot(order, cells, ((1,), (1,))) * widen(valid.astype(F32), c)
        x3[:, 16 * j : 16 * (j + 1), c : 2 * c] = block.astype(BF).reshape(MEL, 16, c)
        return square + sum_rows(block * block * widen(own.astype(F32), c))

    square = jnp.zeros((1, c), F32)
    for j in range(g.win // 16):
        square = place_cells(j, square)
    for m in range(MEL):
        before, after_ = shifted(x3[m, :, c : 2 * c].astype(F32))
        x3[m, :, 0:c] = before.astype(BF)
        x3[m, :, 2 * c : 3 * c] = after_.astype(BF)

    one, two = convolve_sums(g, here, x3, w, pre, True)
    frame_total = 0
    pair_total = 0
    for i in range(g.clips):
        frame_total = frame_total + lens[i]
        pair_total = pair_total + (lens[i] + 1) // 2
    row = misc_row(
        frame_total.astype(F32), pair_total.astype(F32), jnp.sum(square, axis=1, keepdims=True)
    )
    pay[...] = payload(one, two, row, *[gains[i : i + 1] for i in range(4)])


def first(g, lens, gains, maps, w):
    body = functools.partial(first_kernel, g)
    out = [
        arr((MEL, g.win, g.cm), F32),
        arr((MEL, g.win, 3 * g.ci_all), BF),
        arr((1, 2 * g.cm + 5 * 128), F32),
    ]
    args = [lens, gains, *keep_near(w, maps)]
    ins = [SMEM] + [VMEM] * 3
    flops = 2 * 9 * MEL * g.win * g.ci_all * g.cm
    return call(body, out, ins, args, [], 10, flops, 10 * MIB, "first_conv")


MEAN1, INV1, GAMMA1, BETA1, GAMMA2, BETA2, COUNT, PAIRS, SQ0, MEAN2, INV2 = range(11)
TABLE = 16


def half_affine(mean, inverse, gamma, beta):
    scale = 0.5 * gamma * inverse
    return scale, 0.5 * beta - mean * scale


def second_kernel(g, lens, got, pre1, w, pre, x3, table, pay, misc_out):
    here = Here(g, lens)
    c = g.cm
    valid, own = row_masks(g, here, c)
    one, two, rest = total_of(g, got)
    misc = rest[:, :128]
    count = MEL * pick(misc, 0) / g.nch
    pairs = (MEL // 2) * pick(misc, 1) / g.nch
    at = [2 * c + 128 * (1 + i) for i in range(4)]
    vectors = [
        jnp.concatenate([got[zz, :, i : i + g.co] for zz in range(g.nch)], axis=1) for i in at
    ]
    mean = one / count
    inverse = lax.rsqrt(two / count - mean * mean + 1e-05)
    wide = jnp.zeros((1, c), F32)
    table[...] = jnp.concatenate(
        [mean, inverse, *vectors, wide + count, wide + pairs, wide + pick(misc, 2)]
        + [wide] * (TABLE - 9),
        axis=0,
    )
    scale, shift = half_affine(mean, inverse, vectors[0], vectors[1])


    def activate(m, square):
        half = pre1[m] * scale + shift
        act = half * (1.0 + jnp.tanh(half)) * valid
        low = act.astype(BF)
        before, after = shifted(low.astype(F32))
        side_by_side(x3, m, low, c, before, after)
        return square + sum_rows(act * act * own)

    square = jnp.zeros((1, c), F32)
    for m in range(MEL):
        square = activate(m, square)
    one, two = convolve_sums(g, here, x3, w, pre, True)
    pay[...] = payload(one, two)
    misc_out[...] = misc_row(jnp.sum(square, axis=1, keepdims=True))


def second(g, lens, got, pre1, w):
    body = functools.partial(second_kernel, g)
    out = [
        arr((MEL, g.win, g.cm), F32),
        arr((MEL, g.win, 3 * g.cm), BF),
        arr((TABLE, g.cm), F32),
        arr((1, 2 * g.cm), F32),
        arr((1, 128), F32),
    ]
    args = [lens, *keep_near(got, pre1, w)]
    flops = 2 * 9 * MEL * g.win * g.cm * g.cm
    ins = [SMEM, VMEM, VMEM, VMEM]
    return call(body, out, ins, args, [], 10, flops, 17 * MIB, "second_conv")


def pool_kernel(g, lens, got, old_ref, pre2, *rest):
    n, c = g.nch, g.cm
    cs, outs = rest[:n], rest[n : 2 * n]
    local_ref, table, pay, misc_out, held, grads, total, flat = rest[2 * n :]
    here = Here(g, lens)
    for k in range(n):
        held[pl.ds(aligned((here.z ^ k) * g.co), g.co), :] = cs[k][...]
    r = lax.broadcasted_iota(jnp.int32, (256, 128), 0)
    l = lax.broadcasted_iota(jnp.int32, (256, 128), 1)
    spread = (l == (r % 64) // 2 * 4 + r // 64).astype(BF)

    @pl.loop(0, g.cwin // 64)
    def _(j):
        cells = held[:, pl.ds(aligned(128 * j, 128), 128)]
        block = dot(spread, cells, ((1,), (1,)))
        grads[:, pl.ds(aligned(64 * j), 64), :] = block.reshape(MEL // 2, 64, c)

    one, two, _ = total_of(g, got)
    old = old_ref[...]
    count = old[COUNT : COUNT + 1]
    mean = one / count
    inverse = lax.rsqrt(two / count - mean * mean + 1e-05)
    wide = jnp.zeros((1, c), F32)
    table[...] = jnp.concatenate([old[:MEAN2], mean, inverse] + [wide] * (TABLE - 11), axis=0)
    half_gamma, half_beta = 0.5 * old[GAMMA2 : GAMMA2 + 1], 0.5 * old[BETA2 : BETA2 + 1]
    less = -mean * inverse
    side = g.win - g.seg
    segment = pl.ds(aligned(here.off), g.seg)
    sides = [
        aligned(jnp.where(16 * j < here.off, 16 * j, 16 * j + g.seg)) for j in range(side // 16)
    ]

    def weights(rows, start, width):
        frame = lax.broadcasted_iota(jnp.int32, (rows, 128), 0) + (here.start + start)
        valid = (frame < here.length).astype(F32)
        share = jnp.where(here.length - frame // 2 * 2 >= 2, 0.25, 0.5)
        return widen(0.5 * share * valid, width), widen(valid, width)

    half_share, valid = weights(g.seg, here.off, c)
    side_shares = [weights(16, start, c)[0] for start in sides]
    out_row = lax.broadcasted_iota(jnp.int32, (g.seg, 2 * g.seg), 0)
    out_cell = lax.broadcasted_iota(jnp.int32, (g.seg, 2 * g.seg), 1)
    first_cell = out_row // 2 * 4
    frame = out_row + (here.start + here.off)
    out_share = jnp.where(here.length - frame // 2 * 2 >= 2, 0.25, 0.5)
    total[...] = jnp.zeros(total.shape, F32)

    def bent(pre):
        scaled = pre * inverse + less
        half = scaled * half_gamma + half_beta
        bend = jnp.tanh(half)
        twice = 1.0 + bend
        whole = half * twice
        return scaled, whole, twice + whole * (1.0 - bend)

    def step(k, sums):
        beta_sum, gamma_sum, square = sums
        given = grads[k, pl.ds(aligned(here.qoff + here.off), g.seg), :] * half_share
        pair = None
        for i in range(2):
            m = 2 * k + i
            scaled, whole, slope = bent(pre2[m, segment, :])
            act = whole * valid
            square = square + sum_rows(act * act)
            local = given * slope
            local_ref[m, segment, :] = local
            beta_sum = beta_sum + sum_rows(local)
            gamma_sum = gamma_sum + sum_rows(local * scaled)
            pair = act if pair is None else pair + act
            for start, side_share in zip(sides, side_shares, strict=True):
                rows = pl.ds(start, 16)
                _, _, slope = bent(pre2[m, rows, :])
                given_side = grads[k, pl.ds(aligned(here.qoff + start), 16), :] * side_share
                local_ref[m, rows, :] = given_side * slope
        gather = jnp.where(out_cell == first_cell + k, out_share, 0.0).astype(BF)
        total[...] += dot(pair.astype(BF), gather, ((0,), (0,)))
        return beta_sum, gamma_sum, square

    zero = jnp.zeros((1, c), F32)
    beta_sum, gamma_sum, square = lax.fori_loop(0, MEL // 2, step, (zero, zero, zero))
    pooled = total[...]
    flat[...] = pooled.astype(BF)
    for k in range(n):
        outs[k][...] = flat[pl.ds(aligned((here.z ^ k) * g.co), g.co), :]
    pooled_square = sum_rows(jnp.sum(pooled * pooled, axis=1, keepdims=True))
    pay[...] = jnp.broadcast_to(payload(beta_sum, gamma_sum)[None], pay.shape)
    misc_out[...] = misc_row(jnp.sum(square, axis=1, keepdims=True), pooled_square)


def pool(g, lens, got, table, pre2, cs):
    n = g.nch
    body = functools.partial(pool_kernel, g)
    out = [arr((g.co, 2 * g.seg), BF)] * n + [
        arr((MEL, g.win, g.cm), F32),
        arr((TABLE, g.cm), F32),
        arr((g.ndev, 1, 2 * g.cm), F32),
        arr((1, 128), F32),
    ]
    scratch = [
        pltpu.VMEM((g.cm, g.cwin * 2), BF),
        pltpu.VMEM((MEL // 2, g.cwin, g.cm), F32),
        pltpu.VMEM((g.cm, 2 * g.seg), F32),
        pltpu.VMEM((g.cm, 2 * g.seg), BF),
    ]
    args = [lens, *keep_near(got, table, pre2, *cs)]
    ins = [SMEM] + [VMEM] * (len(args) - 1)
    out = call(body, out, ins, args, scratch, 12, 4e9, 8 * MIB, "pool")
    return out[:n], *out[n:]


def terms_kernel(g, depth, norm, lens, got, table, pre, local, x3, after, *refs):
    grad, sums, roots, terms, give = refs
    here = Here(g, lens)
    c = g.cm
    valid, _ = row_masks(g, here, c)
    beta_sum, gamma_sum, rest = total_of(g, got)
    t = table[...]
    mean, inverse, gamma = (t[i : i + 1] for i in norm)
    count = t[COUNT : COUNT + 1]
    sums[...] = jnp.concatenate([beta_sum, gamma_sum] + [jnp.zeros((1, c), F32)] * 6, axis=0)
    if rest.shape[1]:
        second, third = rest[:, :128], rest[:, 128:]
        tops = misc_row(
            pick(t[SQ0 : SQ0 + 1, :128], 0), pick(second, 0), pick(third, 0), pick(third, 1)
        )
        lane = lax.broadcasted_iota(jnp.int32, (1, 128), 1)
        cells, pairs = count[:, :128], t[PAIRS : PAIRS + 1, :128]
        under = jnp.where(lane == 0, cells * g.ci_all, jnp.where(lane == 3, pairs * c, cells * c))
        roots[...] = jnp.broadcast_to(jnp.sqrt(tops / under), (8, 128))
    factor = gamma * inverse
    slope = factor * inverse * gamma_sum / count
    level = factor * beta_sum / count - mean * slope

    @pl.loop(0, MEL)
    def _(m):
        value = valid * (local[m] * factor - pre[m] * slope - level)
        grad[m] = value.astype(BF)

    segment = pl.ds(aligned(here.off), g.seg)

    @pl.loop(0, 3)
    def _(a):
        lanes_of = pl.ds(aligned(a * depth, 128), depth)
        for b in (1, 0, 2):
            low = max(0, 1 - b)
            high = min(MEL, MEL + 1 - b)
            rows = (high - low) * g.seg
            left = grad[low:high, segment, :].reshape(rows, c)
            right = x3[low + b - 1 : high + b - 1, segment, lanes_of].reshape(rows, depth)
            term = dot(left, right, ((0,), (0,))).astype(BF)
            for z in range(g.nch):
                for s in range(2):
                    for p in range(g.planes):
                        at = z * g.co + g.row_of(s, p)
                        terms[s, z, p, 3 * a + b] = term[at : at + g.rows]

    give[...] = terms[1 - here.core]


def terms_of(g, lens, got, table, pre, local, x3, after, depth, norm, name):
    body = functools.partial(terms_kernel, g, depth, norm)
    shape = (g.nch, g.planes, 9, g.rows, depth)
    out = [
        arr((MEL, g.win, g.cm), BF),
        arr((8, g.cm), F32),
        arr((8, 128), F32),
        arr((2, *shape), BF),
        arr(shape, BF),
    ]
    args = [lens, *keep_near(got, table, pre, local, x3), after]
    ins = [SMEM] + [VMEM] * 5 + [ANY]
    flops = 2 * 9 * MEL * g.win * g.cm * depth
    return call(body, out, ins, args, [], 10, flops, 15 * MIB, name)


def back_kernel(g, lens, table, grad, pre1, w, misc2, misc3, after, local1, pay, g3):
    here = Here(g, lens)
    c = g.cm
    valid, own = row_masks(g, here, c)
    t = table[...]

    def row(i):
        return t[i : i + 1]


    for m in range(MEL):
        low = grad[m]
        before, after = shifted(low.astype(F32))
        side_by_side(g3, m, low, c, after, before)

    inverse, less = row(INV1), -row(MEAN1) * row(INV1)
    half_gamma, half_beta = 0.5 * row(GAMMA1), 0.5 * row(BETA1)
    half_valid = 0.5 * valid

    def finish(m, given, sums):
        scaled = pre1[m] * inverse + less
        half = scaled * half_gamma + half_beta
        bend = jnp.tanh(half)
        twice = 1.0 + bend
        local = given * half_valid * (twice + half * twice * (1.0 - bend))
        local1[m] = local
        kept = local * own
        return sums[0] + sum_rows(kept), sums[1] + sum_rows(kept * scaled)

    zero = jnp.zeros((1, c), F32)
    beta_sum, gamma_sum = convolve(g3, w, local1, True, finish, (zero, zero), True)
    pay[...] = payload(beta_sum, gamma_sum, misc2[...], misc3[...])


def back(g, lens, table, grad, pre1, w, misc2, misc3, after):
    body = functools.partial(back_kernel, g)
    out = [arr((MEL, g.win, g.cm), F32), arr((1, 2 * g.cm + 2 * 128), F32)]
    scratch = [pltpu.VMEM((MEL, g.win, 3 * g.cm), BF)]
    args = [lens, *keep_near(table, grad, pre1, w, misc2, misc3), after]
    flops = 2 * 9 * MEL * g.win * g.cm * g.cm
    ins = [SMEM] + [VMEM] * 6 + [ANY]
    return call(body, out, ins, args, scratch, 14, flops, 20 * MIB, "second_back")


def release_kernel(*refs):
    pass


def release_far(gates, x):
    n = len(gates)
    return pl.pallas_call(
        release_kernel,
        out_shape=pltpu.HBM(x.shape, x.dtype),
        in_specs=[ANY] * (n + 1),
        out_specs=ANY,
        input_output_aliases={n: 0},
        compiler_params=pltpu.CompilerParams(vmem_limit_bytes=2 * MIB),
        name="release_far",
    )(*gates, in_hbm(x))


def release(gates, arrays):
    out = [arr(x.shape, x.dtype) for x in arrays]
    n = len(gates)
    ins = [ANY] * n + [VMEM] * len(arrays)
    aliases = {i + n: i for i in range(len(arrays))}
    args = [*gates, *keep_near(*arrays)]
    return call(release_kernel, out, ins, args, [], 2, 0, 1, "release", aliases)


def spectra_kernel(g, lens, grad, after, w, *rest):
    n, c = g.nch, g.cm
    outs, (g3, rows, flat, part) = rest[:n], rest[n:]
    here = Here(g, lens)

    @pl.loop(0, MEL)
    def _(m):
        low = grad[m]
        before, after_ = shifted(low.astype(F32))
        side_by_side(g3, m, low, c, after_, before)

    r = lax.broadcasted_iota(jnp.int32, (g.seg, 128), 0) + here.off + here.start
    valid = widen((r < here.length).astype(F32), g.ci_all)

    def finish(m, total, carry):
        rows[m] = (total * valid).astype(BF)
        return carry

    convolve(g3, w, part, True, finish, 0, False, pl.ds(aligned(here.off), g.seg))
    order = grid_order()

    for j in range(g.seg // 16):
        block = rows[:, 16 * j : 16 * (j + 1), :].reshape(MEL * 16, g.ci_all)
        flat[:, 128 * j : 128 * (j + 1)] = dot(block, order, ((0,), (0,))).astype(BF)

    for k in range(n):
        outs[k][...] = flat[pl.ds(aligned((here.z ^ k) * g.ci), g.ci), :]


def spectra_back(g, lens, grad, after, w):
    n = g.nch
    body = functools.partial(spectra_kernel, g)
    out = [arr((g.ci, g.seg * MEL), BF)] * n
    scratch = [
        pltpu.VMEM((MEL, g.win, 3 * g.cm), BF),
        pltpu.VMEM((MEL, g.seg, g.ci_all), BF),
        pltpu.VMEM((g.ci_all, g.seg * MEL), BF),
        pltpu.VMEM((MEL, g.seg, g.ci_all), F32),
    ]
    grad, w = keep_near(grad, w)
    args = [lens, grad, after, w]
    flops = 2 * 9 * MEL * g.win * g.cm * g.ci_all
    ins = [SMEM, VMEM, ANY, VMEM]
    return call(body, out, ins, args, scratch, 14, flops, 5 * MIB, "spectra_back")


def place_kernel(g, width, *rest):
    n = g.nch
    parts, out, done = rest[:n], rest[n], rest[n + 1]
    z = lax.axis_index("chan")
    done[...] = jnp.zeros(done.shape, F32)
    for k in range(n):
        source = z ^ k
        for zz in range(n):

            @pl.when(source == zz)
            def _():
                at = zz % g.segs * width
                out[zz // g.segs, :, at : at + width] = parts[k][...].astype(out.dtype)


def place(g, parts, dtype, name):
    channels, width = parts[0].shape
    return pl.pallas_call(
        functools.partial(place_kernel, g, width),
        out_shape=[
            jax.ShapeDtypeStruct((g.clips, channels, g.segs * width), dtype),
            jax.ShapeDtypeStruct((8, 128), F32),
        ],
        in_specs=[VMEM] * g.nch,
        out_specs=[VMEM] * 2,
        compiler_params=pltpu.CompilerParams(vmem_limit_bytes=8 * MIB),
        cost_estimate=TINY,
        name=name,
    )(*parts)


def core_sum_kernel(g, terms, got, after, stay, go):
    d, z = lax.axis_index("dp"), lax.axis_index("chan")
    core, plane = lax.rem(d, 2), lax.rem(d, g.pieces) // 2
    half = g.planes // 2
    for e in range(g.planes):
        at = plane ^ g.plane_of(core, e)
        for k in range(g.nch):
            source = z ^ g.zed_of(k)
            value = terms[core, source, at].astype(F32) + got[source, at].astype(F32)
            to = stay if e < half else go
            to[(e % half) * g.nch + k] = value.astype(BF)


def core_sum(g, terms, got, after, name):
    shape = (g.planes // 2 * g.nch, *got.shape[2:])
    return pl.pallas_call(
        functools.partial(core_sum_kernel, g),
        out_shape=[pltpu.VMEM(shape, BF)] * 2,
        in_specs=[VMEM, VMEM, ANY],
        out_specs=[VMEM] * 2,
        compiler_params=pltpu.CompilerParams(vmem_limit_bytes=16 * MIB),
        name=name,
    )(keep_near(terms)[0], got, after)


def quarter_kernel(g, terms, got, *outs):
    d, z = lax.axis_index("dp"), lax.axis_index("chan")
    core, plane = lax.rem(d, 2), lax.rem(d, g.pieces) // 2
    for e in range(g.planes):
        at = plane ^ g.plane_of(core, e)
        for k in range(g.nch):
            source = z ^ g.zed_of(k)
            value = terms[core, source, at].astype(F32) + got[source, at].astype(F32)
            outs[e][k] = value.astype(BF)


def quarters(g, terms, got, name):
    shape = (g.nch, *got.shape[2:])
    return pl.pallas_call(
        functools.partial(quarter_kernel, g),
        out_shape=[pltpu.VMEM(shape, BF)] * g.planes,
        in_specs=[VMEM, VMEM],
        out_specs=[VMEM] * g.planes,
        compiler_params=pltpu.CompilerParams(vmem_limit_bytes=16 * MIB),
        name=name,
    )(keep_near(terms)[0], got)


def add_kernel(n, halves, *rest):
    first = rest[0]
    outs = rest[len(rest) - halves :]
    count = first.shape[0] // halves
    for i in range(first.shape[0]):
        total = first[i].astype(F32)
        for r in rest[1:n]:
            total = total + r[i].astype(F32)
        outs[i // count][i % count] = total.astype(BF)


def add_up(parts, halves, gates, name):
    n = len(parts)
    shape = (parts[0].shape[0] // halves, *parts[0].shape[1:])
    return pl.pallas_call(
        functools.partial(add_kernel, n, halves),
        out_shape=[pltpu.VMEM(shape, BF)] * halves,
        in_specs=[VMEM] * n + [ANY] * len(gates),
        out_specs=[VMEM] * halves,
        compiler_params=pltpu.CompilerParams(vmem_limit_bytes=8 * MIB),
        name=name,
    )(*parts, *gates)


def halve_kernel(stay, got, *rest):
    n = stay.shape[0]
    outs = rest[-2:] if n > 1 else rest[-1:]
    for i in range(n):
        value = stay[i].astype(F32) + got[i].astype(F32)
        if n == 1:
            outs[0][...] = value.astype(BF)
        else:
            outs[i // (n // 2)][i % (n // 2)] = value.astype(BF)


def halve(stay, got, gates, name):
    n = stay.shape[0]
    if n == 1:
        out = [jax.ShapeDtypeStruct(stay.shape[1:], BF)]
    else:
        out = [jax.ShapeDtypeStruct((n // 2, *stay.shape[1:]), BF)] * 2
    return pl.pallas_call(
        halve_kernel,
        out_shape=out,
        in_specs=[VMEM, VMEM] + [ANY] * len(gates),
        out_specs=[VMEM] * len(out),
        compiler_params=pltpu.CompilerParams(vmem_limit_bytes=8 * MIB),
        name=name,
    )(stay, got, *gates)


def spread_kernel(g, mine, other, out, done):
    done[...] = jnp.zeros(done.shape, F32)
    d = lax.axis_index("dp")
    core, plane = lax.rem(d, 2), lax.rem(d, g.pieces) // 2
    for side, part in enumerate((mine, other)):
        c = core if side == 0 else 1 - core
        for e in range(g.planes):
            at = aligned(g.row_of(c, plane ^ g.plane_of(c, e)))
            out[:, pl.ds(at, g.rows), :] = part[e].astype(F32)


def spread_out(g, mine, other, depth, name):
    return pl.pallas_call(
        functools.partial(spread_kernel, g),
        out_shape=[
            jax.ShapeDtypeStruct((9, g.co, depth), F32),
            jax.ShapeDtypeStruct((8, 128), F32),
        ],
        in_specs=[VMEM] * 2,
        out_specs=[VMEM] * 2,
        compiler_params=pltpu.CompilerParams(vmem_limit_bytes=12 * MIB),
        name=name,
    )(mine, other)


def stack_kernel(n, *refs):
    for k, r in enumerate(refs[:n]):
        refs[-1][k] = r[...]


def stack(parts, gates, name):
    n = len(parts)
    out = [arr((n, *parts[0].shape), parts[0].dtype)]
    ins = [VMEM] * n + [ANY] * len(gates)
    body = functools.partial(stack_kernel, n)
    return call(body, out, ins, [*parts, *gates], [], 6, 0, 1e6, name)[0]


class Links:
    def __init__(self, g):
        self.g = g

    def core(self, x):
        return lax.ppermute(x, "dp", [(i, i ^ 1) for i in range(self.g.ndp)])

    def dp(self, x, bit):
        return lax.ppermute(x, "dp", [(i, i ^ bit) for i in range(self.g.ndp)])

    def plane(self, x, turn):
        g = self.g
        return lax.ppermute(x, "dp", [(i, i ^ (2 * g.mask(i & 1, turn))) for i in range(g.ndp)])

    def chan(self, x, k):
        return lax.ppermute(x, "chan", [(i, i ^ k) for i in range(self.g.nch)])

    def exchange(self, parts):
        return [parts[0]] + [self.chan(parts[k], k) for k in range(1, self.g.nch)]

    def gather_planes(self, x, gates=()):
        have = [x]
        for turn in reversed(range(self.g.turns)):
            more = [self.plane(h, turn) for h in have[:1]]
            rest = have[1:]
            if gates and turn == 0 and rest:
                rest = release([*gates, *more], rest)
            have = have + more + [self.plane(h, turn) for h in rest]
        return have

    def gather_cores(self, have):
        return [*have, *[self.core(h) for h in have]]

    def gather_direct(self, x):
        g = self.g
        pairs = [[(i, i ^ (2 * g.plane_of(i & 1, e))) for i in range(g.ndp)] for e in range(g.planes)]
        return [x] + [lax.ppermute(x, "dp", p) for p in pairs[1:]]


def everyone(x):
    return lax.all_to_all(x, ("dp", "chan"), 0, 0)


def make_body(ndp, nch):
    def body(
        spectra, lengths, weight_in, gamma_in, beta_in, weight_mid, gamma_mid, beta_mid, cotangent
    ):
        g = Geometry(
            ndp,
            nch,
            spectra.shape[0],
            spectra.shape[2] // MEL,
            weight_in.shape[2],
            weight_mid.shape[2],
        )
        links = Links(g)
        gains = jnp.stack([gamma_in, beta_in, gamma_mid, beta_mid])
        gains = jnp.pad(gains, ((0, 0), (0, 128 - g.co)))

        piece = cut_weights(g, weight_in, weight_mid)
        cells = cut_maps(g, spectra, piece)
        cots = cut_cot(g, cotangent, cells)
        pieces_in, pieces_mid = sort_pieces(
            g, [links.chan(piece, k) for k in range(1, nch)], [cots[0]]
        )
        maps = lax.all_to_all(release_far([pieces_in], cells), "chan", 0, 0)
        planes_in = links.gather_planes(pieces_in)
        w_in = join(g, weight_in, links.gather_cores(planes_in), g.ci_all, "join_in")
        planes_mid = links.gather_planes(pieces_mid, [maps])

        pre1, x3_in, pay = first(g, lengths, gains, maps, w_in)
        got = everyone(fan(g, pay, cots[0], *planes_mid[1:-1]))
        planes_mid = release([got], planes_mid)
        w_mid = join(g, weight_mid, links.gather_cores(planes_mid), g.cm, "join_mid")
        cs = links.exchange(release([got], cots))
        pre2, x3_mid, table, pay, misc2 = second(g, lengths, got, pre1, w_mid)
        got = everyone(fan(g, pay, *cs[1:]))
        pooled, local2, table, pay, misc3 = pool(g, lengths, got, table, pre2, cs)
        got = everyone(pay)
        pooled = links.exchange(release([got], pooled))
        grad2, sums2, _, terms_mid, give_mid = terms_of(
            g, lengths, got, table, pre2, local2, x3_mid, got, g.cm, (MEAN2, INV2, GAMMA2), "weight_mid_terms"
        )
        got_mid = links.core(give_mid)
        split = g.turns == 2
        if split:
            stay_a, stay_b, go_a, go_b = quarters(g, terms_mid, got_mid, "mid_core_sum")
            got_b = links.plane(go_b, 0)
        else:
            stay_mid, go_b = core_sum(g, terms_mid, got_mid, got_mid, "mid_core_sum")
            got_b = go_b
        local1, pay = back(g, lengths, table, grad2, pre1, w_mid, misc2, misc3, go_b)
        got = everyone(fan(g, pay, got_b, *pooled[1:]))
        block_out, pooled_done = place(g, pooled, BF, "place_pooled")
        if split:
            (go_1,) = add_up([stay_b, got_b], 1, [pay, *pooled[1:]], "mid_sum_b")
            got_1 = early = links.plane(go_1, 1)
            got_a = links.plane(release([got], [go_a])[0], 0)
        else:
            (go_mid,) = release([got], [go_b])
            early = got
        grad1, sums1, roots, terms_in, give_in = terms_of(
            g, lengths, got, table, pre1, local1, x3_in, early, g.ci_all, (MEAN1, INV1, GAMMA1), "weight_in_terms"
        )
        got_in = links.core(give_in)

        class Chain:
            def __init__(self, stay, go, depth, name):
                self.stay, self.go, self.depth, self.name = stay, go, depth, name
                self.turns = [functools.partial(links.plane, turn=t) for t in range(g.turns)]
                self.turns += [functools.partial(links.chan, k=1 << t) for t in range(g.zturns)]

            def turn(self, i, *gates):
                got = self.turns[i](self.go)
                done = halve(self.stay, got, gates, f"{self.name}_sum_{i}")
                self.stay, self.go = done if len(done) == 2 else (done[0], None)
                return self.stay

            def rest(self):
                bit = g.pieces
                while bit < ndp:
                    got = links.dp(self.stay, bit)
                    self.stay = halve(self.stay[None], got[None], [], self.name + "_rest")[0]
                    bit *= 2

            def out(self, planes, *gates):
                mine = stack(planes, gates, self.name + "_stack")
                return spread_out(g, mine, links.core(mine), self.depth, self.name + "_out")

        turns = g.turns + g.zturns
        parts = spectra_back(g, lengths, grad1, grad1, w_in)
        stay_in, go_in = core_sum(g, terms_in, got_in, parts[0], "in_core_sum")
        inner = Chain(stay_in, go_in, g.ci_all, "in")
        parts = links.exchange(parts)
        spectra_grad, spectra_done = place(g, parts, F32, "place_spectra")
        if split:
            halves = add_up([stay_a, got_a, got_1], 2, [stay_in], "mid_sum_1")
            mid = Chain(*halves, g.cm, "mid")
        else:
            mid = Chain(stay_mid, go_mid, g.cm, "mid")
            for i in range(g.turns):
                mid.turn(i, stay_in)
        gates = [parts[2 : nch - 1], [pooled_done]]
        at = mid.stay
        for i in range(g.turns):
            at = inner.turn(i, at, *(gates[i] if i < 2 else []))
            if i == 0:
                at = mid.turn(g.turns, at)
        for i in range(g.turns, turns):
            at = inner.turn(i, at, *(parts[nch - 1 :] if i == g.turns else []))
            if i + 1 < turns:
                at = mid.turn(i + 1, at)
        inner.rest()
        mid.rest()
        planes_in = links.gather_planes(inner.stay)
        weight_mid_grad, mid_done = mid.out(links.gather_direct(mid.stay), *planes_in[1:3], parts[1])
        weight_in_grad, _ = inner.out(planes_in, mid_done, spectra_done)
        z = lax.axis_index("chan")

        def share(sums, i):
            return lax.dynamic_slice_in_dim(sums[i], z * g.co, g.co)

        return (
            block_out,
            spectra_grad,
            weight_in_grad,
            share(sums1, 1),
            share(sums1, 0),
            weight_mid_grad,
            share(sums2, 1),
            share(sums2, 0),
            roots[0, :4],
        )

    return body


def solution(mesh):
    placed = (
        P("dp", "chan", None),
        P("dp"),
        P(None, "chan", None),
        P("chan"),
        P("chan"),
        P(None, "chan", None),
        P("chan"),
        P("chan"),
        P("dp", "chan", None),
    )
    return jax.shard_map(
        make_body(mesh.shape["dp"], mesh.shape["chan"]),
        mesh=mesh,
        in_specs=placed,
        out_specs=(
            P("dp", "chan", None),
            P("dp", "chan", None),
            P(None, "chan", None),
            P("chan"),
            P("chan"),
            P(None, "chan", None),
            P("chan"),
            P("chan"),
            P(),
        ),
        check_vma=False,
    )
```

```python
import functools

import jax
import jax.numpy as jnp
from jax import lax
from jax.experimental import pallas as pl
from jax.experimental.pallas import tpu as pltpu
from jax.sharding import PartitionSpec as P

MEL = 8
HALO = 16
BF = jnp.bfloat16
F32 = jnp.float32
MIB = 1024 * 1024
TINY = pl.CostEstimate(flops=1, bytes_accessed=1, transcendentals=0)

VMEM = pl.BlockSpec(memory_space=pltpu.VMEM)
SMEM = pl.BlockSpec(memory_space=pltpu.SMEM)
ANY = pl.BlockSpec(memory_space=pl.ANY)
HBM = pl.BlockSpec(memory_space=pltpu.HBM)


def bits_of(n):
    return n.bit_length() - 1


class Geometry:
    def __init__(self, ndp, nch, clips, frames, c_in, c_mid):
        self.ndp, self.nch, self.ndev = ndp, nch, ndp * nch
        self.clips, self.frames = clips, frames
        self.ci_all, self.cm = c_in, c_mid
        self.ci, self.co = c_in // nch, c_mid // nch
        self.segs = nch // clips
        self.seg = frames // self.segs
        self.win = self.seg + HALO * min(self.segs - 1, 2)
        starts = [min(max(s * self.seg - HALO, 0), frames - self.win) for s in range(self.segs)]
        self.cwin = min(frames, (self.win + 48 + 63) // 64 * 64)
        assert all(min(s // 64 * 64, frames - self.cwin) + self.cwin >= s + self.win for s in starts)
        self.rows = max(16, self.co // ndp)
        self.pieces = self.co // self.rows
        self.planes = self.pieces // 2
        self.turns = bits_of(self.planes)
        self.zturns = bits_of(nch)

    def mask(self, core, turn):
        low, high = 1 << turn, 1 << (self.turns - 1 - turn)
        return low + core * (high - low)

    def plane_of(self, core, e):
        rel = 0
        for t in range(self.turns):
            if (e >> (self.turns - 1 - t)) & 1:
                rel = rel ^ self.mask(core, t)
        return rel

    def row_of(self, core, plane):
        return core * (self.co // 2) + plane * self.rows

    def zed_of(self, e):
        return sum(1 << t for t in range(self.zturns) if (e >> (self.zturns - 1 - t)) & 1)


class Here:
    def __init__(self, g, lens):
        self.z = lax.axis_index("chan")
        self.d = lax.axis_index("dp")
        self.core = lax.rem(self.d, 2)
        self.plane = lax.rem(self.d, g.pieces) // 2
        clip, seg = self.z // g.segs, lax.rem(self.z, g.segs)
        self.length = lens[clip]
        self.start, self.cstart = g_starts(g, seg)
        self.off = seg * g.seg - self.start
        self.qoff = self.start - self.cstart


def g_starts(g, seg):
    start = jnp.clip(seg * g.seg - HALO, 0, g.frames - g.win)
    return start, jnp.minimum(start // 64 * 64, g.frames - g.cwin)


def aligned(x, n=16):
    return pl.multiple_of(x, n)


def dot(a, b, contract):
    return lax.dot_general(a, b, ((contract[0], contract[1]), ((), ())), preferred_element_type=F32)


def call(body, out, ins, args, scratch, limit, flops, nbytes, name, aliases=None):
    return pl.pallas_call(
        body,
        out_shape=[pltpu.VMEM(o.shape, o.dtype) if isinstance(o, jax.ShapeDtypeStruct) else o for o in out],
        in_specs=ins,
        out_specs=[VMEM if isinstance(o, jax.ShapeDtypeStruct) else ANY for o in out],
        scratch_shapes=scratch,
        input_output_aliases=aliases or {},
        compiler_params=pltpu.CompilerParams(vmem_limit_bytes=limit * MIB),
        cost_estimate=pl.CostEstimate(
            flops=int(flops), bytes_accessed=int(nbytes), transcendentals=0
        ),
        name=name,
    )(*args)


def arr(shape, dtype):
    return jax.ShapeDtypeStruct(shape, dtype)


def keep_near(*xs):
    return [pltpu.with_memory_space_constraint(x, pltpu.VMEM) for x in xs]


class Copies:
    def __init__(self, sems):
        self.sems, self.n, self.open = sems, 0, []

    def start(self, src, dst):
        c = pltpu.make_async_copy(src, dst, self.sems.at[self.n])
        self.n += 1
        c.start()
        self.open.append(c)
        return c

    def wait(self, c):
        self.open = [o for o in self.open if o is not c]
        c.wait()

    def wait_all(self, some=None):
        for c in list(self.open if some is None else some):
            self.wait(c)


def sems(n):
    return pltpu.SemaphoreType.DMA((n,))


def row_masks(g, here, width):
    r = lax.broadcasted_iota(jnp.int32, (g.win, 128), 0)
    valid = (r + here.start) < here.length
    own = valid & (r >= here.off) & (r < here.off + g.seg)
    return widen(valid.astype(F32), width), widen(own.astype(F32), width)


def widen(x, width):
    return jnp.concatenate([x] * (width // 128), axis=1)


def shifted(x):
    n = x.shape[0]
    r = lax.broadcasted_iota(jnp.int32, (8, 1), 0)
    before, after = pltpu.roll(x, 1, 0), pltpu.roll(x, n - 1, 0)
    before = jnp.concatenate([jnp.where(r == 0, 0.0, before[:8]), before[8:]], axis=0)
    after = jnp.concatenate([after[:-8], jnp.where(r == 7, 0.0, after[-8:])], axis=0)
    return before, after


def grid_order(rows=16):
    n = MEL * rows
    r = lax.broadcasted_iota(jnp.int32, (n, n), 0)
    c = lax.broadcasted_iota(jnp.int32, (n, n), 1)
    return (c == (r % rows) * MEL + r // rows).astype(BF)


def misc_row(*scalars):
    lane = lax.broadcasted_iota(jnp.int32, (1, 128), 1)
    row = jnp.zeros((1, 128), F32)
    for i, s in enumerate(scalars):
        row = jnp.where(lane == i, s, row)
    return row


def pick(row, i):
    lane = lax.broadcasted_iota(jnp.int32, (1, 128), 1)
    return jnp.sum(jnp.where(lane == i, row, 0.0), axis=1, keepdims=True)


def sum_rows(x):
    return jnp.sum(x, axis=0, keepdims=True)


def payload(*parts):
    return jnp.concatenate(parts, axis=1)


def fan_kernel(pay, *rest):
    out = rest[-1]
    out[...] = jnp.broadcast_to(pay[...][None], out.shape)


def fan(g, pay, *after):
    out = [arr((g.ndev, *pay.shape), F32)]
    ins = [VMEM] + [ANY] * len(after)
    return call(fan_kernel, out, ins, [pay, *after], [], 4, 0, 1e5, "fan")[0]


def total_of(g, ref):
    row = jnp.sum(ref[...], axis=0)
    return row[:, : g.cm], row[:, g.cm : 2 * g.cm], row[:, 2 * g.cm :]


def side_by_side(x3, m, low, c, first, last):
    x3[m, :, 0:c] = first.astype(BF)
    x3[m, :, c : 2 * c] = low
    x3[m, :, 2 * c : 3 * c] = last.astype(BF)


def cut_weights_kernel(g, w_in, w_mid, out, sem):
    d = lax.axis_index("dp")
    core, plane = lax.rem(d, 2), lax.rem(d, g.pieces) // 2
    rows = pl.ds(aligned(g.row_of(core, plane)), g.rows)
    copies = Copies(sem)
    copies.start(w_in.at[:, rows, :], out.at[:, :, : g.ci_all])
    copies.start(w_mid.at[:, rows, :], out.at[:, :, g.ci_all :])
    copies.wait_all()


def cut_weights(g, w_in, w_mid):
    out = [arr((9, g.rows, g.ci_all + g.cm), BF)]
    args = [in_hbm(w_in), in_hbm(w_mid)]
    body = functools.partial(cut_weights_kernel, g)
    return call(body, out, [ANY] * 2, args, [sems(2)], 4, 0, 4e5, "cut_weights")[0]


def sort_kernel(g, *rest):
    n = g.nch - 1
    parts, first, second = rest[:n], rest[-2], rest[-1]
    for k in range(n):
        first[k] = parts[k][:, :, : g.ci_all]
        second[k] = parts[k][:, :, g.ci_all :]


def sort_pieces(g, parts, gates):
    n = g.nch - 1
    out = [arr((n, 9, g.rows, g.ci_all), BF), arr((n, 9, g.rows, g.cm), BF)]
    body = functools.partial(sort_kernel, g)
    ins = [VMEM] * n + [ANY] * len(gates)
    return call(body, out, ins, [*parts, *gates], [], 4, 0, 1e6, "sort_pieces")


def cut_maps_kernel(g, spec, after, out, held, sem):
    copies = Copies(sem)
    first = []
    for z in range(g.nch):
        start = static_start(g, z % g.segs) * MEL
        first.append(copies.start(spec.at[z // g.segs, :, start : start + g.win * MEL], held.at[z]))
    for z in range(g.nch):
        copies.wait(first[z])
        copies.start(held.at[z], out.at[z])
    copies.wait_all()


def cut_maps(g, spec, after):
    shape = (g.nch, g.ci, g.win * MEL)
    body = functools.partial(cut_maps_kernel, g)
    args = [in_hbm(spec), after]
    scratch = [pltpu.VMEM(shape, BF), sems(2 * g.nch)]
    return call(body, [pltpu.HBM(shape, BF)], [ANY] * 2, args, scratch, 4, 0, 2e6, "cut_maps")[0]


def static_start(g, seg):
    return min(max(seg * g.seg - HALO, 0), g.frames - g.win)


def cut_cot_kernel(g, cot, after, *rest):
    n = g.nch
    cs, sem = rest[:n], rest[n]
    z = lax.axis_index("chan")
    copies = Copies(sem)
    for k in range(n):
        to = z ^ k
        clip, seg = to // g.segs, lax.rem(to, g.segs)
        _, cstart = g_starts(g, seg)
        copies.start(cot.at[clip, :, pl.ds(aligned(cstart * 2, 128), g.cwin * 2)], cs[k])
    copies.wait_all()


def cut_cot(g, cot, after):
    n = g.nch
    out = [arr((g.co, g.cwin * 2), BF)] * n
    body = functools.partial(cut_cot_kernel, g)
    return call(body, out, [ANY] * 2, [in_hbm(cot), after], [sems(n)], 4, 0, 1e6, "cut_cotangent")


def in_hbm(x):
    return pltpu.with_memory_space_constraint(x, pltpu.HBM)


def join_kernel(g, own, *rest):
    parts, w = rest[:-1], rest[-1]
    z, d = lax.axis_index("chan"), lax.axis_index("dp")
    mine, plane = lax.rem(d, 2), lax.rem(d, g.pieces) // 2
    w[:, pl.ds(aligned(z * g.co), g.co), :] = own[...]
    for side in range(2):
        core = mine if side == 0 else 1 - mine
        for e in range(g.planes):
            row = g.row_of(core, plane ^ g.plane_of(core, e))
            for k in range(1, g.nch):
                at = aligned((z ^ k) * g.co + row)
                w[:, pl.ds(at, g.rows), :] = parts[side * g.planes + e][k - 1]


def join(g, own, parts, depth, name):
    body = functools.partial(join_kernel, g)
    args = [*keep_near(own), *parts]
    ins = [VMEM] * len(args)
    return call(body, [arr((9, g.cm, depth), BF)], ins, args, [], 8, 0, 4 * MIB, name)[0]


def convolve(v3, w, part, back, finish, carry, unrolled=False, window=None):
    def taps(t):
        b = 2 - t if back else t
        return jnp.concatenate([w[b], w[3 + b], w[6 + b]], axis=0 if back else 1)

    contract = ((1,), (0,)) if back else ((1,), (1,))
    depth = v3.shape[2]

    size = part.shape[1]
    window = pl.ds(0, size) if window is None else window

    def times(first, n, t):
        return dot(v3[pl.ds(first, n), window, :].reshape(n * size, depth), taps(t), contract)

    def rows_of(term, n):
        return [term[k * size : (k + 1) * size] for k in range(n)]

    if unrolled:
        for i in range(2):
            total = rows_of(times(4 * i, 4, 1), 4)
            side = rows_of(times(1 + 2 * i, 4, 2 - 2 * i), 4)
            edge = rows_of(times(5 * i, 3, 2 * i), 3)
            for k in range(4):
                value = total[k] + side[k]
                if 0 <= k + i - 1 < 3:
                    value = value + edge[k + i - 1]
                carry = finish(4 * i + k, value, carry)
        return carry

    def step(i, carry):
        part[pl.ds(3 * i + 1, 3)] = times(5 * i, 3, 2 * i).reshape(3, size, part.shape[2])
        part[7 * i] = jnp.zeros(part.shape[1:], F32)
        total = times(4 * i, 4, 1) + times(1 + 2 * i, 4, 2 - 2 * i)
        for k in range(4):
            m = 4 * i + k
            carry = finish(m, part[m] + total[k * size : (k + 1) * size], carry)
        return carry

    return lax.fori_loop(0, 2, step, carry)


def convolve_sums(g, here, x3, w, pre, unrolled):
    _, own = row_masks(g, here, g.cm)

    def finish(m, total, sums):
        pre[m] = total
        kept = total * own
        return sums[0] + sum_rows(kept), sums[1] + sum_rows(kept * total)

    zero = jnp.zeros((1, g.cm), F32)
    return convolve(x3, w, pre, False, finish, (zero, zero), unrolled)


def first_kernel(g, lens, gains, w, maps, pre, x3, pay):
    here = Here(g, lens)
    c = g.ci_all
    order = grid_order()
    row = lax.broadcasted_iota(jnp.int32, (MEL * 16, 128), 0) % 16

    def place_cells(j, square):
        cells = maps[:, :, 128 * j : 128 * (j + 1)].reshape(c, 128)
        frame = row + 16 * j
        valid = (frame + here.start) < here.length
        own = (frame >= here.off) & (frame < here.off + g.seg)
        block = dot(order, cells, ((1,), (1,))) * widen(valid.astype(F32), c)
        x3[:, 16 * j : 16 * (j + 1), c : 2 * c] = block.astype(BF).reshape(MEL, 16, c)
        return square + sum_rows(block * block * widen(own.astype(F32), c))

    square = jnp.zeros((1, c), F32)
    for j in range(g.win // 16):
        square = place_cells(j, square)
    for m in range(MEL):
        before, after_ = shifted(x3[m, :, c : 2 * c].astype(F32))
        x3[m, :, 0:c] = before.astype(BF)
        x3[m, :, 2 * c : 3 * c] = after_.astype(BF)

    one, two = convolve_sums(g, here, x3, w, pre, True)
    frame_total = 0
    pair_total = 0
    for i in range(g.clips):
        frame_total = frame_total + lens[i]
        pair_total = pair_total + (lens[i] + 1) // 2
    row = misc_row(
        frame_total.astype(F32), pair_total.astype(F32), jnp.sum(square, axis=1, keepdims=True)
    )
    pay[...] = payload(one, two, row, *[gains[i : i + 1] for i in range(4)])


def first(g, lens, gains, maps, w):
    body = functools.partial(first_kernel, g)
    out = [
        arr((MEL, g.win, g.cm), F32),
        arr((MEL, g.win, 3 * g.ci_all), BF),
        arr((1, 2 * g.cm + 5 * 128), F32),
    ]
    args = [lens, gains, *keep_near(w, maps)]
    ins = [SMEM] + [VMEM] * 3
    flops = 2 * 9 * MEL * g.win * g.ci_all * g.cm
    return call(body, out, ins, args, [], 10, flops, 10 * MIB, "first_conv")


MEAN1, INV1, GAMMA1, BETA1, GAMMA2, BETA2, COUNT, PAIRS, SQ0, MEAN2, INV2 = range(11)
TABLE = 16


def half_affine(mean, inverse, gamma, beta):
    scale = 0.5 * gamma * inverse
    return scale, 0.5 * beta - mean * scale


def second_kernel(g, lens, got, pre1, w, pre, x3, table, pay, misc_out):
    here = Here(g, lens)
    c = g.cm
    valid, own = row_masks(g, here, c)
    one, two, rest = total_of(g, got)
    misc = rest[:, :128]
    count = MEL * pick(misc, 0) / g.nch
    pairs = (MEL // 2) * pick(misc, 1) / g.nch
    at = [2 * c + 128 * (1 + i) for i in range(4)]
    vectors = [
        jnp.concatenate([got[zz, :, i : i + g.co] for zz in range(g.nch)], axis=1) for i in at
    ]
    mean = one / count
    inverse = lax.rsqrt(two / count - mean * mean + 1e-05)
    wide = jnp.zeros((1, c), F32)
    table[...] = jnp.concatenate(
        [mean, inverse, *vectors, wide + count, wide + pairs, wide + pick(misc, 2)]
        + [wide] * (TABLE - 9),
        axis=0,
    )
    scale, shift = half_affine(mean, inverse, vectors[0], vectors[1])


    def activate(m, square):
        half = pre1[m] * scale + shift
        act = half * (1.0 + jnp.tanh(half)) * valid
        low = act.astype(BF)
        before, after = shifted(low.astype(F32))
        side_by_side(x3, m, low, c, before, after)
        return square + sum_rows(act * act * own)

    square = jnp.zeros((1, c), F32)
    for m in range(MEL):
        square = activate(m, square)
    one, two = convolve_sums(g, here, x3, w, pre, True)
    pay[...] = payload(one, two)
    misc_out[...] = misc_row(jnp.sum(square, axis=1, keepdims=True))


def second(g, lens, got, pre1, w):
    body = functools.partial(second_kernel, g)
    out = [
        arr((MEL, g.win, g.cm), F32),
        arr((MEL, g.win, 3 * g.cm), BF),
        arr((TABLE, g.cm), F32),
        arr((1, 2 * g.cm), F32),
        arr((1, 128), F32),
    ]
    args = [lens, *keep_near(got, pre1, w)]
    flops = 2 * 9 * MEL * g.win * g.cm * g.cm
    ins = [SMEM, VMEM, VMEM, VMEM]
    return call(body, out, ins, args, [], 10, flops, 17 * MIB, "second_conv")


def pool_kernel(g, lens, got, old_ref, pre2, *rest):
    n, c = g.nch, g.cm
    cs, outs = rest[:n], rest[n : 2 * n]
    local_ref, table, pay, misc_out, held, grads, total, flat = rest[2 * n :]
    here = Here(g, lens)
    for k in range(n):
        held[pl.ds(aligned((here.z ^ k) * g.co), g.co), :] = cs[k][...]
    r = lax.broadcasted_iota(jnp.int32, (256, 128), 0)
    l = lax.broadcasted_iota(jnp.int32, (256, 128), 1)
    spread = (l == (r % 64) // 2 * 4 + r // 64).astype(BF)

    @pl.loop(0, g.cwin // 64)
    def _(j):
        cells = held[:, pl.ds(aligned(128 * j, 128), 128)]
        block = dot(spread, cells, ((1,), (1,)))
        grads[:, pl.ds(aligned(64 * j), 64), :] = block.reshape(MEL // 2, 64, c)

    one, two, _ = total_of(g, got)
    old = old_ref[...]
    count = old[COUNT : COUNT + 1]
    mean = one / count
    inverse = lax.rsqrt(two / count - mean * mean + 1e-05)
    wide = jnp.zeros((1, c), F32)
    table[...] = jnp.concatenate([old[:MEAN2], mean, inverse] + [wide] * (TABLE - 11), axis=0)
    half_gamma, half_beta = 0.5 * old[GAMMA2 : GAMMA2 + 1], 0.5 * old[BETA2 : BETA2 + 1]
    less = -mean * inverse
    side = g.win - g.seg
    segment = pl.ds(aligned(here.off), g.seg)
    sides = [
        aligned(jnp.where(16 * j < here.off, 16 * j, 16 * j + g.seg)) for j in range(side // 16)
    ]

    def weights(rows, start, width):
        frame = lax.broadcasted_iota(jnp.int32, (rows, 128), 0) + (here.start + start)
        valid = (frame < here.length).astype(F32)
        share = jnp.where(here.length - frame // 2 * 2 >= 2, 0.25, 0.5)
        return widen(0.5 * share * valid, width), widen(valid, width)

    half_share, valid = weights(g.seg, here.off, c)
    side_shares = [weights(16, start, c)[0] for start in sides]
    out_row = lax.broadcasted_iota(jnp.int32, (g.seg, 2 * g.seg), 0)
    out_cell = lax.broadcasted_iota(jnp.int32, (g.seg, 2 * g.seg), 1)
    first_cell = out_row // 2 * 4
    frame = out_row + (here.start + here.off)
    out_share = jnp.where(here.length - frame // 2 * 2 >= 2, 0.25, 0.5)
    total[...] = jnp.zeros(total.shape, F32)

    def bent(pre):
        scaled = pre * inverse + less
        half = scaled * half_gamma + half_beta
        bend = jnp.tanh(half)
        twice = 1.0 + bend
        whole = half * twice
        return scaled, whole, twice + whole * (1.0 - bend)

    def step(k, sums):
        beta_sum, gamma_sum, square = sums
        given = grads[k, pl.ds(aligned(here.qoff + here.off), g.seg), :] * half_share
        pair = None
        for i in range(2):
            m = 2 * k + i
            scaled, whole, slope = bent(pre2[m, segment, :])
            act = whole * valid
            square = square + sum_rows(act * act)
            local = given * slope
            local_ref[m, segment, :] = local
            beta_sum = beta_sum + sum_rows(local)
            gamma_sum = gamma_sum + sum_rows(local * scaled)
            pair = act if pair is None else pair + act
            for start, side_share in zip(sides, side_shares, strict=True):
                rows = pl.ds(start, 16)
                _, _, slope = bent(pre2[m, rows, :])
                given_side = grads[k, pl.ds(aligned(here.qoff + start), 16), :] * side_share
                local_ref[m, rows, :] = given_side * slope
        gather = jnp.where(out_cell == first_cell + k, out_share, 0.0).astype(BF)
        total[...] += dot(pair.astype(BF), gather, ((0,), (0,)))
        return beta_sum, gamma_sum, square

    zero = jnp.zeros((1, c), F32)
    beta_sum, gamma_sum, square = lax.fori_loop(0, MEL // 2, step, (zero, zero, zero))
    pooled = total[...]
    flat[...] = pooled.astype(BF)
    for k in range(n):
        outs[k][...] = flat[pl.ds(aligned((here.z ^ k) * g.co), g.co), :]
    pooled_square = sum_rows(jnp.sum(pooled * pooled, axis=1, keepdims=True))
    pay[...] = jnp.broadcast_to(payload(beta_sum, gamma_sum)[None], pay.shape)
    misc_out[...] = misc_row(jnp.sum(square, axis=1, keepdims=True), pooled_square)


def pool(g, lens, got, table, pre2, cs):
    n = g.nch
    body = functools.partial(pool_kernel, g)
    out = [arr((g.co, 2 * g.seg), BF)] * n + [
        arr((MEL, g.win, g.cm), F32),
        arr((TABLE, g.cm), F32),
        arr((g.ndev, 1, 2 * g.cm), F32),
        arr((1, 128), F32),
    ]
    scratch = [
        pltpu.VMEM((g.cm, g.cwin * 2), BF),
        pltpu.VMEM((MEL // 2, g.cwin, g.cm), F32),
        pltpu.VMEM((g.cm, 2 * g.seg), F32),
        pltpu.VMEM((g.cm, 2 * g.seg), BF),
    ]
    args = [lens, *keep_near(got, table, pre2, *cs)]
    ins = [SMEM] + [VMEM] * (len(args) - 1)
    out = call(body, out, ins, args, scratch, 12, 4e9, 8 * MIB, "pool")
    return out[:n], *out[n:]


def terms_kernel(g, depth, norm, lens, got, table, pre, local, x3, after, *refs):
    grad, sums, roots, terms, give = refs
    here = Here(g, lens)
    c = g.cm
    valid, _ = row_masks(g, here, c)
    beta_sum, gamma_sum, rest = total_of(g, got)
    t = table[...]
    mean, inverse, gamma = (t[i : i + 1] for i in norm)
    count = t[COUNT : COUNT + 1]
    sums[...] = jnp.concatenate([beta_sum, gamma_sum] + [jnp.zeros((1, c), F32)] * 6, axis=0)
    if rest.shape[1]:
        second, third = rest[:, :128], rest[:, 128:]
        tops = misc_row(
            pick(t[SQ0 : SQ0 + 1, :128], 0), pick(second, 0), pick(third, 0), pick(third, 1)
        )
        lane = lax.broadcasted_iota(jnp.int32, (1, 128), 1)
        cells, pairs = count[:, :128], t[PAIRS : PAIRS + 1, :128]
        under = jnp.where(lane == 0, cells * g.ci_all, jnp.where(lane == 3, pairs * c, cells * c))
        roots[...] = jnp.broadcast_to(jnp.sqrt(tops / under), (8, 128))
    factor = gamma * inverse
    slope = factor * inverse * gamma_sum / count
    level = factor * beta_sum / count - mean * slope

    @pl.loop(0, MEL)
    def _(m):
        value = valid * (local[m] * factor - pre[m] * slope - level)
        grad[m] = value.astype(BF)

    segment = pl.ds(aligned(here.off), g.seg)

    @pl.loop(0, 3)
    def _(a):
        lanes_of = pl.ds(aligned(a * depth, 128), depth)
        for b in (1, 0, 2):
            low = max(0, 1 - b)
            high = min(MEL, MEL + 1 - b)
            rows = (high - low) * g.seg
            left = grad[low:high, segment, :].reshape(rows, c)
            right = x3[low + b - 1 : high + b - 1, segment, lanes_of].reshape(rows, depth)
            term = dot(left, right, ((0,), (0,))).astype(BF)
            for z in range(g.nch):
                for s in range(2):
                    for p in range(g.planes):
                        at = z * g.co + g.row_of(s, p)
                        terms[s, z, p, 3 * a + b] = term[at : at + g.rows]

    give[...] = terms[1 - here.core]


def terms_of(g, lens, got, table, pre, local, x3, after, depth, norm, name):
    body = functools.partial(terms_kernel, g, depth, norm)
    shape = (g.nch, g.planes, 9, g.rows, depth)
    out = [
        arr((MEL, g.win, g.cm), BF),
        arr((8, g.cm), F32),
        arr((8, 128), F32),
        arr((2, *shape), BF),
        arr(shape, BF),
    ]
    args = [lens, *keep_near(got, table, pre, local, x3), after]
    ins = [SMEM] + [VMEM] * 5 + [ANY]
    flops = 2 * 9 * MEL * g.win * g.cm * depth
    return call(body, out, ins, args, [], 10, flops, 15 * MIB, name)


def back_kernel(g, lens, table, grad, pre1, w, misc2, misc3, after, local1, pay, g3):
    here = Here(g, lens)
    c = g.cm
    valid, own = row_masks(g, here, c)
    t = table[...]

    def row(i):
        return t[i : i + 1]


    for m in range(MEL):
        low = grad[m]
        before, after = shifted(low.astype(F32))
        side_by_side(g3, m, low, c, after, before)

    inverse, less = row(INV1), -row(MEAN1) * row(INV1)
    half_gamma, half_beta = 0.5 * row(GAMMA1), 0.5 * row(BETA1)
    half_valid = 0.5 * valid

    def finish(m, given, sums):
        scaled = pre1[m] * inverse + less
        half = scaled * half_gamma + half_beta
        bend = jnp.tanh(half)
        twice = 1.0 + bend
        local = given * half_valid * (twice + half * twice * (1.0 - bend))
        local1[m] = local
        kept = local * own
        return sums[0] + sum_rows(kept), sums[1] + sum_rows(kept * scaled)

    zero = jnp.zeros((1, c), F32)
    beta_sum, gamma_sum = convolve(g3, w, local1, True, finish, (zero, zero), True)
    pay[...] = payload(beta_sum, gamma_sum, misc2[...], misc3[...])


def back(g, lens, table, grad, pre1, w, misc2, misc3, after):
    body = functools.partial(back_kernel, g)
    out = [arr((MEL, g.win, g.cm), F32), arr((1, 2 * g.cm + 2 * 128), F32)]
    scratch = [pltpu.VMEM((MEL, g.win, 3 * g.cm), BF)]
    args = [lens, *keep_near(table, grad, pre1, w, misc2, misc3), after]
    flops = 2 * 9 * MEL * g.win * g.cm * g.cm
    ins = [SMEM] + [VMEM] * 6 + [ANY]
    return call(body, out, ins, args, scratch, 14, flops, 20 * MIB, "second_back")


def release_kernel(*refs):
    pass


def release_far(gates, x):
    n = len(gates)
    return pl.pallas_call(
        release_kernel,
        out_shape=pltpu.HBM(x.shape, x.dtype),
        in_specs=[ANY] * (n + 1),
        out_specs=ANY,
        input_output_aliases={n: 0},
        compiler_params=pltpu.CompilerParams(vmem_limit_bytes=2 * MIB),
        name="release_far",
    )(*gates, in_hbm(x))


def release(gates, arrays):
    out = [arr(x.shape, x.dtype) for x in arrays]
    n = len(gates)
    ins = [ANY] * n + [VMEM] * len(arrays)
    aliases = {i + n: i for i in range(len(arrays))}
    args = [*gates, *keep_near(*arrays)]
    return call(release_kernel, out, ins, args, [], 2, 0, 1, "release", aliases)


def spectra_kernel(g, lens, grad, after, w, *rest):
    n, c = g.nch, g.cm
    outs, (g3, rows, flat, part) = rest[:n], rest[n:]
    here = Here(g, lens)

    @pl.loop(0, MEL)
    def _(m):
        low = grad[m]
        before, after_ = shifted(low.astype(F32))
        side_by_side(g3, m, low, c, after_, before)

    r = lax.broadcasted_iota(jnp.int32, (g.seg, 128), 0) + here.off + here.start
    valid = widen((r < here.length).astype(F32), g.ci_all)

    def finish(m, total, carry):
        rows[m] = (total * valid).astype(BF)
        return carry

    convolve(g3, w, part, True, finish, 0, True, pl.ds(aligned(here.off), g.seg))
    order = grid_order()

    for j in range(g.seg // 16):
        block = rows[:, 16 * j : 16 * (j + 1), :].reshape(MEL * 16, g.ci_all)
        flat[:, 128 * j : 128 * (j + 1)] = dot(block, order, ((0,), (0,))).astype(BF)

    for k in range(n):
        outs[k][...] = flat[pl.ds(aligned((here.z ^ k) * g.ci), g.ci), :]


def spectra_back(g, lens, grad, after, w):
    n = g.nch
    body = functools.partial(spectra_kernel, g)
    out = [arr((g.ci, g.seg * MEL), BF)] * n
    scratch = [
        pltpu.VMEM((MEL, g.win, 3 * g.cm), BF),
        pltpu.VMEM((MEL, g.seg, g.ci_all), BF),
        pltpu.VMEM((g.ci_all, g.seg * MEL), BF),
        pltpu.VMEM((MEL, g.seg, g.ci_all), F32),
    ]
    grad, w = keep_near(grad, w)
    args = [lens, grad, after, w]
    flops = 2 * 9 * MEL * g.win * g.cm * g.ci_all
    ins = [SMEM, VMEM, ANY, VMEM]
    return call(body, out, ins, args, scratch, 14, flops, 5 * MIB, "spectra_back")


def place_kernel(g, width, *rest):
    n = g.nch
    parts, out, done = rest[:n], rest[n], rest[n + 1]
    z = lax.axis_index("chan")
    done[...] = jnp.zeros(done.shape, F32)
    for k in range(n):
        source = z ^ k
        for zz in range(n):

            @pl.when(source == zz)
            def _():
                at = zz % g.segs * width
                out[zz // g.segs, :, at : at + width] = parts[k][...].astype(out.dtype)


def place(g, parts, dtype, name):
    channels, width = parts[0].shape
    return pl.pallas_call(
        functools.partial(place_kernel, g, width),
        out_shape=[
            jax.ShapeDtypeStruct((g.clips, channels, g.segs * width), dtype),
            jax.ShapeDtypeStruct((8, 128), F32),
        ],
        in_specs=[VMEM] * g.nch,
        out_specs=[VMEM] * 2,
        compiler_params=pltpu.CompilerParams(vmem_limit_bytes=8 * MIB),
        cost_estimate=TINY,
        name=name,
    )(*parts)


def core_sum_kernel(g, terms, got, after, stay, go):
    d, z = lax.axis_index("dp"), lax.axis_index("chan")
    core, plane = lax.rem(d, 2), lax.rem(d, g.pieces) // 2
    half = g.planes // 2
    for e in range(g.planes):
        at = plane ^ g.plane_of(core, e)
        for k in range(g.nch):
            source = z ^ g.zed_of(k)
            value = terms[core, source, at].astype(F32) + got[source, at].astype(F32)
            to = stay if e < half else go
            to[(e % half) * g.nch + k] = value.astype(BF)


def core_sum(g, terms, got, after, name):
    shape = (g.planes // 2 * g.nch, *got.shape[2:])
    return pl.pallas_call(
        functools.partial(core_sum_kernel, g),
        out_shape=[pltpu.VMEM(shape, BF)] * 2,
        in_specs=[VMEM, VMEM, ANY],
        out_specs=[VMEM] * 2,
        compiler_params=pltpu.CompilerParams(vmem_limit_bytes=16 * MIB),
        name=name,
    )(keep_near(terms)[0], got, after)


def quarter_kernel(g, terms, got, *outs):
    d, z = lax.axis_index("dp"), lax.axis_index("chan")
    core, plane = lax.rem(d, 2), lax.rem(d, g.pieces) // 2
    for e in range(g.planes):
        at = plane ^ g.plane_of(core, e)
        for k in range(g.nch):
            source = z ^ g.zed_of(k)
            value = terms[core, source, at].astype(F32) + got[source, at].astype(F32)
            outs[e][k] = value.astype(BF)


def quarters(g, terms, got, name):
    shape = (g.nch, *got.shape[2:])
    return pl.pallas_call(
        functools.partial(quarter_kernel, g),
        out_shape=[pltpu.VMEM(shape, BF)] * g.planes,
        in_specs=[VMEM, VMEM],
        out_specs=[VMEM] * g.planes,
        compiler_params=pltpu.CompilerParams(vmem_limit_bytes=16 * MIB),
        name=name,
    )(keep_near(terms)[0], got)


def add_kernel(n, halves, *rest):
    first = rest[0]
    outs = rest[len(rest) - halves :]
    count = first.shape[0] // halves
    for i in range(first.shape[0]):
        total = first[i].astype(F32)
        for r in rest[1:n]:
            total = total + r[i].astype(F32)
        outs[i // count][i % count] = total.astype(BF)


def add_up(parts, halves, gates, name):
    n = len(parts)
    shape = (parts[0].shape[0] // halves, *parts[0].shape[1:])
    return pl.pallas_call(
        functools.partial(add_kernel, n, halves),
        out_shape=[pltpu.VMEM(shape, BF)] * halves,
        in_specs=[VMEM] * n + [ANY] * len(gates),
        out_specs=[VMEM] * halves,
        compiler_params=pltpu.CompilerParams(vmem_limit_bytes=8 * MIB),
        name=name,
    )(*parts, *gates)


def halve_kernel(stay, got, *rest):
    n = stay.shape[0]
    outs = rest[-2:] if n > 1 else rest[-1:]
    for i in range(n):
        value = stay[i].astype(F32) + got[i].astype(F32)
        if n == 1:
            outs[0][...] = value.astype(BF)
        else:
            outs[i // (n // 2)][i % (n // 2)] = value.astype(BF)


def halve(stay, got, gates, name):
    n = stay.shape[0]
    if n == 1:
        out = [jax.ShapeDtypeStruct(stay.shape[1:], BF)]
    else:
        out = [jax.ShapeDtypeStruct((n // 2, *stay.shape[1:]), BF)] * 2
    return pl.pallas_call(
        halve_kernel,
        out_shape=out,
        in_specs=[VMEM, VMEM] + [ANY] * len(gates),
        out_specs=[VMEM] * len(out),
        compiler_params=pltpu.CompilerParams(vmem_limit_bytes=8 * MIB),
        name=name,
    )(stay, got, *gates)


def spread_kernel(g, mine, other, out, done):
    done[...] = jnp.zeros(done.shape, F32)
    d = lax.axis_index("dp")
    core, plane = lax.rem(d, 2), lax.rem(d, g.pieces) // 2
    for side, part in enumerate((mine, other)):
        c = core if side == 0 else 1 - core
        for e in range(g.planes):
            at = aligned(g.row_of(c, plane ^ g.plane_of(c, e)))
            out[:, pl.ds(at, g.rows), :] = part[e].astype(F32)


def spread_out(g, mine, other, depth, name):
    return pl.pallas_call(
        functools.partial(spread_kernel, g),
        out_shape=[
            jax.ShapeDtypeStruct((9, g.co, depth), F32),
            jax.ShapeDtypeStruct((8, 128), F32),
        ],
        in_specs=[VMEM] * 2,
        out_specs=[VMEM] * 2,
        compiler_params=pltpu.CompilerParams(vmem_limit_bytes=12 * MIB),
        name=name,
    )(mine, other)


def stack_kernel(n, *refs):
    for k, r in enumerate(refs[:n]):
        refs[-1][k] = r[...]


def stack(parts, gates, name):
    n = len(parts)
    out = [arr((n, *parts[0].shape), parts[0].dtype)]
    ins = [VMEM] * n + [ANY] * len(gates)
    body = functools.partial(stack_kernel, n)
    return call(body, out, ins, [*parts, *gates], [], 6, 0, 1e6, name)[0]


class Links:
    def __init__(self, g):
        self.g = g

    def core(self, x):
        return lax.ppermute(x, "dp", [(i, i ^ 1) for i in range(self.g.ndp)])

    def dp(self, x, bit):
        return lax.ppermute(x, "dp", [(i, i ^ bit) for i in range(self.g.ndp)])

    def plane(self, x, turn):
        g = self.g
        return lax.ppermute(x, "dp", [(i, i ^ (2 * g.mask(i & 1, turn))) for i in range(g.ndp)])

    def chan(self, x, k):
        return lax.ppermute(x, "chan", [(i, i ^ k) for i in range(self.g.nch)])

    def exchange(self, parts):
        return [parts[0]] + [self.chan(parts[k], k) for k in range(1, self.g.nch)]

    def gather_planes(self, x, gates=()):
        have = [x]
        for turn in reversed(range(self.g.turns)):
            more = [self.plane(h, turn) for h in have[:1]]
            rest = have[1:]
            if gates and turn == 0 and rest:
                rest = release([*gates, *more], rest)
            have = have + more + [self.plane(h, turn) for h in rest]
        return have

    def gather_cores(self, have):
        return [*have, *[self.core(h) for h in have]]

    def gather_direct(self, x):
        g = self.g
        pairs = [[(i, i ^ (2 * g.plane_of(i & 1, e))) for i in range(g.ndp)] for e in range(g.planes)]
        return [x] + [lax.ppermute(x, "dp", p) for p in pairs[1:]]


def everyone(x):
    return lax.all_to_all(x, ("dp", "chan"), 0, 0)


def make_body(ndp, nch):
    def body(
        spectra, lengths, weight_in, gamma_in, beta_in, weight_mid, gamma_mid, beta_mid, cotangent
    ):
        g = Geometry(
            ndp,
            nch,
            spectra.shape[0],
            spectra.shape[2] // MEL,
            weight_in.shape[2],
            weight_mid.shape[2],
        )
        links = Links(g)
        gains = jnp.stack([gamma_in, beta_in, gamma_mid, beta_mid])
        gains = jnp.pad(gains, ((0, 0), (0, 128 - g.co)))

        piece = cut_weights(g, weight_in, weight_mid)
        cells = cut_maps(g, spectra, piece)
        cots = cut_cot(g, cotangent, cells)
        pieces_in, pieces_mid = sort_pieces(
            g, [links.chan(piece, k) for k in range(1, nch)], [cots[0]]
        )
        maps = lax.all_to_all(release_far([pieces_in], cells), "chan", 0, 0)
        planes_in = links.gather_planes(pieces_in)
        w_in = join(g, weight_in, links.gather_cores(planes_in), g.ci_all, "join_in")
        planes_mid = links.gather_planes(pieces_mid, [maps])

        pre1, x3_in, pay = first(g, lengths, gains, maps, w_in)
        got = everyone(fan(g, pay, cots[0], *planes_mid[1:-1]))
        planes_mid = release([got], planes_mid)
        w_mid = join(g, weight_mid, links.gather_cores(planes_mid), g.cm, "join_mid")
        cs = links.exchange(release([got], cots))
        pre2, x3_mid, table, pay, misc2 = second(g, lengths, got, pre1, w_mid)
        got = everyone(fan(g, pay, *cs[1:]))
        pooled, local2, table, pay, misc3 = pool(g, lengths, got, table, pre2, cs)
        got = everyone(pay)
        pooled = links.exchange(release([got], pooled))
        grad2, sums2, _, terms_mid, give_mid = terms_of(
            g, lengths, got, table, pre2, local2, x3_mid, got, g.cm, (MEAN2, INV2, GAMMA2), "weight_mid_terms"
        )
        got_mid = links.core(give_mid)
        split = g.turns == 2
        if split:
            stay_a, stay_b, go_a, go_b = quarters(g, terms_mid, got_mid, "mid_core_sum")
            got_b = links.plane(go_b, 0)
        else:
            stay_mid, go_b = core_sum(g, terms_mid, got_mid, got_mid, "mid_core_sum")
            got_b = go_b
        local1, pay = back(g, lengths, table, grad2, pre1, w_mid, misc2, misc3, go_b)
        got = everyone(fan(g, pay, got_b, *pooled[1:]))
        block_out, pooled_done = place(g, pooled, BF, "place_pooled")
        if split:
            (go_1,) = add_up([stay_b, got_b], 1, [pay, *pooled[1:]], "mid_sum_b")
            got_1 = early = links.plane(go_1, 1)
            got_a = links.plane(release([got], [go_a])[0], 0)
        else:
            (go_mid,) = release([got], [go_b])
            early = got
        grad1, sums1, roots, terms_in, give_in = terms_of(
            g, lengths, got, table, pre1, local1, x3_in, early, g.ci_all, (MEAN1, INV1, GAMMA1), "weight_in_terms"
        )
        got_in = links.core(give_in)

        class Chain:
            def __init__(self, stay, go, depth, name):
                self.stay, self.go, self.depth, self.name = stay, go, depth, name
                self.turns = [functools.partial(links.plane, turn=t) for t in range(g.turns)]
                self.turns += [functools.partial(links.chan, k=1 << t) for t in range(g.zturns)]

            def turn(self, i, *gates):
                got = self.turns[i](self.go)
                done = halve(self.stay, got, gates, f"{self.name}_sum_{i}")
                self.stay, self.go = done if len(done) == 2 else (done[0], None)
                return self.stay

            def rest(self):
                bit = g.pieces
                while bit < ndp:
                    got = links.dp(self.stay, bit)
                    self.stay = halve(self.stay[None], got[None], [], self.name + "_rest")[0]
                    bit *= 2

            def out(self, planes, *gates):
                mine = stack(planes, gates, self.name + "_stack")
                return spread_out(g, mine, links.core(mine), self.depth, self.name + "_out")

        turns = g.turns + g.zturns
        parts = spectra_back(g, lengths, grad1, grad1, w_in)
        stay_in, go_in = core_sum(g, terms_in, got_in, parts[0], "in_core_sum")
        inner = Chain(stay_in, go_in, g.ci_all, "in")
        parts = links.exchange(parts)
        spectra_grad, spectra_done = place(g, parts, F32, "place_spectra")
        if split:
            halves = add_up([stay_a, got_a, got_1], 2, [stay_in], "mid_sum_1")
            mid = Chain(*halves, g.cm, "mid")
        else:
            mid = Chain(stay_mid, go_mid, g.cm, "mid")
            for i in range(g.turns):
                mid.turn(i, stay_in)
        gates = [parts[2 : nch - 1], [pooled_done]]
        at = mid.stay
        for i in range(g.turns):
            at = inner.turn(i, at, *(gates[i] if i < 2 else []))
            if i == 0:
                at = mid.turn(g.turns, at)
        for i in range(g.turns, turns):
            at = inner.turn(i, at, *(parts[nch - 1 :] if i == g.turns else []))
            if i + 1 < turns:
                at = mid.turn(i + 1, at)
        inner.rest()
        mid.rest()
        planes_in = links.gather_planes(inner.stay)
        weight_mid_grad, mid_done = mid.out(links.gather_direct(mid.stay), *planes_in[1:3], parts[1])
        weight_in_grad, _ = inner.out(planes_in, mid_done, spectra_done)
        z = lax.axis_index("chan")

        def share(sums, i):
            return lax.dynamic_slice_in_dim(sums[i], z * g.co, g.co)

        return (
            block_out,
            spectra_grad,
            weight_in_grad,
            share(sums1, 1),
            share(sums1, 0),
            weight_mid_grad,
            share(sums2, 1),
            share(sums2, 0),
            roots[0, :4],
        )

    return body


def solution(mesh):
    placed = (
        P("dp", "chan", None),
        P("dp"),
        P(None, "chan", None),
        P("chan"),
        P("chan"),
        P(None, "chan", None),
        P("chan"),
        P("chan"),
        P("dp", "chan", None),
    )
    return jax.shard_map(
        make_body(mesh.shape["dp"], mesh.shape["chan"]),
        mesh=mesh,
        in_specs=placed,
        out_specs=(
            P("dp", "chan", None),
            P("dp", "chan", None),
            P(None, "chan", None),
            P("chan"),
            P("chan"),
            P(None, "chan", None),
            P("chan"),
            P("chan"),
            P(),
        ),
        check_vma=False,
    )
```
